32 devices in a mesh: dp: 16 (over z, y, x), mp: 2 (over core).
Axes of the slice: x: 2, y: 2, z: 4, core: 2. Of those that a mesh axis runs over, the one named last changes fastest.
Arguments:
- residual_in: bfloat16 [32768, 512], P(('dp', 'mp')), may hold values from -6 to 6
- memory: bfloat16 [32768, 512], P(('dp', 'mp')), may hold values from -6 to 6
- lengths: int32 [256], P('dp'), may hold values from 1 to 256, as said below
- targets: int32 [32768], P(('dp', 'mp')), may hold values from 0 to 522
- attn_in: float32 [2, 3, 512, 512], P(None, None, None, 'mp'), may hold values from -0.25 to 0.25
- attn_out: float32 [2, 512, 512], P(None, 'mp'), may hold values from -0.75 to 0.75
- ffn_in: float32 [512, 2048], P(None, 'mp'), may hold values from -0.25 to 0.25
- ffn_out: float32 [2048, 512], P('mp'), may hold values from -0.125 to 0.125
- vocab_head: float32 [512, 523], replicated, may hold values from -0.25 to 0.25
- norm_gain: float32 [4, 512], replicated, may hold values from 0.5 to 1.5
- norm_bias: float32 [4, 512], replicated, may hold values from -4 to 4
- attn_in_moment: float32 [2, 3, 512, 512], P(None, None, None, 'mp'), may hold values from -56 to 56
- attn_out_moment: float32 [2, 512, 512], P(None, 'mp'), may hold values from -56 to 56
- ffn_in_moment: float32 [512, 2048], P(None, 'mp'), may hold values from -56 to 56
- ffn_out_moment: float32 [2048, 512], P('mp'), may hold values from -56 to 56
- head_moment: float32 [512, 523], replicated, may hold values from -56 to 56
- norm_moment: float32 [2, 4, 512], replicated, may hold values from -56 to 56
Outputs:
- output: bfloat16 [32768, 512], P(('dp', 'mp'))
- input_grad: float32 [32768, 512], P(('dp', 'mp'))
- memory_grad: float32 [32768, 512], P(('dp', 'mp'))
- moment_attn_in: float32 [2, 3, 512, 512], P(None, None, None, 'mp')
- new_attn_in: float32 [2, 3, 512, 512], P(None, None, None, 'mp')
- moment_attn_out: float32 [2, 512, 512], P(None, 'mp')
- new_attn_out: float32 [2, 512, 512], P(None, 'mp')
- moment_ffn_in: float32 [512, 2048], P(None, 'mp')
- new_ffn_in: float32 [512, 2048], P(None, 'mp')
- moment_ffn_out: float32 [2048, 512], P('mp')
- new_ffn_out: float32 [2048, 512], P('mp')
- moment_head: float32 [512, 523], replicated
- new_head: float32 [512, 523], replicated
- moment_norms: float32 [2, 4, 512], replicated
- new_norms: float32 [2, 4, 512], replicated
- token_counts: int32 [523], replicated
The draws below stay inside these ranges and needn't reach their ends.
Inputs may be any that keep to these rules, and one draw needn't show every extreme that they name: `lengths`: in each group the first 8 slots hold 1 to 64 tokens, the next 4 1 to 128, the last 4 1 to 256; in every group each bucket has one full slot.
All inputs are finite; a program needn't handle non-finite values.
Results may differ from the reference program's by a relative error of at most 0.017.
Values may be sent and summed in bfloat16 or wider, within the bound.
A program may use at most 256 MiB of HBM per device.

```python
import math
import jax
import jax.numpy as jnp
from jax import lax

D = 512
HEADS = 8
HEAD = 64
FF = 2048
VOCAB = 523
CAP_S = 64
CAP_M = 128
CAP_L = 256
MEM = 128
SETS = 4
NS_STEPS = 5
SLOTS = 16
ROWS = 2048
MROWS = 2048
TOKENS = 32768
N_DP = 16


def draw_lengths(key, part):
    key = jax.random.fold_in(key, 17)
    first_key, second_key = jax.random.split(key)
    slot_caps = jnp.concatenate([jnp.full((2 * SETS,), CAP_S, jnp.int32), jnp.full((SETS,), CAP_M, jnp.int32), jnp.full((SETS,), CAP_L, jnp.int32)])
    bucket_ids = jnp.concatenate([jnp.zeros((2 * SETS,), jnp.int32), jnp.ones((SETS,), jnp.int32), jnp.full((SETS,), 2, jnp.int32)])
    starts = jnp.concatenate([jnp.zeros((2 * SETS,), jnp.int32), jnp.full((SETS,), 2 * SETS, jnp.int32), jnp.full((SETS,), 3 * SETS, jnp.int32)])
    within = jnp.arange(4 * SETS, dtype=jnp.int32) - starts
    drawn_lengths = jax.random.randint(first_key, (N_DP, 4 * SETS), 1, slot_caps[None, :] + 1)
    bucket_sizes = jnp.array([2 * SETS, SETS, SETS], jnp.int32)
    chosen = jax.random.randint(second_key, (N_DP, 3), 0, bucket_sizes[None, :])
    full_slot = jnp.take(chosen, bucket_ids, axis=1) == within[None, :]
    return jnp.where(full_slot, slot_caps[None, :], drawn_lengths).reshape(-1)


def touch_ends(drawn, key, smallest, largest):
    longest = drawn.shape.index(max(drawn.shape))
    spots = []
    for shift in (0, 1):
        where = [jax.random.randint(jax.random.fold_in(key, axis), (), 0, length) for axis, length in enumerate(drawn.shape)]
        where[longest] = (where[longest] + shift) % drawn.shape[longest]
        spots.append(tuple(where))
    return drawn.at[spots[0]].set(smallest).at[spots[1]].set(largest)


def levels(rng, dims, cuts, smallest, high):
    level = 1.0
    for dim, parts in cuts:
        draws = jax.random.uniform(jax.random.fold_in(jax.random.fold_in(rng, 6), dim), (parts,), jnp.float32, smallest / len(cuts), high / len(cuts))
        level = level * jnp.repeat(jnp.exp(draws), dims[dim] // parts).reshape((-1,) + (1,) * (len(dims) - 1 - dim))
    return level


def scatter_about(rng, shape, deviation, limit, shards=(), kind=jnp.bfloat16):
    values = jax.random.normal(rng, shape, jnp.float32) * deviation
    if len(shards) > 0:
        values = levels(rng, shape, shards, -0.22, 0.18) * values
    return jnp.clip(values, min=-limit, max=limit).astype(kind)


def setup_inputs(seed: int = 0) -> dict:
    keys = jax.random.split(jax.random.key(seed), 18)
    return {
        "residual_in": scatter_about(keys[0], (TOKENS, D), 1.0, 6.0, ((0, 32),)),
        "memory": scatter_about(keys[1], (N_DP * MROWS, D), 1.0, 6.0, ((0, 32),)),
        "lengths": draw_lengths(jax.random.fold_in(keys[17], 71), 0),
        "targets": touch_ends(jax.random.randint(keys[3], (TOKENS,), 0, VOCAB), jax.random.fold_in(keys[3], 1), 0, VOCAB - 1).astype(jnp.int32),
        "attn_in": scatter_about(keys[4], (2, 3, D, D), D ** -0.5, 0.25, ((3, 2),), jnp.float32),
        "attn_out": scatter_about(keys[5], (2, D, D), (D // 8) ** -0.5, 0.75, ((1, 2),), jnp.float32),
        "ffn_in": scatter_about(keys[6], (D, FF), D ** -0.5, 0.25, ((1, 2),), jnp.float32),
        "ffn_out": scatter_about(keys[7], (FF, D), FF ** -0.5, 0.125, ((0, 2),), jnp.float32),
        "vocab_head": scatter_about(keys[8], (D, VOCAB), D ** -0.5, 0.25, (), jnp.float32),
        "norm_gain": jnp.clip(1.0 + 0.1 * jax.random.normal(keys[9], (4, D), jnp.float32), 0.5, 1.5),
        "norm_bias": scatter_about(keys[10], (4, D), 0.3, 4.0, (), jnp.float32),
        "attn_in_moment": scatter_about(keys[11], (2, 3, D, D), (0.05 * TOKENS ** 0.5), 56.0, ((3, 2),), jnp.float32),
        "attn_out_moment": scatter_about(keys[12], (2, D, D), (0.05 * TOKENS ** 0.5), 56.0, ((1, 2),), jnp.float32),
        "ffn_in_moment": scatter_about(keys[13], (D, FF), (0.05 * TOKENS ** 0.5), 56.0, ((1, 2),), jnp.float32),
        "ffn_out_moment": scatter_about(keys[14], (FF, D), (0.05 * TOKENS ** 0.5), 56.0, ((0, 2),), jnp.float32),
        "head_moment": scatter_about(keys[15], (D, VOCAB), (0.05 * TOKENS ** 0.5), 56.0, (), jnp.float32),
        "norm_moment": scatter_about(keys[16], (2, 4, D), (0.05 * TOKENS ** 0.5), 56.0, (), jnp.float32),
    }


@jax.custom_vjp
def low(v):
    return lax.optimization_barrier(v.astype(jnp.bfloat16)).astype(jnp.float32)

@jax.custom_vjp
def low_back(v):
    return v

def low_keep(v):
    return (low(v), None)

def low_pass(kept, grad):
    return (grad,)

def back_keep(v):
    return (v, None)

def back_low(kept, grad):
    return (low(grad),)
low.defvjp(low_keep, low_pass)
low_back.defvjp(back_keep, back_low)
HIGHEST = lax.Precision.HIGHEST
NS_A = 3.4445
NS_B = -4.775
NS_C = 2.0315
muon_rate = 0.5
vector_rate = 0.05

def matrix_times(left_side, right_side):
    return jnp.dot(left_side, right_side, precision=HIGHEST, preferred_element_type=jnp.float32)

def rounded(value):
    return low_back(low(value))

def layer_norm(value, gain, bias):
    average = lax.optimization_barrier(jnp.mean(value, axis=-1, keepdims=True))
    centred = value - average
    variance = lax.optimization_barrier(jnp.mean(centred * centred, axis=-1, keepdims=True))
    return centred * lax.rsqrt(variance + 1e-05) * gain + bias

def bucket_plan():
    return ((2 * SETS, CAP_S, 0, 0), (SETS, CAP_M, 2 * SETS * CAP_S, 2 * SETS), (SETS, CAP_L, 2 * SETS * CAP_S + SETS * CAP_M, 3 * SETS))

def live_rows(slot_lengths):
    pieces = []
    for seq_count, slot_cap, row_start, slot_start in bucket_plan():
        positions = jnp.arange(slot_cap, dtype=jnp.int32)
        pieces.append((positions[None, :] < slot_lengths[slot_start:slot_start + seq_count, None]).reshape(-1))
    return jnp.concatenate(pieces)

def causal_mask(slot_cap, slot_lengths):
    positions = jnp.arange(slot_cap, dtype=jnp.int32)
    return (positions[None, None, :] <= positions[None, :, None]) & (positions[None, None, :] < slot_lengths[:, None, None])

def attend(query_block, key_block, value_block, allowed):
    scores = jnp.einsum('nqhe,nkhe->nhqk', query_block, key_block, precision=HIGHEST) * 0.125
    scores = jnp.where(allowed[:, None], low_back(scores), -1000000000.0)
    row_max = lax.optimization_barrier(jnp.max(scores, axis=-1, keepdims=True))
    exp_scores = jnp.exp(scores - row_max)
    attn_probs = low(exp_scores / lax.optimization_barrier(jnp.sum(exp_scores, axis=-1, keepdims=True)))
    return jnp.einsum('nhqk,nkhe->nqhe', attn_probs, value_block, precision=HIGHEST)

def self_branch(normed, query_weight, key_weight, value_weight, out_weight, slot_lengths):
    queries = rounded(matrix_times(normed, query_weight))
    key_rows = rounded(matrix_times(normed, key_weight))
    value_rows = rounded(matrix_times(normed, value_weight))
    results = []
    for seq_count, slot_cap, row_start, slot_start in bucket_plan():
        row_end = row_start + seq_count * slot_cap
        block_shape = (seq_count, slot_cap, HEADS, HEAD)
        allowed = causal_mask(slot_cap, slot_lengths[slot_start:slot_start + seq_count])
        attended = attend(queries[row_start:row_end].reshape(block_shape), key_rows[row_start:row_end].reshape(block_shape), value_rows[row_start:row_end].reshape(block_shape), allowed)
        results.append(attended.reshape(seq_count * slot_cap, D))
    return low_back(matrix_times(rounded(jnp.concatenate(results, 0)), out_weight))

def cross_branch(normed, memory_rows, query_weight, key_weight, value_weight, out_weight):
    queries = rounded(matrix_times(normed, query_weight))
    key_rows = rounded(matrix_times(memory_rows, key_weight))
    value_rows = rounded(matrix_times(memory_rows, value_weight))
    results = []
    for seq_count, slot_cap, row_start, slot_start in bucket_plan():
        row_end = row_start + seq_count * slot_cap
        mem_start = slot_start * MEM
        mem_end = (slot_start + seq_count) * MEM
        allowed = jnp.ones((seq_count, slot_cap, MEM), dtype=jnp.bool_)
        attended = attend(queries[row_start:row_end].reshape(seq_count, slot_cap, HEADS, HEAD), key_rows[mem_start:mem_end].reshape(seq_count, MEM, HEADS, HEAD), value_rows[mem_start:mem_end].reshape(seq_count, MEM, HEADS, HEAD), allowed)
        results.append(attended.reshape(seq_count * slot_cap, D))
    return low_back(matrix_times(rounded(jnp.concatenate(results, 0)), out_weight))

def group_loss(weights, residual, memory_rows, slot_lengths, slot_targets):
    attn_in, attn_out, ffn_in, ffn_out, vocab_head, norm_gain, norm_bias = weights
    normed = low(layer_norm(residual, norm_gain[0], norm_bias[0]))
    resid_one = residual + self_branch(normed, attn_in[0, 0], attn_in[0, 1], attn_in[0, 2], attn_out[0], slot_lengths)
    normed = low(layer_norm(resid_one, norm_gain[1], norm_bias[1]))
    resid_two = resid_one + cross_branch(normed, memory_rows, attn_in[1, 0], attn_in[1, 1], attn_in[1, 2], attn_out[1])
    normed = low(layer_norm(resid_two, norm_gain[2], norm_bias[2]))
    hidden_pre = low_back(matrix_times(normed, ffn_in))
    active = low(jax.nn.gelu(hidden_pre, approximate=False))
    resid_three = resid_two + low_back(matrix_times(active, ffn_out))
    final_rows = low(layer_norm(resid_three, norm_gain[3], norm_bias[3]))
    logits = low_back(matrix_times(final_rows, vocab_head))
    row_max = lax.optimization_barrier(jnp.max(logits, axis=-1, keepdims=True))
    log_total = row_max[:, 0] + jnp.log(lax.optimization_barrier(jnp.sum(jnp.exp(logits - row_max), axis=-1)))
    onehot = slot_targets[:, None] == jnp.arange(VOCAB, dtype=jnp.int32)[None, :]
    picked = lax.optimization_barrier(jnp.sum(jnp.where(onehot, logits, 0.0), axis=-1))
    live_mask = live_rows(slot_lengths)
    return (jnp.sum(jnp.where(live_mask, log_total - picked, 0.0)), resid_three)

def orthogonal(moment_matrix):
    frobenius = jnp.sqrt(jnp.sum(moment_matrix * moment_matrix))
    iterate = moment_matrix / (frobenius + 1e-07)
    for iteration in range(NS_STEPS):
        gram_matrix = matrix_times(iterate, iterate.T)
        polynomial = NS_B * gram_matrix + NS_C * matrix_times(gram_matrix, gram_matrix)
        iterate = NS_A * iterate + matrix_times(polynomial, iterate)
    return iterate

def muon_update(weight, old_moment, gradient):
    moment_new = 0.5 * old_moment + gradient
    direction = orthogonal(moment_new)
    step_rate = muon_rate * math.sqrt(weight.shape[1] / weight.shape[0])
    return (moment_new, weight - step_rate * direction)

def reference(residual_in, memory, lengths, targets, attn_in, attn_out, ffn_in, ffn_out, vocab_head, norm_gain, norm_bias, attn_in_moment, attn_out_moment, ffn_in_moment, ffn_out_moment, head_moment, norm_moment):
    group_lengths = lengths.reshape(N_DP, SLOTS)
    group_targets = targets.reshape(N_DP, ROWS)
    live_all = jax.vmap(live_rows)(group_lengths).reshape(-1)
    token_counts = jax.ops.segment_sum(live_all.astype(jnp.int32), targets, num_segments=VOCAB)
    loss_scale = TOKENS / jnp.sum(token_counts).astype(jnp.float32)

    def forward(matrices, vectors, inputs_f, memory_f):
        weights = tuple((low(matrix) for matrix in matrices)) + vectors

        def one_group(running, group_item):
            residual, memory_rows, slot_lengths, slot_targets = group_item
            ce_sum, result = jax.checkpoint(group_loss)(weights, residual, memory_rows, slot_lengths, slot_targets)
            return (running + ce_sum, result)
        ce_total, results = lax.scan(one_group, jnp.zeros((), jnp.float32), (inputs_f.reshape(N_DP, ROWS, D), memory_f.reshape(N_DP, MROWS, D), group_lengths, group_targets))
        return (ce_total * loss_scale, results.reshape(TOKENS, D))
    matrices = (attn_in, attn_out, ffn_in, ffn_out, vocab_head)
    loss_value, pullback, layer_out = jax.vjp(forward, matrices, (norm_gain, norm_bias), residual_in.astype(jnp.float32), memory.astype(jnp.float32), has_aux=True)
    grad_matrices, grad_vectors, input_grad, memory_grad = pullback(jnp.ones((), jnp.float32))
    grad_in, grad_out, grad_up, grad_down, grad_head = grad_matrices
    in_moments, in_weights = ([], [])
    for branch in range(2):
        for which in range(3):
            moment_new, weight_new = muon_update(attn_in[branch, which], attn_in_moment[branch, which], grad_in[branch, which])
            in_moments.append(moment_new)
            in_weights.append(weight_new)
    out_moments, out_weights = ([], [])
    for branch in range(2):
        moment_new, weight_new = muon_update(attn_out[branch].T, attn_out_moment[branch].T, grad_out[branch].T)
        out_moments.append(moment_new.T)
        out_weights.append(weight_new.T)
    moment_up, new_up = muon_update(ffn_in, ffn_in_moment, grad_up)
    moment_down, new_down = muon_update(ffn_out.T, ffn_out_moment.T, grad_down.T)
    moment_head, new_head = muon_update(vocab_head, head_moment, grad_head)
    moment_norms = 0.5 * norm_moment + jnp.stack([grad_vectors[0], grad_vectors[1]])
    old_vector = jnp.stack([norm_gain, norm_bias])
    new_norms = old_vector - vector_rate * moment_norms * lax.rsqrt(lax.optimization_barrier(jnp.mean(moment_norms * moment_norms, axis=-1, keepdims=True)) + 1e-06)
    return (layer_out.astype(jnp.bfloat16), input_grad, memory_grad, jnp.stack(in_moments).reshape(2, 3, D, D), jnp.stack(in_weights).reshape(2, 3, D, D), jnp.stack(out_moments), jnp.stack(out_weights), moment_up, new_up, moment_down.T, new_down.T, moment_head, new_head, moment_norms, new_norms, token_counts)
```

```python
from functools import partial
import math

import jax
import jax.numpy as jnp
from jax import lax
from jax.experimental import pallas as pl
from jax.experimental.pallas import tpu as pltpu
from jax.sharding import PartitionSpec as P

HEAD = 64
CAP_S = 64
CAP_M = 128
CAP_L = 256
MEM = 128
SETS = 4
NS_STEPS = 5
NS_A = 3.4445
NS_B = -4.775
NS_C = 2.0315
muon_rate = 0.5
vector_rate = 0.05

D = 512
BLK = 256
WIDE = 512
VOC = 640
HROWS = 320
HPART = 160
MIB = 1024 * 1024
bf16 = jnp.bfloat16
f32 = jnp.float32
VMEM = pltpu.VMEM


def mm(a, b):
    return jnp.dot(a, b, preferred_element_type=f32)


def mm_nt(a, b):
    return lax.dot_general(a, b, (((1,), (1,)), ((), ())), preferred_element_type=f32)


def mm_tn(a, b):
    return lax.dot_general(a, b, (((0,), (0,)), ((), ())), preferred_element_type=f32)


def norm_stats(value):
    average = jnp.mean(value, axis=-1, keepdims=True)
    centred = value - average
    variance = jnp.mean(centred * centred, axis=-1, keepdims=True)
    inverse = lax.rsqrt(variance + 1e-05)
    return centred * inverse, inverse


def norm_back(gradient, normed, inverse, gain):
    scaled = gradient * gain
    return inverse * (
        scaled
        - jnp.mean(scaled, axis=-1, keepdims=True)
        - normed * jnp.mean(scaled * normed, axis=-1, keepdims=True)
    )


def lane_masks(width):
    lanes = lax.broadcasted_iota(jnp.int32, (1, width), 1)
    return [(lanes // HEAD == h).astype(f32).astype(bf16) for h in range(width // HEAD)]


def spread(block, masks):
    return jnp.concatenate([block * m for m in masks], axis=0)


def pick(stacked, masks, rows):
    total = stacked[:rows] * masks[0].astype(f32)
    for h in range(1, len(masks)):
        total = total + stacked[h * rows : (h + 1) * rows] * masks[h].astype(f32)
    return total


def softmax_rows(scores):
    top = jnp.max(scores, axis=-1, keepdims=True)
    exps = jnp.exp(scores - top)
    return exps * (1.0 / jnp.sum(exps, axis=-1, keepdims=True))


def mem_slot(core, block, unit):
    on_first = jnp.where(block < 2, 4 * block + unit, 8 + 2 * (block - 2) + unit // 2)
    return jnp.where(core == 0, on_first, block)


def row_limits(core, block, lengths_ref):
    unit = lax.broadcasted_iota(jnp.int32, (BLK, 1), 0) // CAP_S
    low = jnp.zeros((BLK, 1), jnp.int32)
    length = jnp.zeros((BLK, 1), jnp.int32)
    for u in range(BLK // CAP_S):
        on_first = jnp.where(block < 2, u * CAP_S, u // 2 * CAP_M)
        slot = mem_slot(core, block, u) + jnp.where(core == 0, 0, 3 * SETS)
        low = jnp.where(unit == u, jnp.where(core == 0, on_first, 0), low)
        length = jnp.where(unit == u, lengths_ref[slot], length)
    return low, length


def rows_live(core, first, blocks, lengths_ref):
    pieces = []
    for j in range(blocks):
        low, length = row_limits(core, first + j, lengths_ref)
        place = lax.broadcasted_iota(jnp.int32, (BLK, 1), 0)
        pieces.append((place - low < length).astype(f32))
    return jnp.concatenate(pieces, axis=0)


def forward_kernel(
    lengths_ref, x_ref, mem_ref, wa0, wa1, wo0, wo1, gain_ref, bias_ref,
    h1_ref, qkv_ref, p_ref, o_ref, x1_ref, h2_ref, cq_ref, kv_ref, pc_ref, oc_ref, x2_ref,
):
    core = lax.axis_index("mp")
    step = pl.program_id(0)
    wa = (wa0, wa1)

    @pl.when(step == 0)
    def _():
        def fill(i, carry):
            rows = pl.ds(pl.multiple_of(i * WIDE, WIDE), WIDE)
            for half in range(2):
                for which in range(2):
                    kv_ref[rows, pl.ds(which * D + half * 256, 256)] = mm(
                        mem_ref[rows, :], wa[half][4 + which]
                    ).astype(bf16)
            return carry

        lax.fori_loop(0, jnp.where(core == 0, 3, 1), fill, 0)

    normed, _ = norm_stats(x_ref[...].astype(f32))
    h1_ref[...] = (normed * gain_ref[0:1, :] + bias_ref[0:1, :]).astype(bf16)
    for half in range(2):
        for which in range(3):
            qkv_ref[:, pl.ds(which * D + half * 256, 256)] = mm(h1_ref[...], wa[half][which]).astype(bf16)
    pair = lane_masks(128)
    for j in range(WIDE // BLK):
        rows = pl.ds(j * BLK, BLK)
        low, length = row_limits(core, step * (WIDE // BLK) + j, lengths_ref)
        keys = lax.broadcasted_iota(jnp.int32, (BLK, BLK), 1)
        queries = lax.broadcasted_iota(jnp.int32, (BLK, BLK), 0)
        allowed = (keys >= low) & (keys < low + length) & (keys <= queries)
        for i in range(4):
            q = qkv_ref[rows, pl.ds(i * 128, 128)] * jnp.bfloat16(0.125)
            k = qkv_ref[rows, pl.ds(D + i * 128, 128)]
            v = qkv_ref[rows, pl.ds(2 * D + i * 128, 128)]
            scores = mm_nt(spread(q, pair), k).reshape(2, BLK, BLK)
            scores = jnp.where(allowed[None], scores, -1000000000.0)
            probs = softmax_rows(scores).astype(bf16).reshape(2 * BLK, BLK)
            p_ref[j, i] = probs
            o_ref[rows, pl.ds(i * 128, 128)] = pick(mm(probs, v), pair, BLK).astype(bf16)
    x1 = x_ref[...].astype(f32) + mm(o_ref[:, :256], wo0[0]) + mm(o_ref[:, 256:], wo1[0])
    x1_ref[...] = x1
    normed, _ = norm_stats(x1)
    h2_ref[...] = (normed * gain_ref[1:2, :] + bias_ref[1:2, :]).astype(bf16)
    for half in range(2):
        cq_ref[:, pl.ds(half * 256, 256)] = mm(h2_ref[...], wa[half][3]).astype(bf16)
    quad = lane_masks(256)
    for u in range(WIDE // 64):
        rows = pl.ds(u * 64, 64)
        block = step * (WIDE // BLK) + u // 4
        slot = pl.ds(pl.multiple_of(mem_slot(core, block, u % 4) * MEM, MEM), MEM)
        for j in range(2):
            q = cq_ref[rows, pl.ds(j * 256, 256)] * jnp.bfloat16(0.125)
            k = kv_ref[slot, pl.ds(j * 256, 256)]
            v = kv_ref[slot, pl.ds(D + j * 256, 256)]
            probs = softmax_rows(mm_nt(spread(q, quad), k)).astype(bf16)
            pc_ref[u // 4, u % 4 * 2 + j] = probs
            oc_ref[rows, pl.ds(j * 256, 256)] = pick(mm(probs, v), quad, 64).astype(bf16)
    x2_ref[...] = x1_ref[...] + mm(oc_ref[:, :256], wo0[1]) + mm(oc_ref[:, 256:], wo1[1])


def gelu_parts(u):
    z = jnp.abs(u) * (1.0 / math.sqrt(2.0))
    t = 1.0 / (1.0 + 0.3275911 * z)
    gauss = jnp.exp(-0.5 * u * u)
    poly = t * (
        0.254829592 + t * (-0.284496736 + t * (1.421413741 + t * (-1.453152027 + t * 1.061405429)))
    )
    tail = 0.5 * poly * gauss
    cdf = jnp.where(u < 0, tail, 1.0 - tail)
    return u * cdf, cdf + u * gauss * (1.0 / math.sqrt(2.0 * math.pi))


def middle_kernel(
    vocab, tokens, lengths_ref, total_ref, x2_ref, targets_ref, wi0, wi1, wf0, wf1, wh_ref, gain_ref, bias_ref,
    out_ref, g2_ref, gw_ref, ghead_ref, gnorm_ref, count_ref,
    h3_all, a_all, dy_all, du_all, z_all, gl_all, slope,
):
    block = pl.program_id(0)
    rows = pl.ds(pl.multiple_of(block * WIDE, WIDE), WIDE)
    wi = (wi0, wi1)
    wf = (wf0, wf1)
    x2 = x2_ref[...]
    normed2, inverse2 = norm_stats(x2)
    h3 = (normed2 * gain_ref[2:3, :] + bias_ref[2:3, :]).astype(bf16)
    h3_all[rows, :] = h3
    for half in range(2):
        for j in range(2):
            wide = pl.ds(half * 1024 + j * 512, 512)
            active, grad = gelu_parts(mm(h3, wi[half][:, j * 512 : (j + 1) * 512]))
            a_all[rows, wide] = active.astype(bf16)
            slope[:, wide] = grad
    x3 = x2_ref[...] + mm(a_all[rows, 0:1024], wf0[...]) + mm(a_all[rows, 1024:2048], wf1[...])
    out_ref[...] = x3.astype(bf16)
    normed3, inverse3 = norm_stats(x3)
    z = (normed3 * gain_ref[3:4, :] + bias_ref[3:4, :]).astype(bf16)
    z_all[rows, :] = z
    logits = mm_nt(z, wh_ref[...])
    columns = lax.broadcasted_iota(jnp.int32, (WIDE, VOC), 1)
    logits = jnp.where(columns < vocab, logits, -1e30)
    probs = softmax_rows(logits)
    onehot = (columns == targets_ref[...]).astype(f32)
    live = rows_live(lax.axis_index("mp"), block * (WIDE // BLK), WIDE // BLK, lengths_ref)
    gl = (tokens / total_ref[0:1, 0:1] * live * (probs - onehot)).astype(bf16)
    gl_all[rows, :] = gl
    counts = jnp.sum(onehot * live, axis=0, keepdims=True)
    gz = mm(gl, wh_ref[...])
    gain3 = jnp.sum(gz * normed3, axis=0, keepdims=True)
    bias3 = jnp.sum(gz, axis=0, keepdims=True)
    g3 = norm_back(gz, normed3, inverse3, gain_ref[3:4, :])
    dy = g3.astype(bf16)
    dy_all[rows, :] = dy
    g2_ref[...] = g3
    for half in range(2):
        for j in range(2):
            wide = pl.ds(half * 1024 + j * 512, 512)
            back = mm_nt(dy, wf[half][j * 512 : (j + 1) * 512, :])
            du_all[rows, wide] = (slope[:, wide] * back).astype(bf16)
    dh = mm_nt(du_all[rows, 0:1024], wi0[...]) + mm_nt(du_all[rows, 1024:2048], wi1[...])
    normed2, inverse2 = norm_stats(x2_ref[...])
    gain2 = jnp.sum(dh * normed2, axis=0, keepdims=True)
    bias2 = jnp.sum(dh, axis=0, keepdims=True)
    g2_ref[...] = g2_ref[...] + norm_back(dh, normed2, inverse2, gain_ref[2:3, :])

    @pl.when(block == 0)
    def _():
        gnorm_ref[...] = jnp.zeros_like(gnorm_ref)
        count_ref[...] = jnp.zeros_like(count_ref)

    gnorm_ref[0:1, :] += gain2
    gnorm_ref[1:2, :] += gain3
    gnorm_ref[2:3, :] += bias2
    gnorm_ref[3:4, :] += bias3
    count_ref[0:1, :] += counts

    @pl.when(block == pl.num_programs(0) - 1)
    def _():
        for half in range(2):
            for j in range(2):
                col = pl.ds(half * 1024 + j * 512, 512)
                gw_ref[half, 0, j] = mm_tn(du_all[:, col], h3_all[...]).astype(bf16)
                gw_ref[half, 1, j] = mm_tn(a_all[:, col], dy_all[...]).astype(bf16)
        ghead_ref[...] = mm_tn(gl_all[...], z_all[...]).astype(bf16)


def attend_back(queries, keys, values, probs, grads, masks, rows):
    q = spread(queries, masks)
    do = spread(grads, masks)
    dprobs = mm_nt(do, values)
    p = probs.astype(f32)
    weighted = p * dprobs
    ds = (weighted - p * jnp.sum(weighted, axis=-1, keepdims=True)).astype(bf16)
    dv = mm_tn(probs, do)
    dq = pick(mm(ds, keys), masks, rows) * 0.125
    dk = mm_tn(ds, q) * 0.125
    return dq, dk, dv


def backward_kernel(
    dims, g2_ref, x_ref, x1_ref, h1_ref, qkv_ref, p_ref, o_ref, h2_ref, cq_ref, kv_ref, pc_ref, oc_ref,
    mem_ref, wa0, wa1, wo0, wo1, gain_ref, gw_ref, ghead_ref,
    dx_ref, dmem_ref, dlow_ref, gs_ref, gnorm_ref, wide_out, head_out,
    dyc_all, dcq_all, dys_all, dqkv_all, dkv_all, dkv_low,
    early_acc, early_core, early_first, early_second, head_acc, head_core, head_first, head_second,
    send_sems, recv_sems, local_sems,
):
    core = lax.axis_index("mp")
    block = pl.program_id(0)
    early = EarlySum(
        Net(dims, send_sems, recv_sems), gw_ref, ghead_ref, wide_out, head_out,
        (
            early_acc, early_core, early_first, early_second, head_acc, head_core, head_first, head_second,
            local_sems,
        ),
    )
    pl.when(block == 0)(early.start)
    rows = pl.ds(pl.multiple_of(block * BLK, BLK), BLK)
    wa = (wa0, wa1)
    wo = (wo0, wo1)

    @pl.when(block == 0)
    def _():
        gnorm_ref[...] = jnp.zeros_like(gnorm_ref)
        dkv_all[...] = jnp.zeros_like(dkv_all)

    g2 = g2_ref[...]
    dyc = g2.astype(bf16)
    dyc_all[rows, :] = dyc
    quad = lane_masks(256)
    for j in range(2):
        lanes = pl.ds(j * 256, 256)
        do = mm_nt(dyc, wo[j][1]).astype(bf16)
        for u in range(4):
            base = pl.multiple_of(block * BLK + u * 64, 64)
            slot = pl.ds(pl.multiple_of(mem_slot(core, block, u) * MEM, MEM), MEM)
            dq, dk, dv = attend_back(
                cq_ref[u * 64 : (u + 1) * 64, lanes],
                kv_ref[slot, lanes],
                kv_ref[slot, pl.ds(D + j * 256, 256)],
                pc_ref[0, u * 2 + j],
                do[u * 64 : (u + 1) * 64],
                quad,
                64,
            )
            dcq_all[pl.ds(base, 64), lanes] = dq.astype(bf16)
            dkv_all[slot, lanes] += dk
            dkv_all[slot, pl.ds(D + j * 256, 256)] += dv
    dcq = dcq_all[rows, :]
    dh = mm_nt(dcq[:, :256], wa0[3]) + mm_nt(dcq[:, 256:], wa1[3])
    normed, inverse = norm_stats(x1_ref[...])
    gnorm_ref[1:2, :] += jnp.sum(dh * normed, axis=0, keepdims=True)
    gnorm_ref[3:4, :] += jnp.sum(dh, axis=0, keepdims=True)
    g1 = g2 + norm_back(dh, normed, inverse, gain_ref[1:2, :])
    pl.when(block == 0)(early.one)
    dys = g1.astype(bf16)
    dys_all[rows, :] = dys
    pair = lane_masks(128)
    for half in range(2):
        do_half = mm_nt(dys, wo[half][0]).astype(bf16)
        for i in range(2):
            first = half * 256 + i * 128
            dq, dk, dv = attend_back(
                qkv_ref[:, pl.ds(first, 128)],
                qkv_ref[:, pl.ds(D + first, 128)],
                qkv_ref[:, pl.ds(2 * D + first, 128)],
                p_ref[0, half * 2 + i],
                do_half[:, i * 128 : (i + 1) * 128],
                pair,
                BLK,
            )
            dqkv_all[rows, pl.ds(first, 128)] = dq.astype(bf16)
            dqkv_all[rows, pl.ds(D + first, 128)] = dk.astype(bf16)
            dqkv_all[rows, pl.ds(2 * D + first, 128)] = dv.astype(bf16)
    dqkv = dqkv_all[rows, :]
    dh = jnp.zeros((BLK, D), f32)
    for half in range(2):
        for which in range(3):
            first = which * D + half * 256
            dh = dh + mm_nt(dqkv[:, first : first + 256], wa[half][which])
    normed, inverse = norm_stats(x_ref[...].astype(f32))
    gnorm_ref[0:1, :] += jnp.sum(dh * normed, axis=0, keepdims=True)
    gnorm_ref[2:3, :] += jnp.sum(dh, axis=0, keepdims=True)
    dx_ref[...] = g1 + norm_back(dh, normed, inverse, gain_ref[0:1, :])
    pl.when(block == 1)(early.two)
    pl.when(block == 3)(early.three)

    @pl.when(block == pl.num_programs(0) - 1)
    def _():
        def memory_rows(i, carry):
            part = pl.ds(pl.multiple_of(i * BLK, BLK), BLK)
            low = dkv_all[part, :].astype(bf16)
            dkv_low[part, :] = low
            total = jnp.zeros((BLK, D), f32)
            for half in range(2):
                for which in range(2):
                    first = which * D + half * 256
                    total = total + mm_nt(low[:, first : first + 256], wa[half][4 + which])
            dmem_ref[part, :] = total
            return carry

        lax.fori_loop(0, jnp.where(core == 0, 6, 2), memory_rows, 0)

        @pl.when(core != 0)
        def _():
            dkv_low[512:, :] = jnp.zeros((1024, 2 * D), bf16)
            dmem_ref[512:, :] = jnp.zeros((1024, D), f32)

        dlow_ref[...] = dmem_ref[1024:, :].astype(bf16)

        for half in range(2):
            for which in range(3):
                col = pl.ds(which * D + half * 256, 256)
                gs_ref[half, 0, which] = mm_tn(dqkv_all[:, col], h1_ref[...]).astype(bf16)
            col = pl.ds(half * 256, 256)
            gs_ref[half, 0, 3] = mm_tn(dcq_all[:, col], h2_ref[...]).astype(bf16)
            for which in range(2):
                wide = pl.ds(which * D + half * 256, 256)
                gs_ref[half, 1, which] = mm_tn(dkv_low[:, wide], mem_ref[...]).astype(bf16)
            gs_ref[half, 1, 2] = mm_tn(o_ref[:, col], dys_all[...]).astype(bf16)
            gs_ref[half, 1, 3] = mm_tn(oc_ref[:, col], dyc_all[...]).astype(bf16)
        early.end()


def whole(shape):
    return pl.BlockSpec(shape, lambda i: (0,) * len(shape), pipeline_mode=pl.Buffered(1))


def by_rows(width):
    return pl.BlockSpec((BLK, width), lambda i: (i, 0))


def wide_rows(width):
    return pl.BlockSpec((WIDE, width), lambda i: (i, 0))


def sds(shape, dtype):
    return jax.ShapeDtypeStruct(shape, dtype)


def run_forward(lengths, x, mem, wa, wo, gain, bias):
    rows = x.shape[0]
    steps = rows // WIDE
    outs = [
        (sds((rows, D), bf16), wide_rows(D)),
        (sds((rows, 3 * D), bf16), wide_rows(3 * D)),
        (sds((rows // BLK, 4, 512, 256), bf16), pl.BlockSpec((2, 4, 512, 256), lambda i: (i, 0, 0, 0))),
        (sds((rows, D), bf16), wide_rows(D)),
        (sds((rows, D), f32), wide_rows(D)),
        (sds((rows, D), bf16), wide_rows(D)),
        (sds((rows, D), bf16), wide_rows(D)),
        (sds((1536, 2 * D), bf16), whole((1536, 2 * D))),
        (sds((rows // BLK, 8, 256, 128), bf16), pl.BlockSpec((2, 8, 256, 128), lambda i: (i, 0, 0, 0))),
        (sds((rows, D), bf16), wide_rows(D)),
        (sds((rows, D), f32), wide_rows(D)),
    ]
    return pl.pallas_call(
        forward_kernel,
        grid=(steps,),
        in_specs=[
            pl.BlockSpec(memory_space=pltpu.SMEM), wide_rows(D), whole((1536, D)),
            whole((6, D, 256)), whole((6, D, 256)), whole((2, 256, D)), whole((2, 256, D)),
            whole((4, D)), whole((4, D)),
        ],
        out_specs=[o[1] for o in outs],
        out_shape=[o[0] for o in outs],
        compiler_params=pltpu.CompilerParams(vmem_limit_bytes=60 * MIB),
        cost_estimate=pl.CostEstimate(flops=9 * 10**9, bytes_accessed=22 * MIB, transcendentals=3 * 10**6),
        name="layer_forward",
    )(lengths, x, mem, wa[0], wa[1], wo[0], wo[1], gain, bias)


def run_middle(lengths, total, x2, targets, wi, wf, wh, gain, bias, vocab, tokens):
    rows = x2.shape[0]
    steps = rows // WIDE
    outs = [
        (sds((rows, D), bf16), wide_rows(D)),
        (sds((rows, D), f32), wide_rows(D)),
        (sds((2, 2, 2, 512, D), bf16), whole((2, 2, 2, 512, D))),
        (sds((VOC, D), bf16), whole((VOC, D))),
        (sds((8, D), f32), whole((8, D))),
        (sds((8, VOC), f32), whole((8, VOC))),
    ]
    return pl.pallas_call(
        partial(middle_kernel, vocab, tokens),
        grid=(steps,),
        in_specs=[
            pl.BlockSpec(memory_space=pltpu.SMEM), whole((8, 128)), wide_rows(D), wide_rows(1),
            whole((D, 1024)), whole((D, 1024)), whole((1024, D)), whole((1024, D)), whole((VOC, D)),
            whole((4, D)), whole((4, D)),
        ],
        out_specs=[o[1] for o in outs],
        out_shape=[o[0] for o in outs],
        scratch_shapes=[
            VMEM((rows, D), bf16), VMEM((rows, 2048), bf16), VMEM((rows, D), bf16),
            VMEM((rows, 2048), bf16), VMEM((rows, D), bf16), VMEM((rows, VOC), bf16),
            VMEM((WIDE, 2048), f32),
        ],
        compiler_params=pltpu.CompilerParams(vmem_limit_bytes=60 * MIB),
        cost_estimate=pl.CostEstimate(flops=15 * 10**9, bytes_accessed=18 * MIB, transcendentals=5 * 10**6),
        name="ffn_head",
    )(lengths, total, x2, targets, wi[0], wi[1], wf[0], wf[1], wh, gain, bias)


def run_backward(dims, g2, x, x1, h1, qkv, p, o, h2, cq, kv, pc, oc, mem, wa, wo, gain, gw, ghead):
    rows = x.shape[0]
    steps = rows // BLK
    outs = [
        (sds((rows, D), f32), by_rows(D)),
        (sds((1536, D), f32), whole((1536, D))),
        (sds((512, D), bf16), whole((512, D))),
        (sds((2, 2, 4, 256, D), bf16), whole((2, 2, 4, 256, D))),
        (sds((8, D), f32), whole((8, D))),
        (sds((2, 512, D), bf16), pl.BlockSpec(memory_space=pl.ANY)),
        (sds((2, HPART, D), bf16), pl.BlockSpec(memory_space=pl.ANY)),
    ]
    nz, ny, nx = dims
    slots = max(nx, ny) - 1
    return pl.pallas_call(
        partial(backward_kernel, dims),
        grid=(steps,),
        in_specs=[
            by_rows(D), by_rows(D), by_rows(D), whole((rows, D)), by_rows(3 * D),
            pl.BlockSpec((1, 4, 512, 256), lambda i: (i, 0, 0, 0)), whole((rows, D)), whole((rows, D)),
            by_rows(D), whole((1536, 2 * D)), pl.BlockSpec((1, 8, 256, 128), lambda i: (i, 0, 0, 0)),
            whole((rows, D)), whole((1536, D)),
            whole((6, D, 256)), whole((6, D, 256)), whole((2, 256, D)), whole((2, 256, D)), whole((4, D)),
            pl.BlockSpec(memory_space=pl.ANY), pl.BlockSpec(memory_space=pl.ANY),
        ],
        out_specs=[o_[1] for o_ in outs],
        out_shape=[o_[0] for o_ in outs],
        scratch_shapes=[
            VMEM((rows, D), bf16), VMEM((rows, D), bf16), VMEM((rows, D), bf16),
            VMEM((rows, 3 * D), bf16), VMEM((1536, 2 * D), f32), VMEM((1536, 2 * D), bf16),
            VMEM((2, 2, 512, D), bf16), VMEM((2, 2, 512, D), bf16),
            VMEM((2, slots, 512, D), bf16), VMEM((2, slots, 512, D), bf16),
            VMEM((2, HPART, D), bf16), VMEM((2, HPART, D), bf16),
            VMEM((2, slots, HPART, D), bf16), VMEM((2, slots, HPART, D), bf16),
            pltpu.SemaphoreType.DMA((48,)), pltpu.SemaphoreType.DMA((32,)), pltpu.SemaphoreType.DMA((6,)),
        ],
        compiler_params=pltpu.CompilerParams(
            vmem_limit_bytes=62 * MIB, collective_id=2, has_side_effects=True
        ),
        cost_estimate=pl.CostEstimate(flops=18 * 10**9, bytes_accessed=30 * MIB, transcendentals=0),
        name="attention_backward",
    )(g2, x, x1, h1, qkv, p, o, h2, cq, kv, pc, oc, mem, wa[0], wa[1], wo[0], wo[1], gain, gw, ghead)


MESH = pl.DeviceIdType.MESH
OWN = 2


def chip_dims(count):
    nz = 4
    side = math.isqrt(count // nz)
    return nz, count // nz // side, side


class Net:
    def __init__(self, dims, send_sems, recv_sems):
        self.nz, self.ny, self.nx = dims
        self.chip = lax.axis_index("dp")
        self.core = lax.axis_index("mp")
        self.x = lax.rem(self.chip, self.nx)
        self.y = lax.rem(lax.div(self.chip, self.nx), self.ny)
        self.z = lax.div(self.chip, self.nx * self.ny)
        self.place = {"x": self.x, "y": self.y, "z": self.z}
        self.count = {"x": self.nx, "y": self.ny, "z": self.nz}
        self.sibling = {"dp": self.chip, "mp": 1 - self.core}
        self.send_sems, self.recv_sems = send_sems, recv_sems
        self.sent, self.received = 0, 0
        self.unsent = []
        self.ending = False

    def at(self, **moved):
        p = {**self.place, **moved}
        return {"dp": (p["z"] * self.ny + p["y"]) * self.nx + p["x"], "mp": self.core}

    def further(self, axis, d):
        return lax.rem(self.place[axis] + d, self.count[axis])

    def on(self, condition, body):
        if condition is True:
            body()
        else:
            pl.when(condition)(body)

    def both(self, *conditions):
        result = True
        for c in conditions:
            if c is not True:
                result = c if result is True else jnp.logical_and(result, c)
        return result

    def inside(self, axis):
        return True if self.count[axis] == OWN else self.place[axis] < OWN

    def goes_inside(self, axis, d):
        return True if self.count[axis] == OWN else self.further(axis, d) < OWN

    def clipped(self, axis):
        return self.place[axis] if self.count[axis] == OWN else jnp.minimum(self.place[axis], OWN - 1)

    def send_sem(self, amount):
        self.sent += amount
        return self.sent - amount

    def recv_sem(self, amount):
        self.received += amount
        return self.received - amount

    def remote(self, src, dst, send_sem, recv_sem, device):
        return pltpu.make_async_remote_copy(
            src_ref=src, dst_ref=dst, send_sem=self.send_sems.at[send_sem],
            recv_sem=self.recv_sems.at[recv_sem], device_id=device, device_id_type=MESH,
        )

    def send(self, condition, src, dst, recv_sem, device):
        sem = self.send_sem(1)
        copy = lambda: self.remote(src, dst, sem, recv_sem, device)
        if self.ending:
            self.on(condition, lambda: copy().wait_send())
            return
        self.on(condition, lambda: copy().start())
        self.unsent.append((condition, copy))

    def landed(self, condition, dst, recv_sem):
        self.on(condition, lambda: self.remote(dst, dst, 0, recv_sem, self.sibling).wait_recv())

    def spread(self, axis, condition, ref, recv_sem):
        for d in range(1, self.count[axis]):
            self.send(condition, ref, ref, recv_sem, self.at(**{axis: self.further(axis, d)}))

    def all_sent(self):
        for condition, copy in self.unsent:
            self.on(condition, lambda copy=copy: copy().wait_send())
        self.unsent = []
        assert self.sent <= self.send_sems.shape[0] and self.received <= self.recv_sems.shape[0]

    def barrier(self):
        partners = [self.sibling]
        for axis in ("x", "y", "z"):
            for d in range(1, self.count[axis]):
                partners.append(self.at(**{axis: self.further(axis, d)}))
        barrier = pltpu.get_barrier_semaphore()
        for partner in partners:
            pl.semaphore_signal(barrier, inc=1, device_id=partner, device_id_type=MESH)
        pl.semaphore_wait(barrier, len(partners))


def add_into(dst, sources, step):
    rows = dst.shape[0]

    def body(i, carry):
        part = pl.ds(pl.multiple_of(i * step, step), step)
        total = dst[part, :].astype(f32)
        for s in sources:
            total = total + s[part, :].astype(f32)
        dst[part, :] = total.astype(bf16)
        return carry

    lax.fori_loop(0, rows // step, body, 0)


HEAD_X, HEAD_Y, HEAD_Z = 1, 0, 0


class EarlySum:
    def __init__(self, net, gw, ghead, wide_out, head_out, scratch):
        (
            self.acc, self.core_in, self.first_in, self.second_in,
            self.head_acc, self.head_core, self.head_first, self.head_second, self.local,
        ) = scratch
        self.net, self.gw, self.ghead, self.wide_out, self.head_out = net, gw, ghead, wide_out, head_out
        n = net
        self.core_sem = n.recv_sem(6)
        self.first_sem = [n.recv_sem(n.nx - 1), n.recv_sem(n.ny - 1)]
        self.second_sem = [n.recv_sem(n.ny - 1), n.recv_sem(n.nx - 1)]
        self.head_first_sem = [n.recv_sem(n.nx - 1), n.recv_sem(n.ny - 1)]
        self.head_second_sem = [n.recv_sem(n.ny - 1), n.recv_sem(n.nx - 1)]
        self.sums = ((0, "x", "y"), (1, "y", "x"))
        self.goal = {"x": HEAD_X, "y": HEAD_Y}

    def head_rows(self, core, f):
        return self.ghead.at[pl.ds(pl.multiple_of(core * HROWS + f * HPART, HPART), HPART)]

    def own_copies(self):
        core = self.net.core
        return [
            pltpu.make_async_copy(self.gw.at[0, m, f], self.acc.at[m, f], self.local.at[2 * m + f])
            for m in range(2)
            for f in range(2)
        ] + [
            pltpu.make_async_copy(self.head_rows(core, f), self.head_acc.at[f], self.local.at[4 + f]) for f in range(2)
        ]

    def start(self):
        self.net.barrier()
        for copy in self.own_copies():
            copy.start()
        self.core_sends()

    def core_sends(self):
        n = self.net
        for m in range(2):
            for f in range(2):
                n.send(True, self.gw.at[1, m, f], self.core_in.at[m, f], self.core_sem + 2 * m + f, n.sibling)
        for f in range(2):
            n.send(True, self.head_rows(1 - n.core, f), self.head_core.at[f], self.core_sem + 4 + f, n.sibling)

    def one(self):
        n = self.net
        for copy in self.own_copies():
            copy.wait()
        for m in range(2):
            for f in range(2):
                n.landed(True, self.core_in.at[m, f], self.core_sem + 2 * m + f)
                add_into(self.acc.at[m, f], [self.core_in.at[m, f]], 128)
        for f in range(2):
            n.landed(True, self.head_core.at[f], self.core_sem + 4 + f)
            add_into(self.head_acc.at[f], [self.head_core.at[f]], HPART)
        self.first_sends()

    def first_sends(self):
        n = self.net
        for f, axis, other in self.sums:
            for d in range(1, n.count[axis]):
                target = jnp.minimum(n.further(axis, d), OWN - 1)
                n.send(
                    n.goes_inside(axis, d), self.acc.at[target, f], self.first_in.at[f, d - 1],
                    self.first_sem[f] + d - 1, n.at(**{axis: n.further(axis, d)}),
                )
            goal = self.goal[axis]
            for d in range(1, n.count[axis]):
                n.send(
                    n.place[axis] == (goal + d) % n.count[axis], self.head_acc.at[f],
                    self.head_first.at[f, d - 1], self.head_first_sem[f] + d - 1, n.at(**{axis: goal}),
                )

    def two(self):
        n = self.net
        for f, axis, other in self.sums:
            matrix = n.clipped(axis)

            def take(f=f, axis=axis, matrix=matrix):
                slots = [self.first_in.at[f, d - 1] for d in range(1, n.count[axis])]
                for d in range(1, n.count[axis]):
                    n.landed(True, slots[d - 1], self.first_sem[f] + d - 1)
                add_into(self.acc.at[matrix, f], slots, 128)

            n.on(n.inside(axis), take)

            def take_head(f=f, axis=axis):
                slots = [self.head_first.at[f, d - 1] for d in range(1, n.count[axis])]
                for d in range(1, n.count[axis]):
                    n.landed(True, slots[d - 1], self.head_first_sem[f] + d - 1)
                add_into(self.head_acc.at[f], slots, HPART)

            n.on(n.place[axis] == self.goal[axis], take_head)
        self.second_sends()

    def second_sends(self):
        n = self.net
        for f, axis, other in self.sums:
            matrix = n.clipped(axis)
            distance = lax.rem(n.place[other] - matrix + n.count[other], n.count[other])
            slot = jnp.maximum(distance, 1) - 1
            n.send(
                n.both(n.inside(axis), distance != 0), self.acc.at[matrix, f], self.second_in.at[f, slot],
                self.second_sem[f] + slot, n.at(**{other: matrix}),
            )
            goal = self.goal[other]
            for d in range(1, n.count[other]):
                n.send(
                    n.both(n.place[axis] == self.goal[axis], n.place[other] == (goal + d) % n.count[other]),
                    self.head_acc.at[f], self.head_second.at[f, d - 1], self.head_second_sem[f] + d - 1,
                    n.at(**{other: goal}),
                )

    def columns(self):
        n = self.net
        wide = n.both(n.inside("x"), n.inside("y"), n.x == n.y)
        return wide, n.both(n.x == HEAD_X, n.y == HEAD_Y)

    def out_copies(self):
        n = self.net
        wide, head = self.columns()
        copies = [
            (wide, pltpu.make_async_copy(self.acc.at[n.clipped(axis), f], self.wide_out.at[f], self.local.at[f]))
            for f, axis, other in self.sums
        ]
        return copies + [(head, pltpu.make_async_copy(self.head_acc, self.head_out, self.local.at[4]))]

    def three(self):
        n = self.net
        wide, head = self.columns()
        for f, axis, other in self.sums:

            def take(f=f, axis=axis, other=other):
                slots = [self.second_in.at[f, d - 1] for d in range(1, n.count[other])]
                for d in range(1, n.count[other]):
                    n.landed(True, slots[d - 1], self.second_sem[f] + d - 1)
                add_into(self.acc.at[n.clipped(axis), f], slots, 128)

            n.on(wide, take)

            def take_head(f=f, other=other):
                slots = [self.head_second.at[f, d - 1] for d in range(1, n.count[other])]
                for d in range(1, n.count[other]):
                    n.landed(True, slots[d - 1], self.head_second_sem[f] + d - 1)
                add_into(self.head_acc.at[f], slots, HPART)

            n.on(head, take_head)
        for condition, copy in self.out_copies():
            n.on(condition, copy.start)

    def end(self):
        for condition, copy in self.out_copies():
            self.net.on(condition, copy.wait)
        self.net.sent, self.net.ending = 0, True
        self.core_sends()
        self.first_sends()
        self.second_sends()


def prepare_kernel(
    dims, lengths_ref, ai_ref, ao_ref, fi_ref, fo_ref, vh_ref, mem_ref,
    wa0, wa1, wo0, wo1, wi0, wi1, wf0, wf1, mem_out, wh_ref, total_ref,
    ai_in, ao_in, fi_in, fo_in, vh_in, mem_in, ai_low, ao_low, fi_low, fo_low, totals,
    load_sems, keep_sems, send_sems, recv_sems,
):
    nz, ny, nx = dims
    chip = lax.axis_index("dp")
    core = lax.axis_index("mp")
    place = {"x": lax.rem(chip, nx), "y": lax.rem(lax.div(chip, nx), ny), "z": lax.div(chip, nx * ny)}
    count = {"x": nx, "y": ny, "z": nz}
    sibling = {"dp": chip, "mp": 1 - core}

    def at(axis, target):
        p = {**place, axis: target}
        return {"dp": (p["z"] * ny + p["y"]) * nx + p["x"], "mp": core}

    arrays = (
        (ai_ref, ai_in, ai_low, wa0, wa1),
        (ao_ref, ao_in, ao_low, wo0, wo1),
        (fi_ref, fi_in, fi_low, wi0, wi1),
        (fo_ref, fo_in, fo_low, wf0, wf1),
    )
    loads = [
        pltpu.make_async_copy(src, dst, load_sems.at[i])
        for i, (src, dst) in enumerate([a[:2] for a in arrays] + [(vh_ref, vh_in), (mem_ref, mem_in)])
    ]
    for load in loads:
        load.start()
    partners = [sibling]
    for axis in ("x", "y", "z"):
        for d in range(1, count[axis]):
            partners.append(at(axis, lax.rem(place[axis] + d, count[axis])))
    barrier = pltpu.get_barrier_semaphore()
    for partner in partners:
        pl.semaphore_signal(barrier, inc=1, device_id=partner, device_id_type=MESH)
    pl.semaphore_wait(barrier, len(partners))

    def remote(src, dst, send_sem, recv_sem, device):
        return pltpu.make_async_remote_copy(
            src_ref=src, dst_ref=dst, send_sem=send_sems.at[send_sem], recv_sem=recv_sems.at[recv_sem],
            device_id=device, device_id_type=MESH,
        )

    tokens = lengths_ref[0]
    for s in range(1, lengths_ref.shape[0]):
        tokens = tokens + lengths_ref[s]

    base = {}
    used = 8
    for axis in ("x", "y", "z"):
        base[axis] = used
        used += count[axis]
    pending = []

    def spread_total(level, axis, value):
        totals[level, place[axis]] = value
        for d in range(1, count[axis]):
            copy = remote(
                totals.at[level, place[axis]], totals.at[level, place[axis]], base[axis] + d,
                base[axis] + place[axis], at(axis, lax.rem(place[axis] + d, count[axis])),
            )
            copy.start()
            pending.append(copy)

    def add_total(level, axis):
        for d in range(1, count[axis]):
            source = lax.rem(place[axis] + d, count[axis])
            remote(
                totals.at[level, source], totals.at[level, source], base[axis] + d,
                base[axis] + source, sibling,
            ).wait_recv()
        value = totals[level, 0]
        for s in range(1, count[axis]):
            value = value + totals[level, s]
        return value

    def memory_moves():
        return (
            (core == 0, pltpu.make_async_copy(mem_in, mem_out.at[pl.ds(0, 1024)], keep_sems.at[4])),
            (
                core == 1,
                pltpu.make_async_copy(mem_in.at[pl.ds(512, 512)], mem_out.at[pl.ds(0, 512)], keep_sems.at[4]),
            ),
            (core == 1, pltpu.make_async_copy(mem_in, mem_out.at[pl.ds(512, 1024)], keep_sems.at[5])),
        )

    def memory_send():
        return remote(mem_in.at[pl.ds(0, 512)], mem_out.at[pl.ds(1024, 512)], 4, 4, sibling)

    spread_total(0, "x", jnp.full((8, 128), tokens.astype(f32)))
    loads[5].wait()
    for condition, copy in memory_moves():
        pl.when(condition)(copy.start)
    pl.when(core == 1)(lambda: memory_send().start())
    sends = []
    keeps = []
    for i, (src, staged, low, mine, others) in enumerate(arrays):
        loads[i].wait()
        low[...] = staged[...].astype(bf16)
        copy = remote(low, others, i, i, sibling)
        copy.start()
        sends.append(copy)
        keep = pltpu.make_async_copy(low, mine, keep_sems.at[i])
        keep.start()
        keeps.append(keep)
        if i < 2:
            spread_total(i + 1, ("y", "z")[i], add_total(i, ("x", "y")[i]))
    loads[4].wait()
    vocab = vh_in.shape[0]
    wh_ref[512:, :] = jnp.zeros((VOC - 512, D), bf16)
    wh_ref[0:vocab, :] = vh_in[...].astype(bf16)
    total_ref[...] = add_total(2, "z")
    for condition, copy in memory_moves():
        pl.when(condition)(copy.wait)
    pl.when(core == 1)(lambda: memory_send().wait_send())
    pl.when(core == 0)(lambda: memory_send().wait_recv())
    for copy in keeps:
        copy.wait()
    for copy in sends:
        copy.wait()
    for copy in pending:
        copy.wait_send()


def run_prepare(dims, lengths, ai, ao, fi, fo, vh, mem):
    hbm = pl.BlockSpec(memory_space=pl.ANY)
    vmem = pl.BlockSpec(memory_space=VMEM)
    weights = [sds(w.shape, bf16) for w in (ai, ao, fi, fo) for _ in range(2)]
    nz, ny, nx = dims
    return pl.pallas_call(
        partial(prepare_kernel, dims),
        in_specs=[pl.BlockSpec(memory_space=pltpu.SMEM)] + [hbm] * 6,
        out_specs=[hbm] * 9 + [vmem, vmem],
        out_shape=weights + [sds((1536, D), bf16), sds((VOC, D), bf16), sds((8, 128), f32)],
        scratch_shapes=[VMEM(w.shape, f32) for w in (ai, ao, fi, fo, vh)]
        + [VMEM(mem.shape, bf16)]
        + [VMEM(w.shape, bf16) for w in (ai, ao, fi, fo)]
        + [
            VMEM((3, max(dims), 8, 128), f32),
            pltpu.SemaphoreType.DMA((6,)), pltpu.SemaphoreType.DMA((6,)),
            pltpu.SemaphoreType.DMA((8 + nx + ny + nz,)), pltpu.SemaphoreType.DMA((8 + nx + ny + nz,)),
        ],
        compiler_params=pltpu.CompilerParams(
            vmem_limit_bytes=60 * MIB, collective_id=1, has_side_effects=True
        ),
        cost_estimate=pl.CostEstimate(flops=10**6, bytes_accessed=24 * MIB, transcendentals=0),
        name="prepare_weights",
    )(lengths, ai, ao, fi, fo, vh, mem)


PIECE = 256
SMALL = 24


def split_two(value):
    high = value.astype(bf16)
    return high, (value - high.astype(f32)).astype(bf16)


class SquareBack:
    def __init__(self, net, low, land):
        self.net, self.low, self.land = net, low, land
        self.axes = (("x", "y"), ("y", "x"))
        self.z_sem = [net.recv_sem(2) for _ in range(2)]
        self.one_sem = [net.recv_sem(2 * OWN) for _ in range(2)]
        self.two_sem = [net.recv_sem(2 * OWN) for _ in range(2)]
        self.valid = net.both(net.inside("x"), net.inside("y"))

    def chunk(self, f):
        first, second = self.axes[f]
        return self.net.clipped(first) * 2 + self.net.clipped(second)

    def rows(self, p):
        return pl.ds(p * 128, 128)

    def start(self, p):
        n = self.net
        for f in range(2):
            owner = n.both(self.valid, n.z == 1 + f)

            def keep(f=f):
                self.land[f, self.chunk(f), self.rows(p), :] = self.low[self.rows(p), :]

            n.on(owner, keep)
            n.spread("z", owner, self.land.at[f, self.chunk(f), self.rows(p)], self.z_sem[f] + p)

    def one(self, p):
        n = self.net
        for f in range(2):
            mine = self.land.at[f, self.chunk(f), self.rows(p)]
            n.landed(n.both(self.valid, n.z != 1 + f), mine, self.z_sem[f] + p)
            second = self.axes[f][1]
            n.spread(second, self.valid, mine, self.one_sem[f] + p * OWN + n.clipped(second))

    def two(self, p):
        n = self.net
        for f in range(2):
            first, second = self.axes[f]
            for s in range(OWN):
                n.landed(
                    n.both(n.inside(first), n.place[second] != s),
                    self.land.at[f, n.clipped(first) * 2 + s, self.rows(p)], self.one_sem[f] + p * OWN + s,
                )
            n.spread(
                first, n.inside(first), self.land.at[f, pl.ds(n.clipped(first) * 2, 2), self.rows(p)],
                self.two_sem[f] + p * OWN + n.clipped(first),
            )

    def end(self):
        n = self.net
        for p in range(2):
            for f in range(2):
                first = self.axes[f][0]
                for s in range(OWN):
                    n.landed(
                        n.place[first] != s, self.land.at[f, pl.ds(s * 2, 2), self.rows(p)],
                        self.two_sem[f] + p * OWN + s,
                    )


class WideBack:
    def __init__(self, net, low, spot, pieces, rows):
        self.net, self.low, self.spot, self.pieces, self.rows = net, low, spot, pieces, rows
        self.axes = (("x", "y"), ("y", "x"))
        self.hop_sem = [net.recv_sem(1) for _ in range(pieces)]
        self.one_sem = [net.recv_sem(1) for _ in range(pieces)]
        self.two_sem = [net.recv_sem(OWN) for _ in range(pieces)]
        self.wide = net.both(net.inside("x"), net.inside("y"), net.x == net.y)
        self.far = jnp.where(net.x == 0, net.z, net.nz - 1 - net.z)
        self.onward = jnp.where(net.x == 0, net.z + 1, net.z - 1)

    def hop(self, k):
        n = self.net
        here = n.both(self.wide, self.far == k)
        for p in range(self.pieces):
            mine = self.spot(n.clipped("x"), p)
            if k == 0:

                def keep(p=p, mine=mine):
                    mine[...] = self.low[pl.ds(p * self.rows, self.rows), :]

                n.on(here, keep)
            else:
                n.landed(here, mine, self.hop_sem[p])
            if k < n.nz - 1:
                n.send(here, mine, mine, self.hop_sem[p], n.at(z=self.onward))

    def one(self):
        n = self.net
        for p in range(self.pieces):
            first, second = self.axes[2 * p // self.pieces]
            n.spread(second, self.wide, self.spot(n.clipped(first), p), self.one_sem[p])

    def two(self):
        n = self.net
        for p in range(self.pieces):
            first, second = self.axes[2 * p // self.pieces]
            mine = self.spot(n.clipped(first), p)
            n.landed(
                n.both(n.inside(first), n.place[first] != n.place[second]), mine, self.one_sem[p]
            )
            n.spread(first, n.inside(first), mine, self.two_sem[p] + n.clipped(first))

    def end(self):
        n = self.net
        for p in range(self.pieces):
            first = self.axes[2 * p // self.pieces][0]
            for m in range(OWN):
                n.landed(n.place[first] != m, self.spot(m, p), self.two_sem[p] + m)


class HeadBack:
    def __init__(self, net, low, land):
        self.net, self.low = net, low
        self.hop_sem, self.one_sem, self.two_sem = net.recv_sem(2), net.recv_sem(2), net.recv_sem(2)
        self.core_sem = net.recv_sem(1)
        self.axes = (("x", "y"), ("y", "x"))
        self.goal = {"x": HEAD_X, "y": HEAD_Y}
        self.spots = [
            land.at[pl.ds(pl.multiple_of(net.core * HROWS + p * HPART, HPART), HPART)] for p in range(2)
        ]
        self.mine = land.at[pl.ds(pl.multiple_of(net.core * HROWS, HROWS), HROWS)]
        self.theirs = land.at[pl.ds(pl.multiple_of((1 - net.core) * HROWS, HROWS), HROWS)]
        self.column = net.both(net.x == HEAD_X, net.y == HEAD_Y)

    def hop(self, k):
        n = self.net
        here = n.both(self.column, n.z == k)
        for p in range(2):
            if k == 0:

                def keep(p=p):
                    self.spots[p][...] = self.low[pl.ds(p * HPART, HPART), :]

                n.on(here, keep)
            else:
                n.landed(here, self.spots[p], self.hop_sem + p)
            if k < n.nz - 1:
                n.send(here, self.spots[p], self.spots[p], self.hop_sem + p, n.at(z=k + 1))

    def one(self):
        n = self.net
        for p in range(2):
            n.spread(self.axes[p][1], self.column, self.spots[p], self.one_sem + p)

    def two(self):
        n = self.net
        for p in range(2):
            first, second = self.axes[p]
            plane = n.place[first] == self.goal[first]
            n.landed(n.both(plane, n.place[second] != self.goal[second]), self.spots[p], self.one_sem + p)
            n.spread(first, plane, self.spots[p], self.two_sem + p)

    def three(self):
        n = self.net
        for p in range(2):
            first = self.axes[p][0]
            n.landed(n.place[first] != self.goal[first], self.spots[p], self.two_sem + p)
        n.send(True, self.mine, self.mine, self.core_sem, n.sibling)

    def end(self):
        self.net.landed(True, self.theirs, self.core_sem)


def muon_kernel(
    dims, gs_ref, wide_ref, headg_ref, na_ref, nf_ref, count_ref, dlow_ref, mi_ref, mo_ref, mu_ref, md_ref, mh_ref,
    ms_all, xs_all, mw_all, q_all, mh_all, xh_all, d_in, small_out,
    acc, core_in, first_in, second_in, band_in, wide_acc, wide_in, head_acc, head_in, small_buf,
    old_turned, old_plain, old_head, own, gram, gram_in, mats, m_low, x_low,
    ms_land, xs_land, mw_land, q_land, mh_land, xh_land,
    send_sems, recv_sems, local_sems,
):
    n = Net(dims, send_sems, recv_sems)
    nz = n.nz
    x, y, z, core = n.x, n.y, n.z, n.core
    on, both = n.on, n.both
    n.barrier()
    valid = both(n.inside("x"), n.inside("y"))
    wide = both(valid, x == y)
    far = jnp.where(x == 0, z, nz - 1 - z)
    inward = jnp.where(x == 0, z - 1, z + 1)
    wide_owner = both(wide, far == 0)
    square = both(valid, jnp.logical_or(z == 1, z == 2))
    task = jnp.where(z == 1, n.clipped("x") * 2 + n.clipped("y"), 4 + n.clipped("y") * 2 + n.clipped("x"))
    head_column = both(x == HEAD_X, y == HEAD_Y)
    head_owner = both(head_column, z == HEAD_Z)
    axes = (("x", "y"), ("y", "x"))

    core_sem = n.recv_sem(4)
    blocks = []
    for k in range(4):
        f = k % 2
        axis = axes[f][0]
        if n.count[axis] == OWN:
            which = 1 - n.place[axis] if k < 2 else n.place[axis]
        else:
            which = k // 2
        blocks.append((f, which * 2))
    own_copies = []
    for k, (f, first) in enumerate(blocks):
        n.send(True, gs_ref.at[1, f, pl.ds(first, 2)], core_in.at[f, pl.ds(first, 2)], core_sem + k, n.sibling)
        own_copies.append(
            pltpu.make_async_copy(gs_ref.at[0, f, pl.ds(first, 2)], acc.at[f, pl.ds(first, 2)], local_sems.at[k])
        )
        own_copies[-1].start()

    def wide_load():
        return pltpu.make_async_copy(wide_ref, wide_acc, local_sems.at[4])

    def head_load():
        return pltpu.make_async_copy(headg_ref, head_acc, local_sems.at[5])

    def old_copies():
        sem = local_sems.at[6]
        return (
            (both(wide_owner, x == 0), lambda: pltpu.make_async_copy(mu_ref, old_turned, sem)),
            (both(wide_owner, x != 0), lambda: pltpu.make_async_copy(md_ref, old_plain, sem)),
            (
                both(square, task < 6),
                lambda: pltpu.make_async_copy(
                    mi_ref.at[jnp.minimum(task, 5)], old_turned.at[:, pl.ds(0, PIECE)], sem
                ),
            ),
            (
                both(square, task >= 6),
                lambda: pltpu.make_async_copy(
                    mo_ref.at[jnp.maximum(task, 6) - 6], old_plain.at[pl.ds(0, PIECE)], sem
                ),
            ),
            (head_owner, lambda: pltpu.make_async_copy(mh_ref, old_head, sem)),
        )

    on(wide, lambda: wide_load().start())
    on(head_column, lambda: head_load().start())
    for condition, copy in old_copies():
        on(condition, lambda copy=copy: copy().start())
    d_sem = n.recv_sem(1)
    n.send(core == 0, dlow_ref, d_in, d_sem, n.sibling)

    on(wide, lambda: wide_load().wait())
    wide_sem = n.recv_sem(4)

    def piece(k):
        return wide_acc.at[k // 2, pl.ds((k % 2) * PIECE, PIECE)]

    def wide_pass(distance, k):
        here = both(wide, far == distance)
        if distance < nz - 1:

            def take():
                n.landed(True, wide_in.at[k], wide_sem + k)
                add_into(piece(k), [wide_in.at[k]], 128)

            on(here, take)
        n.send(here, piece(k), wide_in.at[k], wide_sem + k, n.at(z=inward))

    for k in range(4):
        wide_pass(nz - 1, k)
    on(head_column, lambda: head_load().wait())
    head_sem = n.recv_sem(2)

    def head_pass(distance):
        here = both(head_column, z == distance)
        for p in range(2):
            if distance < nz - 1:

                def take(p=p):
                    n.landed(True, head_in.at[p], head_sem + p)
                    add_into(head_acc.at[p], [head_in.at[p]], HPART)

                on(here, take)
            n.send(here, head_acc.at[p], head_in.at[p], head_sem + p, n.at(z=distance - 1))

    head_pass(nz - 1)

    small_core = n.recv_sem(1)
    small_sem = {axis: n.recv_sem(n.count[axis]) for axis in ("x", "y", "z")}
    small_buf[0, 0] = jnp.zeros((SMALL, VOC), f32)
    small_buf[0, 0, 0:8, 0:D] = na_ref[...]
    small_buf[0, 0, 8:16, 0:D] = nf_ref[...]
    small_buf[0, 0, 16:24, :] = count_ref[...]
    n.send(True, small_buf.at[0, 0], small_buf.at[0, 1], small_core, n.sibling)

    def small_go(level, axis, value):
        small_buf[level, n.place[axis]] = value
        n.spread(axis, True, small_buf.at[level, n.place[axis]], small_sem[axis] + n.place[axis])

    def small_add(level, axis):
        for d in range(1, n.count[axis]):
            source = n.further(axis, d)
            n.landed(True, small_buf.at[level, source], small_sem[axis] + source)
        total = small_buf[level, 0]
        for s in range(1, n.count[axis]):
            total = total + small_buf[level, s]
        return total

    first_sem = [n.recv_sem(2 * (n.count[axes[f][0]] - 1)) for f in range(2)]
    second_sem = [n.recv_sem(2 * (n.count[axes[f][1]] - 1)) for f in range(2)]

    def half_rows(p):
        return pl.ds(p * 128, 128)

    def start_first(f, p):
        axis = axes[f][0]
        for d in range(1, n.count[axis]):
            target = jnp.minimum(n.further(axis, d), OWN - 1)
            n.send(
                n.goes_inside(axis, d), acc.at[f, pl.ds(target * 2, 2), half_rows(p)],
                first_in.at[f, d - 1, :, half_rows(p)], first_sem[f] + 2 * (d - 1) + p,
                n.at(**{axis: n.further(axis, d)}),
            )

    for k, (f, first) in enumerate(blocks):
        n.landed(True, core_in.at[f, pl.ds(first, 2)], core_sem + k)
        own_copies[k].wait()
        for j in range(2):
            add_into(acc.at[f, first + j], [core_in.at[f, first + j]], 128)
        if n.nx == OWN and n.ny == OWN:
            if k < 2:
                start_first(f, 0)
                start_first(f, 1)
        elif k == 3:
            for p in range(2):
                start_first(0, p)
                start_first(1, p)
    n.landed(True, small_buf.at[0, 1], small_core)
    small_go(1, "x", small_buf[0, 0] + small_buf[0, 1])
    wide_pass(2, 0)
    wide_pass(2, 1)
    wide_pass(1, 0)
    head_pass(2)
    for p in range(2):
        for f in range(2):
            first, second = axes[f]
            mine = n.clipped(first) * 2

            def take(f=f, p=p, first=first, mine=mine):
                for d in range(1, n.count[first]):
                    n.landed(True, first_in.at[f, d - 1, :, half_rows(p)], first_sem[f] + 2 * (d - 1) + p)
                for j in range(2):
                    add_into(
                        acc.at[f, mine + j, half_rows(p)],
                        [first_in.at[f, d - 1, j, half_rows(p)] for d in range(1, n.count[first])], 128,
                    )

            on(n.inside(first), take)
            for d in range(1, n.count[second]):
                target = jnp.minimum(n.further(second, d), OWN - 1)
                n.send(
                    both(n.inside(first), n.goes_inside(second, d)), acc.at[f, mine + target, half_rows(p)],
                    second_in.at[f, d - 1, half_rows(p)], second_sem[f] + 2 * (d - 1) + p,
                    n.at(**{second: n.further(second, d)}),
                )
    small_go(2, "y", small_add(1, "x"))
    wide_pass(2, 2)
    wide_pass(2, 3)
    wide_pass(1, 1)
    wide_pass(1, 2)
    head_pass(1)

    def chunk(f):
        first, second = axes[f]
        return n.clipped(first) * 2 + n.clipped(second)

    band_sem = [n.recv_sem(2 * (nz - 1)) for _ in range(2)]
    for p in range(2):
        for f in range(2):
            second = axes[f][1]

            def take_second(f=f, p=p, second=second):
                for d in range(1, n.count[second]):
                    n.landed(True, second_in.at[f, d - 1, half_rows(p)], second_sem[f] + 2 * (d - 1) + p)
                add_into(
                    acc.at[f, chunk(f), half_rows(p)],
                    [second_in.at[f, d - 1, half_rows(p)] for d in range(1, n.count[second])], 128,
                )

            on(valid, take_second)
            for d in range(1, nz):
                n.send(
                    both(valid, z == (1 + f + d) % nz), acc.at[f, chunk(f), half_rows(p)],
                    band_in.at[d - 1, half_rows(p)], band_sem[f] + 2 * (d - 1) + p, n.at(z=1 + f),
                )
    small_go(3, "z", small_add(2, "y"))
    wide_pass(1, 3)

    own[...] = jnp.zeros_like(own)
    for condition, copy in old_copies():
        on(condition, lambda copy=copy: copy().wait())

    def turned(k):
        return jnp.swapaxes(old_turned[:, k * PIECE : (k + 1) * PIECE], 0, 1)

    def finish_wide(k, old):
        own[pl.ds(k * PIECE, PIECE), :] = piece(k)[...].astype(f32) + wide_in[k].astype(f32) + 0.5 * old

    for k in range(4):
        n.landed(wide_owner, wide_in.at[k], wide_sem + k)
        on(both(wide_owner, x == 0), lambda k=k: finish_wide(k, turned(k)))
        on(both(wide_owner, x != 0), lambda k=k: finish_wide(k, old_plain[pl.ds(k * PIECE, PIECE), :]))
    for p in range(2):
        n.landed(head_owner, head_in.at[p], head_sem + p)

    def finish_head():
        old_plain[pl.ds(512, 128), :] = jnp.zeros((128, D), f32)
        old_plain[pl.ds(0, old_head.shape[0]), :] = old_head[...]
        for p in range(2):
            here = pl.ds(pl.multiple_of(core * HROWS + p * HPART, HPART), HPART)
            total = head_acc[p].astype(f32) + head_in[p].astype(f32)
            own[pl.ds(p * HPART, HPART), :] = total + 0.5 * old_plain[here, :]

    on(head_owner, finish_head)

    def finish_square(old):
        f = z - 1
        mine = jnp.where(z == 1, chunk(0), chunk(1))
        total = acc[f, mine].astype(f32)
        for d in range(1, nz):
            total = total + band_in[d - 1].astype(f32)
        own[pl.ds(0, PIECE), :] = total + 0.5 * old

    for f in range(2):
        for d in range(1, nz):
            for p in range(2):
                n.landed(both(valid, z == 1 + f), band_in.at[d - 1, half_rows(p)], band_sem[f] + 2 * (d - 1) + p)
    on(both(square, task < 6), lambda: finish_square(turned(0)))
    on(both(square, task >= 6), lambda: finish_square(old_plain[pl.ds(0, PIECE), :]))
    m_low[...] = own[...].astype(bf16)

    back_ms = SquareBack(n, m_low, ms_land)
    back_mw = WideBack(
        n, m_low, lambda m, p: mw_land.at[m, p // 2, pl.ds((p % 2) * PIECE, PIECE)], 4, PIECE
    )
    back_mh = HeadBack(n, m_low, mh_land)
    back_xs = SquareBack(n, x_low, xs_land)
    back_q = WideBack(n, x_low, lambda m, p: q_land.at[m, core, p], 2, 128)
    back_xh = HeadBack(n, x_low, xh_land)
    back_ms.start(0)
    back_ms.start(1)
    back_mw.hop(0)
    back_mh.hop(0)

    blocks_used = jnp.where(wide_owner, 4, jnp.where(head_owner, 2, 1))
    gram[...] = jnp.zeros_like(gram)

    def gram_step(i, carry):
        high, low = split_two(own[pl.ds(pl.multiple_of(i * PIECE, PIECE), PIECE), :])
        gram[...] += mm_tn(high, high) + (mm_tn(high, low) + mm_tn(low, high))
        return carry

    lax.fori_loop(0, blocks_used, gram_step, 0)
    gram_sem = n.recv_sem(1)
    n.send(True, gram, gram_in, gram_sem, n.sibling)
    back_mw.hop(1)
    back_mh.hop(1)
    small_out[...] = small_add(3, "z")
    n.landed(True, gram_in, gram_sem)

    def eye_rows(first, rows):
        place = lax.broadcasted_iota(jnp.int32, (rows, D), 0) + first
        return (place == lax.broadcasted_iota(jnp.int32, (rows, D), 1)).astype(f32)

    def put(m, value):
        high, low = split_two(value)
        mats[m, 0] = high
        mats[m, 1] = low

    def product(a, b):
        ah, al = mats[a, 0], mats[a, 1]
        left_h, left_l = mats[b, 0, :, 0:256], mats[b, 1, :, 0:256]
        left = mm(ah, left_h) + (mm(ah, left_l) + mm(al, left_h))
        right_h, right_l = mats[b, 0, :, 256:512], mats[b, 1, :, 256:512]
        corner = mm(ah[256:], right_h) + (mm(ah[256:], right_l) + mm(al[256:], right_h))
        right = jnp.concatenate([jnp.swapaxes(left[256:], 0, 1), corner], axis=0)
        return jnp.concatenate([left, right], axis=1)

    both_halves = gram[...] + gram_in[...]
    total = jnp.sum(jnp.sum(both_halves * eye_rows(0, D), axis=0, keepdims=True), axis=1, keepdims=True)
    scale = 1.0 / (jnp.sqrt(total) + 1e-07)
    put(0, both_halves * scale * scale)
    for iteration in range(NS_STEPS):
        q_now, q_next = (2, 4) if iteration % 2 == 0 else (4, 2)
        a = mats[0, 0].astype(f32) + mats[0, 1].astype(f32)
        put(1, NS_A * eye_rows(0, D) + NS_B * a + NS_C * product(0, 0))
        if iteration == 0:
            mats[q_next] = mats[1]
        else:
            put(q_next, product(1, q_now))
        if iteration < NS_STEPS - 1:
            put(3, product(0, 1))
            put(0, product(3, 1))
        if iteration == 0:
            back_ms.one(0)
            back_ms.one(1)
            back_mw.hop(2)
            back_mh.hop(2)
        if iteration == 1:
            back_ms.two(0)
            back_ms.two(1)
            back_mw.hop(3)
            back_mh.hop(3)
            back_mh.one()
        if iteration == 2:
            back_mw.one()
            back_mh.two()
        if iteration == 3:
            back_mw.two()
            back_mh.three()

    last = 4 if NS_STEPS % 2 == 1 else 2

    def direction(first, rows):
        part = pl.ds(first, rows)
        high, low = split_two(own[part, :] * scale)
        value = mm(high, mats[last, 0]) + (mm(high, mats[last, 1]) + mm(low, mats[last, 0]))
        x_low[part, :] = value.astype(bf16)

    def wide_polynomial():
        rows = pl.ds(pl.multiple_of(core * PIECE, PIECE), PIECE)
        value = mats[last, 0, rows, :].astype(f32) + mats[last, 1, rows, :].astype(f32)
        x_low[pl.ds(0, PIECE), :] = (value * scale).astype(bf16)

    on(wide_owner, wide_polynomial)
    on(head_owner, partial(direction, 0, 512))
    on(square, partial(direction, 0, 128))
    back_xs.start(0)
    on(square, partial(direction, 128, 128))
    back_xs.start(1)
    back_q.hop(0)
    back_xh.hop(0)
    back_q.hop(1)
    back_xh.hop(1)
    back_ms.end()
    back_mh.end()
    outs = [
        pltpu.make_async_copy(src, dst, local_sems.at[i])
        for i, (src, dst) in enumerate(
            (
                (ms_land, ms_all), (mh_land, mh_all), (mw_land, mw_all), (xs_land, xs_all), (q_land, q_all),
                (xh_land, xh_all),
            )
        )
    ]
    outs[0].start()
    outs[1].start()
    back_xs.one(0)
    back_q.hop(2)
    back_xh.hop(2)
    back_xs.one(1)
    back_q.hop(3)
    back_q.one()
    back_xs.two(0)
    back_xh.hop(3)
    back_xh.one()
    back_xs.two(1)
    back_q.two()
    back_xh.two()
    back_mw.end()
    outs[2].start()
    back_q.end()
    q_sem = n.recv_sem(2)
    for m in range(2):
        n.send(True, q_land.at[m, core], q_land.at[m, core], q_sem + m, n.sibling)
    back_xh.three()
    back_xs.end()
    outs[3].start()
    for m in range(2):
        n.landed(True, q_land.at[m, 1 - core], q_sem + m)
    outs[4].start()
    back_xh.end()
    outs[5].start()
    n.landed(core == 1, d_in, d_sem)
    n.all_sent()
    for copy in outs:
        copy.wait()


def run_muon(dims, gs, wide, headg, na, nf, count, dlow, mi, mo, mu, md, mh):
    nz, ny, nx = dims
    hbm = pl.BlockSpec(memory_space=pl.ANY)
    vmem = pl.BlockSpec(memory_space=VMEM)
    slots = max(nx, ny) - 1
    most = max(nx, ny, nz, 2)
    squares = (2, 4, PIECE, D)
    lands = [squares, squares, (2, 2, 512, D), (2, 2, 2, 128, D), (VOC, D), (VOC, D)]
    return pl.pallas_call(
        partial(muon_kernel, dims),
        in_specs=[hbm] * 3 + [vmem] * 3 + [hbm] * 6,
        out_specs=[hbm] * 7 + [vmem],
        out_shape=[sds(s, bf16) for s in lands] + [sds((512, D), bf16), sds((SMALL, VOC), f32)],
        scratch_shapes=[
            VMEM(squares, bf16),
            VMEM(squares, bf16),
            VMEM((2, slots, 2, PIECE, D), bf16),
            VMEM((2, slots, PIECE, D), bf16),
            VMEM((nz - 1, PIECE, D), bf16),
            VMEM((2, 512, D), bf16),
            VMEM((4, PIECE, D), bf16),
            VMEM((2, HPART, D), bf16),
            VMEM((2, HPART, D), bf16),
            VMEM((4, most, SMALL, VOC), f32),
            VMEM((D, 1024), f32),
            VMEM((1024, D), f32),
            VMEM(mh.shape, f32),
            VMEM((1024, D), f32),
            VMEM((D, D), f32),
            VMEM((D, D), f32),
            VMEM((5, 2, D, D), bf16),
            VMEM((1024, D), bf16),
            VMEM((512, D), bf16),
        ]
        + [VMEM(s, bf16) for s in lands]
        + [
            pltpu.SemaphoreType.DMA((400,)), pltpu.SemaphoreType.DMA((160,)), pltpu.SemaphoreType.DMA((8,)),
        ],
        compiler_params=pltpu.CompilerParams(
            vmem_limit_bytes=60 * MIB, collective_id=0, has_side_effects=True
        ),
        cost_estimate=pl.CostEstimate(flops=20 * 10**9, bytes_accessed=40 * MIB, transcendentals=0),
        name="reduce_muon_spread",
    )(gs, wide, headg, na, nf, count, dlow, mi, mo, mu, md, mh)


def finish_kernel(
    wide_rate, head_rate, core_ref,
    mu, md, mb, q_ref, xb, mh, xh, ai, ao, fi, fo, vh, small, gain, bias, nm, dm, dr,
    mi_out, ni_out, mo_out, no_out, mu_out, nu_out, md_out, nd_out, mh_out, nh_out,
    mn_out, nn_out, counts_out, dm_out,
):
    i = pl.program_id(0)
    same = lax.broadcasted_iota(jnp.int32, (D, D), 0) == lax.broadcasted_iota(jnp.int32, (D, D), 1)
    eye = same.astype(f32).astype(bf16)
    mu_out[...] = mm_nt(eye, mu[0, 0])
    nu_out[...] = fi[...] - wide_rate * mm_nt(q_ref[0], mu[0, 0])
    md_out[...] = md[0, 0].astype(f32)
    nd_out[...] = fo[...] - wide_rate * mm(md[0, 0], q_ref[1])

    @pl.when(i < 6)
    def _():
        mi_out[0] = mm_nt(eye, mb[0, 0])
        ni_out[0] = ai[0] - muon_rate * mm_nt(eye, xb[0, 0])

    @pl.when(i >= 6)
    def _():
        mo_out[0] = mb[0, 0].astype(f32)
        no_out[0] = ao[0] - muon_rate * xb[0, 0].astype(f32)

    dm_out[...] = jnp.where((core_ref[0] == 0) | (i >= 4), dm[...], dr[...].astype(f32))

    @pl.when(i == 0)
    def _():
        vocab = vh.shape[0]
        mh_out[...] = mh[0:vocab, :].astype(f32)
        nh_out[...] = vh[...] - head_rate * xh[0:vocab, :].astype(f32)
        for kind, old in enumerate((gain, bias)):
            first = 2 * kind
            total = jnp.concatenate([small[first : first + 2, 0:D], small[first + 8 : first + 10, 0:D]], axis=0)
            moment = 0.5 * nm[kind] + total
            mn_out[kind] = moment
            nn_out[kind] = old[...] - vector_rate * moment * lax.rsqrt(
                jnp.mean(moment * moment, axis=-1, keepdims=True) + 1e-06
            )
        counts_out[...] = small[16:17, 0:vocab].astype(jnp.int32)


def run_finish(core, ms, xs, mw, q, m_head, x_head, ai, ao, fi, fo, vh, small, gain, bias, nm, dmem, d_in):
    vocab = vh.shape[0]
    wide_rate = muon_rate * math.sqrt(2 * fi.shape[1] / D)
    head_rate = muon_rate * math.sqrt(vocab / D)

    def spec(shape, index):
        return pl.BlockSpec(shape, index)

    def fixed(shape):
        return pl.BlockSpec(shape, lambda i, c: (0,) * len(shape))

    up = spec((1, 1, 128, D), lambda i, c: (0, i // 4, i % 4, 0))
    down = spec((1, 1, 128, D), lambda i, c: (1, i // 4, i % 4, 0))
    bands = spec((1, 1, 256, D), lambda i, c: (i // 4, i % 4, 0, 0))
    inner = spec((1, D, 256), lambda i, c: (jnp.minimum(i, 5), 0, 0))
    outer = spec((1, 256, D), lambda i, c: (jnp.maximum(i, 6) - 6, 0, 0))
    cols = spec((D, 128), lambda i, c: (0, i))
    rows = spec((128, D), lambda i, c: (i, 0))
    head = fixed((vocab, D))
    shapes = [
        (sds((6, D, 256), f32), inner), (sds((6, D, 256), f32), inner),
        (sds((2, 256, D), f32), outer), (sds((2, 256, D), f32), outer),
        (sds(fi.shape, f32), cols), (sds(fi.shape, f32), cols),
        (sds(fo.shape, f32), rows), (sds(fo.shape, f32), rows),
        (sds((vocab, D), f32), head), (sds((vocab, D), f32), head),
        (sds((2, 4, D), f32), fixed((2, 4, D))), (sds((2, 4, D), f32), fixed((2, 4, D))),
        (sds((1, vocab), jnp.int32), fixed((1, vocab))),
        (sds((1024, D), f32), rows),
    ]
    return pl.pallas_call(
        partial(finish_kernel, wide_rate, head_rate),
        grid_spec=pltpu.PrefetchScalarGridSpec(
            num_scalar_prefetch=1,
            grid=(8,),
            in_specs=[
                up, down, bands, fixed((2, D, D)), bands, fixed((VOC, D)), fixed((VOC, D)),
                inner, outer, cols, rows, head, fixed((SMALL, VOC)), fixed((4, D)), fixed((4, D)), fixed((2, 4, D)),
                spec((128, D), lambda i, c: (jnp.where(c[0] == 0, i, jnp.maximum(i - 4, 0)), 0)),
                spec((128, D), lambda i, c: (jnp.minimum(i, 3), 0)),
            ],
            out_specs=[s[1] for s in shapes],
        ),
        out_shape=[s[0] for s in shapes],
        compiler_params=pltpu.CompilerParams(vmem_limit_bytes=60 * MIB),
        cost_estimate=pl.CostEstimate(flops=10**7, bytes_accessed=40 * MIB, transcendentals=0),
        name="finish_weights",
    )(core, mw, mw, ms, q.reshape(2, D, D), xs, m_head, x_head, ai, ao, fi, fo, vh, small,
      gain, bias, nm, dmem, d_in)


def local(
    residual_in, memory, lengths, targets, attn_in, attn_out, ffn_in, ffn_out, vocab_head,
    norm_gain, norm_bias, attn_in_moment, attn_out_moment, ffn_in_moment, ffn_out_moment,
    head_moment, norm_moment,
):
    dims = chip_dims(lax.axis_size("dp"))
    core = lax.axis_index("mp")
    tokens = residual_in.shape[0] * lax.axis_size("mp") * lax.axis_size("dp")
    vocab = vocab_head.shape[1]
    inner = attn_in.reshape(6, D, 256)
    wa0, wa1, wo0, wo1, wi0, wi1, wf0, wf1, mem, wh, total = run_prepare(
        dims, lengths, inner, attn_out, ffn_in, ffn_out, vocab_head.T, memory
    )
    wa, wo, wi, wf = (wa0, wa1), (wo0, wo1), (wi0, wi1), (wf0, wf1)
    h1, qkv, p, o, x1, h2, cq, kv, pc, oc, x2 = run_forward(
        lengths, residual_in, mem, wa, wo, norm_gain, norm_bias
    )
    out, g2, gw, ghead, gnorm_ffn, counts = run_middle(
        lengths, total, x2, targets[:, None], wi, wf, wh, norm_gain, norm_bias, vocab, float(tokens)
    )
    dx, dmem, dlow, gs, gnorm_attn, wide, head_part = run_backward(
        dims, g2, residual_in, x1, h1, qkv, p, o, h2, cq, kv, pc, oc, mem, wa, wo, norm_gain, gw, ghead
    )
    ms, xs, mw, q, head_m, head_x, d_in, small = run_muon(
        dims, gs, wide, head_part, gnorm_attn, gnorm_ffn, counts, dlow,
        attn_in_moment.reshape(6, D, 256), attn_out_moment, ffn_in_moment, ffn_out_moment, head_moment.T,
    )
    (
        moment_in, new_in, moment_out, new_out, moment_up, new_up, moment_down, new_down,
        moment_head, new_head, moment_norms, new_norms, token_counts, memory_grad,
    ) = run_finish(
        core.reshape(1), ms, xs, mw, q, head_m, head_x, inner, attn_out, ffn_in, ffn_out,
        vocab_head.T, small, norm_gain, norm_bias, norm_moment, dmem, d_in,
    )
    return (
        out, dx, memory_grad, moment_in.reshape(attn_in.shape), new_in.reshape(attn_in.shape),
        moment_out, new_out, moment_up, new_up, moment_down, new_down, moment_head.T, new_head.T,
        moment_norms, new_norms,
        token_counts.reshape(vocab),
    )


def solution(mesh):
    rows = P(("dp", "mp"), None)
    placed = (
        rows, rows, P("dp"), P(("dp", "mp")),
        P(None, None, None, "mp"), P(None, "mp", None), P(None, "mp"), P("mp", None), P(), P(), P(),
        P(None, None, None, "mp"), P(None, "mp", None), P(None, "mp"), P("mp", None), P(), P(),
    )
    return jax.shard_map(
        local,
        mesh=mesh,
        in_specs=placed,
        out_specs=(
            rows, rows, rows,
            P(None, None, None, "mp"), P(None, None, None, "mp"),
            P(None, "mp", None), P(None, "mp", None),
            P(None, "mp"), P(None, "mp"), P("mp", None), P("mp", None),
            P(), P(), P(), P(), P(),
        ),
        check_vma=False,
    )
```

```python
from functools import partial
import math

import jax
import jax.numpy as jnp
from jax import lax
from jax.experimental import pallas as pl
from jax.experimental.pallas import tpu as pltpu
from jax.sharding import PartitionSpec as P

HEAD = 64
CAP_S = 64
CAP_M = 128
CAP_L = 256
MEM = 128
SETS = 4
NS_STEPS = 5
NS_A = 3.4445
NS_B = -4.775
NS_C = 2.0315
muon_rate = 0.5
vector_rate = 0.05

D = 512
BLK = 256
WIDE = 512
VOC = 640
HROWS = 320
HPART = 160
MIB = 1024 * 1024
bf16 = jnp.bfloat16
f32 = jnp.float32
VMEM = pltpu.VMEM


def mm(a, b):
    return jnp.dot(a, b, preferred_element_type=f32)


def mm_nt(a, b):
    return lax.dot_general(a, b, (((1,), (1,)), ((), ())), preferred_element_type=f32)


def mm_tn(a, b):
    return lax.dot_general(a, b, (((0,), (0,)), ((), ())), preferred_element_type=f32)


def norm_stats(value):
    average = jnp.mean(value, axis=-1, keepdims=True)
    centred = value - average
    variance = jnp.mean(centred * centred, axis=-1, keepdims=True)
    inverse = lax.rsqrt(variance + 1e-05)
    return centred * inverse, inverse


def norm_back(gradient, normed, inverse, gain):
    scaled = gradient * gain
    return inverse * (
        scaled
        - jnp.mean(scaled, axis=-1, keepdims=True)
        - normed * jnp.mean(scaled * normed, axis=-1, keepdims=True)
    )


def lane_masks(width):
    lanes = lax.broadcasted_iota(jnp.int32, (1, width), 1)
    return [(lanes // HEAD == h).astype(f32).astype(bf16) for h in range(width // HEAD)]


def spread(block, masks):
    return jnp.concatenate([block * m for m in masks], axis=0)


def pick(stacked, masks, rows):
    total = stacked[:rows] * masks[0].astype(f32)
    for h in range(1, len(masks)):
        total = total + stacked[h * rows : (h + 1) * rows] * masks[h].astype(f32)
    return total


def softmax_rows(scores):
    top = jnp.max(scores, axis=-1, keepdims=True)
    exps = jnp.exp(scores - top)
    return exps * (1.0 / jnp.sum(exps, axis=-1, keepdims=True))


def mem_slot(core, block, unit):
    on_first = jnp.where(block < 2, 4 * block + unit, 8 + 2 * (block - 2) + unit // 2)
    return jnp.where(core == 0, on_first, block)


def row_limits(core, block, lengths_ref):
    unit = lax.broadcasted_iota(jnp.int32, (BLK, 1), 0) // CAP_S
    low = jnp.zeros((BLK, 1), jnp.int32)
    length = jnp.zeros((BLK, 1), jnp.int32)
    for u in range(BLK // CAP_S):
        on_first = jnp.where(block < 2, u * CAP_S, u // 2 * CAP_M)
        slot = mem_slot(core, block, u) + jnp.where(core == 0, 0, 3 * SETS)
        low = jnp.where(unit == u, jnp.where(core == 0, on_first, 0), low)
        length = jnp.where(unit == u, lengths_ref[slot], length)
    return low, length


def rows_live(core, first, blocks, lengths_ref):
    pieces = []
    for j in range(blocks):
        low, length = row_limits(core, first + j, lengths_ref)
        place = lax.broadcasted_iota(jnp.int32, (BLK, 1), 0)
        pieces.append((place - low < length).astype(f32))
    return jnp.concatenate(pieces, axis=0)


def forward_kernel(
    lengths_ref, x_ref, mem_ref, wa0, wa1, wo0, wo1, gain_ref, bias_ref,
    h1_ref, qkv_ref, p_ref, o_ref, x1_ref, h2_ref, cq_ref, kv_ref, pc_ref, oc_ref, x2_ref,
):
    core = lax.axis_index("mp")
    step = pl.program_id(0)
    wa = (wa0, wa1)

    @pl.when(step == 0)
    def _():
        def fill(i, carry):
            rows = pl.ds(pl.multiple_of(i * WIDE, WIDE), WIDE)
            for half in range(2):
                for which in range(2):
                    kv_ref[rows, pl.ds(which * D + half * 256, 256)] = mm(
                        mem_ref[rows, :], wa[half][4 + which]
                    ).astype(bf16)
            return carry

        lax.fori_loop(0, jnp.where(core == 0, 3, 1), fill, 0)

    normed, _ = norm_stats(x_ref[...].astype(f32))
    h1_ref[...] = (normed * gain_ref[0:1, :] + bias_ref[0:1, :]).astype(bf16)
    for half in range(2):
        for which in range(3):
            qkv_ref[:, pl.ds(which * D + half * 256, 256)] = mm(h1_ref[...], wa[half][which]).astype(bf16)
    pair = lane_masks(128)
    for j in range(WIDE // BLK):
        rows = pl.ds(j * BLK, BLK)
        low, length = row_limits(core, step * (WIDE // BLK) + j, lengths_ref)
        keys = lax.broadcasted_iota(jnp.int32, (BLK, BLK), 1)
        queries = lax.broadcasted_iota(jnp.int32, (BLK, BLK), 0)
        allowed = (keys >= low) & (keys < low + length) & (keys <= queries)
        for i in range(4):
            q = qkv_ref[rows, pl.ds(i * 128, 128)] * jnp.bfloat16(0.125)
            k = qkv_ref[rows, pl.ds(D + i * 128, 128)]
            v = qkv_ref[rows, pl.ds(2 * D + i * 128, 128)]
            scores = mm_nt(spread(q, pair), k).reshape(2, BLK, BLK)
            scores = jnp.where(allowed[None], scores, -1000000000.0)
            probs = softmax_rows(scores).astype(bf16).reshape(2 * BLK, BLK)
            p_ref[j, i] = probs
            o_ref[rows, pl.ds(i * 128, 128)] = pick(mm(probs, v), pair, BLK).astype(bf16)
    x1 = x_ref[...].astype(f32) + mm(o_ref[:, :256], wo0[0]) + mm(o_ref[:, 256:], wo1[0])
    x1_ref[...] = x1
    normed, _ = norm_stats(x1)
    h2_ref[...] = (normed * gain_ref[1:2, :] + bias_ref[1:2, :]).astype(bf16)
    for half in range(2):
        cq_ref[:, pl.ds(half * 256, 256)] = mm(h2_ref[...], wa[half][3]).astype(bf16)
    quad = lane_masks(256)
    for u in range(WIDE // 64):
        rows = pl.ds(u * 64, 64)
        block = step * (WIDE // BLK) + u // 4
        slot = pl.ds(pl.multiple_of(mem_slot(core, block, u % 4) * MEM, MEM), MEM)
        for j in range(2):
            q = cq_ref[rows, pl.ds(j * 256, 256)] * jnp.bfloat16(0.125)
            k = kv_ref[slot, pl.ds(j * 256, 256)]
            v = kv_ref[slot, pl.ds(D + j * 256, 256)]
            probs = softmax_rows(mm_nt(spread(q, quad), k)).astype(bf16)
            pc_ref[u // 4, u % 4 * 2 + j] = probs
            oc_ref[rows, pl.ds(j * 256, 256)] = pick(mm(probs, v), quad, 64).astype(bf16)
    x2_ref[...] = x1_ref[...] + mm(oc_ref[:, :256], wo0[1]) + mm(oc_ref[:, 256:], wo1[1])


def gelu_parts(u):
    z = jnp.abs(u) * math.sqrt(0.5 / math.log(2.0))
    below = 1.0 + (0.3275911 * math.sqrt(math.log(2.0))) * z
    guess = pl.reciprocal(below, approx=True)
    t = guess * (2.0 - below * guess)
    gauss = jnp.exp2(-(z * z))
    tail = gauss * (
        t * (0.127414796 + t * (-0.142248368 + t * (0.7107068705 + t * (-0.7265760135 + t * 0.5307027145))))
    )
    cdf = jnp.where(u < 0, tail, 1.0 - tail)
    return u * cdf, cdf + u * (gauss * (1.0 / math.sqrt(2.0 * math.pi)))


def middle_kernel(
    vocab, tokens, lengths_ref, total_ref, x2_ref, targets_ref, wi0, wi1, wf0, wf1, wh_ref, gain_ref, bias_ref,
    out_ref, g2_ref, gw_ref, ghead_ref, gnorm_ref, count_ref,
    h3_all, a_all, dy_all, du_all, z_all, gl_all, slope,
):
    block = pl.program_id(0)
    rows = pl.ds(pl.multiple_of(block * WIDE, WIDE), WIDE)
    wi = (wi0, wi1)
    wf = (wf0, wf1)
    x2 = x2_ref[...]
    normed2, inverse2 = norm_stats(x2)
    h3 = (normed2 * gain_ref[2:3, :] + bias_ref[2:3, :]).astype(bf16)
    h3_all[rows, :] = h3
    for half in range(2):
        for j in range(2):
            wide = pl.ds(half * 1024 + j * 512, 512)
            active, grad = gelu_parts(mm(h3, wi[half][:, j * 512 : (j + 1) * 512]))
            a_all[rows, wide] = active.astype(bf16)
            slope[:, wide] = grad
    x3 = x2_ref[...] + mm(a_all[rows, 0:1024], wf0[...]) + mm(a_all[rows, 1024:2048], wf1[...])
    out_ref[...] = x3.astype(bf16)
    normed3, inverse3 = norm_stats(x3)
    z = (normed3 * gain_ref[3:4, :] + bias_ref[3:4, :]).astype(bf16)
    z_all[rows, :] = z
    logits = mm_nt(z, wh_ref[...])
    columns = lax.broadcasted_iota(jnp.int32, (WIDE, VOC), 1)
    logits = jnp.where(columns < vocab, logits, -1e30)
    probs = softmax_rows(logits)
    onehot = (columns == targets_ref[...]).astype(f32)
    live = rows_live(lax.axis_index("mp"), block * (WIDE // BLK), WIDE // BLK, lengths_ref)
    gl = (tokens / total_ref[0:1, 0:1] * live * (probs - onehot)).astype(bf16)
    gl_all[rows, :] = gl
    counts = jnp.sum(onehot * live, axis=0, keepdims=True)
    gz = mm(gl, wh_ref[...])
    gain3 = jnp.sum(gz * normed3, axis=0, keepdims=True)
    bias3 = jnp.sum(gz, axis=0, keepdims=True)
    g3 = norm_back(gz, normed3, inverse3, gain_ref[3:4, :])
    dy = g3.astype(bf16)
    dy_all[rows, :] = dy
    g2_ref[...] = g3
    for half in range(2):
        for j in range(2):
            wide = pl.ds(half * 1024 + j * 512, 512)
            back = mm_nt(dy, wf[half][j * 512 : (j + 1) * 512, :])
            du_all[rows, wide] = (slope[:, wide] * back).astype(bf16)
    dh = mm_nt(du_all[rows, 0:1024], wi0[...]) + mm_nt(du_all[rows, 1024:2048], wi1[...])
    normed2, inverse2 = norm_stats(x2_ref[...])
    gain2 = jnp.sum(dh * normed2, axis=0, keepdims=True)
    bias2 = jnp.sum(dh, axis=0, keepdims=True)
    g2_ref[...] = g2_ref[...] + norm_back(dh, normed2, inverse2, gain_ref[2:3, :])

    @pl.when(block == 0)
    def _():
        gnorm_ref[...] = jnp.zeros_like(gnorm_ref)
        count_ref[...] = jnp.zeros_like(count_ref)

    gnorm_ref[0:1, :] += gain2
    gnorm_ref[1:2, :] += gain3
    gnorm_ref[2:3, :] += bias2
    gnorm_ref[3:4, :] += bias3
    count_ref[0:1, :] += counts

    @pl.when(block == pl.num_programs(0) - 1)
    def _():
        for half in range(2):
            for j in range(2):
                col = pl.ds(half * 1024 + j * 512, 512)
                gw_ref[half, 0, j] = mm_tn(du_all[:, col], h3_all[...]).astype(bf16)
                gw_ref[half, 1, j] = mm_tn(a_all[:, col], dy_all[...]).astype(bf16)
        ghead_ref[...] = mm_tn(gl_all[...], z_all[...]).astype(bf16)


def attend_back(queries, keys, values, probs, grads, masks, rows):
    q = spread(queries, masks)
    do = spread(grads, masks)
    dprobs = mm_nt(do, values)
    p = probs.astype(f32)
    weighted = p * dprobs
    ds = (weighted - p * jnp.sum(weighted, axis=-1, keepdims=True)).astype(bf16)
    dv = mm_tn(probs, do)
    dq = pick(mm(ds, keys), masks, rows) * 0.125
    dk = mm_tn(ds, q) * 0.125
    return dq, dk, dv


def backward_kernel(
    dims, g2_ref, x_ref, x1_ref, h1_ref, qkv_ref, p_ref, o_ref, h2_ref, cq_ref, kv_ref, pc_ref, oc_ref,
    mem_ref, wa0, wa1, wo0, wo1, gain_ref, gw_ref, ghead_ref,
    dx_ref, dmem_ref, dlow_ref, gs_ref, gnorm_ref, wide_out, head_out,
    dyc_all, dcq_all, dys_all, dqkv_all, dkv_all, dkv_low,
    early_acc, early_core, early_first, early_second, head_acc, head_core, head_first, head_second,
    gs_away, gs_in, send_sems, recv_sems, local_sems,
):
    core = lax.axis_index("mp")
    block = pl.program_id(0)
    early = EarlySum(
        Net(dims, send_sems, recv_sems), gw_ref, ghead_ref, wide_out, head_out,
        (
            early_acc, early_core, early_first, early_second, head_acc, head_core, head_first, head_second,
            local_sems,
        ),
    )
    band_sem = early.net.recv_sem(4)
    pl.when(block == 0)(early.start)
    rows = pl.ds(pl.multiple_of(block * BLK, BLK), BLK)
    wa = (wa0, wa1)
    wo = (wo0, wo1)

    @pl.when(block == 0)
    def _():
        gnorm_ref[...] = jnp.zeros_like(gnorm_ref)
        dkv_all[...] = jnp.zeros_like(dkv_all)

    g2 = g2_ref[...]
    dyc = g2.astype(bf16)
    dyc_all[rows, :] = dyc
    quad = lane_masks(256)
    for j in range(2):
        lanes = pl.ds(j * 256, 256)
        do = mm_nt(dyc, wo[j][1]).astype(bf16)
        for u in range(4):
            base = pl.multiple_of(block * BLK + u * 64, 64)
            slot = pl.ds(pl.multiple_of(mem_slot(core, block, u) * MEM, MEM), MEM)
            dq, dk, dv = attend_back(
                cq_ref[u * 64 : (u + 1) * 64, lanes],
                kv_ref[slot, lanes],
                kv_ref[slot, pl.ds(D + j * 256, 256)],
                pc_ref[0, u * 2 + j],
                do[u * 64 : (u + 1) * 64],
                quad,
                64,
            )
            dcq_all[pl.ds(base, 64), lanes] = dq.astype(bf16)
            dkv_all[slot, lanes] += dk
            dkv_all[slot, pl.ds(D + j * 256, 256)] += dv
    dcq = dcq_all[rows, :]
    dh = mm_nt(dcq[:, :256], wa0[3]) + mm_nt(dcq[:, 256:], wa1[3])
    normed, inverse = norm_stats(x1_ref[...])
    gnorm_ref[1:2, :] += jnp.sum(dh * normed, axis=0, keepdims=True)
    gnorm_ref[3:4, :] += jnp.sum(dh, axis=0, keepdims=True)
    g1 = g2 + norm_back(dh, normed, inverse, gain_ref[1:2, :])
    pl.when(block == 0)(early.one)
    dys = g1.astype(bf16)
    dys_all[rows, :] = dys
    pair = lane_masks(128)
    for half in range(2):
        do_half = mm_nt(dys, wo[half][0]).astype(bf16)
        for i in range(2):
            first = half * 256 + i * 128
            dq, dk, dv = attend_back(
                qkv_ref[:, pl.ds(first, 128)],
                qkv_ref[:, pl.ds(D + first, 128)],
                qkv_ref[:, pl.ds(2 * D + first, 128)],
                p_ref[0, half * 2 + i],
                do_half[:, i * 128 : (i + 1) * 128],
                pair,
                BLK,
            )
            dqkv_all[rows, pl.ds(first, 128)] = dq.astype(bf16)
            dqkv_all[rows, pl.ds(D + first, 128)] = dk.astype(bf16)
            dqkv_all[rows, pl.ds(2 * D + first, 128)] = dv.astype(bf16)
    dqkv = dqkv_all[rows, :]
    dh = jnp.zeros((BLK, D), f32)
    for half in range(2):
        for which in range(3):
            first = which * D + half * 256
            dh = dh + mm_nt(dqkv[:, first : first + 256], wa[half][which])
    normed, inverse = norm_stats(x_ref[...].astype(f32))
    gnorm_ref[0:1, :] += jnp.sum(dh * normed, axis=0, keepdims=True)
    gnorm_ref[2:3, :] += jnp.sum(dh, axis=0, keepdims=True)
    dx_ref[...] = g1 + norm_back(dh, normed, inverse, gain_ref[0:1, :])
    pl.when(block == 2)(early.two)

    @pl.when(block == pl.num_programs(0) - 1)
    def _():
        def memory_rows(i, carry):
            part = pl.ds(pl.multiple_of(i * BLK, BLK), BLK)
            low = dkv_all[part, :].astype(bf16)
            dkv_low[part, :] = low
            total = jnp.zeros((BLK, D), f32)
            for half in range(2):
                for which in range(2):
                    first = which * D + half * 256
                    total = total + mm_nt(low[:, first : first + 256], wa[half][4 + which])
            dmem_ref[part, :] = total
            return carry

        lax.fori_loop(0, jnp.where(core == 0, 6, 2), memory_rows, 0)

        @pl.when(core != 0)
        def _():
            dkv_low[512:, :] = jnp.zeros((1024, 2 * D), bf16)
            dmem_ref[512:, :] = jnp.zeros((1024, D), f32)

        dlow_ref[...] = dmem_ref[1024:, :].astype(bf16)

        def bands(half, put):
            col = pl.ds(half * 256, 256)
            for which in range(3):
                put(0, which, mm_tn(dqkv_all[:, pl.ds(which * D + half * 256, 256)], h1_ref[...]))
            put(0, 3, mm_tn(dcq_all[:, col], h2_ref[...]))
            for which in range(2):
                put(1, which, mm_tn(dkv_low[:, pl.ds(which * D + half * 256, 256)], mem_ref[...]))
            put(1, 2, mm_tn(o_ref[:, col], dys_all[...]))
            put(1, 3, mm_tn(oc_ref[:, col], dyc_all[...]))

        def put_away(f, j, value):
            gs_away[f, j] = value.astype(bf16)
            if j % 2 == 1:
                pair = pl.ds(j - 1, 2)
                early.net.send(
                    True, gs_away.at[f, pair], gs_in.at[f, pair], band_sem + 2 * f + j // 2, early.net.sibling
                )

        def put_here(f, j, value):
            gs_ref[f, j] = value.astype(bf16)

        early.keep_sends()
        bands(1, put_away)
        bands(0, put_here)
        early.three()
        for f in range(2):
            for j in range(4):
                if j % 2 == 0:
                    early.net.landed(True, gs_in.at[f, pl.ds(j, 2)], band_sem + 2 * f + j // 2)
                add_into(gs_ref.at[f, j], [gs_in.at[f, j]], 128)
        early.net.all_sent()
        early.end()


def whole(shape):
    return pl.BlockSpec(shape, lambda i: (0,) * len(shape), pipeline_mode=pl.Buffered(1))


def by_rows(width):
    return pl.BlockSpec((BLK, width), lambda i: (i, 0))


def wide_rows(width):
    return pl.BlockSpec((WIDE, width), lambda i: (i, 0))


def sds(shape, dtype):
    return jax.ShapeDtypeStruct(shape, dtype)


def run_forward(lengths, x, mem, wa, wo, gain, bias):
    rows = x.shape[0]
    steps = rows // WIDE
    outs = [
        (sds((rows, D), bf16), wide_rows(D)),
        (sds((rows, 3 * D), bf16), wide_rows(3 * D)),
        (sds((rows // BLK, 4, 512, 256), bf16), pl.BlockSpec((2, 4, 512, 256), lambda i: (i, 0, 0, 0))),
        (sds((rows, D), bf16), wide_rows(D)),
        (sds((rows, D), f32), wide_rows(D)),
        (sds((rows, D), bf16), wide_rows(D)),
        (sds((rows, D), bf16), wide_rows(D)),
        (sds((1536, 2 * D), bf16), whole((1536, 2 * D))),
        (sds((rows // BLK, 8, 256, 128), bf16), pl.BlockSpec((2, 8, 256, 128), lambda i: (i, 0, 0, 0))),
        (sds((rows, D), bf16), wide_rows(D)),
        (sds((rows, D), f32), wide_rows(D)),
    ]
    return pl.pallas_call(
        forward_kernel,
        grid=(steps,),
        in_specs=[
            pl.BlockSpec(memory_space=pltpu.SMEM), wide_rows(D), whole((1536, D)),
            whole((6, D, 256)), whole((6, D, 256)), whole((2, 256, D)), whole((2, 256, D)),
            whole((4, D)), whole((4, D)),
        ],
        out_specs=[o[1] for o in outs],
        out_shape=[o[0] for o in outs],
        compiler_params=pltpu.CompilerParams(vmem_limit_bytes=60 * MIB),
        cost_estimate=pl.CostEstimate(flops=9 * 10**9, bytes_accessed=22 * MIB, transcendentals=3 * 10**6),
        name="layer_forward",
    )(lengths, x, mem, wa[0], wa[1], wo[0], wo[1], gain, bias)


def run_middle(lengths, total, x2, targets, wi, wf, wh, gain, bias, vocab, tokens):
    rows = x2.shape[0]
    steps = rows // WIDE
    outs = [
        (sds((rows, D), bf16), wide_rows(D)),
        (sds((rows, D), f32), wide_rows(D)),
        (sds((2, 2, 2, 512, D), bf16), whole((2, 2, 2, 512, D))),
        (sds((VOC, D), bf16), whole((VOC, D))),
        (sds((8, D), f32), whole((8, D))),
        (sds((8, VOC), f32), whole((8, VOC))),
    ]
    return pl.pallas_call(
        partial(middle_kernel, vocab, tokens),
        grid=(steps,),
        in_specs=[
            pl.BlockSpec(memory_space=pltpu.SMEM), whole((8, 128)), wide_rows(D), wide_rows(1),
            whole((D, 1024)), whole((D, 1024)), whole((1024, D)), whole((1024, D)), whole((VOC, D)),
            whole((4, D)), whole((4, D)),
        ],
        out_specs=[o[1] for o in outs],
        out_shape=[o[0] for o in outs],
        scratch_shapes=[
            VMEM((rows, D), bf16), VMEM((rows, 2048), bf16), VMEM((rows, D), bf16),
            VMEM((rows, 2048), bf16), VMEM((rows, D), bf16), VMEM((rows, VOC), bf16),
            VMEM((WIDE, 2048), f32),
        ],
        compiler_params=pltpu.CompilerParams(vmem_limit_bytes=60 * MIB),
        cost_estimate=pl.CostEstimate(flops=15 * 10**9, bytes_accessed=18 * MIB, transcendentals=5 * 10**6),
        name="ffn_head",
    )(lengths, total, x2, targets, wi[0], wi[1], wf[0], wf[1], wh, gain, bias)


def run_backward(dims, g2, x, x1, h1, qkv, p, o, h2, cq, kv, pc, oc, mem, wa, wo, gain, gw, ghead):
    rows = x.shape[0]
    steps = rows // BLK
    outs = [
        (sds((rows, D), f32), by_rows(D)),
        (sds((1536, D), f32), whole((1536, D))),
        (sds((512, D), bf16), whole((512, D))),
        (sds((2, 4, 256, D), bf16), whole((2, 4, 256, D))),
        (sds((8, D), f32), whole((8, D))),
        (sds((2, 512, D), bf16), pl.BlockSpec(memory_space=pl.ANY)),
        (sds((2, HPART, D), bf16), pl.BlockSpec(memory_space=pl.ANY)),
    ]
    nz, ny, nx = dims
    slots = max(nx, ny) - 1
    return pl.pallas_call(
        partial(backward_kernel, dims),
        grid=(steps,),
        in_specs=[
            by_rows(D), by_rows(D), by_rows(D), whole((rows, D)), by_rows(3 * D),
            pl.BlockSpec((1, 4, 512, 256), lambda i: (i, 0, 0, 0)), whole((rows, D)), whole((rows, D)),
            by_rows(D), whole((1536, 2 * D)), pl.BlockSpec((1, 8, 256, 128), lambda i: (i, 0, 0, 0)),
            whole((rows, D)), whole((1536, D)),
            whole((6, D, 256)), whole((6, D, 256)), whole((2, 256, D)), whole((2, 256, D)), whole((4, D)),
            pl.BlockSpec(memory_space=pl.ANY), pl.BlockSpec(memory_space=pl.ANY),
        ],
        out_specs=[o_[1] for o_ in outs],
        out_shape=[o_[0] for o_ in outs],
        scratch_shapes=[
            VMEM((rows, D), bf16), VMEM((rows, D), bf16), VMEM((rows, D), bf16),
            VMEM((rows, 3 * D), bf16), VMEM((1536, 2 * D), f32), VMEM((1536, 2 * D), bf16),
            VMEM((2, 2, 512, D), bf16), VMEM((2, 2, 512, D), bf16),
            VMEM((2, slots, 512, D), bf16), VMEM((2, slots, 512, D), bf16),
            VMEM((2, HPART, D), bf16), VMEM((2, HPART, D), bf16),
            VMEM((2, slots, HPART, D), bf16), VMEM((2, slots, HPART, D), bf16),
            VMEM((2, 4, 256, D), bf16), VMEM((2, 4, 256, D), bf16),
            pltpu.SemaphoreType.DMA((48,)), pltpu.SemaphoreType.DMA((40,)), pltpu.SemaphoreType.DMA((6,)),
        ],
        compiler_params=pltpu.CompilerParams(
            vmem_limit_bytes=62 * MIB, collective_id=2, has_side_effects=True,
        ),
        cost_estimate=pl.CostEstimate(flops=18 * 10**9, bytes_accessed=30 * MIB, transcendentals=0),
        name="attention_backward",
    )(g2, x, x1, h1, qkv, p, o, h2, cq, kv, pc, oc, mem, wa[0], wa[1], wo[0], wo[1], gain, gw, ghead)


MESH = pl.DeviceIdType.MESH
OWN = 2


def chip_dims(count):
    nz = 4
    side = math.isqrt(count // nz)
    return nz, count // nz // side, side


class Net:
    def __init__(self, dims, send_sems, recv_sems):
        self.nz, self.ny, self.nx = dims
        self.chip = lax.axis_index("dp")
        self.core = lax.axis_index("mp")
        self.x = lax.rem(self.chip, self.nx)
        self.y = lax.rem(lax.div(self.chip, self.nx), self.ny)
        self.z = lax.div(self.chip, self.nx * self.ny)
        self.place = {"x": self.x, "y": self.y, "z": self.z}
        self.count = {"x": self.nx, "y": self.ny, "z": self.nz}
        self.sibling = {"dp": self.chip, "mp": 1 - self.core}
        self.send_sems, self.recv_sems = send_sems, recv_sems
        self.sent, self.received = 0, 0
        self.unsent = []
        self.ending, self.keeping = False, True

    def at(self, **moved):
        p = {**self.place, **moved}
        return {"dp": (p["z"] * self.ny + p["y"]) * self.nx + p["x"], "mp": self.core}

    def further(self, axis, d):
        return lax.rem(self.place[axis] + d, self.count[axis])

    def on(self, condition, body):
        if condition is True:
            body()
        else:
            pl.when(condition)(body)

    def both(self, *conditions):
        result = True
        for c in conditions:
            if c is not True:
                result = c if result is True else jnp.logical_and(result, c)
        return result

    def inside(self, axis):
        return True if self.count[axis] == OWN else self.place[axis] < OWN

    def goes_inside(self, axis, d):
        return True if self.count[axis] == OWN else self.further(axis, d) < OWN

    def clipped(self, axis):
        return self.place[axis] if self.count[axis] == OWN else jnp.minimum(self.place[axis], OWN - 1)

    def send_sem(self, amount):
        self.sent += amount
        return self.sent - amount

    def recv_sem(self, amount):
        self.received += amount
        return self.received - amount

    def remote(self, src, dst, send_sem, recv_sem, device):
        return pltpu.make_async_remote_copy(
            src_ref=src, dst_ref=dst, send_sem=self.send_sems.at[send_sem],
            recv_sem=self.recv_sems.at[recv_sem], device_id=device, device_id_type=MESH,
        )

    def send(self, condition, src, dst, recv_sem, device):
        sem = self.send_sem(1)
        copy = lambda: self.remote(src, dst, sem, recv_sem, device)
        if self.ending:
            self.on(condition, lambda: copy().wait_send())
            return
        self.on(condition, lambda: copy().start())
        if self.keeping:
            self.unsent.append((condition, copy))

    def landed(self, condition, dst, recv_sem):
        self.on(condition, lambda: self.remote(dst, dst, 0, recv_sem, self.sibling).wait_recv())

    def spread(self, axis, condition, ref, recv_sem):
        for d in range(1, self.count[axis]):
            self.send(condition, ref, ref, recv_sem, self.at(**{axis: self.further(axis, d)}))

    def all_sent(self):
        for condition, copy in self.unsent:
            self.on(condition, lambda copy=copy: copy().wait_send())
        self.unsent = []
        assert self.sent <= self.send_sems.shape[0] and self.received <= self.recv_sems.shape[0]

    def barrier(self):
        partners = [self.sibling]
        for axis in ("x", "y", "z"):
            for d in range(1, self.count[axis]):
                partners.append(self.at(**{axis: self.further(axis, d)}))
        barrier = pltpu.get_barrier_semaphore()
        for partner in partners:
            pl.semaphore_signal(barrier, inc=1, device_id=partner, device_id_type=MESH)
        pl.semaphore_wait(barrier, len(partners))


def add_into(dst, sources, step):
    rows = dst.shape[0]

    def body(i, carry):
        part = pl.ds(pl.multiple_of(i * step, step), step)
        total = dst[part, :].astype(f32)
        for s in sources:
            total = total + s[part, :].astype(f32)
        dst[part, :] = total.astype(bf16)
        return carry

    lax.fori_loop(0, rows // step, body, 0)


HEAD_X, HEAD_Y, HEAD_Z = 1, 0, 0


class EarlySum:
    def __init__(self, net, gw, ghead, wide_out, head_out, scratch):
        (
            self.acc, self.core_in, self.first_in, self.second_in,
            self.head_acc, self.head_core, self.head_first, self.head_second, self.local,
        ) = scratch
        self.net, self.gw, self.ghead, self.wide_out, self.head_out = net, gw, ghead, wide_out, head_out
        n = net
        self.core_sem = n.recv_sem(6)
        self.first_sem = [n.recv_sem(n.nx - 1), n.recv_sem(n.ny - 1)]
        self.second_sem = [n.recv_sem(n.ny - 1), n.recv_sem(n.nx - 1)]
        self.head_first_sem = [n.recv_sem(n.nx - 1), n.recv_sem(n.ny - 1)]
        self.head_second_sem = [n.recv_sem(n.ny - 1), n.recv_sem(n.nx - 1)]
        self.sums = ((0, "x", "y"), (1, "y", "x"))
        self.goal = {"x": HEAD_X, "y": HEAD_Y}

    def head_rows(self, core, f):
        return self.ghead.at[pl.ds(pl.multiple_of(core * HROWS + f * HPART, HPART), HPART)]

    def own_copies(self):
        core = self.net.core
        return [
            pltpu.make_async_copy(self.gw.at[0, m, f], self.acc.at[m, f], self.local.at[2 * m + f])
            for m in range(2)
            for f in range(2)
        ] + [
            pltpu.make_async_copy(self.head_rows(core, f), self.head_acc.at[f], self.local.at[4 + f]) for f in range(2)
        ]

    def start(self):
        self.net.keeping = False
        self.net.barrier()
        for copy in self.own_copies():
            copy.start()
        self.core_sends()

    def core_sends(self):
        n = self.net
        for m in range(2):
            for f in range(2):
                n.send(True, self.gw.at[1, m, f], self.core_in.at[m, f], self.core_sem + 2 * m + f, n.sibling)
        for f in range(2):
            n.send(True, self.head_rows(1 - n.core, f), self.head_core.at[f], self.core_sem + 4 + f, n.sibling)

    def one(self):
        n = self.net
        for copy in self.own_copies():
            copy.wait()
        for m in range(2):
            for f in range(2):
                n.landed(True, self.core_in.at[m, f], self.core_sem + 2 * m + f)
                add_into(self.acc.at[m, f], [self.core_in.at[m, f]], 128)
        for f in range(2):
            n.landed(True, self.head_core.at[f], self.core_sem + 4 + f)
            add_into(self.head_acc.at[f], [self.head_core.at[f]], HPART)
        self.first_sends()

    def first_sends(self):
        n = self.net
        for f, axis, other in self.sums:
            for d in range(1, n.count[axis]):
                target = jnp.minimum(n.further(axis, d), OWN - 1)
                n.send(
                    n.goes_inside(axis, d), self.acc.at[target, f], self.first_in.at[f, d - 1],
                    self.first_sem[f] + d - 1, n.at(**{axis: n.further(axis, d)}),
                )
            goal = self.goal[axis]
            for d in range(1, n.count[axis]):
                n.send(
                    n.place[axis] == (goal + d) % n.count[axis], self.head_acc.at[f],
                    self.head_first.at[f, d - 1], self.head_first_sem[f] + d - 1, n.at(**{axis: goal}),
                )

    def two(self):
        n = self.net
        for f, axis, other in self.sums:
            matrix = n.clipped(axis)

            def take(f=f, axis=axis, matrix=matrix):
                slots = [self.first_in.at[f, d - 1] for d in range(1, n.count[axis])]
                for d in range(1, n.count[axis]):
                    n.landed(True, slots[d - 1], self.first_sem[f] + d - 1)
                add_into(self.acc.at[matrix, f], slots, 128)

            n.on(n.inside(axis), take)

            def take_head(f=f, axis=axis):
                slots = [self.head_first.at[f, d - 1] for d in range(1, n.count[axis])]
                for d in range(1, n.count[axis]):
                    n.landed(True, slots[d - 1], self.head_first_sem[f] + d - 1)
                add_into(self.head_acc.at[f], slots, HPART)

            n.on(n.place[axis] == self.goal[axis], take_head)
        self.second_sends()

    def second_sends(self):
        n = self.net
        for f, axis, other in self.sums:
            matrix = n.clipped(axis)
            distance = lax.rem(n.place[other] - matrix + n.count[other], n.count[other])
            slot = jnp.maximum(distance, 1) - 1
            n.send(
                n.both(n.inside(axis), distance != 0), self.acc.at[matrix, f], self.second_in.at[f, slot],
                self.second_sem[f] + slot, n.at(**{other: matrix}),
            )
            goal = self.goal[other]
            for d in range(1, n.count[other]):
                n.send(
                    n.both(n.place[axis] == self.goal[axis], n.place[other] == (goal + d) % n.count[other]),
                    self.head_acc.at[f], self.head_second.at[f, d - 1], self.head_second_sem[f] + d - 1,
                    n.at(**{other: goal}),
                )

    def columns(self):
        n = self.net
        wide = n.both(n.inside("x"), n.inside("y"), n.x == n.y)
        return wide, n.both(n.x == HEAD_X, n.y == HEAD_Y)

    def out_copies(self):
        n = self.net
        wide, head = self.columns()
        copies = [
            (wide, pltpu.make_async_copy(self.acc.at[n.clipped(axis), f], self.wide_out.at[f], self.local.at[f]))
            for f, axis, other in self.sums
        ]
        return copies + [(head, pltpu.make_async_copy(self.head_acc, self.head_out, self.local.at[4]))]

    def three(self):
        n = self.net
        wide, head = self.columns()
        for f, axis, other in self.sums:

            def take(f=f, axis=axis, other=other):
                slots = [self.second_in.at[f, d - 1] for d in range(1, n.count[other])]
                for d in range(1, n.count[other]):
                    n.landed(True, slots[d - 1], self.second_sem[f] + d - 1)
                add_into(self.acc.at[n.clipped(axis), f], slots, 128)

            n.on(wide, take)

            def take_head(f=f, other=other):
                slots = [self.head_second.at[f, d - 1] for d in range(1, n.count[other])]
                for d in range(1, n.count[other]):
                    n.landed(True, slots[d - 1], self.head_second_sem[f] + d - 1)
                add_into(self.head_acc.at[f], slots, HPART)

            n.on(head, take_head)
        for condition, copy in self.out_copies():
            n.on(condition, copy.start)

    def keep_sends(self):
        self.net.keeping = True

    def end(self):
        for condition, copy in self.out_copies():
            self.net.on(condition, copy.wait)
        self.net.sent, self.net.ending = 0, True
        self.core_sends()
        self.first_sends()
        self.second_sends()


def prepare_kernel(
    dims, lengths_ref, ai_ref, ao_ref, fi_ref, fo_ref, vh_ref, mem_ref,
    wa0, wa1, wo0, wo1, wi0, wi1, wf0, wf1, mem_out, wh_ref, total_ref,
    ai_in, ao_in, fi_in, fo_in, vh_in, mem_in, ai_low, ao_low, fi_low, fo_low, totals,
    load_sems, keep_sems, send_sems, recv_sems,
):
    nz, ny, nx = dims
    chip = lax.axis_index("dp")
    core = lax.axis_index("mp")
    place = {"x": lax.rem(chip, nx), "y": lax.rem(lax.div(chip, nx), ny), "z": lax.div(chip, nx * ny)}
    count = {"x": nx, "y": ny, "z": nz}
    sibling = {"dp": chip, "mp": 1 - core}

    def at(axis, target):
        p = {**place, axis: target}
        return {"dp": (p["z"] * ny + p["y"]) * nx + p["x"], "mp": core}

    arrays = (
        (ai_ref, ai_in, ai_low, wa0, wa1),
        (ao_ref, ao_in, ao_low, wo0, wo1),
        (fi_ref, fi_in, fi_low, wi0, wi1),
        (fo_ref, fo_in, fo_low, wf0, wf1),
    )
    loads = [
        pltpu.make_async_copy(src, dst, load_sems.at[i])
        for i, (src, dst) in enumerate([a[:2] for a in arrays] + [(vh_ref, vh_in), (mem_ref, mem_in)])
    ]
    for load in loads:
        load.start()
    partners = [sibling]
    for axis in ("x", "y", "z"):
        for d in range(1, count[axis]):
            partners.append(at(axis, lax.rem(place[axis] + d, count[axis])))
    barrier = pltpu.get_barrier_semaphore()
    for partner in partners:
        pl.semaphore_signal(barrier, inc=1, device_id=partner, device_id_type=MESH)
    pl.semaphore_wait(barrier, len(partners))

    def remote(src, dst, send_sem, recv_sem, device):
        return pltpu.make_async_remote_copy(
            src_ref=src, dst_ref=dst, send_sem=send_sems.at[send_sem], recv_sem=recv_sems.at[recv_sem],
            device_id=device, device_id_type=MESH,
        )

    tokens = lengths_ref[0]
    for s in range(1, lengths_ref.shape[0]):
        tokens = tokens + lengths_ref[s]

    base = {}
    used = 8
    for axis in ("x", "y", "z"):
        base[axis] = used
        used += count[axis]
    pending = []

    def spread_total(level, axis, value):
        totals[level, place[axis]] = value
        for d in range(1, count[axis]):
            copy = remote(
                totals.at[level, place[axis]], totals.at[level, place[axis]], base[axis] + d,
                base[axis] + place[axis], at(axis, lax.rem(place[axis] + d, count[axis])),
            )
            copy.start()
            pending.append(copy)

    def add_total(level, axis):
        for d in range(1, count[axis]):
            source = lax.rem(place[axis] + d, count[axis])
            remote(
                totals.at[level, source], totals.at[level, source], base[axis] + d,
                base[axis] + source, sibling,
            ).wait_recv()
        value = totals[level, 0]
        for s in range(1, count[axis]):
            value = value + totals[level, s]
        return value

    def memory_moves():
        return (
            (core == 0, pltpu.make_async_copy(mem_in, mem_out.at[pl.ds(0, 1024)], keep_sems.at[4])),
            (
                core == 1,
                pltpu.make_async_copy(mem_in.at[pl.ds(512, 512)], mem_out.at[pl.ds(0, 512)], keep_sems.at[4]),
            ),
            (core == 1, pltpu.make_async_copy(mem_in, mem_out.at[pl.ds(512, 1024)], keep_sems.at[5])),
        )

    def memory_send():
        return remote(mem_in.at[pl.ds(0, 512)], mem_out.at[pl.ds(1024, 512)], 4, 4, sibling)

    spread_total(0, "x", jnp.full((8, 128), tokens.astype(f32)))
    loads[5].wait()
    for condition, copy in memory_moves():
        pl.when(condition)(copy.start)
    pl.when(core == 1)(lambda: memory_send().start())
    sends = []
    keeps = []
    for i, (src, staged, low, mine, others) in enumerate(arrays):
        loads[i].wait()
        low[...] = staged[...].astype(bf16)
        copy = remote(low, others, i, i, sibling)
        copy.start()
        sends.append(copy)
        keep = pltpu.make_async_copy(low, mine, keep_sems.at[i])
        keep.start()
        keeps.append(keep)
        if i < 2:
            spread_total(i + 1, ("y", "z")[i], add_total(i, ("x", "y")[i]))
    loads[4].wait()
    vocab = vh_in.shape[0]
    wh_ref[512:, :] = jnp.zeros((VOC - 512, D), bf16)
    wh_ref[0:vocab, :] = vh_in[...].astype(bf16)
    total_ref[...] = add_total(2, "z")
    for condition, copy in memory_moves():
        pl.when(condition)(copy.wait)
    pl.when(core == 1)(lambda: memory_send().wait_send())
    pl.when(core == 0)(lambda: memory_send().wait_recv())
    for copy in keeps:
        copy.wait()
    for copy in sends:
        copy.wait()
    for copy in pending:
        copy.wait_send()


def run_prepare(dims, lengths, ai, ao, fi, fo, vh, mem):
    hbm = pl.BlockSpec(memory_space=pl.ANY)
    vmem = pl.BlockSpec(memory_space=VMEM)
    weights = [sds(w.shape, bf16) for w in (ai, ao, fi, fo) for _ in range(2)]
    nz, ny, nx = dims
    return pl.pallas_call(
        partial(prepare_kernel, dims),
        in_specs=[pl.BlockSpec(memory_space=pltpu.SMEM)] + [hbm] * 6,
        out_specs=[hbm] * 9 + [vmem, vmem],
        out_shape=weights + [sds((1536, D), bf16), sds((VOC, D), bf16), sds((8, 128), f32)],
        scratch_shapes=[VMEM(w.shape, f32) for w in (ai, ao, fi, fo, vh)]
        + [VMEM(mem.shape, bf16)]
        + [VMEM(w.shape, bf16) for w in (ai, ao, fi, fo)]
        + [
            VMEM((3, max(dims), 8, 128), f32),
            pltpu.SemaphoreType.DMA((6,)), pltpu.SemaphoreType.DMA((6,)),
            pltpu.SemaphoreType.DMA((8 + nx + ny + nz,)), pltpu.SemaphoreType.DMA((8 + nx + ny + nz,)),
        ],
        compiler_params=pltpu.CompilerParams(
            vmem_limit_bytes=60 * MIB, collective_id=1, has_side_effects=True
        ),
        cost_estimate=pl.CostEstimate(flops=10**6, bytes_accessed=24 * MIB, transcendentals=0),
        name="prepare_weights",
    )(lengths, ai, ao, fi, fo, vh, mem)


PIECE = 256
SMALL = 24


def split_two(value):
    high = value.astype(bf16)
    return high, (value - high.astype(f32)).astype(bf16)


def wide_roles(n):
    left = n.x == 0
    return (
        jnp.where(left, 1, 2), jnp.where(left, 0, 3), jnp.where(left, 2, 1), jnp.where(left, 3, 0)
    )


def square_owners(n):
    beside = n.x == n.y
    return (
        jnp.where(beside, jnp.where(n.x == 0, 2, 1), 1),
        jnp.where(beside, jnp.where(n.x == 0, 0, 3), 2),
    )


class SquareBack:
    def __init__(self, net, low, land):
        self.net, self.low, self.land = net, low, land
        self.axes = (("x", "y"), ("y", "x"))
        self.z_sem = [net.recv_sem(2) for _ in range(2)]
        self.one_sem = [net.recv_sem(2 * OWN) for _ in range(2)]
        self.two_sem = [net.recv_sem(2 * OWN) for _ in range(2)]
        self.valid = net.both(net.inside("x"), net.inside("y"))
        self.owners = square_owners(net)

    def chunk(self, f):
        first, second = self.axes[f]
        return self.net.clipped(first) * 2 + self.net.clipped(second)

    def rows(self, p):
        return pl.ds(p * 128, 128)

    def start(self, p):
        n = self.net
        for f in range(2):
            owner = n.both(self.valid, n.z == self.owners[f])

            def keep(f=f):
                self.land[f, self.chunk(f), self.rows(p), :] = self.low[self.rows(p), :]

            n.on(owner, keep)
            n.spread("z", owner, self.land.at[f, self.chunk(f), self.rows(p)], self.z_sem[f] + p)

    def one(self, p):
        n = self.net
        for f in range(2):
            mine = self.land.at[f, self.chunk(f), self.rows(p)]
            n.landed(n.both(self.valid, n.z != self.owners[f]), mine, self.z_sem[f] + p)
            second = self.axes[f][1]
            n.spread(second, self.valid, mine, self.one_sem[f] + p * OWN + n.clipped(second))

    def two(self, p):
        n = self.net
        for f in range(2):
            first, second = self.axes[f]
            for s in range(OWN):
                n.landed(
                    n.both(n.inside(first), n.place[second] != s),
                    self.land.at[f, n.clipped(first) * 2 + s, self.rows(p)], self.one_sem[f] + p * OWN + s,
                )
            n.spread(
                first, n.inside(first), self.land.at[f, pl.ds(n.clipped(first) * 2, 2), self.rows(p)],
                self.two_sem[f] + p * OWN + n.clipped(first),
            )

    def end(self):
        n = self.net
        for p in range(2):
            for f in range(2):
                first = self.axes[f][0]
                for s in range(OWN):
                    n.landed(
                        n.place[first] != s, self.land.at[f, pl.ds(s * 2, 2), self.rows(p)],
                        self.two_sem[f] + p * OWN + s,
                    )


class WideBack:
    def __init__(self, net, low, spot, pieces, rows):
        self.net, self.low, self.spot, self.pieces, self.rows = net, low, spot, pieces, rows
        self.axes = (("x", "y"), ("y", "x"))
        self.hop_sem = net.recv_sem(pieces)
        self.one_sem = net.recv_sem(pieces)
        self.two_sem = [net.recv_sem(OWN) for _ in range(pieces)]
        self.wide = net.both(net.inside("x"), net.inside("y"), net.x == net.y)
        self.owner, self.near, self.middle, self.far = wide_roles(net)

    def stands(self, position):
        return self.net.both(self.wide, self.net.z == position)

    def mine(self, p):
        return self.spot(self.net.clipped("x"), p)

    def start(self, p):
        n = self.net

        def keep():
            self.mine(p)[...] = self.low[pl.ds(p * self.rows, self.rows), :]

        owner = self.stands(self.owner)
        n.on(owner, keep)
        n.send(owner, self.mine(p), self.mine(p), self.hop_sem + p, n.at(z=self.middle))
        n.send(owner, self.mine(p), self.mine(p), self.hop_sem + p, n.at(z=self.near))

    def onward(self, p):
        n = self.net
        here = self.stands(self.middle)
        n.landed(here, self.mine(p), self.hop_sem + p)
        n.send(here, self.mine(p), self.mine(p), self.hop_sem + p, n.at(z=self.far))

    def one(self, p):
        n = self.net
        n.landed(self.stands(self.near), self.mine(p), self.hop_sem + p)
        n.landed(self.stands(self.far), self.mine(p), self.hop_sem + p)
        first, second = self.axes[2 * p // self.pieces]
        n.spread(second, self.wide, self.spot(n.clipped(first), p), self.one_sem + p)

    def two(self, p):
        n = self.net
        first, second = self.axes[2 * p // self.pieces]
        mine = self.spot(n.clipped(first), p)
        n.landed(n.both(n.inside(first), n.place[first] != n.place[second]), mine, self.one_sem + p)
        n.spread(first, n.inside(first), mine, self.two_sem[p] + n.clipped(first))

    def end(self):
        n = self.net
        for p in range(self.pieces):
            first = self.axes[2 * p // self.pieces][0]
            for m in range(OWN):
                n.landed(n.place[first] != m, self.spot(m, p), self.two_sem[p] + m)


class HeadBack:
    def __init__(self, net, low, land):
        self.net, self.low = net, low
        self.hop_sem, self.one_sem, self.two_sem = net.recv_sem(2), net.recv_sem(2), net.recv_sem(2)
        self.core_sem = net.recv_sem(1)
        self.axes = (("x", "y"), ("y", "x"))
        self.goal = {"x": HEAD_X, "y": HEAD_Y}
        self.spots = [
            land.at[pl.ds(pl.multiple_of(net.core * HROWS + p * HPART, HPART), HPART)] for p in range(2)
        ]
        self.mine = land.at[pl.ds(pl.multiple_of(net.core * HROWS, HROWS), HROWS)]
        self.theirs = land.at[pl.ds(pl.multiple_of((1 - net.core) * HROWS, HROWS), HROWS)]
        self.column = net.both(net.x == HEAD_X, net.y == HEAD_Y)

    def hop(self, k):
        n = self.net
        here = n.both(self.column, n.z == k)
        for p in range(2):
            if k == 0:

                def keep(p=p):
                    self.spots[p][...] = self.low[pl.ds(p * HPART, HPART), :]

                n.on(here, keep)
            else:
                n.landed(here, self.spots[p], self.hop_sem + p)
            if k < n.nz - 1:
                n.send(here, self.spots[p], self.spots[p], self.hop_sem + p, n.at(z=k + 1))

    def one(self):
        n = self.net
        for p in range(2):
            n.spread(self.axes[p][1], self.column, self.spots[p], self.one_sem + p)

    def two(self):
        n = self.net
        for p in range(2):
            first, second = self.axes[p]
            plane = n.place[first] == self.goal[first]
            n.landed(n.both(plane, n.place[second] != self.goal[second]), self.spots[p], self.one_sem + p)
            n.spread(first, plane, self.spots[p], self.two_sem + p)

    def three(self):
        n = self.net
        for p in range(2):
            first = self.axes[p][0]
            n.landed(n.place[first] != self.goal[first], self.spots[p], self.two_sem + p)
        n.send(True, self.mine, self.mine, self.core_sem, n.sibling)

    def end(self):
        self.net.landed(True, self.theirs, self.core_sem)


def muon_kernel(
    dims, gs_ref, wide_ref, headg_ref, na_ref, nf_ref, count_ref, dlow_ref, mi_ref, mo_ref, mu_ref, md_ref, mh_ref,
    ms_all, xs_all, mw_all, q_all, mh_all, xh_all, d_in, small_out,
    acc, first_in, second_in, band_in, wide_acc, wide_in, head_acc, head_in, small_buf,
    old_turned, old_plain, old_head, own, gram, gram_in, mats, m_low, x_low,
    ms_land, xs_land, mw_land, q_land, mh_land, xh_land,
    send_sems, recv_sems, local_sems,
):
    n = Net(dims, send_sems, recv_sems)
    nz = n.nz
    x, y, z, core = n.x, n.y, n.z, n.core
    on, both = n.on, n.both
    n.barrier()
    valid = both(n.inside("x"), n.inside("y"))
    wide = both(valid, x == y)
    wide_z, near_z, middle_z, far_z = wide_roles(n)
    wide_owner = both(wide, z == wide_z)
    square_z = square_owners(n)
    owns = [both(valid, z == square_z[f]) for f in range(2)]
    square = jnp.logical_or(owns[0], owns[1])
    task = jnp.where(
        z == square_z[0], n.clipped("x") * 2 + n.clipped("y"), 4 + n.clipped("y") * 2 + n.clipped("x")
    )
    head_column = both(x == HEAD_X, y == HEAD_Y)
    head_owner = both(head_column, z == HEAD_Z)
    axes = (("x", "y"), ("y", "x"))

    first_sem = [n.recv_sem(2 * (n.count[axes[f][0]] - 1)) for f in range(2)]
    second_sem = [n.recv_sem(2 * (n.count[axes[f][1]] - 1)) for f in range(2)]

    def half_rows(p):
        return pl.ds(p * 128, 128)

    for p in range(2):
        for f in range(2):
            axis = axes[f][0]
            for d in range(1, n.count[axis]):
                target = jnp.minimum(n.further(axis, d), OWN - 1)
                n.send(
                    n.goes_inside(axis, d), gs_ref.at[f, pl.ds(target * 2, 2), half_rows(p)],
                    first_in.at[f, d - 1, :, half_rows(p)], first_sem[f] + 2 * (d - 1) + p,
                    n.at(**{axis: n.further(axis, d)}),
                )
    own_copies = [
        pltpu.make_async_copy(gs_ref.at[f], acc.at[f], local_sems.at[f]) for f in range(2)
    ]
    for copy in own_copies:
        copy.start()

    def wide_load():
        return pltpu.make_async_copy(wide_ref, wide_acc, local_sems.at[4])

    def head_load():
        return pltpu.make_async_copy(headg_ref, head_acc, local_sems.at[5])

    def old_copies():
        sem = local_sems.at[6]
        return (
            (both(wide_owner, x == 0), lambda: pltpu.make_async_copy(mu_ref, old_turned, sem)),
            (both(wide_owner, x != 0), lambda: pltpu.make_async_copy(md_ref, old_plain, sem)),
            (
                both(square, task < 6),
                lambda: pltpu.make_async_copy(
                    mi_ref.at[jnp.minimum(task, 5)], old_turned.at[:, pl.ds(0, PIECE)], sem
                ),
            ),
            (
                both(square, task >= 6),
                lambda: pltpu.make_async_copy(
                    mo_ref.at[jnp.maximum(task, 6) - 6], old_plain.at[pl.ds(0, PIECE)], sem
                ),
            ),
            (head_owner, lambda: pltpu.make_async_copy(mh_ref, old_head, sem)),
        )

    on(wide, lambda: wide_load().start())
    on(head_column, lambda: head_load().start())
    for condition, copy in old_copies():
        on(condition, lambda copy=copy: copy().start())
    d_sem = n.recv_sem(1)
    n.send(core == 0, dlow_ref, d_in, d_sem, n.sibling)

    on(wide, lambda: wide_load().wait())
    near_sem, middle_sem, far_sem = n.recv_sem(4), n.recv_sem(4), n.recv_sem(4)

    def piece(k):
        return wide_acc.at[k // 2, pl.ds((k % 2) * PIECE, PIECE)]

    for k in range(4):
        n.send(both(wide, z == far_z), piece(k), wide_in.at[1, k], far_sem + k, n.at(z=middle_z))
        n.send(both(wide, z == near_z), piece(k), wide_in.at[0, k], near_sem + k, n.at(z=wide_z))

    def wide_pass(k):
        here = both(wide, z == middle_z)

        def take():
            n.landed(True, wide_in.at[1, k], far_sem + k)
            add_into(piece(k), [wide_in.at[1, k]], 128)

        on(here, take)
        n.send(here, piece(k), wide_in.at[1, k], middle_sem + k, n.at(z=wide_z))

    on(head_column, lambda: head_load().wait())
    head_sem = n.recv_sem(2)

    def head_pass(distance):
        here = both(head_column, z == distance)
        for p in range(2):
            if distance < nz - 1:

                def take(p=p):
                    n.landed(True, head_in.at[p], head_sem + p)
                    add_into(head_acc.at[p], [head_in.at[p]], HPART)

                on(here, take)
            n.send(here, head_acc.at[p], head_in.at[p], head_sem + p, n.at(z=distance - 1))

    head_pass(nz - 1)

    small_core = n.recv_sem(1)
    small_sem = {axis: n.recv_sem(n.count[axis]) for axis in ("x", "y", "z")}
    small_buf[0, 0] = jnp.zeros((SMALL, VOC), f32)
    small_buf[0, 0, 0:8, 0:D] = na_ref[...]
    small_buf[0, 0, 8:16, 0:D] = nf_ref[...]
    small_buf[0, 0, 16:24, :] = count_ref[...]
    n.send(True, small_buf.at[0, 0], small_buf.at[0, 1], small_core, n.sibling)

    def small_go(level, axis, value):
        small_buf[level, n.place[axis]] = value
        n.spread(axis, True, small_buf.at[level, n.place[axis]], small_sem[axis] + n.place[axis])

    def small_add(level, axis):
        for d in range(1, n.count[axis]):
            source = n.further(axis, d)
            n.landed(True, small_buf.at[level, source], small_sem[axis] + source)
        total = small_buf[level, 0]
        for s in range(1, n.count[axis]):
            total = total + small_buf[level, s]
        return total

    for copy in own_copies:
        copy.wait()
    n.landed(True, small_buf.at[0, 1], small_core)
    small_go(1, "x", small_buf[0, 0] + small_buf[0, 1])
    wide_pass(0)
    for p in range(2):
        for f in range(2):
            first, second = axes[f]
            mine = n.clipped(first) * 2

            def take(f=f, p=p, first=first, mine=mine):
                for d in range(1, n.count[first]):
                    n.landed(True, first_in.at[f, d - 1, :, half_rows(p)], first_sem[f] + 2 * (d - 1) + p)
                for j in range(2):
                    add_into(
                        acc.at[f, mine + j, half_rows(p)],
                        [first_in.at[f, d - 1, j, half_rows(p)] for d in range(1, n.count[first])], 128,
                    )

            on(n.inside(first), take)
            for d in range(1, n.count[second]):
                target = jnp.minimum(n.further(second, d), OWN - 1)
                n.send(
                    both(n.inside(first), n.goes_inside(second, d)), acc.at[f, mine + target, half_rows(p)],
                    second_in.at[f, d - 1, half_rows(p)], second_sem[f] + 2 * (d - 1) + p,
                    n.at(**{second: n.further(second, d)}),
                )
        wide_pass(1 + p)
        head_pass(2 - p)
    small_go(2, "y", small_add(1, "x"))

    def chunk(f):
        first, second = axes[f]
        return n.clipped(first) * 2 + n.clipped(second)

    band_sem = [n.recv_sem(2 * (nz - 1)) for _ in range(2)]
    for p in range(2):
        for f in range(2):
            second = axes[f][1]

            def take_second(f=f, p=p, second=second):
                for d in range(1, n.count[second]):
                    n.landed(True, second_in.at[f, d - 1, half_rows(p)], second_sem[f] + 2 * (d - 1) + p)
                add_into(
                    acc.at[f, chunk(f), half_rows(p)],
                    [second_in.at[f, d - 1, half_rows(p)] for d in range(1, n.count[second])], 128,
                )

            on(valid, take_second)
            for d in range(1, nz):
                n.send(
                    both(valid, z == lax.rem(square_z[f] + d, nz)), acc.at[f, chunk(f), half_rows(p)],
                    band_in.at[d - 1, half_rows(p)], band_sem[f] + 2 * (d - 1) + p, n.at(z=square_z[f]),
                )
    small_go(3, "z", small_add(2, "y"))
    wide_pass(3)

    own[...] = jnp.zeros_like(own)
    for condition, copy in old_copies():
        on(condition, lambda copy=copy: copy().wait())

    def turned(k):
        return jnp.swapaxes(old_turned[:, k * PIECE : (k + 1) * PIECE], 0, 1)

    back_ms = SquareBack(n, m_low, ms_land)
    back_mw = WideBack(
        n, m_low, lambda m, p: mw_land.at[m, p // 2, pl.ds((p % 2) * PIECE, PIECE)], 4, PIECE
    )
    back_mh = HeadBack(n, m_low, mh_land)
    back_xs = SquareBack(n, x_low, xs_land)
    back_q = WideBack(n, x_low, lambda m, p: q_land.at[m, core, p], 2, 128)
    back_xh = HeadBack(n, x_low, xh_land)

    def keep_moment(rows, value):
        own[rows, :] = value
        m_low[rows, :] = value.astype(bf16)

    def finish_wide(k, old):
        total = piece(k)[...].astype(f32) + wide_in[0, k].astype(f32) + wide_in[1, k].astype(f32)
        keep_moment(pl.ds(k * PIECE, PIECE), total + 0.5 * old)

    def wide_moment(k):
        n.landed(wide_owner, wide_in.at[0, k], near_sem + k)
        n.landed(wide_owner, wide_in.at[1, k], middle_sem + k)
        on(both(wide_owner, x == 0), lambda: finish_wide(k, turned(k)))
        on(both(wide_owner, x != 0), lambda: finish_wide(k, old_plain[pl.ds(k * PIECE, PIECE), :]))
        back_mw.start(k)

    def finish_square(p, old):
        f = jnp.where(owns[0], 0, 1)
        mine = jnp.where(owns[0], chunk(0), chunk(1))
        total = acc[f, mine, half_rows(p), :].astype(f32)
        for d in range(1, nz):
            total = total + band_in[d - 1, half_rows(p), :].astype(f32)
        keep_moment(half_rows(p), total + 0.5 * old)

    def square_moment(p):
        for f in range(2):
            for d in range(1, nz):
                n.landed(owns[f], band_in.at[d - 1, half_rows(p)], band_sem[f] + 2 * (d - 1) + p)
        on(
            both(square, task < 6),
            lambda: finish_square(p, jnp.swapaxes(old_turned[:, p * 128 : (p + 1) * 128], 0, 1)),
        )
        on(both(square, task >= 6), lambda: finish_square(p, old_plain[half_rows(p), :]))
        back_ms.start(p)

    def finish_head():
        old_plain[pl.ds(512, 128), :] = jnp.zeros((128, D), f32)
        old_plain[pl.ds(0, old_head.shape[0]), :] = old_head[...]
        for p in range(2):
            here = pl.ds(pl.multiple_of(core * HROWS + p * HPART, HPART), HPART)
            total = head_acc[p].astype(f32) + head_in[p].astype(f32)
            keep_moment(pl.ds(p * HPART, HPART), total + 0.5 * old_plain[here, :])

    wide_moment(0)
    for p in range(2):
        n.landed(head_owner, head_in.at[p], head_sem + p)
    on(head_owner, finish_head)
    back_mh.hop(0)
    square_moment(0)
    wide_moment(1)
    wide_moment(2)
    square_moment(1)
    wide_moment(3)

    blocks_used = jnp.where(wide_owner, 4, jnp.where(head_owner, 2, 1))
    gram[...] = jnp.zeros_like(gram)

    def gram_step(i, carry):
        high, low = split_two(own[pl.ds(pl.multiple_of(i * PIECE, PIECE), PIECE), :])
        gram[...] += mm_tn(high, high) + (mm_tn(high, low) + mm_tn(low, high))
        return carry

    lax.fori_loop(0, blocks_used, gram_step, 0)
    gram_sem = n.recv_sem(1)
    n.send(True, gram, gram_in, gram_sem, n.sibling)
    small_out[...] = small_add(3, "z")
    n.landed(True, gram_in, gram_sem)

    def eye_rows(first, rows):
        place = lax.broadcasted_iota(jnp.int32, (rows, D), 0) + first
        return (place == lax.broadcasted_iota(jnp.int32, (rows, D), 1)).astype(f32)

    def put(m, value):
        high, low = split_two(value)
        mats[m, 0] = high
        mats[m, 1] = low

    def product(a, b):
        ah, al = mats[a, 0], mats[a, 1]
        left_h, left_l = mats[b, 0, :, 0:256], mats[b, 1, :, 0:256]
        left = mm(ah, left_h) + (mm(ah, left_l) + mm(al, left_h))
        right_h, right_l = mats[b, 0, :, 256:512], mats[b, 1, :, 256:512]
        corner = mm(ah[256:], right_h) + (mm(ah[256:], right_l) + mm(al[256:], right_h))
        right = jnp.concatenate([jnp.swapaxes(left[256:], 0, 1), corner], axis=0)
        return jnp.concatenate([left, right], axis=1)

    both_halves = gram[...] + gram_in[...]
    total = jnp.sum(jnp.sum(both_halves * eye_rows(0, D), axis=0, keepdims=True), axis=1, keepdims=True)
    scale = 1.0 / (jnp.sqrt(total) + 1e-07)
    put(0, both_halves * scale * scale)
    on(square, lambda: own.__setitem__((pl.ds(0, PIECE), slice(None)), own[pl.ds(0, PIECE), :] * scale))
    for iteration in range(NS_STEPS):
        q_now, q_next = (2, 4) if iteration % 2 == 0 else (4, 2)
        a = mats[0, 0].astype(f32) + mats[0, 1].astype(f32)
        put(1, NS_A * eye_rows(0, D) + NS_B * a + NS_C * product(0, 0))

        def update_rows():
            high, low = split_two(own[pl.ds(0, PIECE), :])
            ph, pll = mats[1, 0], mats[1, 1]
            own[pl.ds(0, PIECE), :] = mm(high, ph) + (mm(high, pll) + mm(low, ph))

        def update_q():
            if iteration == 0:
                mats[q_next] = mats[1]
            else:
                put(q_next, product(1, q_now))

        on(square, update_rows)
        on(jnp.logical_not(square), update_q)
        if iteration < NS_STEPS - 1:
            put(3, product(0, 1))
            put(0, product(3, 1))
        if iteration == 0:
            back_ms.one(0)
            back_mh.hop(1)
        if iteration == 1:
            back_ms.one(1)
            back_mw.onward(0)
            back_mw.onward(1)
            back_mh.hop(2)
        if iteration == 2:
            back_ms.two(0)
            back_mw.onward(2)
            back_mw.one(0)
            back_mh.hop(3)
        if iteration == 3:
            back_ms.two(1)
            back_mw.onward(3)
            back_mw.one(1)
            back_mh.one()

    last = 4 if NS_STEPS % 2 == 1 else 2

    def direction():
        part = pl.ds(0, 512)
        high, low = split_two(own[part, :] * scale)
        value = mm(high, mats[last, 0]) + (mm(high, mats[last, 1]) + mm(low, mats[last, 0]))
        x_low[part, :] = value.astype(bf16)

    def wide_polynomial():
        rows = pl.ds(pl.multiple_of(core * PIECE, PIECE), PIECE)
        value = mats[last, 0, rows, :].astype(f32) + mats[last, 1, rows, :].astype(f32)
        x_low[pl.ds(0, PIECE), :] = (value * scale).astype(bf16)

    on(wide_owner, wide_polynomial)
    on(head_owner, direction)

    def keep_rows():
        x_low[pl.ds(0, PIECE), :] = own[pl.ds(0, PIECE), :].astype(bf16)

    on(square, keep_rows)
    back_xs.start(0)
    back_xs.start(1)
    back_q.start(0)
    back_q.start(1)
    back_xh.hop(0)
    back_mw.one(2)
    back_mw.two(0)
    back_mh.two()
    back_q.onward(0)
    back_q.onward(1)
    back_xh.hop(1)
    outs = [
        pltpu.make_async_copy(src, dst, local_sems.at[i])
        for i, (src, dst) in enumerate(
            (
                (ms_land, ms_all), (mh_land, mh_all), (mw_land, mw_all), (xs_land, xs_all), (q_land, q_all),
                (xh_land, xh_all),
            )
        )
    ]
    back_xs.one(0)
    back_xh.hop(2)
    back_mw.one(3)
    back_mw.two(1)
    back_xs.one(1)
    back_q.one(0)
    back_q.one(1)
    back_xs.two(0)
    back_xh.hop(3)
    back_xh.one()
    back_mw.two(2)
    back_xs.two(1)
    back_q.two(0)
    back_q.two(1)
    back_mw.two(3)
    back_xh.two()
    back_mh.three()
    back_ms.end()
    outs[0].start()
    back_mh.end()
    outs[1].start()
    back_mw.end()
    outs[2].start()
    back_q.end()
    q_sem = n.recv_sem(2)
    for m in range(2):
        n.send(True, q_land.at[m, core], q_land.at[m, core], q_sem + m, n.sibling)
    back_xh.three()
    back_xs.end()
    outs[3].start()
    for m in range(2):
        n.landed(True, q_land.at[m, 1 - core], q_sem + m)
    outs[4].start()
    back_xh.end()
    outs[5].start()
    n.landed(core == 1, d_in, d_sem)
    n.all_sent()
    for copy in outs:
        copy.wait()


def run_muon(dims, gs, wide, headg, na, nf, count, dlow, mi, mo, mu, md, mh):
    nz, ny, nx = dims
    hbm = pl.BlockSpec(memory_space=pl.ANY)
    vmem = pl.BlockSpec(memory_space=VMEM)
    slots = max(nx, ny) - 1
    most = max(nx, ny, nz, 2)
    squares = (2, 4, PIECE, D)
    lands = [squares, squares, (2, 2, 512, D), (2, 2, 2, 128, D), (VOC, D), (VOC, D)]
    return pl.pallas_call(
        partial(muon_kernel, dims),
        in_specs=[hbm] * 3 + [vmem] * 3 + [hbm] * 6,
        out_specs=[hbm] * 7 + [vmem],
        out_shape=[sds(s, bf16) for s in lands] + [sds((512, D), bf16), sds((SMALL, VOC), f32)],
        scratch_shapes=[
            VMEM(squares, bf16),
            VMEM((2, slots, 2, PIECE, D), bf16),
            VMEM((2, slots, PIECE, D), bf16),
            VMEM((nz - 1, PIECE, D), bf16),
            VMEM((2, 512, D), bf16),
            VMEM((2, 4, PIECE, D), bf16),
            VMEM((2, HPART, D), bf16),
            VMEM((2, HPART, D), bf16),
            VMEM((4, most, SMALL, VOC), f32),
            VMEM((D, 1024), f32),
            VMEM((1024, D), f32),
            VMEM(mh.shape, f32),
            VMEM((1024, D), f32),
            VMEM((D, D), f32),
            VMEM((D, D), f32),
            VMEM((5, 2, D, D), bf16),
            VMEM((1024, D), bf16),
            VMEM((512, D), bf16),
        ]
        + [VMEM(s, bf16) for s in lands]
        + [
            pltpu.SemaphoreType.DMA((400,)), pltpu.SemaphoreType.DMA((160,)), pltpu.SemaphoreType.DMA((8,)),
        ],
        compiler_params=pltpu.CompilerParams(
            vmem_limit_bytes=60 * MIB, collective_id=0, has_side_effects=True
        ),
        cost_estimate=pl.CostEstimate(flops=20 * 10**9, bytes_accessed=40 * MIB, transcendentals=0),
        name="reduce_muon_spread",
    )(gs, wide, headg, na, nf, count, dlow, mi, mo, mu, md, mh)


def finish_kernel(
    wide_rate, head_rate, core_ref,
    mu, md, mb, q_ref, xb, mh, xh, ai, ao, fi, fo, vh, small, gain, bias, nm, dm, dr,
    mi_out, ni_out, mo_out, no_out, mu_out, nu_out, md_out, nd_out, mh_out, nh_out,
    mn_out, nn_out, counts_out, dm_out,
):
    i = pl.program_id(0)
    same = lax.broadcasted_iota(jnp.int32, (D, D), 0) == lax.broadcasted_iota(jnp.int32, (D, D), 1)
    eye = same.astype(f32).astype(bf16)
    mu_out[...] = mm_nt(eye, mu[0, 0])
    nu_out[...] = fi[...] - wide_rate * mm_nt(q_ref[0], mu[0, 0])
    md_out[...] = md[0, 0].astype(f32)
    nd_out[...] = fo[...] - wide_rate * mm(md[0, 0], q_ref[1])

    @pl.when(i < 3)
    def _():
        for j in range(2):
            mi_out[j] = mm_nt(eye, mb[0, j])
            ni_out[j] = ai[j] - muon_rate * mm_nt(eye, xb[0, j])

    @pl.when(i == 3)
    def _():
        for j in range(2):
            mo_out[j] = mb[0, j].astype(f32)
            no_out[j] = ao[j] - muon_rate * xb[0, j].astype(f32)

    dm_out[...] = jnp.where((core_ref[0] == 0) | (i >= 2), dm[...], dr[...].astype(f32))

    @pl.when(i == 0)
    def _():
        vocab = vh.shape[0]
        mh_out[...] = mh[0:vocab, :].astype(f32)
        nh_out[...] = vh[...] - head_rate * xh[0:vocab, :].astype(f32)
        for kind, old in enumerate((gain, bias)):
            first = 2 * kind
            total = jnp.concatenate([small[first : first + 2, 0:D], small[first + 8 : first + 10, 0:D]], axis=0)
            moment = 0.5 * nm[kind] + total
            mn_out[kind] = moment
            nn_out[kind] = old[...] - vector_rate * moment * lax.rsqrt(
                jnp.mean(moment * moment, axis=-1, keepdims=True) + 1e-06
            )
        counts_out[...] = small[16:17, 0:vocab].astype(jnp.int32)


def run_finish(core, ms, xs, mw, q, m_head, x_head, ai, ao, fi, fo, vh, small, gain, bias, nm, dmem, d_in):
    vocab = vh.shape[0]
    wide_rate = muon_rate * math.sqrt(2 * fi.shape[1] / D)
    head_rate = muon_rate * math.sqrt(vocab / D)

    def spec(shape, index):
        return pl.BlockSpec(shape, index)

    def fixed(shape):
        return pl.BlockSpec(shape, lambda i, c: (0,) * len(shape))

    up = spec((1, 1, 256, D), lambda i, c: (0, i // 2, i % 2, 0))
    down = spec((1, 1, 256, D), lambda i, c: (1, i // 2, i % 2, 0))
    bands = spec((1, 2, 256, D), lambda i, c: (i // 2, i % 2, 0, 0))
    inner = spec((2, D, 256), lambda i, c: (jnp.minimum(i, 2), 0, 0))
    outer = spec((2, 256, D), lambda i, c: (0, 0, 0))
    cols = spec((D, 256), lambda i, c: (0, i))
    rows = spec((256, D), lambda i, c: (i, 0))
    head = fixed((vocab, D))
    shapes = [
        (sds((6, D, 256), f32), inner), (sds((6, D, 256), f32), inner),
        (sds((2, 256, D), f32), outer), (sds((2, 256, D), f32), outer),
        (sds(fi.shape, f32), cols), (sds(fi.shape, f32), cols),
        (sds(fo.shape, f32), rows), (sds(fo.shape, f32), rows),
        (sds((vocab, D), f32), head), (sds((vocab, D), f32), head),
        (sds((2, 4, D), f32), fixed((2, 4, D))), (sds((2, 4, D), f32), fixed((2, 4, D))),
        (sds((1, vocab), jnp.int32), fixed((1, vocab))),
        (sds((1024, D), f32), rows),
    ]
    return pl.pallas_call(
        partial(finish_kernel, wide_rate, head_rate),
        grid_spec=pltpu.PrefetchScalarGridSpec(
            num_scalar_prefetch=1,
            grid=(4,),
            in_specs=[
                up, down, bands, fixed((2, D, D)), bands, fixed((VOC, D)), fixed((VOC, D)),
                inner, outer, cols, rows, head, fixed((SMALL, VOC)), fixed((4, D)), fixed((4, D)), fixed((2, 4, D)),
                spec((256, D), lambda i, c: (jnp.where(c[0] == 0, i, jnp.maximum(i - 2, 0)), 0)),
                spec((256, D), lambda i, c: (jnp.minimum(i, 1), 0)),
            ],
            out_specs=[s[1] for s in shapes],
        ),
        out_shape=[s[0] for s in shapes],
        compiler_params=pltpu.CompilerParams(vmem_limit_bytes=60 * MIB),
        cost_estimate=pl.CostEstimate(flops=10**7, bytes_accessed=40 * MIB, transcendentals=0),
        name="finish_weights",
    )(core, mw, mw, ms, q.reshape(2, D, D), xs, m_head, x_head, ai, ao, fi, fo, vh, small,
      gain, bias, nm, dmem, d_in)


def local(
    residual_in, memory, lengths, targets, attn_in, attn_out, ffn_in, ffn_out, vocab_head,
    norm_gain, norm_bias, attn_in_moment, attn_out_moment, ffn_in_moment, ffn_out_moment,
    head_moment, norm_moment,
):
    dims = chip_dims(lax.axis_size("dp"))
    core = lax.axis_index("mp")
    tokens = residual_in.shape[0] * lax.axis_size("mp") * lax.axis_size("dp")
    vocab = vocab_head.shape[1]
    inner = attn_in.reshape(6, D, 256)
    wa0, wa1, wo0, wo1, wi0, wi1, wf0, wf1, mem, wh, total = run_prepare(
        dims, lengths, inner, attn_out, ffn_in, ffn_out, vocab_head.T, memory
    )
    wa, wo, wi, wf = (wa0, wa1), (wo0, wo1), (wi0, wi1), (wf0, wf1)
    h1, qkv, p, o, x1, h2, cq, kv, pc, oc, x2 = run_forward(
        lengths, residual_in, mem, wa, wo, norm_gain, norm_bias
    )
    out, g2, gw, ghead, gnorm_ffn, counts = run_middle(
        lengths, total, x2, targets[:, None], wi, wf, wh, norm_gain, norm_bias, vocab, float(tokens)
    )
    dx, dmem, dlow, gs, gnorm_attn, wide, head_part = run_backward(
        dims, g2, residual_in, x1, h1, qkv, p, o, h2, cq, kv, pc, oc, mem, wa, wo, norm_gain, gw, ghead
    )
    ms, xs, mw, q, head_m, head_x, d_in, small = run_muon(
        dims, gs, wide, head_part, gnorm_attn, gnorm_ffn, counts, dlow,
        attn_in_moment.reshape(6, D, 256), attn_out_moment, ffn_in_moment, ffn_out_moment, head_moment.T,
    )
    (
        moment_in, new_in, moment_out, new_out, moment_up, new_up, moment_down, new_down,
        moment_head, new_head, moment_norms, new_norms, token_counts, memory_grad,
    ) = run_finish(
        core.reshape(1), ms, xs, mw, q, head_m, head_x, inner, attn_out, ffn_in, ffn_out,
        vocab_head.T, small, norm_gain, norm_bias, norm_moment, dmem, d_in,
    )
    return (
        out, dx, memory_grad, moment_in.reshape(attn_in.shape), new_in.reshape(attn_in.shape),
        moment_out, new_out, moment_up, new_up, moment_down, new_down, moment_head.T, new_head.T,
        moment_norms, new_norms,
        token_counts.reshape(vocab),
    )


def solution(mesh):
    rows = P(("dp", "mp"), None)
    placed = (
        rows, rows, P("dp"), P(("dp", "mp")),
        P(None, None, None, "mp"), P(None, "mp", None), P(None, "mp"), P("mp", None), P(), P(), P(),
        P(None, None, None, "mp"), P(None, "mp", None), P(None, "mp"), P("mp", None), P(), P(),
    )
    return jax.shard_map(
        local,
        mesh=mesh,
        in_specs=placed,
        out_specs=(
            rows, rows, rows,
            P(None, None, None, "mp"), P(None, None, None, "mp"),
            P(None, "mp", None), P(None, "mp", None),
            P(None, "mp"), P(None, "mp"), P("mp", None), P("mp", None),
            P(), P(), P(), P(), P(),
        ),
        check_vma=False,
    )
```

```python
from functools import partial
import math

import jax
import jax.numpy as jnp
from jax import lax
from jax.experimental import pallas as pl
from jax.experimental.pallas import tpu as pltpu
from jax.sharding import PartitionSpec as P

HEAD = 64
CAP_S = 64
CAP_M = 128
CAP_L = 256
MEM = 128
SETS = 4
NS_STEPS = 5
NS_A = 3.4445
NS_B = -4.775
NS_C = 2.0315
muon_rate = 0.5
vector_rate = 0.05

D = 512
BLK = 256
WIDE = 512
TALL = 1024
VOC = 640
HROWS = 320
HPART = 160
MIB = 1024 * 1024
bf16 = jnp.bfloat16
f32 = jnp.float32
VMEM = pltpu.VMEM


def mm(a, b):
    return jnp.dot(a, b, preferred_element_type=f32)


def mm_nt(a, b):
    return lax.dot_general(a, b, (((1,), (1,)), ((), ())), preferred_element_type=f32)


def mm_tn(a, b):
    return lax.dot_general(a, b, (((0,), (0,)), ((), ())), preferred_element_type=f32)


def norm_stats(value):
    average = jnp.mean(value, axis=-1, keepdims=True)
    centred = value - average
    variance = jnp.mean(centred * centred, axis=-1, keepdims=True)
    inverse = lax.rsqrt(variance + 1e-05)
    return centred * inverse, inverse


def norm_back(gradient, normed, inverse, gain):
    scaled = gradient * gain
    return inverse * (
        scaled
        - jnp.mean(scaled, axis=-1, keepdims=True)
        - normed * jnp.mean(scaled * normed, axis=-1, keepdims=True)
    )


def lane_masks(width):
    lanes = lax.broadcasted_iota(jnp.int32, (1, width), 1)
    return [(lanes // HEAD == h).astype(f32).astype(bf16) for h in range(width // HEAD)]


def spread(block, masks):
    return jnp.concatenate([block * m for m in masks], axis=0)


def pick(stacked, masks, rows):
    total = stacked[:rows] * masks[0].astype(f32)
    for h in range(1, len(masks)):
        total = total + stacked[h * rows : (h + 1) * rows] * masks[h].astype(f32)
    return total


def softmax_rows(scores):
    top = jnp.max(scores, axis=-1, keepdims=True)
    exps = jnp.exp(scores - top)
    return exps * (1.0 / jnp.sum(exps, axis=-1, keepdims=True))


def mem_slot(core, block, unit):
    on_first = jnp.where(block < 2, 4 * block + unit, 8 + 2 * (block - 2) + unit // 2)
    return jnp.where(core == 0, on_first, block)


def row_limits(core, block, lengths_ref):
    unit = lax.broadcasted_iota(jnp.int32, (BLK, 1), 0) // CAP_S
    low = jnp.zeros((BLK, 1), jnp.int32)
    length = jnp.zeros((BLK, 1), jnp.int32)
    for u in range(BLK // CAP_S):
        on_first = jnp.where(block < 2, u * CAP_S, u // 2 * CAP_M)
        slot = mem_slot(core, block, u) + jnp.where(core == 0, 0, 3 * SETS)
        low = jnp.where(unit == u, jnp.where(core == 0, on_first, 0), low)
        length = jnp.where(unit == u, lengths_ref[slot], length)
    return low, length


def rows_live(core, first, blocks, lengths_ref):
    pieces = []
    for j in range(blocks):
        low, length = row_limits(core, first + j, lengths_ref)
        place = lax.broadcasted_iota(jnp.int32, (BLK, 1), 0)
        pieces.append((place - low < length).astype(f32))
    return jnp.concatenate(pieces, axis=0)


def forward_kernel(
    lengths_ref, x_ref, mem_ref, wa0, wa1, wo0, wo1, gain_ref, bias_ref,
    h1_ref, qkv_ref, p_ref, o_ref, x1_ref, h2_ref, cq_ref, kv_ref, pc_ref, oc_ref, x2_ref,
):
    core = lax.axis_index("mp")
    step = pl.program_id(0)
    wa = (wa0, wa1)

    @pl.when(step == 0)
    def _():
        def fill(i, carry):
            rows = pl.ds(pl.multiple_of(i * WIDE, WIDE), WIDE)
            for half in range(2):
                for which in range(2):
                    kv_ref[rows, pl.ds(which * D + half * 256, 256)] = mm(
                        mem_ref[rows, :], wa[half][4 + which]
                    ).astype(bf16)
            return carry

        lax.fori_loop(0, jnp.where(core == 0, 3, 1), fill, 0)

    normed, _ = norm_stats(x_ref[...].astype(f32))
    h1_ref[...] = (normed * gain_ref[0:1, :] + bias_ref[0:1, :]).astype(bf16)
    for half in range(2):
        for which in range(3):
            qkv_ref[:, pl.ds(which * D + half * 256, 256)] = mm(h1_ref[...], wa[half][which]).astype(bf16)
    pair = lane_masks(128)
    for j in range(WIDE // BLK):
        rows = pl.ds(j * BLK, BLK)
        low, length = row_limits(core, step * (WIDE // BLK) + j, lengths_ref)
        keys = lax.broadcasted_iota(jnp.int32, (BLK, BLK), 1)
        queries = lax.broadcasted_iota(jnp.int32, (BLK, BLK), 0)
        allowed = (keys >= low) & (keys < low + length) & (keys <= queries)
        for i in range(4):
            q = qkv_ref[rows, pl.ds(i * 128, 128)] * jnp.bfloat16(0.125)
            k = qkv_ref[rows, pl.ds(D + i * 128, 128)]
            v = qkv_ref[rows, pl.ds(2 * D + i * 128, 128)]
            scores = mm_nt(spread(q, pair), k).reshape(2, BLK, BLK)
            scores = jnp.where(allowed[None], scores, -1000000000.0)
            probs = softmax_rows(scores).astype(bf16).reshape(2 * BLK, BLK)
            p_ref[j, i] = probs
            o_ref[rows, pl.ds(i * 128, 128)] = pick(mm(probs, v), pair, BLK).astype(bf16)
    x1 = x_ref[...].astype(f32) + mm(o_ref[:, :256], wo0[0]) + mm(o_ref[:, 256:], wo1[0])
    x1_ref[...] = x1
    normed, _ = norm_stats(x1)
    h2_ref[...] = (normed * gain_ref[1:2, :] + bias_ref[1:2, :]).astype(bf16)
    for half in range(2):
        cq_ref[:, pl.ds(half * 256, 256)] = mm(h2_ref[...], wa[half][3]).astype(bf16)
    quad = lane_masks(256)
    for u in range(WIDE // 64):
        rows = pl.ds(u * 64, 64)
        block = step * (WIDE // BLK) + u // 4
        slot = pl.ds(pl.multiple_of(mem_slot(core, block, u % 4) * MEM, MEM), MEM)
        for j in range(2):
            q = cq_ref[rows, pl.ds(j * 256, 256)] * jnp.bfloat16(0.125)
            k = kv_ref[slot, pl.ds(j * 256, 256)]
            v = kv_ref[slot, pl.ds(D + j * 256, 256)]
            probs = softmax_rows(mm_nt(spread(q, quad), k)).astype(bf16)
            pc_ref[u // 4, u % 4 * 2 + j] = probs
            oc_ref[rows, pl.ds(j * 256, 256)] = pick(mm(probs, v), quad, 64).astype(bf16)
    x2_ref[...] = x1_ref[...] + mm(oc_ref[:, :256], wo0[1]) + mm(oc_ref[:, 256:], wo1[1])


def gelu_parts(u):
    z = jnp.abs(u) * math.sqrt(0.5 / math.log(2.0))
    below = 1.0 + (0.3275911 * math.sqrt(math.log(2.0))) * z
    guess = pl.reciprocal(below, approx=True)
    t = guess * (2.0 - below * guess)
    gauss = jnp.exp2(-(z * z))
    tail = gauss * (
        t * (0.127414796 + t * (-0.142248368 + t * (0.7107068705 + t * (-0.7265760135 + t * 0.5307027145))))
    )
    cdf = jnp.where(u < 0, tail, 1.0 - tail)
    return u * cdf, cdf + u * (gauss * (1.0 / math.sqrt(2.0 * math.pi)))


def middle_kernel(
    vocab, tokens, lengths_ref, total_ref, x2_ref, targets_ref, wi0, wi1, wf0, wf1, wh_ref, gain_ref, bias_ref,
    out_ref, g2_ref, gw_ref, ghead_ref, gnorm_ref, count_ref,
    h3_all, a_all, dy_all, du_all, z_all, gl_all, slope,
):
    block = pl.program_id(0)
    rows = pl.ds(pl.multiple_of(block * TALL, TALL), TALL)
    wi = (wi0, wi1)
    wf = (wf0, wf1)
    x2 = x2_ref[...]
    normed2, inverse2 = norm_stats(x2)
    h3 = (normed2 * gain_ref[2:3, :] + bias_ref[2:3, :]).astype(bf16)
    h3_all[rows, :] = h3
    for half in range(2):
        for j in range(2):
            wide = pl.ds(half * 1024 + j * 512, 512)
            active, grad = gelu_parts(mm(h3, wi[half][:, j * 512 : (j + 1) * 512]))
            a_all[rows, wide] = active.astype(bf16)
            slope[:, wide] = grad
    x3 = x2_ref[...] + mm(a_all[rows, 0:1024], wf0[...]) + mm(a_all[rows, 1024:2048], wf1[...])
    out_ref[...] = x3.astype(bf16)
    normed3, inverse3 = norm_stats(x3)
    z = (normed3 * gain_ref[3:4, :] + bias_ref[3:4, :]).astype(bf16)
    z_all[rows, :] = z
    logits = mm_nt(z, wh_ref[...])
    columns = lax.broadcasted_iota(jnp.int32, (TALL, VOC), 1)
    logits = jnp.where(columns < vocab, logits, -1e30)
    probs = softmax_rows(logits)
    onehot = (columns == targets_ref[...]).astype(f32)
    live = rows_live(lax.axis_index("mp"), block * (TALL // BLK), TALL // BLK, lengths_ref)
    gl = (tokens / total_ref[0:1, 0:1] * live * (probs - onehot)).astype(bf16)
    gl_all[rows, :] = gl
    counts = jnp.sum(onehot * live, axis=0, keepdims=True)
    gz = mm(gl, wh_ref[...])
    gain3 = jnp.sum(gz * normed3, axis=0, keepdims=True)
    bias3 = jnp.sum(gz, axis=0, keepdims=True)
    g3 = norm_back(gz, normed3, inverse3, gain_ref[3:4, :])
    dy = g3.astype(bf16)
    dy_all[rows, :] = dy
    g2_ref[...] = g3
    for half in range(2):
        for j in range(2):
            wide = pl.ds(half * 1024 + j * 512, 512)
            back = mm_nt(dy, wf[half][j * 512 : (j + 1) * 512, :])
            du_all[rows, wide] = (slope[:, wide] * back).astype(bf16)
    dh = mm_nt(du_all[rows, 0:1024], wi0[...]) + mm_nt(du_all[rows, 1024:2048], wi1[...])
    normed2, inverse2 = norm_stats(x2_ref[...])
    gain2 = jnp.sum(dh * normed2, axis=0, keepdims=True)
    bias2 = jnp.sum(dh, axis=0, keepdims=True)
    g2_ref[...] = g2_ref[...] + norm_back(dh, normed2, inverse2, gain_ref[2:3, :])

    @pl.when(block == 0)
    def _():
        gnorm_ref[...] = jnp.zeros_like(gnorm_ref)
        count_ref[...] = jnp.zeros_like(count_ref)

    gnorm_ref[0:1, :] += gain2
    gnorm_ref[1:2, :] += gain3
    gnorm_ref[2:3, :] += bias2
    gnorm_ref[3:4, :] += bias3
    count_ref[0:1, :] += counts

    @pl.when(block == pl.num_programs(0) - 1)
    def _():
        for half in range(2):
            for j in range(2):
                col = pl.ds(half * 1024 + j * 512, 512)
                gw_ref[half, 0, j] = mm_tn(du_all[:, col], h3_all[...]).astype(bf16)
                gw_ref[half, 1, j] = mm_tn(a_all[:, col], dy_all[...]).astype(bf16)
        ghead_ref[...] = mm_tn(gl_all[...], z_all[...]).astype(bf16)


def attend_back(queries, keys, values, probs, grads, masks, rows):
    q = spread(queries, masks)
    do = spread(grads, masks)
    dprobs = mm_nt(do, values)
    p = probs.astype(f32)
    weighted = p * dprobs
    ds = (weighted - p * jnp.sum(weighted, axis=-1, keepdims=True)).astype(bf16)
    dv = mm_tn(probs, do)
    dq = pick(mm(ds, keys), masks, rows) * 0.125
    dk = mm_tn(ds, q) * 0.125
    return dq, dk, dv


def backward_kernel(
    dims, g2_ref, x_ref, x1_ref, h1_ref, qkv_ref, p_ref, o_ref, h2_ref, cq_ref, kv_ref, pc_ref, oc_ref,
    mem_ref, wa0, wa1, wo0, wo1, gain_ref, gw_ref, ghead_ref,
    dx_ref, dmem_ref, dlow_ref, gs_ref, gnorm_ref, wide_out, head_out,
    dyc_all, dcq_all, dys_all, dqkv_all, dkv_all, dkv_low,
    early_acc, early_core, early_first, early_second, head_acc, head_core, head_first, head_second,
    gs_away, gs_in, send_sems, recv_sems, local_sems,
):
    core = lax.axis_index("mp")
    block = pl.program_id(0)
    early = EarlySum(
        Net(dims, send_sems, recv_sems), gw_ref, ghead_ref, wide_out, head_out,
        (
            early_acc, early_core, early_first, early_second, head_acc, head_core, head_first, head_second,
            local_sems,
        ),
    )
    band_sem = early.net.recv_sem(4)
    pl.when(block == 0)(early.start)
    rows = pl.ds(pl.multiple_of(block * BLK, BLK), BLK)
    wa = (wa0, wa1)
    wo = (wo0, wo1)

    @pl.when(block == 0)
    def _():
        gnorm_ref[...] = jnp.zeros_like(gnorm_ref)
        dkv_all[...] = jnp.zeros_like(dkv_all)

    g2 = g2_ref[...]
    dyc = g2.astype(bf16)
    dyc_all[rows, :] = dyc
    quad = lane_masks(256)
    for j in range(2):
        lanes = pl.ds(j * 256, 256)
        do = mm_nt(dyc, wo[j][1]).astype(bf16)
        for u in range(4):
            base = pl.multiple_of(block * BLK + u * 64, 64)
            slot = pl.ds(pl.multiple_of(mem_slot(core, block, u) * MEM, MEM), MEM)
            dq, dk, dv = attend_back(
                cq_ref[u * 64 : (u + 1) * 64, lanes],
                kv_ref[slot, lanes],
                kv_ref[slot, pl.ds(D + j * 256, 256)],
                pc_ref[0, u * 2 + j],
                do[u * 64 : (u + 1) * 64],
                quad,
                64,
            )
            dcq_all[pl.ds(base, 64), lanes] = dq.astype(bf16)
            dkv_all[slot, lanes] += dk
            dkv_all[slot, pl.ds(D + j * 256, 256)] += dv
    dcq = dcq_all[rows, :]
    dh = mm_nt(dcq[:, :256], wa0[3]) + mm_nt(dcq[:, 256:], wa1[3])
    normed, inverse = norm_stats(x1_ref[...])
    gnorm_ref[1:2, :] += jnp.sum(dh * normed, axis=0, keepdims=True)
    gnorm_ref[3:4, :] += jnp.sum(dh, axis=0, keepdims=True)
    g1 = g2 + norm_back(dh, normed, inverse, gain_ref[1:2, :])
    pl.when(block == 0)(early.one)
    dys = g1.astype(bf16)
    dys_all[rows, :] = dys
    pair = lane_masks(128)
    for half in range(2):
        do_half = mm_nt(dys, wo[half][0]).astype(bf16)
        for i in range(2):
            first = half * 256 + i * 128
            dq, dk, dv = attend_back(
                qkv_ref[:, pl.ds(first, 128)],
                qkv_ref[:, pl.ds(D + first, 128)],
                qkv_ref[:, pl.ds(2 * D + first, 128)],
                p_ref[0, half * 2 + i],
                do_half[:, i * 128 : (i + 1) * 128],
                pair,
                BLK,
            )
            dqkv_all[rows, pl.ds(first, 128)] = dq.astype(bf16)
            dqkv_all[rows, pl.ds(D + first, 128)] = dk.astype(bf16)
            dqkv_all[rows, pl.ds(2 * D + first, 128)] = dv.astype(bf16)
    dqkv = dqkv_all[rows, :]
    dh = jnp.zeros((BLK, D), f32)
    for half in range(2):
        for which in range(3):
            first = which * D + half * 256
            dh = dh + mm_nt(dqkv[:, first : first + 256], wa[half][which])
    normed, inverse = norm_stats(x_ref[...].astype(f32))
    gnorm_ref[0:1, :] += jnp.sum(dh * normed, axis=0, keepdims=True)
    gnorm_ref[2:3, :] += jnp.sum(dh, axis=0, keepdims=True)
    dx_ref[...] = g1 + norm_back(dh, normed, inverse, gain_ref[0:1, :])
    pl.when(block == 2)(early.two)

    @pl.when(block == pl.num_programs(0) - 1)
    def _():
        def memory_rows(i, carry):
            part = pl.ds(pl.multiple_of(i * BLK, BLK), BLK)
            low = dkv_all[part, :].astype(bf16)
            dkv_low[part, :] = low
            total = jnp.zeros((BLK, D), f32)
            for half in range(2):
                for which in range(2):
                    first = which * D + half * 256
                    total = total + mm_nt(low[:, first : first + 256], wa[half][4 + which])
            dmem_ref[part, :] = total
            return carry

        lax.fori_loop(0, jnp.where(core == 0, 6, 2), memory_rows, 0)

        @pl.when(core != 0)
        def _():
            dkv_low[512:, :] = jnp.zeros((1024, 2 * D), bf16)
            dmem_ref[512:, :] = jnp.zeros((1024, D), f32)

        dlow_ref[...] = dmem_ref[1024:, :].astype(bf16)

        def bands(half, put):
            col = pl.ds(half * 256, 256)
            for which in range(3):
                put(0, which, mm_tn(dqkv_all[:, pl.ds(which * D + half * 256, 256)], h1_ref[...]))
            put(0, 3, mm_tn(dcq_all[:, col], h2_ref[...]))
            for which in range(2):
                put(1, which, mm_tn(dkv_low[:, pl.ds(which * D + half * 256, 256)], mem_ref[...]))
            put(1, 2, mm_tn(o_ref[:, col], dys_all[...]))
            put(1, 3, mm_tn(oc_ref[:, col], dyc_all[...]))

        def put_away(f, j, value):
            gs_away[f, j] = value.astype(bf16)
            if j % 2 == 1:
                pair = pl.ds(j - 1, 2)
                early.net.send(
                    True, gs_away.at[f, pair], gs_in.at[f, pair], band_sem + 2 * f + j // 2, early.net.sibling
                )

        def put_here(f, j, value):
            gs_ref[f, j] = value.astype(bf16)

        early.keep_sends()
        bands(1, put_away)
        bands(0, put_here)
        early.three()
        for f in range(2):
            for j in range(4):
                if j % 2 == 0:
                    early.net.landed(True, gs_in.at[f, pl.ds(j, 2)], band_sem + 2 * f + j // 2)
                add_into(gs_ref.at[f, j], [gs_in.at[f, j]], 128)
        early.net.all_sent()
        early.end()


def whole(shape):
    return pl.BlockSpec(shape, lambda i: (0,) * len(shape), pipeline_mode=pl.Buffered(1))


def by_rows(width):
    return pl.BlockSpec((BLK, width), lambda i: (i, 0))


def wide_rows(width):
    return pl.BlockSpec((WIDE, width), lambda i: (i, 0))


def tall_rows(width):
    return pl.BlockSpec((TALL, width), lambda i: (i, 0))


def sds(shape, dtype):
    return jax.ShapeDtypeStruct(shape, dtype)


def run_forward(lengths, x, mem, wa, wo, gain, bias):
    rows = x.shape[0]
    steps = rows // WIDE
    outs = [
        (sds((rows, D), bf16), wide_rows(D)),
        (sds((rows, 3 * D), bf16), wide_rows(3 * D)),
        (sds((rows // BLK, 4, 512, 256), bf16), pl.BlockSpec((2, 4, 512, 256), lambda i: (i, 0, 0, 0))),
        (sds((rows, D), bf16), wide_rows(D)),
        (sds((rows, D), f32), wide_rows(D)),
        (sds((rows, D), bf16), wide_rows(D)),
        (sds((rows, D), bf16), wide_rows(D)),
        (sds((1536, 2 * D), bf16), whole((1536, 2 * D))),
        (sds((rows // BLK, 8, 256, 128), bf16), pl.BlockSpec((2, 8, 256, 128), lambda i: (i, 0, 0, 0))),
        (sds((rows, D), bf16), wide_rows(D)),
        (sds((rows, D), f32), wide_rows(D)),
    ]
    return pl.pallas_call(
        forward_kernel,
        grid=(steps,),
        in_specs=[
            pl.BlockSpec(memory_space=pltpu.SMEM), wide_rows(D), whole((1536, D)),
            whole((6, D, 256)), whole((6, D, 256)), whole((2, 256, D)), whole((2, 256, D)),
            whole((4, D)), whole((4, D)),
        ],
        out_specs=[o[1] for o in outs],
        out_shape=[o[0] for o in outs],
        compiler_params=pltpu.CompilerParams(vmem_limit_bytes=60 * MIB),
        cost_estimate=pl.CostEstimate(flops=9 * 10**9, bytes_accessed=22 * MIB, transcendentals=3 * 10**6),
        name="layer_forward",
    )(lengths, x, mem, wa[0], wa[1], wo[0], wo[1], gain, bias)


def run_middle(lengths, total, x2, targets, wi, wf, wh, gain, bias, vocab, tokens):
    rows = x2.shape[0]
    steps = rows // TALL
    outs = [
        (sds((rows, D), bf16), tall_rows(D)),
        (sds((rows, D), f32), tall_rows(D)),
        (sds((2, 2, 2, 512, D), bf16), whole((2, 2, 2, 512, D))),
        (sds((VOC, D), bf16), whole((VOC, D))),
        (sds((8, D), f32), whole((8, D))),
        (sds((8, VOC), f32), whole((8, VOC))),
    ]
    return pl.pallas_call(
        partial(middle_kernel, vocab, tokens),
        grid=(steps,),
        in_specs=[
            pl.BlockSpec(memory_space=pltpu.SMEM), whole((8, 128)), tall_rows(D), tall_rows(1),
            whole((D, 1024)), whole((D, 1024)), whole((1024, D)), whole((1024, D)), whole((VOC, D)),
            whole((4, D)), whole((4, D)),
        ],
        out_specs=[o[1] for o in outs],
        out_shape=[o[0] for o in outs],
        scratch_shapes=[
            VMEM((rows, D), bf16), VMEM((rows, 2048), bf16), VMEM((rows, D), bf16),
            VMEM((rows, 2048), bf16), VMEM((rows, D), bf16), VMEM((rows, VOC), bf16),
            VMEM((TALL, 2048), f32),
        ],
        compiler_params=pltpu.CompilerParams(vmem_limit_bytes=60 * MIB),
        cost_estimate=pl.CostEstimate(flops=15 * 10**9, bytes_accessed=18 * MIB, transcendentals=5 * 10**6),
        name="ffn_head",
    )(lengths, total, x2, targets, wi[0], wi[1], wf[0], wf[1], wh, gain, bias)


def run_backward(dims, g2, x, x1, h1, qkv, p, o, h2, cq, kv, pc, oc, mem, wa, wo, gain, gw, ghead):
    rows = x.shape[0]
    steps = rows // BLK
    outs = [
        (sds((rows, D), f32), by_rows(D)),
        (sds((1536, D), f32), whole((1536, D))),
        (sds((512, D), bf16), whole((512, D))),
        (sds((2, 4, 256, D), bf16), whole((2, 4, 256, D))),
        (sds((8, D), f32), whole((8, D))),
        (sds((2, 512, D), bf16), pl.BlockSpec(memory_space=pl.ANY)),
        (sds((2, HPART, D), bf16), pl.BlockSpec(memory_space=pl.ANY)),
    ]
    nz, ny, nx = dims
    slots = max(nx, ny) - 1
    return pl.pallas_call(
        partial(backward_kernel, dims),
        grid=(steps,),
        in_specs=[
            by_rows(D), by_rows(D), by_rows(D), whole((rows, D)), by_rows(3 * D),
            pl.BlockSpec((1, 4, 512, 256), lambda i: (i, 0, 0, 0)), whole((rows, D)), whole((rows, D)),
            by_rows(D), whole((1536, 2 * D)), pl.BlockSpec((1, 8, 256, 128), lambda i: (i, 0, 0, 0)),
            whole((rows, D)), whole((1536, D)),
            whole((6, D, 256)), whole((6, D, 256)), whole((2, 256, D)), whole((2, 256, D)), whole((4, D)),
            pl.BlockSpec(memory_space=pl.ANY), pl.BlockSpec(memory_space=pl.ANY),
        ],
        out_specs=[o_[1] for o_ in outs],
        out_shape=[o_[0] for o_ in outs],
        scratch_shapes=[
            VMEM((rows, D), bf16), VMEM((rows, D), bf16), VMEM((rows, D), bf16),
            VMEM((rows, 3 * D), bf16), VMEM((1536, 2 * D), f32), VMEM((1536, 2 * D), bf16),
            VMEM((2, 2, 512, D), bf16), VMEM((2, 2, 512, D), bf16),
            VMEM((2, slots, 512, D), bf16), VMEM((2, slots, 512, D), bf16),
            VMEM((2, HPART, D), bf16), VMEM((2, HPART, D), bf16),
            VMEM((2, slots, HPART, D), bf16), VMEM((2, slots, HPART, D), bf16),
            VMEM((2, 4, 256, D), bf16), VMEM((2, 4, 256, D), bf16),
            pltpu.SemaphoreType.DMA((48,)), pltpu.SemaphoreType.DMA((40,)), pltpu.SemaphoreType.DMA((6,)),
        ],
        compiler_params=pltpu.CompilerParams(
            vmem_limit_bytes=62 * MIB, collective_id=2, has_side_effects=True,
        ),
        cost_estimate=pl.CostEstimate(flops=18 * 10**9, bytes_accessed=30 * MIB, transcendentals=0),
        name="attention_backward",
    )(g2, x, x1, h1, qkv, p, o, h2, cq, kv, pc, oc, mem, wa[0], wa[1], wo[0], wo[1], gain, gw, ghead)


MESH = pl.DeviceIdType.MESH
OWN = 2


def chip_dims(count):
    nz = 4
    side = math.isqrt(count // nz)
    return nz, count // nz // side, side


class Net:
    def __init__(self, dims, send_sems, recv_sems):
        self.nz, self.ny, self.nx = dims
        self.chip = lax.axis_index("dp")
        self.core = lax.axis_index("mp")
        self.x = lax.rem(self.chip, self.nx)
        self.y = lax.rem(lax.div(self.chip, self.nx), self.ny)
        self.z = lax.div(self.chip, self.nx * self.ny)
        self.place = {"x": self.x, "y": self.y, "z": self.z}
        self.count = {"x": self.nx, "y": self.ny, "z": self.nz}
        self.sibling = {"dp": self.chip, "mp": 1 - self.core}
        self.send_sems, self.recv_sems = send_sems, recv_sems
        self.sent, self.received = 0, 0
        self.unsent = []
        self.ending, self.keeping = False, True

    def at(self, **moved):
        p = {**self.place, **moved}
        return {"dp": (p["z"] * self.ny + p["y"]) * self.nx + p["x"], "mp": self.core}

    def further(self, axis, d):
        return lax.rem(self.place[axis] + d, self.count[axis])

    def on(self, condition, body):
        if condition is True:
            body()
        else:
            pl.when(condition)(body)

    def both(self, *conditions):
        result = True
        for c in conditions:
            if c is not True:
                result = c if result is True else jnp.logical_and(result, c)
        return result

    def inside(self, axis):
        return True if self.count[axis] == OWN else self.place[axis] < OWN

    def goes_inside(self, axis, d):
        return True if self.count[axis] == OWN else self.further(axis, d) < OWN

    def clipped(self, axis):
        return self.place[axis] if self.count[axis] == OWN else jnp.minimum(self.place[axis], OWN - 1)

    def send_sem(self, amount):
        self.sent += amount
        return self.sent - amount

    def recv_sem(self, amount):
        self.received += amount
        return self.received - amount

    def remote(self, src, dst, send_sem, recv_sem, device):
        return pltpu.make_async_remote_copy(
            src_ref=src, dst_ref=dst, send_sem=self.send_sems.at[send_sem],
            recv_sem=self.recv_sems.at[recv_sem], device_id=device, device_id_type=MESH,
        )

    def send(self, condition, src, dst, recv_sem, device):
        sem = self.send_sem(1)
        copy = lambda: self.remote(src, dst, sem, recv_sem, device)
        if self.ending:
            self.on(condition, lambda: copy().wait_send())
            return
        self.on(condition, lambda: copy().start())
        if self.keeping:
            self.unsent.append((condition, copy))

    def landed(self, condition, dst, recv_sem):
        self.on(condition, lambda: self.remote(dst, dst, 0, recv_sem, self.sibling).wait_recv())

    def spread(self, axis, condition, ref, recv_sem):
        for d in range(1, self.count[axis]):
            self.send(condition, ref, ref, recv_sem, self.at(**{axis: self.further(axis, d)}))

    def all_sent(self):
        for condition, copy in self.unsent:
            self.on(condition, lambda copy=copy: copy().wait_send())
        self.unsent = []
        assert self.sent <= self.send_sems.shape[0] and self.received <= self.recv_sems.shape[0]

    def barrier(self):
        partners = [self.sibling]
        for axis in ("x", "y", "z"):
            for d in range(1, self.count[axis]):
                partners.append(self.at(**{axis: self.further(axis, d)}))
        barrier = pltpu.get_barrier_semaphore()
        for partner in partners:
            pl.semaphore_signal(barrier, inc=1, device_id=partner, device_id_type=MESH)
        pl.semaphore_wait(barrier, len(partners))


def add_into(dst, sources, step):
    rows = dst.shape[0]

    def body(i, carry):
        part = pl.ds(pl.multiple_of(i * step, step), step)
        total = dst[part, :].astype(f32)
        for s in sources:
            total = total + s[part, :].astype(f32)
        dst[part, :] = total.astype(bf16)
        return carry

    lax.fori_loop(0, rows // step, body, 0)


HEAD_X, HEAD_Y, HEAD_Z = 1, 0, 0


class EarlySum:
    def __init__(self, net, gw, ghead, wide_out, head_out, scratch):
        (
            self.acc, self.core_in, self.first_in, self.second_in,
            self.head_acc, self.head_core, self.head_first, self.head_second, self.local,
        ) = scratch
        self.net, self.gw, self.ghead, self.wide_out, self.head_out = net, gw, ghead, wide_out, head_out
        n = net
        self.core_sem = n.recv_sem(6)
        self.first_sem = [n.recv_sem(n.nx - 1), n.recv_sem(n.ny - 1)]
        self.second_sem = [n.recv_sem(n.ny - 1), n.recv_sem(n.nx - 1)]
        self.head_first_sem = [n.recv_sem(n.nx - 1), n.recv_sem(n.ny - 1)]
        self.head_second_sem = [n.recv_sem(n.ny - 1), n.recv_sem(n.nx - 1)]
        self.sums = ((0, "x", "y"), (1, "y", "x"))
        self.goal = {"x": HEAD_X, "y": HEAD_Y}

    def head_rows(self, core, f):
        return self.ghead.at[pl.ds(pl.multiple_of(core * HROWS + f * HPART, HPART), HPART)]

    def own_copies(self):
        core = self.net.core
        return [
            pltpu.make_async_copy(self.gw.at[0, m, f], self.acc.at[m, f], self.local.at[2 * m + f])
            for m in range(2)
            for f in range(2)
        ] + [
            pltpu.make_async_copy(self.head_rows(core, f), self.head_acc.at[f], self.local.at[4 + f]) for f in range(2)
        ]

    def start(self):
        self.net.keeping = False
        self.net.barrier()
        for copy in self.own_copies():
            copy.start()
        self.core_sends()

    def core_sends(self):
        n = self.net
        for m in range(2):
            for f in range(2):
                n.send(True, self.gw.at[1, m, f], self.core_in.at[m, f], self.core_sem + 2 * m + f, n.sibling)
        for f in range(2):
            n.send(True, self.head_rows(1 - n.core, f), self.head_core.at[f], self.core_sem + 4 + f, n.sibling)

    def one(self):
        n = self.net
        for copy in self.own_copies():
            copy.wait()
        for m in range(2):
            for f in range(2):
                n.landed(True, self.core_in.at[m, f], self.core_sem + 2 * m + f)
                add_into(self.acc.at[m, f], [self.core_in.at[m, f]], 128)
        for f in range(2):
            n.landed(True, self.head_core.at[f], self.core_sem + 4 + f)
            add_into(self.head_acc.at[f], [self.head_core.at[f]], HPART)
        self.first_sends()

    def first_sends(self):
        n = self.net
        for f, axis, other in self.sums:
            for d in range(1, n.count[axis]):
                target = jnp.minimum(n.further(axis, d), OWN - 1)
                n.send(
                    n.goes_inside(axis, d), self.acc.at[target, f], self.first_in.at[f, d - 1],
                    self.first_sem[f] + d - 1, n.at(**{axis: n.further(axis, d)}),
                )
            goal = self.goal[axis]
            for d in range(1, n.count[axis]):
                n.send(
                    n.place[axis] == (goal + d) % n.count[axis], self.head_acc.at[f],
                    self.head_first.at[f, d - 1], self.head_first_sem[f] + d - 1, n.at(**{axis: goal}),
                )

    def two(self):
        n = self.net
        for f, axis, other in self.sums:
            matrix = n.clipped(axis)

            def take(f=f, axis=axis, matrix=matrix):
                slots = [self.first_in.at[f, d - 1] for d in range(1, n.count[axis])]
                for d in range(1, n.count[axis]):
                    n.landed(True, slots[d - 1], self.first_sem[f] + d - 1)
                add_into(self.acc.at[matrix, f], slots, 128)

            n.on(n.inside(axis), take)

            def take_head(f=f, axis=axis):
                slots = [self.head_first.at[f, d - 1] for d in range(1, n.count[axis])]
                for d in range(1, n.count[axis]):
                    n.landed(True, slots[d - 1], self.head_first_sem[f] + d - 1)
                add_into(self.head_acc.at[f], slots, HPART)

            n.on(n.place[axis] == self.goal[axis], take_head)
        self.second_sends()

    def second_sends(self):
        n = self.net
        for f, axis, other in self.sums:
            matrix = n.clipped(axis)
            distance = lax.rem(n.place[other] - matrix + n.count[other], n.count[other])
            slot = jnp.maximum(distance, 1) - 1
            n.send(
                n.both(n.inside(axis), distance != 0), self.acc.at[matrix, f], self.second_in.at[f, slot],
                self.second_sem[f] + slot, n.at(**{other: matrix}),
            )
            goal = self.goal[other]
            for d in range(1, n.count[other]):
                n.send(
                    n.both(n.place[axis] == self.goal[axis], n.place[other] == (goal + d) % n.count[other]),
                    self.head_acc.at[f], self.head_second.at[f, d - 1], self.head_second_sem[f] + d - 1,
                    n.at(**{other: goal}),
                )

    def columns(self):
        n = self.net
        wide = n.both(n.inside("x"), n.inside("y"), n.x == n.y)
        return wide, n.both(n.x == HEAD_X, n.y == HEAD_Y)

    def out_copies(self):
        n = self.net
        wide, head = self.columns()
        copies = [
            (wide, pltpu.make_async_copy(self.acc.at[n.clipped(axis), f], self.wide_out.at[f], self.local.at[f]))
            for f, axis, other in self.sums
        ]
        return copies + [(head, pltpu.make_async_copy(self.head_acc, self.head_out, self.local.at[4]))]

    def three(self):
        n = self.net
        wide, head = self.columns()
        for f, axis, other in self.sums:

            def take(f=f, axis=axis, other=other):
                slots = [self.second_in.at[f, d - 1] for d in range(1, n.count[other])]
                for d in range(1, n.count[other]):
                    n.landed(True, slots[d - 1], self.second_sem[f] + d - 1)
                add_into(self.acc.at[n.clipped(axis), f], slots, 128)

            n.on(wide, take)

            def take_head(f=f, other=other):
                slots = [self.head_second.at[f, d - 1] for d in range(1, n.count[other])]
                for d in range(1, n.count[other]):
                    n.landed(True, slots[d - 1], self.head_second_sem[f] + d - 1)
                add_into(self.head_acc.at[f], slots, HPART)

            n.on(head, take_head)
        for condition, copy in self.out_copies():
            n.on(condition, copy.start)

    def keep_sends(self):
        self.net.keeping = True

    def end(self):
        for condition, copy in self.out_copies():
            self.net.on(condition, copy.wait)
        self.net.sent, self.net.ending = 0, True
        self.core_sends()
        self.first_sends()
        self.second_sends()


def prepare_kernel(
    dims, lengths_ref, ai_ref, ao_ref, fi_ref, fo_ref, vh_ref, mem_ref,
    wa0, wa1, wo0, wo1, wi0, wi1, wf0, wf1, mem_out, wh_ref, total_ref,
    ai_in, ao_in, fi_in, fo_in, vh_in, mem_in, ai_low, ao_low, fi_low, fo_low, totals,
    load_sems, keep_sems, send_sems, recv_sems,
):
    nz, ny, nx = dims
    chip = lax.axis_index("dp")
    core = lax.axis_index("mp")
    place = {"x": lax.rem(chip, nx), "y": lax.rem(lax.div(chip, nx), ny), "z": lax.div(chip, nx * ny)}
    count = {"x": nx, "y": ny, "z": nz}
    sibling = {"dp": chip, "mp": 1 - core}

    def at(axis, target):
        p = {**place, axis: target}
        return {"dp": (p["z"] * ny + p["y"]) * nx + p["x"], "mp": core}

    arrays = (
        (ai_ref, ai_in, ai_low, wa0, wa1),
        (ao_ref, ao_in, ao_low, wo0, wo1),
        (fi_ref, fi_in, fi_low, wi0, wi1),
        (fo_ref, fo_in, fo_low, wf0, wf1),
    )
    loads = [
        pltpu.make_async_copy(src, dst, load_sems.at[i])
        for i, (src, dst) in enumerate([a[:2] for a in arrays] + [(vh_ref, vh_in), (mem_ref, mem_in)])
    ]
    for load in loads:
        load.start()
    partners = [sibling]
    for axis in ("x", "y", "z"):
        for d in range(1, count[axis]):
            partners.append(at(axis, lax.rem(place[axis] + d, count[axis])))
    barrier = pltpu.get_barrier_semaphore()
    for partner in partners:
        pl.semaphore_signal(barrier, inc=1, device_id=partner, device_id_type=MESH)
    pl.semaphore_wait(barrier, len(partners))

    def remote(src, dst, send_sem, recv_sem, device):
        return pltpu.make_async_remote_copy(
            src_ref=src, dst_ref=dst, send_sem=send_sems.at[send_sem], recv_sem=recv_sems.at[recv_sem],
            device_id=device, device_id_type=MESH,
        )

    tokens = lengths_ref[0]
    for s in range(1, lengths_ref.shape[0]):
        tokens = tokens + lengths_ref[s]

    base = {}
    used = 8
    for axis in ("x", "y", "z"):
        base[axis] = used
        used += count[axis]
    pending = []

    def spread_total(level, axis, value):
        totals[level, place[axis]] = value
        for d in range(1, count[axis]):
            copy = remote(
                totals.at[level, place[axis]], totals.at[level, place[axis]], base[axis] + d,
                base[axis] + place[axis], at(axis, lax.rem(place[axis] + d, count[axis])),
            )
            copy.start()
            pending.append(copy)

    def add_total(level, axis):
        for d in range(1, count[axis]):
            source = lax.rem(place[axis] + d, count[axis])
            remote(
                totals.at[level, source], totals.at[level, source], base[axis] + d,
                base[axis] + source, sibling,
            ).wait_recv()
        value = totals[level, 0]
        for s in range(1, count[axis]):
            value = value + totals[level, s]
        return value

    def memory_moves():
        return (
            (core == 0, pltpu.make_async_copy(mem_in, mem_out.at[pl.ds(0, 1024)], keep_sems.at[4])),
            (
                core == 1,
                pltpu.make_async_copy(mem_in.at[pl.ds(512, 512)], mem_out.at[pl.ds(0, 512)], keep_sems.at[4]),
            ),
            (core == 1, pltpu.make_async_copy(mem_in, mem_out.at[pl.ds(512, 1024)], keep_sems.at[5])),
        )

    def memory_send():
        return remote(mem_in.at[pl.ds(0, 512)], mem_out.at[pl.ds(1024, 512)], 4, 4, sibling)

    spread_total(0, "x", jnp.full((8, 128), tokens.astype(f32)))
    loads[5].wait()
    for condition, copy in memory_moves():
        pl.when(condition)(copy.start)
    pl.when(core == 1)(lambda: memory_send().start())
    sends = []
    keeps = []
    for i, (src, staged, low, mine, others) in enumerate(arrays):
        loads[i].wait()
        low[...] = staged[...].astype(bf16)
        copy = remote(low, others, i, i, sibling)
        copy.start()
        sends.append(copy)
        keep = pltpu.make_async_copy(low, mine, keep_sems.at[i])
        keep.start()
        keeps.append(keep)
        if i < 2:
            spread_total(i + 1, ("y", "z")[i], add_total(i, ("x", "y")[i]))
    loads[4].wait()
    vocab = vh_in.shape[0]
    wh_ref[512:, :] = jnp.zeros((VOC - 512, D), bf16)
    wh_ref[0:vocab, :] = vh_in[...].astype(bf16)
    total_ref[...] = add_total(2, "z")
    for condition, copy in memory_moves():
        pl.when(condition)(copy.wait)
    pl.when(core == 1)(lambda: memory_send().wait_send())
    pl.when(core == 0)(lambda: memory_send().wait_recv())
    for copy in keeps:
        copy.wait()
    for copy in sends:
        copy.wait()
    for copy in pending:
        copy.wait_send()


def run_prepare(dims, lengths, ai, ao, fi, fo, vh, mem):
    hbm = pl.BlockSpec(memory_space=pl.ANY)
    vmem = pl.BlockSpec(memory_space=VMEM)
    weights = [sds(w.shape, bf16) for w in (ai, ao, fi, fo) for _ in range(2)]
    nz, ny, nx = dims
    return pl.pallas_call(
        partial(prepare_kernel, dims),
        in_specs=[pl.BlockSpec(memory_space=pltpu.SMEM)] + [hbm] * 6,
        out_specs=[hbm] * 9 + [vmem, vmem],
        out_shape=weights + [sds((1536, D), bf16), sds((VOC, D), bf16), sds((8, 128), f32)],
        scratch_shapes=[VMEM(w.shape, f32) for w in (ai, ao, fi, fo, vh)]
        + [VMEM(mem.shape, bf16)]
        + [VMEM(w.shape, bf16) for w in (ai, ao, fi, fo)]
        + [
            VMEM((3, max(dims), 8, 128), f32),
            pltpu.SemaphoreType.DMA((6,)), pltpu.SemaphoreType.DMA((6,)),
            pltpu.SemaphoreType.DMA((8 + nx + ny + nz,)), pltpu.SemaphoreType.DMA((8 + nx + ny + nz,)),
        ],
        compiler_params=pltpu.CompilerParams(
            vmem_limit_bytes=60 * MIB, collective_id=1, has_side_effects=True
        ),
        cost_estimate=pl.CostEstimate(flops=10**6, bytes_accessed=24 * MIB, transcendentals=0),
        name="prepare_weights",
    )(lengths, ai, ao, fi, fo, vh, mem)


PIECE = 256
SMALL = 24


def split_two(value):
    high = value.astype(bf16)
    return high, (value - high.astype(f32)).astype(bf16)


def wide_roles(n):
    left = n.x == 0
    return (
        jnp.where(left, 1, 2), jnp.where(left, 0, 3), jnp.where(left, 2, 1), jnp.where(left, 3, 0)
    )


def square_owners(n):
    beside = n.x == n.y
    return (
        jnp.where(beside, jnp.where(n.x == 0, 2, 1), 1),
        jnp.where(beside, jnp.where(n.x == 0, 0, 3), 2),
    )


class SquareBack:
    def __init__(self, net, low, land):
        self.net, self.low, self.land = net, low, land
        self.axes = (("x", "y"), ("y", "x"))
        self.z_sem = [net.recv_sem(2) for _ in range(2)]
        self.one_sem = [net.recv_sem(2 * OWN) for _ in range(2)]
        self.two_sem = [net.recv_sem(2 * OWN) for _ in range(2)]
        self.valid = net.both(net.inside("x"), net.inside("y"))
        self.owners = square_owners(net)

    def chunk(self, f):
        first, second = self.axes[f]
        return self.net.clipped(first) * 2 + self.net.clipped(second)

    def rows(self, p):
        return pl.ds(p * 128, 128)

    def start(self, p):
        n = self.net
        for f in range(2):
            owner = n.both(self.valid, n.z == self.owners[f])

            def keep(f=f):
                self.land[f, self.chunk(f), self.rows(p), :] = self.low[self.rows(p), :]

            n.on(owner, keep)
            n.spread("z", owner, self.land.at[f, self.chunk(f), self.rows(p)], self.z_sem[f] + p)

    def one(self, p):
        n = self.net
        for f in range(2):
            mine = self.land.at[f, self.chunk(f), self.rows(p)]
            n.landed(n.both(self.valid, n.z != self.owners[f]), mine, self.z_sem[f] + p)
            second = self.axes[f][1]
            n.spread(second, self.valid, mine, self.one_sem[f] + p * OWN + n.clipped(second))

    def two(self, p):
        n = self.net
        for f in range(2):
            first, second = self.axes[f]
            for s in range(OWN):
                n.landed(
                    n.both(n.inside(first), n.place[second] != s),
                    self.land.at[f, n.clipped(first) * 2 + s, self.rows(p)], self.one_sem[f] + p * OWN + s,
                )
            n.spread(
                first, n.inside(first), self.land.at[f, pl.ds(n.clipped(first) * 2, 2), self.rows(p)],
                self.two_sem[f] + p * OWN + n.clipped(first),
            )

    def end(self):
        n = self.net
        for p in range(2):
            for f in range(2):
                first = self.axes[f][0]
                for s in range(OWN):
                    n.landed(
                        n.place[first] != s, self.land.at[f, pl.ds(s * 2, 2), self.rows(p)],
                        self.two_sem[f] + p * OWN + s,
                    )


class WideBack:
    def __init__(self, net, low, spot, pieces, rows):
        self.net, self.low, self.spot, self.pieces, self.rows = net, low, spot, pieces, rows
        self.axes = (("x", "y"), ("y", "x"))
        self.hop_sem = net.recv_sem(pieces)
        self.one_sem = net.recv_sem(pieces)
        self.two_sem = [net.recv_sem(OWN) for _ in range(pieces)]
        self.wide = net.both(net.inside("x"), net.inside("y"), net.x == net.y)
        self.owner, self.near, self.middle, self.far = wide_roles(net)

    def stands(self, position):
        return self.net.both(self.wide, self.net.z == position)

    def mine(self, p):
        return self.spot(self.net.clipped("x"), p)

    def start(self, p):
        n = self.net

        def keep():
            self.mine(p)[...] = self.low[pl.ds(p * self.rows, self.rows), :]

        owner = self.stands(self.owner)
        n.on(owner, keep)
        n.send(owner, self.mine(p), self.mine(p), self.hop_sem + p, n.at(z=self.middle))
        n.send(owner, self.mine(p), self.mine(p), self.hop_sem + p, n.at(z=self.near))

    def onward(self, p):
        n = self.net
        here = self.stands(self.middle)
        n.landed(here, self.mine(p), self.hop_sem + p)
        n.send(here, self.mine(p), self.mine(p), self.hop_sem + p, n.at(z=self.far))

    def one(self, p):
        n = self.net
        n.landed(self.stands(self.near), self.mine(p), self.hop_sem + p)
        n.landed(self.stands(self.far), self.mine(p), self.hop_sem + p)
        first, second = self.axes[2 * p // self.pieces]
        n.spread(second, self.wide, self.spot(n.clipped(first), p), self.one_sem + p)

    def two(self, p):
        n = self.net
        first, second = self.axes[2 * p // self.pieces]
        mine = self.spot(n.clipped(first), p)
        n.landed(n.both(n.inside(first), n.place[first] != n.place[second]), mine, self.one_sem + p)
        n.spread(first, n.inside(first), mine, self.two_sem[p] + n.clipped(first))

    def end(self):
        n = self.net
        for p in range(self.pieces):
            first = self.axes[2 * p // self.pieces][0]
            for m in range(OWN):
                n.landed(n.place[first] != m, self.spot(m, p), self.two_sem[p] + m)


class HeadBack:
    def __init__(self, net, low, land):
        self.net, self.low = net, low
        self.hop_sem, self.one_sem, self.two_sem = net.recv_sem(2), net.recv_sem(2), net.recv_sem(2)
        self.core_sem = net.recv_sem(1)
        self.axes = (("x", "y"), ("y", "x"))
        self.goal = {"x": HEAD_X, "y": HEAD_Y}
        self.spots = [
            land.at[pl.ds(pl.multiple_of(net.core * HROWS + p * HPART, HPART), HPART)] for p in range(2)
        ]
        self.mine = land.at[pl.ds(pl.multiple_of(net.core * HROWS, HROWS), HROWS)]
        self.theirs = land.at[pl.ds(pl.multiple_of((1 - net.core) * HROWS, HROWS), HROWS)]
        self.column = net.both(net.x == HEAD_X, net.y == HEAD_Y)

    def hop(self, k):
        n = self.net
        here = n.both(self.column, n.z == k)
        for p in range(2):
            if k == 0:

                def keep(p=p):
                    self.spots[p][...] = self.low[pl.ds(p * HPART, HPART), :]

                n.on(here, keep)
            else:
                n.landed(here, self.spots[p], self.hop_sem + p)
            if k < n.nz - 1:
                n.send(here, self.spots[p], self.spots[p], self.hop_sem + p, n.at(z=k + 1))

    def one(self):
        n = self.net
        for p in range(2):
            n.spread(self.axes[p][1], self.column, self.spots[p], self.one_sem + p)

    def two(self):
        n = self.net
        for p in range(2):
            first, second = self.axes[p]
            plane = n.place[first] == self.goal[first]
            n.landed(n.both(plane, n.place[second] != self.goal[second]), self.spots[p], self.one_sem + p)
            n.spread(first, plane, self.spots[p], self.two_sem + p)

    def three(self):
        n = self.net
        for p in range(2):
            first = self.axes[p][0]
            n.landed(n.place[first] != self.goal[first], self.spots[p], self.two_sem + p)
        n.send(True, self.mine, self.mine, self.core_sem, n.sibling)

    def end(self):
        self.net.landed(True, self.theirs, self.core_sem)


def muon_kernel(
    dims, gs_ref, wide_ref, headg_ref, na_ref, nf_ref, count_ref, dlow_ref, mi_ref, mo_ref, mu_ref, md_ref, mh_ref,
    ms_all, xs_all, mw_all, q_all, mh_all, xh_all, d_in, small_out,
    acc, first_in, second_in, band_in, wide_acc, wide_in, head_acc, head_in, small_buf,
    old_turned, old_plain, old_head, own, gram, gram_in, mats, m_low, x_low,
    ms_land, xs_land, mw_land, q_land, mh_land, xh_land,
    send_sems, recv_sems, local_sems,
):
    n = Net(dims, send_sems, recv_sems)
    nz = n.nz
    x, y, z, core = n.x, n.y, n.z, n.core
    on, both = n.on, n.both
    n.barrier()
    valid = both(n.inside("x"), n.inside("y"))
    wide = both(valid, x == y)
    wide_z, near_z, middle_z, far_z = wide_roles(n)
    wide_owner = both(wide, z == wide_z)
    square_z = square_owners(n)
    owns = [both(valid, z == square_z[f]) for f in range(2)]
    square = jnp.logical_or(owns[0], owns[1])
    task = jnp.where(
        z == square_z[0], n.clipped("x") * 2 + n.clipped("y"), 4 + n.clipped("y") * 2 + n.clipped("x")
    )
    head_column = both(x == HEAD_X, y == HEAD_Y)
    head_owner = both(head_column, z == HEAD_Z)
    axes = (("x", "y"), ("y", "x"))

    first_sem = [n.recv_sem(2 * (n.count[axes[f][0]] - 1)) for f in range(2)]
    second_sem = [n.recv_sem(2 * (n.count[axes[f][1]] - 1)) for f in range(2)]

    def half_rows(p):
        return pl.ds(p * 128, 128)

    for p in range(2):
        for f in range(2):
            axis = axes[f][0]
            for d in range(1, n.count[axis]):
                target = jnp.minimum(n.further(axis, d), OWN - 1)
                n.send(
                    n.goes_inside(axis, d), gs_ref.at[f, pl.ds(target * 2, 2), half_rows(p)],
                    first_in.at[f, d - 1, :, half_rows(p)], first_sem[f] + 2 * (d - 1) + p,
                    n.at(**{axis: n.further(axis, d)}),
                )
    own_copies = [
        pltpu.make_async_copy(gs_ref.at[f], acc.at[f], local_sems.at[f]) for f in range(2)
    ]
    for copy in own_copies:
        copy.start()

    def wide_load():
        return pltpu.make_async_copy(wide_ref, wide_acc, local_sems.at[4])

    def head_load():
        return pltpu.make_async_copy(headg_ref, head_acc, local_sems.at[5])

    def old_copies():
        sem = local_sems.at[6]
        return (
            (both(wide_owner, x == 0), lambda: pltpu.make_async_copy(mu_ref, old_turned, sem)),
            (both(wide_owner, x != 0), lambda: pltpu.make_async_copy(md_ref, old_plain, sem)),
            (
                both(square, task < 6),
                lambda: pltpu.make_async_copy(
                    mi_ref.at[jnp.minimum(task, 5)], old_turned.at[:, pl.ds(0, PIECE)], sem
                ),
            ),
            (
                both(square, task >= 6),
                lambda: pltpu.make_async_copy(
                    mo_ref.at[jnp.maximum(task, 6) - 6], old_plain.at[pl.ds(0, PIECE)], sem
                ),
            ),
            (head_owner, lambda: pltpu.make_async_copy(mh_ref, old_head, sem)),
        )

    on(wide, lambda: wide_load().start())
    on(head_column, lambda: head_load().start())
    for condition, copy in old_copies():
        on(condition, lambda copy=copy: copy().start())
    d_sem = n.recv_sem(1)
    n.send(core == 0, dlow_ref, d_in, d_sem, n.sibling)

    on(wide, lambda: wide_load().wait())
    near_sem, middle_sem, far_sem = n.recv_sem(4), n.recv_sem(4), n.recv_sem(4)

    def piece(k):
        return wide_acc.at[k // 2, pl.ds((k % 2) * PIECE, PIECE)]

    for k in range(4):
        n.send(both(wide, z == far_z), piece(k), wide_in.at[1, k], far_sem + k, n.at(z=middle_z))
        n.send(both(wide, z == near_z), piece(k), wide_in.at[0, k], near_sem + k, n.at(z=wide_z))

    def wide_pass(k):
        here = both(wide, z == middle_z)

        def take():
            n.landed(True, wide_in.at[1, k], far_sem + k)
            add_into(piece(k), [wide_in.at[1, k]], 128)

        on(here, take)
        n.send(here, piece(k), wide_in.at[1, k], middle_sem + k, n.at(z=wide_z))

    on(head_column, lambda: head_load().wait())
    head_sem = n.recv_sem(2)

    def head_pass(distance):
        here = both(head_column, z == distance)
        for p in range(2):
            if distance < nz - 1:

                def take(p=p):
                    n.landed(True, head_in.at[p], head_sem + p)
                    add_into(head_acc.at[p], [head_in.at[p]], HPART)

                on(here, take)
            n.send(here, head_acc.at[p], head_in.at[p], head_sem + p, n.at(z=distance - 1))

    head_pass(nz - 1)

    small_core = n.recv_sem(1)
    small_sem = {axis: n.recv_sem(n.count[axis]) for axis in ("x", "y", "z")}
    small_buf[0, 0] = jnp.zeros((SMALL, VOC), f32)
    small_buf[0, 0, 0:8, 0:D] = na_ref[...]
    small_buf[0, 0, 8:16, 0:D] = nf_ref[...]
    small_buf[0, 0, 16:24, :] = count_ref[...]
    n.send(True, small_buf.at[0, 0], small_buf.at[0, 1], small_core, n.sibling)

    def small_go(level, axis, value):
        small_buf[level, n.place[axis]] = value
        n.spread(axis, True, small_buf.at[level, n.place[axis]], small_sem[axis] + n.place[axis])

    def small_add(level, axis):
        for d in range(1, n.count[axis]):
            source = n.further(axis, d)
            n.landed(True, small_buf.at[level, source], small_sem[axis] + source)
        total = small_buf[level, 0]
        for s in range(1, n.count[axis]):
            total = total + small_buf[level, s]
        return total

    for copy in own_copies:
        copy.wait()
    n.landed(True, small_buf.at[0, 1], small_core)
    small_go(1, "x", small_buf[0, 0] + small_buf[0, 1])
    wide_pass(0)
    for p in range(2):
        for f in range(2):
            first, second = axes[f]
            mine = n.clipped(first) * 2

            def take(f=f, p=p, first=first, mine=mine):
                for d in range(1, n.count[first]):
                    n.landed(True, first_in.at[f, d - 1, :, half_rows(p)], first_sem[f] + 2 * (d - 1) + p)
                for j in range(2):
                    add_into(
                        acc.at[f, mine + j, half_rows(p)],
                        [first_in.at[f, d - 1, j, half_rows(p)] for d in range(1, n.count[first])], 128,
                    )

            on(n.inside(first), take)
            for d in range(1, n.count[second]):
                target = jnp.minimum(n.further(second, d), OWN - 1)
                n.send(
                    both(n.inside(first), n.goes_inside(second, d)), acc.at[f, mine + target, half_rows(p)],
                    second_in.at[f, d - 1, half_rows(p)], second_sem[f] + 2 * (d - 1) + p,
                    n.at(**{second: n.further(second, d)}),
                )
        wide_pass(1 + p)
        head_pass(2 - p)
    small_go(2, "y", small_add(1, "x"))

    def chunk(f):
        first, second = axes[f]
        return n.clipped(first) * 2 + n.clipped(second)

    band_sem = [n.recv_sem(2 * (nz - 1)) for _ in range(2)]
    for p in range(2):
        for f in range(2):
            second = axes[f][1]

            def take_second(f=f, p=p, second=second):
                for d in range(1, n.count[second]):
                    n.landed(True, second_in.at[f, d - 1, half_rows(p)], second_sem[f] + 2 * (d - 1) + p)
                add_into(
                    acc.at[f, chunk(f), half_rows(p)],
                    [second_in.at[f, d - 1, half_rows(p)] for d in range(1, n.count[second])], 128,
                )

            on(valid, take_second)
            for d in range(1, nz):
                n.send(
                    both(valid, z == lax.rem(square_z[f] + d, nz)), acc.at[f, chunk(f), half_rows(p)],
                    band_in.at[d - 1, half_rows(p)], band_sem[f] + 2 * (d - 1) + p, n.at(z=square_z[f]),
                )
    small_go(3, "z", small_add(2, "y"))
    wide_pass(3)

    own[...] = jnp.zeros_like(own)
    for condition, copy in old_copies():
        on(condition, lambda copy=copy: copy().wait())

    def turned(k):
        return jnp.swapaxes(old_turned[:, k * PIECE : (k + 1) * PIECE], 0, 1)

    back_ms = SquareBack(n, m_low, ms_land)
    back_mw = WideBack(
        n, m_low, lambda m, p: mw_land.at[m, p // 2, pl.ds((p % 2) * PIECE, PIECE)], 4, PIECE
    )
    back_mh = HeadBack(n, m_low, mh_land)
    back_xs = SquareBack(n, x_low, xs_land)
    back_q = WideBack(n, x_low, lambda m, p: q_land.at[m, core, p], 2, 128)
    back_xh = HeadBack(n, x_low, xh_land)

    def keep_moment(rows, value):
        own[rows, :] = value
        m_low[rows, :] = value.astype(bf16)

    def finish_wide(k, old):
        total = piece(k)[...].astype(f32) + wide_in[0, k].astype(f32) + wide_in[1, k].astype(f32)
        keep_moment(pl.ds(k * PIECE, PIECE), total + 0.5 * old)

    def wide_moment(k):
        n.landed(wide_owner, wide_in.at[0, k], near_sem + k)
        n.landed(wide_owner, wide_in.at[1, k], middle_sem + k)
        on(both(wide_owner, x == 0), lambda: finish_wide(k, turned(k)))
        on(both(wide_owner, x != 0), lambda: finish_wide(k, old_plain[pl.ds(k * PIECE, PIECE), :]))
        back_mw.start(k)

    def finish_square(p, old):
        f = jnp.where(owns[0], 0, 1)
        mine = jnp.where(owns[0], chunk(0), chunk(1))
        total = acc[f, mine, half_rows(p), :].astype(f32)
        for d in range(1, nz):
            total = total + band_in[d - 1, half_rows(p), :].astype(f32)
        keep_moment(half_rows(p), total + 0.5 * old)

    def square_moment(p):
        for f in range(2):
            for d in range(1, nz):
                n.landed(owns[f], band_in.at[d - 1, half_rows(p)], band_sem[f] + 2 * (d - 1) + p)
        on(
            both(square, task < 6),
            lambda: finish_square(p, jnp.swapaxes(old_turned[:, p * 128 : (p + 1) * 128], 0, 1)),
        )
        on(both(square, task >= 6), lambda: finish_square(p, old_plain[half_rows(p), :]))
        back_ms.start(p)

    def finish_head():
        old_plain[pl.ds(512, 128), :] = jnp.zeros((128, D), f32)
        old_plain[pl.ds(0, old_head.shape[0]), :] = old_head[...]
        for p in range(2):
            here = pl.ds(pl.multiple_of(core * HROWS + p * HPART, HPART), HPART)
            total = head_acc[p].astype(f32) + head_in[p].astype(f32)
            keep_moment(pl.ds(p * HPART, HPART), total + 0.5 * old_plain[here, :])

    wide_moment(0)
    for p in range(2):
        n.landed(head_owner, head_in.at[p], head_sem + p)
    on(head_owner, finish_head)
    back_mh.hop(0)
    square_moment(0)
    wide_moment(1)
    wide_moment(2)
    square_moment(1)
    wide_moment(3)

    blocks_used = jnp.where(wide_owner, 4, jnp.where(head_owner, 2, 1))
    gram[...] = jnp.zeros_like(gram)

    def gram_step(i, carry):
        high, low = split_two(own[pl.ds(pl.multiple_of(i * PIECE, PIECE), PIECE), :])
        gram[...] += mm_tn(high, high) + (mm_tn(high, low) + mm_tn(low, high))
        return carry

    lax.fori_loop(0, blocks_used, gram_step, 0)
    gram_sem = n.recv_sem(1)
    n.send(True, gram, gram_in, gram_sem, n.sibling)
    small_out[...] = small_add(3, "z")
    n.landed(True, gram_in, gram_sem)

    def eye_rows(first, rows):
        place = lax.broadcasted_iota(jnp.int32, (rows, D), 0) + first
        return (place == lax.broadcasted_iota(jnp.int32, (rows, D), 1)).astype(f32)

    def put(m, value):
        high, low = split_two(value)
        mats[m, 0] = high
        mats[m, 1] = low

    def product(a, b):
        ah, al = mats[a, 0], mats[a, 1]
        left_h, left_l = mats[b, 0, :, 0:256], mats[b, 1, :, 0:256]
        left = mm(ah, left_h) + (mm(ah, left_l) + mm(al, left_h))
        right_h, right_l = mats[b, 0, :, 256:512], mats[b, 1, :, 256:512]
        corner = mm(ah[256:], right_h) + (mm(ah[256:], right_l) + mm(al[256:], right_h))
        right = jnp.concatenate([jnp.swapaxes(left[256:], 0, 1), corner], axis=0)
        return jnp.concatenate([left, right], axis=1)

    busy = jnp.logical_or(square, jnp.logical_or(wide_owner, head_owner))
    total = jnp.sum(
        jnp.sum((gram[...] + gram_in[...]) * eye_rows(0, D), axis=0, keepdims=True), axis=1, keepdims=True
    )
    scale = 1.0 / (jnp.sqrt(total) + 1e-07)

    def begin():
        put(0, (gram[...] + gram_in[...]) * scale * scale)

    def begin_rows():
        own[pl.ds(0, PIECE), :] = own[pl.ds(0, PIECE), :] * scale

    on(busy, begin)
    on(square, begin_rows)
    between = {
        (0, 0): [partial(back_ms.one, 0), partial(back_mw.onward, 0)],
        (0, 1): [partial(back_mw.one, 0)],
        (0, 2): [partial(back_mw.onward, 1), partial(back_mh.hop, 1)],
        (0, 3): [partial(back_ms.one, 1), partial(back_mw.one, 1)],
        (1, 0): [partial(back_ms.two, 0), partial(back_mw.onward, 2)],
        (1, 1): [partial(back_mw.two, 0)],
        (1, 2): [partial(back_mh.hop, 2), partial(back_mw.one, 2)],
        (1, 3): [partial(back_ms.two, 1), partial(back_mw.two, 1)],
        (2, 0): [partial(back_mw.onward, 3)],
        (2, 1): [partial(back_mh.hop, 3)],
        (2, 2): [partial(back_mw.one, 3)],
        (2, 3): [back_mh.one, partial(back_mw.two, 2)],
        (3, 1): [partial(back_mw.two, 3)],
        (3, 3): [back_mh.two],
    }
    for iteration in range(NS_STEPS):
        q_now, q_next = (2, 4) if iteration % 2 == 0 else (4, 2)

        def polynomial():
            a = mats[0, 0].astype(f32) + mats[0, 1].astype(f32)
            put(1, NS_A * eye_rows(0, D) + NS_B * a + NS_C * product(0, 0))

        def update_rows():
            high, low = split_two(own[pl.ds(0, PIECE), :])
            ph, pll = mats[1, 0], mats[1, 1]
            own[pl.ds(0, PIECE), :] = mm(high, ph) + (mm(high, pll) + mm(low, ph))

        def update_q():
            if iteration == 0:
                mats[q_next] = mats[1]
            else:
                put(q_next, product(1, q_now))

        def first_factor():
            put(3, product(0, 1))

        def next_gram():
            put(0, product(3, 1))

        steps = [[(busy, polynomial)], [(square, update_rows), (jnp.logical_or(wide_owner, head_owner), update_q)]]
        if iteration < NS_STEPS - 1:
            steps += [[(busy, first_factor)], [(busy, next_gram)]]
        for j, step in enumerate(steps):
            for condition, body in step:
                on(condition, body)
            for move in between.get((iteration, j), ()):
                move()

    last = 4 if NS_STEPS % 2 == 1 else 2

    def direction():
        part = pl.ds(0, 512)
        high, low = split_two(own[part, :] * scale)
        value = mm(high, mats[last, 0]) + (mm(high, mats[last, 1]) + mm(low, mats[last, 0]))
        x_low[part, :] = value.astype(bf16)

    def wide_polynomial():
        rows = pl.ds(pl.multiple_of(core * PIECE, PIECE), PIECE)
        value = mats[last, 0, rows, :].astype(f32) + mats[last, 1, rows, :].astype(f32)
        x_low[pl.ds(0, PIECE), :] = (value * scale).astype(bf16)

    on(wide_owner, wide_polynomial)
    on(head_owner, direction)

    def keep_rows():
        x_low[pl.ds(0, PIECE), :] = own[pl.ds(0, PIECE), :].astype(bf16)

    on(square, keep_rows)
    back_xs.start(0)
    back_xs.start(1)
    back_q.start(0)
    back_q.start(1)
    back_xh.hop(0)
    back_q.onward(0)
    back_q.onward(1)
    back_xh.hop(1)
    outs = [
        pltpu.make_async_copy(src, dst, local_sems.at[i])
        for i, (src, dst) in enumerate(
            (
                (ms_land, ms_all), (mh_land, mh_all), (mw_land, mw_all), (xs_land, xs_all), (q_land, q_all),
                (xh_land, xh_all),
            )
        )
    ]
    back_xs.one(0)
    back_xh.hop(2)
    back_xs.one(1)
    back_q.one(0)
    back_q.one(1)
    back_xs.two(0)
    back_xh.hop(3)
    back_xh.one()
    back_xs.two(1)
    back_q.two(0)
    back_q.two(1)
    back_xh.two()
    back_mh.three()
    back_ms.end()
    outs[0].start()
    back_mh.end()
    outs[1].start()
    back_mw.end()
    outs[2].start()
    back_q.end()
    q_sem = n.recv_sem(2)
    for m in range(2):
        n.send(True, q_land.at[m, core], q_land.at[m, core], q_sem + m, n.sibling)
    back_xh.three()
    back_xs.end()
    outs[3].start()
    for m in range(2):
        n.landed(True, q_land.at[m, 1 - core], q_sem + m)
    outs[4].start()
    back_xh.end()
    outs[5].start()
    n.landed(core == 1, d_in, d_sem)
    n.all_sent()
    for copy in outs:
        copy.wait()


def run_muon(dims, gs, wide, headg, na, nf, count, dlow, mi, mo, mu, md, mh):
    nz, ny, nx = dims
    hbm = pl.BlockSpec(memory_space=pl.ANY)
    vmem = pl.BlockSpec(memory_space=VMEM)
    slots = max(nx, ny) - 1
    most = max(nx, ny, nz, 2)
    squares = (2, 4, PIECE, D)
    lands = [squares, squares, (2, 2, 512, D), (2, 2, 2, 128, D), (VOC, D), (VOC, D)]
    return pl.pallas_call(
        partial(muon_kernel, dims),
        in_specs=[hbm] * 3 + [vmem] * 3 + [hbm] * 6,
        out_specs=[hbm] * 7 + [vmem],
        out_shape=[sds(s, bf16) for s in lands] + [sds((512, D), bf16), sds((SMALL, VOC), f32)],
        scratch_shapes=[
            VMEM(squares, bf16),
            VMEM((2, slots, 2, PIECE, D), bf16),
            VMEM((2, slots, PIECE, D), bf16),
            VMEM((nz - 1, PIECE, D), bf16),
            VMEM((2, 512, D), bf16),
            VMEM((2, 4, PIECE, D), bf16),
            VMEM((2, HPART, D), bf16),
            VMEM((2, HPART, D), bf16),
            VMEM((4, most, SMALL, VOC), f32),
            VMEM((D, 1024), f32),
            VMEM((1024, D), f32),
            VMEM(mh.shape, f32),
            VMEM((1024, D), f32),
            VMEM((D, D), f32),
            VMEM((D, D), f32),
            VMEM((5, 2, D, D), bf16),
            VMEM((1024, D), bf16),
            VMEM((512, D), bf16),
        ]
        + [VMEM(s, bf16) for s in lands]
        + [
            pltpu.SemaphoreType.DMA((400,)), pltpu.SemaphoreType.DMA((160,)), pltpu.SemaphoreType.DMA((8,)),
        ],
        compiler_params=pltpu.CompilerParams(
            vmem_limit_bytes=60 * MIB, collective_id=0, has_side_effects=True
        ),
        cost_estimate=pl.CostEstimate(flops=20 * 10**9, bytes_accessed=40 * MIB, transcendentals=0),
        name="reduce_muon_spread",
    )(gs, wide, headg, na, nf, count, dlow, mi, mo, mu, md, mh)


def finish_kernel(
    wide_rate, head_rate, core_ref,
    mu, md, mb, q_ref, xb, mh, xh, ai, ao, fi, fo, vh, small, gain, bias, nm, dm, dr,
    mi_out, ni_out, mo_out, no_out, mu_out, nu_out, md_out, nd_out, mh_out, nh_out,
    mn_out, nn_out, counts_out, dm_out,
):
    i = pl.program_id(0)
    same = lax.broadcasted_iota(jnp.int32, (D, D), 0) == lax.broadcasted_iota(jnp.int32, (D, D), 1)
    eye = same.astype(f32).astype(bf16)
    mu_out[...] = mm_nt(eye, mu[0, 0])
    nu_out[...] = fi[...] - wide_rate * mm_nt(q_ref[0], mu[0, 0])
    md_out[...] = md[0, 0].astype(f32)
    nd_out[...] = fo[...] - wide_rate * mm(md[0, 0], q_ref[1])

    @pl.when(i < 3)
    def _():
        for j in range(2):
            mi_out[j] = mm_nt(eye, mb[0, j])
            ni_out[j] = ai[j] - muon_rate * mm_nt(eye, xb[0, j])

    @pl.when(i == 3)
    def _():
        for j in range(2):
            mo_out[j] = mb[0, j].astype(f32)
            no_out[j] = ao[j] - muon_rate * xb[0, j].astype(f32)

    dm_out[...] = jnp.where((core_ref[0] == 0) | (i >= 2), dm[...], dr[...].astype(f32))

    @pl.when(i == 0)
    def _():
        vocab = vh.shape[0]
        mh_out[...] = mh[0:vocab, :].astype(f32)
        nh_out[...] = vh[...] - head_rate * xh[0:vocab, :].astype(f32)
        for kind, old in enumerate((gain, bias)):
            first = 2 * kind
            total = jnp.concatenate([small[first : first + 2, 0:D], small[first + 8 : first + 10, 0:D]], axis=0)
            moment = 0.5 * nm[kind] + total
            mn_out[kind] = moment
            nn_out[kind] = old[...] - vector_rate * moment * lax.rsqrt(
                jnp.mean(moment * moment, axis=-1, keepdims=True) + 1e-06
            )
        counts_out[...] = small[16:17, 0:vocab].astype(jnp.int32)


def run_finish(core, ms, xs, mw, q, m_head, x_head, ai, ao, fi, fo, vh, small, gain, bias, nm, dmem, d_in):
    vocab = vh.shape[0]
    wide_rate = muon_rate * math.sqrt(2 * fi.shape[1] / D)
    head_rate = muon_rate * math.sqrt(vocab / D)

    def spec(shape, index):
        return pl.BlockSpec(shape, index)

    def fixed(shape):
        return pl.BlockSpec(shape, lambda i, c: (0,) * len(shape))

    up = spec((1, 1, 256, D), lambda i, c: (0, i // 2, i % 2, 0))
    down = spec((1, 1, 256, D), lambda i, c: (1, i // 2, i % 2, 0))
    bands = spec((1, 2, 256, D), lambda i, c: (i // 2, i % 2, 0, 0))
    inner = spec((2, D, 256), lambda i, c: (jnp.minimum(i, 2), 0, 0))
    outer = spec((2, 256, D), lambda i, c: (0, 0, 0))
    cols = spec((D, 256), lambda i, c: (0, i))
    rows = spec((256, D), lambda i, c: (i, 0))
    head = fixed((vocab, D))
    shapes = [
        (sds((6, D, 256), f32), inner), (sds((6, D, 256), f32), inner),
        (sds((2, 256, D), f32), outer), (sds((2, 256, D), f32), outer),
        (sds(fi.shape, f32), cols), (sds(fi.shape, f32), cols),
        (sds(fo.shape, f32), rows), (sds(fo.shape, f32), rows),
        (sds((vocab, D), f32), head), (sds((vocab, D), f32), head),
        (sds((2, 4, D), f32), fixed((2, 4, D))), (sds((2, 4, D), f32), fixed((2, 4, D))),
        (sds((1, vocab), jnp.int32), fixed((1, vocab))),
        (sds((1024, D), f32), rows),
    ]
    return pl.pallas_call(
        partial(finish_kernel, wide_rate, head_rate),
        grid_spec=pltpu.PrefetchScalarGridSpec(
            num_scalar_prefetch=1,
            grid=(4,),
            in_specs=[
                up, down, bands, fixed((2, D, D)), bands, fixed((VOC, D)), fixed((VOC, D)),
                inner, outer, cols, rows, head, fixed((SMALL, VOC)), fixed((4, D)), fixed((4, D)), fixed((2, 4, D)),
                spec((256, D), lambda i, c: (jnp.where(c[0] == 0, i, jnp.maximum(i - 2, 0)), 0)),
                spec((256, D), lambda i, c: (jnp.minimum(i, 1), 0)),
            ],
            out_specs=[s[1] for s in shapes],
        ),
        out_shape=[s[0] for s in shapes],
        compiler_params=pltpu.CompilerParams(vmem_limit_bytes=60 * MIB),
        cost_estimate=pl.CostEstimate(flops=10**7, bytes_accessed=40 * MIB, transcendentals=0),
        name="finish_weights",
    )(core, mw, mw, ms, q.reshape(2, D, D), xs, m_head, x_head, ai, ao, fi, fo, vh, small,
      gain, bias, nm, dmem, d_in)


def local(
    residual_in, memory, lengths, targets, attn_in, attn_out, ffn_in, ffn_out, vocab_head,
    norm_gain, norm_bias, attn_in_moment, attn_out_moment, ffn_in_moment, ffn_out_moment,
    head_moment, norm_moment,
):
    dims = chip_dims(lax.axis_size("dp"))
    core = lax.axis_index("mp")
    tokens = residual_in.shape[0] * lax.axis_size("mp") * lax.axis_size("dp")
    vocab = vocab_head.shape[1]
    inner = attn_in.reshape(6, D, 256)
    wa0, wa1, wo0, wo1, wi0, wi1, wf0, wf1, mem, wh, total = run_prepare(
        dims, lengths, inner, attn_out, ffn_in, ffn_out, vocab_head.T, memory
    )
    wa, wo, wi, wf = (wa0, wa1), (wo0, wo1), (wi0, wi1), (wf0, wf1)
    h1, qkv, p, o, x1, h2, cq, kv, pc, oc, x2 = run_forward(
        lengths, residual_in, mem, wa, wo, norm_gain, norm_bias
    )
    out, g2, gw, ghead, gnorm_ffn, counts = run_middle(
        lengths, total, x2, targets[:, None], wi, wf, wh, norm_gain, norm_bias, vocab, float(tokens)
    )
    dx, dmem, dlow, gs, gnorm_attn, wide, head_part = run_backward(
        dims, g2, residual_in, x1, h1, qkv, p, o, h2, cq, kv, pc, oc, mem, wa, wo, norm_gain, gw, ghead
    )
    ms, xs, mw, q, head_m, head_x, d_in, small = run_muon(
        dims, gs, wide, head_part, gnorm_attn, gnorm_ffn, counts, dlow,
        attn_in_moment.reshape(6, D, 256), attn_out_moment, ffn_in_moment, ffn_out_moment, head_moment.T,
    )
    (
        moment_in, new_in, moment_out, new_out, moment_up, new_up, moment_down, new_down,
        moment_head, new_head, moment_norms, new_norms, token_counts, memory_grad,
    ) = run_finish(
        core.reshape(1), ms, xs, mw, q, head_m, head_x, inner, attn_out, ffn_in, ffn_out,
        vocab_head.T, small, norm_gain, norm_bias, norm_moment, dmem, d_in,
    )
    return (
        out, dx, memory_grad, moment_in.reshape(attn_in.shape), new_in.reshape(attn_in.shape),
        moment_out, new_out, moment_up, new_up, moment_down, new_down, moment_head.T, new_head.T,
        moment_norms, new_norms,
        token_counts.reshape(vocab),
    )


def solution(mesh):
    rows = P(("dp", "mp"), None)
    placed = (
        rows, rows, P("dp"), P(("dp", "mp")),
        P(None, None, None, "mp"), P(None, "mp", None), P(None, "mp"), P("mp", None), P(), P(), P(),
        P(None, None, None, "mp"), P(None, "mp", None), P(None, "mp"), P("mp", None), P(), P(),
    )
    return jax.shard_map(
        local,
        mesh=mesh,
        in_specs=placed,
        out_specs=(
            rows, rows, rows,
            P(None, None, None, "mp"), P(None, None, None, "mp"),
            P(None, "mp", None), P(None, "mp", None),
            P(None, "mp"), P(None, "mp"), P("mp", None), P("mp", None),
            P(), P(), P(), P(), P(),
        ),
        check_vma=False,
    )
```

```python
from functools import partial
import math

import jax
import jax.numpy as jnp
from jax import lax
from jax.experimental import pallas as pl
from jax.experimental.pallas import tpu as pltpu
from jax.sharding import PartitionSpec as P

HEAD = 64
CAP_S = 64
CAP_M = 128
CAP_L = 256
MEM = 128
SETS = 4
NS_STEPS = 5
NS_A = 3.4445
NS_B = -4.775
NS_C = 2.0315
muon_rate = 0.5
vector_rate = 0.05

D = 512
BLK = 256
WIDE = 512
TALL = 1024
VOC = 640
HROWS = 320
HPART = 160
MIB = 1024 * 1024
bf16 = jnp.bfloat16
f32 = jnp.float32
VMEM = pltpu.VMEM


def mm(a, b):
    return jnp.dot(a, b, preferred_element_type=f32)


def mm_nt(a, b):
    return lax.dot_general(a, b, (((1,), (1,)), ((), ())), preferred_element_type=f32)


def mm_tn(a, b):
    return lax.dot_general(a, b, (((0,), (0,)), ((), ())), preferred_element_type=f32)


def norm_stats(value):
    average = jnp.mean(value, axis=-1, keepdims=True)
    centred = value - average
    variance = jnp.mean(centred * centred, axis=-1, keepdims=True)
    inverse = lax.rsqrt(variance + 1e-05)
    return centred * inverse, inverse


def norm_back(gradient, normed, inverse, gain):
    scaled = gradient * gain
    return inverse * (
        scaled
        - jnp.mean(scaled, axis=-1, keepdims=True)
        - normed * jnp.mean(scaled * normed, axis=-1, keepdims=True)
    )


def lane_masks(width):
    lanes = lax.broadcasted_iota(jnp.int32, (1, width), 1)
    return [(lanes // HEAD == h).astype(f32).astype(bf16) for h in range(width // HEAD)]


def spread(block, masks):
    return jnp.concatenate([block * m for m in masks], axis=0)


def pick(stacked, masks, rows):
    total = stacked[:rows] * masks[0].astype(f32)
    for h in range(1, len(masks)):
        total = total + stacked[h * rows : (h + 1) * rows] * masks[h].astype(f32)
    return total


def softmax_rows(scores):
    top = jnp.max(scores, axis=-1, keepdims=True)
    exps = jnp.exp(scores - top)
    return exps * (1.0 / jnp.sum(exps, axis=-1, keepdims=True))


def mem_slot(core, block, unit):
    on_first = jnp.where(block < 2, 4 * block + unit, 8 + 2 * (block - 2) + unit // 2)
    return jnp.where(core == 0, on_first, block)


def row_limits(core, block, lengths_ref):
    unit = lax.broadcasted_iota(jnp.int32, (BLK, 1), 0) // CAP_S
    low = jnp.zeros((BLK, 1), jnp.int32)
    length = jnp.zeros((BLK, 1), jnp.int32)
    for u in range(BLK // CAP_S):
        on_first = jnp.where(block < 2, u * CAP_S, u // 2 * CAP_M)
        slot = mem_slot(core, block, u) + jnp.where(core == 0, 0, 3 * SETS)
        low = jnp.where(unit == u, jnp.where(core == 0, on_first, 0), low)
        length = jnp.where(unit == u, lengths_ref[slot], length)
    return low, length


def rows_live(core, first, blocks, lengths_ref):
    pieces = []
    for j in range(blocks):
        low, length = row_limits(core, first + j, lengths_ref)
        place = lax.broadcasted_iota(jnp.int32, (BLK, 1), 0)
        pieces.append((place - low < length).astype(f32))
    return jnp.concatenate(pieces, axis=0)


def forward_kernel(
    lengths_ref, x_ref, mem_ref, wa0, wa1, wo0, wo1, gain_ref, bias_ref, fi_ref, fo_ref,
    h1_ref, qkv_ref, p_ref, o_ref, x1_ref, h2_ref, cq_ref, kv_ref, pc_ref, oc_ref, x2_ref, wi0, wi1, wf0, wf1,
    fi_in, fo_in, fi_low, fo_low, load_sems, keep_sems, send_sems, recv_sems,
):
    core = lax.axis_index("mp")
    step = pl.program_id(0)
    wa = (wa0, wa1)
    sibling = {"mp": 1 - core}

    def weight_copies():
        triples = ((fi_ref, fi_in, fi_low, wi0, wi1), (fo_ref, fo_in, fo_low, wf0, wf1))
        return [
            (
                pltpu.make_async_copy(src, staged, load_sems.at[i]),
                pltpu.make_async_copy(low, mine, keep_sems.at[i]),
                pltpu.make_async_remote_copy(
                    src_ref=low, dst_ref=others, send_sem=send_sems.at[i], recv_sem=recv_sems.at[i],
                    device_id=sibling, device_id_type=pl.DeviceIdType.MESH,
                ),
            )
            for i, (src, staged, low, mine, others) in enumerate(triples)
        ]

    @pl.when(step == 0)
    def _():
        for load, _, _ in weight_copies():
            load.start()
        barrier = pltpu.get_barrier_semaphore()
        pl.semaphore_signal(barrier, inc=1, device_id=sibling, device_id_type=pl.DeviceIdType.MESH)
        pl.semaphore_wait(barrier, 1)
        def fill(i, carry):
            rows = pl.ds(pl.multiple_of(i * WIDE, WIDE), WIDE)
            for half in range(2):
                for which in range(2):
                    kv_ref[rows, pl.ds(which * D + half * 256, 256)] = mm(
                        mem_ref[rows, :], wa[half][4 + which]
                    ).astype(bf16)
            return carry

        lax.fori_loop(0, jnp.where(core == 0, 3, 1), fill, 0)
        for (load, keep, send), staged, low in zip(weight_copies(), (fi_in, fo_in), (fi_low, fo_low)):
            load.wait()
            low[...] = staged[...].astype(bf16)
            send.start()
            keep.start()

    normed, _ = norm_stats(x_ref[...].astype(f32))
    h1_ref[...] = (normed * gain_ref[0:1, :] + bias_ref[0:1, :]).astype(bf16)
    for half in range(2):
        for which in range(3):
            qkv_ref[:, pl.ds(which * D + half * 256, 256)] = mm(h1_ref[...], wa[half][which]).astype(bf16)
    pair = lane_masks(128)
    for j in range(WIDE // BLK):
        rows = pl.ds(j * BLK, BLK)
        low, length = row_limits(core, step * (WIDE // BLK) + j, lengths_ref)
        keys = lax.broadcasted_iota(jnp.int32, (BLK, BLK), 1)
        queries = lax.broadcasted_iota(jnp.int32, (BLK, BLK), 0)
        allowed = (keys >= low) & (keys < low + length) & (keys <= queries)
        for i in range(4):
            q = qkv_ref[rows, pl.ds(i * 128, 128)] * jnp.bfloat16(0.125)
            k = qkv_ref[rows, pl.ds(D + i * 128, 128)]
            v = qkv_ref[rows, pl.ds(2 * D + i * 128, 128)]
            scores = mm_nt(spread(q, pair), k).reshape(2, BLK, BLK)
            scores = jnp.where(allowed[None], scores, -1000000000.0)
            probs = softmax_rows(scores).astype(bf16).reshape(2 * BLK, BLK)
            p_ref[j, i] = probs
            o_ref[rows, pl.ds(i * 128, 128)] = pick(mm(probs, v), pair, BLK).astype(bf16)
    x1 = x_ref[...].astype(f32) + mm(o_ref[:, :256], wo0[0]) + mm(o_ref[:, 256:], wo1[0])
    x1_ref[...] = x1
    normed, _ = norm_stats(x1)
    h2_ref[...] = (normed * gain_ref[1:2, :] + bias_ref[1:2, :]).astype(bf16)
    for half in range(2):
        cq_ref[:, pl.ds(half * 256, 256)] = mm(h2_ref[...], wa[half][3]).astype(bf16)
    quad = lane_masks(256)
    for u in range(WIDE // 64):
        rows = pl.ds(u * 64, 64)
        block = step * (WIDE // BLK) + u // 4
        slot = pl.ds(pl.multiple_of(mem_slot(core, block, u % 4) * MEM, MEM), MEM)
        for j in range(2):
            q = cq_ref[rows, pl.ds(j * 256, 256)] * jnp.bfloat16(0.125)
            k = kv_ref[slot, pl.ds(j * 256, 256)]
            v = kv_ref[slot, pl.ds(D + j * 256, 256)]
            probs = softmax_rows(mm_nt(spread(q, quad), k)).astype(bf16)
            pc_ref[u // 4, u % 4 * 2 + j] = probs
            oc_ref[rows, pl.ds(j * 256, 256)] = pick(mm(probs, v), quad, 64).astype(bf16)
    x2_ref[...] = x1_ref[...] + mm(oc_ref[:, :256], wo0[1]) + mm(oc_ref[:, 256:], wo1[1])

    @pl.when(step == pl.num_programs(0) - 1)
    def _():
        for _, keep, send in weight_copies():
            keep.wait()
            send.wait()


def gelu_parts(u):
    z = jnp.abs(u) * math.sqrt(0.5 / math.log(2.0))
    below = 1.0 + (0.3275911 * math.sqrt(math.log(2.0))) * z
    guess = pl.reciprocal(below, approx=True)
    t = guess * (2.0 - below * guess)
    gauss = jnp.exp2(-(z * z))
    tail = gauss * (
        t * (0.127414796 + t * (-0.142248368 + t * (0.7107068705 + t * (-0.7265760135 + t * 0.5307027145))))
    )
    cdf = jnp.where(u < 0, tail, 1.0 - tail)
    return u * cdf, cdf + u * (gauss * (1.0 / math.sqrt(2.0 * math.pi)))


def middle_kernel(
    vocab, tokens, lengths_ref, total_ref, x2_ref, targets_ref, wi0, wi1, wf0, wf1, wh_ref, gain_ref, bias_ref,
    out_ref, g2_ref, gw_ref, ghead_ref, gnorm_ref, count_ref,
    h3_all, a_all, dy_all, du_all, z_all, gl_all, slope,
):
    block = pl.program_id(0)
    rows = pl.ds(pl.multiple_of(block * TALL, TALL), TALL)
    wi = (wi0, wi1)
    wf = (wf0, wf1)
    x2 = x2_ref[...]
    normed2, inverse2 = norm_stats(x2)
    h3 = (normed2 * gain_ref[2:3, :] + bias_ref[2:3, :]).astype(bf16)
    h3_all[rows, :] = h3
    for half in range(2):
        for j in range(2):
            wide = pl.ds(half * 1024 + j * 512, 512)
            active, grad = gelu_parts(mm(h3, wi[half][:, j * 512 : (j + 1) * 512]))
            a_all[rows, wide] = active.astype(bf16)
            slope[:, wide] = grad
    x3 = x2_ref[...] + mm(a_all[rows, 0:1024], wf0[...]) + mm(a_all[rows, 1024:2048], wf1[...])
    out_ref[...] = x3.astype(bf16)
    normed3, inverse3 = norm_stats(x3)
    z = (normed3 * gain_ref[3:4, :] + bias_ref[3:4, :]).astype(bf16)
    z_all[rows, :] = z
    logits = mm_nt(z, wh_ref[...])
    columns = lax.broadcasted_iota(jnp.int32, (TALL, VOC), 1)
    logits = jnp.where(columns < vocab, logits, -1e30)
    probs = softmax_rows(logits)
    onehot = (columns == targets_ref[...]).astype(f32)
    live = rows_live(lax.axis_index("mp"), block * (TALL // BLK), TALL // BLK, lengths_ref)
    gl = (tokens / total_ref[0:1, 0:1] * live * (probs - onehot)).astype(bf16)
    gl_all[rows, :] = gl
    counts = jnp.sum(onehot * live, axis=0, keepdims=True)
    gz = mm(gl, wh_ref[...])
    gain3 = jnp.sum(gz * normed3, axis=0, keepdims=True)
    bias3 = jnp.sum(gz, axis=0, keepdims=True)
    g3 = norm_back(gz, normed3, inverse3, gain_ref[3:4, :])
    dy = g3.astype(bf16)
    dy_all[rows, :] = dy
    g2_ref[...] = g3
    for half in range(2):
        for j in range(2):
            wide = pl.ds(half * 1024 + j * 512, 512)
            back = mm_nt(dy, wf[half][j * 512 : (j + 1) * 512, :])
            du_all[rows, wide] = (slope[:, wide] * back).astype(bf16)
    dh = mm_nt(du_all[rows, 0:1024], wi0[...]) + mm_nt(du_all[rows, 1024:2048], wi1[...])
    normed2, inverse2 = norm_stats(x2_ref[...])
    gain2 = jnp.sum(dh * normed2, axis=0, keepdims=True)
    bias2 = jnp.sum(dh, axis=0, keepdims=True)
    g2_ref[...] = g2_ref[...] + norm_back(dh, normed2, inverse2, gain_ref[2:3, :])

    @pl.when(block == 0)
    def _():
        gnorm_ref[...] = jnp.zeros_like(gnorm_ref)
        count_ref[...] = jnp.zeros_like(count_ref)

    gnorm_ref[0:1, :] += gain2
    gnorm_ref[1:2, :] += gain3
    gnorm_ref[2:3, :] += bias2
    gnorm_ref[3:4, :] += bias3
    count_ref[0:1, :] += counts

    @pl.when(block == pl.num_programs(0) - 1)
    def _():
        for half in range(2):
            for j in range(2):
                col = pl.ds(half * 1024 + j * 512, 512)
                gw_ref[half, 0, j] = mm_tn(du_all[:, col], h3_all[...]).astype(bf16)
                gw_ref[half, 1, j] = mm_tn(a_all[:, col], dy_all[...]).astype(bf16)
        ghead_ref[...] = mm_tn(gl_all[...], z_all[...]).astype(bf16)


def attend_back(queries, keys, values, probs, grads, masks, rows):
    q = spread(queries, masks)
    do = spread(grads, masks)
    dprobs = mm_nt(do, values)
    p = probs.astype(f32)
    weighted = p * dprobs
    ds = (weighted - p * jnp.sum(weighted, axis=-1, keepdims=True)).astype(bf16)
    dv = mm_tn(probs, do)
    dq = pick(mm(ds, keys), masks, rows) * 0.125
    dk = mm_tn(ds, q) * 0.125
    return dq, dk, dv


def backward_kernel(
    dims, g2_ref, x_ref, x1_ref, h1_ref, qkv_ref, p_ref, o_ref, h2_ref, cq_ref, kv_ref, pc_ref, oc_ref,
    mem_ref, wa0, wa1, wo0, wo1, gain_ref, gw_ref, ghead_ref,
    dx_ref, dmem_ref, dlow_ref, gs_ref, gnorm_ref, wide_out, head_out,
    dyc_all, dcq_all, dys_all, dqkv_all, dkv_all, dkv_low,
    early_acc, early_core, early_first, early_second, head_acc, head_core, head_first, head_second,
    gs_away, gs_in, send_sems, recv_sems, local_sems,
):
    core = lax.axis_index("mp")
    block = pl.program_id(0)
    early = EarlySum(
        Net(dims, send_sems, recv_sems), gw_ref, ghead_ref, wide_out, head_out,
        (
            early_acc, early_core, early_first, early_second, head_acc, head_core, head_first, head_second,
            local_sems,
        ),
    )
    band_sem = early.net.recv_sem(4)
    pl.when(block == 0)(early.start)
    rows = pl.ds(pl.multiple_of(block * BLK, BLK), BLK)
    wa = (wa0, wa1)
    wo = (wo0, wo1)

    @pl.when(block == 0)
    def _():
        gnorm_ref[...] = jnp.zeros_like(gnorm_ref)
        dkv_all[...] = jnp.zeros_like(dkv_all)

    g2 = g2_ref[...]
    dyc = g2.astype(bf16)
    dyc_all[rows, :] = dyc
    quad = lane_masks(256)
    for j in range(2):
        lanes = pl.ds(j * 256, 256)
        do = mm_nt(dyc, wo[j][1]).astype(bf16)
        for u in range(4):
            base = pl.multiple_of(block * BLK + u * 64, 64)
            slot = pl.ds(pl.multiple_of(mem_slot(core, block, u) * MEM, MEM), MEM)
            dq, dk, dv = attend_back(
                cq_ref[u * 64 : (u + 1) * 64, lanes],
                kv_ref[slot, lanes],
                kv_ref[slot, pl.ds(D + j * 256, 256)],
                pc_ref[0, u * 2 + j],
                do[u * 64 : (u + 1) * 64],
                quad,
                64,
            )
            dcq_all[pl.ds(base, 64), lanes] = dq.astype(bf16)
            dkv_all[slot, lanes] += dk
            dkv_all[slot, pl.ds(D + j * 256, 256)] += dv
    dcq = dcq_all[rows, :]
    dh = mm_nt(dcq[:, :256], wa0[3]) + mm_nt(dcq[:, 256:], wa1[3])
    normed, inverse = norm_stats(x1_ref[...])
    gnorm_ref[1:2, :] += jnp.sum(dh * normed, axis=0, keepdims=True)
    gnorm_ref[3:4, :] += jnp.sum(dh, axis=0, keepdims=True)
    g1 = g2 + norm_back(dh, normed, inverse, gain_ref[1:2, :])
    pl.when(block == 0)(early.one)
    dys = g1.astype(bf16)
    dys_all[rows, :] = dys
    pair = lane_masks(128)
    for half in range(2):
        do_half = mm_nt(dys, wo[half][0]).astype(bf16)
        for i in range(2):
            first = half * 256 + i * 128
            dq, dk, dv = attend_back(
                qkv_ref[:, pl.ds(first, 128)],
                qkv_ref[:, pl.ds(D + first, 128)],
                qkv_ref[:, pl.ds(2 * D + first, 128)],
                p_ref[0, half * 2 + i],
                do_half[:, i * 128 : (i + 1) * 128],
                pair,
                BLK,
            )
            dqkv_all[rows, pl.ds(first, 128)] = dq.astype(bf16)
            dqkv_all[rows, pl.ds(D + first, 128)] = dk.astype(bf16)
            dqkv_all[rows, pl.ds(2 * D + first, 128)] = dv.astype(bf16)
    dqkv = dqkv_all[rows, :]
    dh = jnp.zeros((BLK, D), f32)
    for half in range(2):
        for which in range(3):
            first = which * D + half * 256
            dh = dh + mm_nt(dqkv[:, first : first + 256], wa[half][which])
    normed, inverse = norm_stats(x_ref[...].astype(f32))
    gnorm_ref[0:1, :] += jnp.sum(dh * normed, axis=0, keepdims=True)
    gnorm_ref[2:3, :] += jnp.sum(dh, axis=0, keepdims=True)
    dx_ref[...] = g1 + norm_back(dh, normed, inverse, gain_ref[0:1, :])
    pl.when(block == 2)(early.two)

    @pl.when(block == pl.num_programs(0) - 1)
    def _():
        def memory_rows(i, carry):
            part = pl.ds(pl.multiple_of(i * BLK, BLK), BLK)
            low = dkv_all[part, :].astype(bf16)
            dkv_low[part, :] = low
            total = jnp.zeros((BLK, D), f32)
            for half in range(2):
                for which in range(2):
                    first = which * D + half * 256
                    total = total + mm_nt(low[:, first : first + 256], wa[half][4 + which])
            dmem_ref[part, :] = total
            return carry

        lax.fori_loop(0, jnp.where(core == 0, 6, 2), memory_rows, 0)

        @pl.when(core != 0)
        def _():
            dkv_low[512:, :] = jnp.zeros((1024, 2 * D), bf16)
            dmem_ref[512:, :] = jnp.zeros((1024, D), f32)

        dlow_ref[...] = dmem_ref[1024:, :].astype(bf16)

        def bands(half, put):
            col = pl.ds(half * 256, 256)
            for which in range(3):
                put(0, which, mm_tn(dqkv_all[:, pl.ds(which * D + half * 256, 256)], h1_ref[...]))
            put(0, 3, mm_tn(dcq_all[:, col], h2_ref[...]))
            for which in range(2):
                put(1, which, mm_tn(dkv_low[:, pl.ds(which * D + half * 256, 256)], mem_ref[...]))
            put(1, 2, mm_tn(o_ref[:, col], dys_all[...]))
            put(1, 3, mm_tn(oc_ref[:, col], dyc_all[...]))

        def put_away(f, j, value):
            gs_away[f, j] = value.astype(bf16)
            if j % 2 == 1:
                pair = pl.ds(j - 1, 2)
                early.net.send(
                    True, gs_away.at[f, pair], gs_in.at[f, pair], band_sem + 2 * f + j // 2, early.net.sibling
                )

        def put_here(f, j, value):
            gs_ref[f, j] = value.astype(bf16)

        early.keep_sends()
        bands(1, put_away)
        bands(0, put_here)
        early.three()
        for f in range(2):
            for j in range(4):
                if j % 2 == 0:
                    early.net.landed(True, gs_in.at[f, pl.ds(j, 2)], band_sem + 2 * f + j // 2)
                add_into(gs_ref.at[f, j], [gs_in.at[f, j]], 128)
        early.net.all_sent()
        early.end()


def whole(shape):
    return pl.BlockSpec(shape, lambda i: (0,) * len(shape), pipeline_mode=pl.Buffered(1))


def by_rows(width):
    return pl.BlockSpec((BLK, width), lambda i: (i, 0))


def wide_rows(width):
    return pl.BlockSpec((WIDE, width), lambda i: (i, 0))


def tall_rows(width):
    return pl.BlockSpec((TALL, width), lambda i: (i, 0))


def sds(shape, dtype):
    return jax.ShapeDtypeStruct(shape, dtype)


def run_forward(lengths, x, mem, wa, wo, gain, bias, fi, fo):
    rows = x.shape[0]
    steps = rows // WIDE
    outs = [
        (sds((rows, D), bf16), wide_rows(D)),
        (sds((rows, 3 * D), bf16), wide_rows(3 * D)),
        (sds((rows // BLK, 4, 512, 256), bf16), pl.BlockSpec((2, 4, 512, 256), lambda i: (i, 0, 0, 0))),
        (sds((rows, D), bf16), wide_rows(D)),
        (sds((rows, D), f32), wide_rows(D)),
        (sds((rows, D), bf16), wide_rows(D)),
        (sds((rows, D), bf16), wide_rows(D)),
        (sds((1536, 2 * D), bf16), whole((1536, 2 * D))),
        (sds((rows // BLK, 8, 256, 128), bf16), pl.BlockSpec((2, 8, 256, 128), lambda i: (i, 0, 0, 0))),
        (sds((rows, D), bf16), wide_rows(D)),
        (sds((rows, D), f32), wide_rows(D)),
    ] + [(sds(w.shape, bf16), pl.BlockSpec(memory_space=pl.ANY)) for w in (fi, fi, fo, fo)]
    return pl.pallas_call(
        forward_kernel,
        grid=(steps,),
        in_specs=[
            pl.BlockSpec(memory_space=pltpu.SMEM), wide_rows(D), whole((1536, D)),
            whole((6, D, 256)), whole((6, D, 256)), whole((2, 256, D)), whole((2, 256, D)),
            whole((4, D)), whole((4, D)),
            pl.BlockSpec(memory_space=pl.ANY), pl.BlockSpec(memory_space=pl.ANY),
        ],
        out_specs=[o[1] for o in outs],
        out_shape=[o[0] for o in outs],
        scratch_shapes=[
            VMEM(fi.shape, f32), VMEM(fo.shape, f32), VMEM(fi.shape, bf16), VMEM(fo.shape, bf16),
            pltpu.SemaphoreType.DMA((2,)), pltpu.SemaphoreType.DMA((2,)),
            pltpu.SemaphoreType.DMA((2,)), pltpu.SemaphoreType.DMA((2,)),
        ],
        compiler_params=pltpu.CompilerParams(
            vmem_limit_bytes=60 * MIB, collective_id=3, has_side_effects=True
        ),
        cost_estimate=pl.CostEstimate(flops=9 * 10**9, bytes_accessed=22 * MIB, transcendentals=3 * 10**6),
        name="layer_forward",
    )(lengths, x, mem, wa[0], wa[1], wo[0], wo[1], gain, bias, fi, fo)


def run_middle(lengths, total, x2, targets, wi, wf, wh, gain, bias, vocab, tokens):
    rows = x2.shape[0]
    steps = rows // TALL
    outs = [
        (sds((rows, D), bf16), tall_rows(D)),
        (sds((rows, D), f32), tall_rows(D)),
        (sds((2, 2, 2, 512, D), bf16), whole((2, 2, 2, 512, D))),
        (sds((VOC, D), bf16), whole((VOC, D))),
        (sds((8, D), f32), whole((8, D))),
        (sds((8, VOC), f32), whole((8, VOC))),
    ]
    return pl.pallas_call(
        partial(middle_kernel, vocab, tokens),
        grid=(steps,),
        in_specs=[
            pl.BlockSpec(memory_space=pltpu.SMEM), whole((8, 128)), tall_rows(D), tall_rows(1),
            whole((D, 1024)), whole((D, 1024)), whole((1024, D)), whole((1024, D)), whole((VOC, D)),
            whole((4, D)), whole((4, D)),
        ],
        out_specs=[o[1] for o in outs],
        out_shape=[o[0] for o in outs],
        scratch_shapes=[
            VMEM((rows, D), bf16), VMEM((rows, 2048), bf16), VMEM((rows, D), bf16),
            VMEM((rows, 2048), bf16), VMEM((rows, D), bf16), VMEM((rows, VOC), bf16),
            VMEM((TALL, 2048), f32),
        ],
        compiler_params=pltpu.CompilerParams(vmem_limit_bytes=60 * MIB),
        cost_estimate=pl.CostEstimate(flops=15 * 10**9, bytes_accessed=18 * MIB, transcendentals=5 * 10**6),
        name="ffn_head",
    )(lengths, total, x2, targets, wi[0], wi[1], wf[0], wf[1], wh, gain, bias)


def run_backward(dims, g2, x, x1, h1, qkv, p, o, h2, cq, kv, pc, oc, mem, wa, wo, gain, gw, ghead):
    rows = x.shape[0]
    steps = rows // BLK
    outs = [
        (sds((rows, D), f32), by_rows(D)),
        (sds((1536, D), f32), whole((1536, D))),
        (sds((512, D), bf16), whole((512, D))),
        (sds((2, 4, 256, D), bf16), whole((2, 4, 256, D))),
        (sds((8, D), f32), whole((8, D))),
        (sds((2, 512, D), bf16), pl.BlockSpec(memory_space=pl.ANY)),
        (sds((2, HPART, D), bf16), pl.BlockSpec(memory_space=pl.ANY)),
    ]
    nz, ny, nx = dims
    slots = max(nx, ny) - 1
    return pl.pallas_call(
        partial(backward_kernel, dims),
        grid=(steps,),
        in_specs=[
            by_rows(D), by_rows(D), by_rows(D), whole((rows, D)), by_rows(3 * D),
            pl.BlockSpec((1, 4, 512, 256), lambda i: (i, 0, 0, 0)), whole((rows, D)), whole((rows, D)),
            by_rows(D), whole((1536, 2 * D)), pl.BlockSpec((1, 8, 256, 128), lambda i: (i, 0, 0, 0)),
            whole((rows, D)), whole((1536, D)),
            whole((6, D, 256)), whole((6, D, 256)), whole((2, 256, D)), whole((2, 256, D)), whole((4, D)),
            pl.BlockSpec(memory_space=pl.ANY), pl.BlockSpec(memory_space=pl.ANY),
        ],
        out_specs=[o_[1] for o_ in outs],
        out_shape=[o_[0] for o_ in outs],
        scratch_shapes=[
            VMEM((rows, D), bf16), VMEM((rows, D), bf16), VMEM((rows, D), bf16),
            VMEM((rows, 3 * D), bf16), VMEM((1536, 2 * D), f32), VMEM((1536, 2 * D), bf16),
            VMEM((2, 2, 512, D), bf16), VMEM((2, 2, 512, D), bf16),
            VMEM((2, slots, 512, D), bf16), VMEM((2, slots, 512, D), bf16),
            VMEM((2, HPART, D), bf16), VMEM((2, HPART, D), bf16),
            VMEM((2, slots, HPART, D), bf16), VMEM((2, slots, HPART, D), bf16),
            VMEM((2, 4, 256, D), bf16), VMEM((2, 4, 256, D), bf16),
            pltpu.SemaphoreType.DMA((48,)), pltpu.SemaphoreType.DMA((40,)), pltpu.SemaphoreType.DMA((6,)),
        ],
        compiler_params=pltpu.CompilerParams(
            vmem_limit_bytes=62 * MIB, collective_id=2, has_side_effects=True,
        ),
        cost_estimate=pl.CostEstimate(flops=18 * 10**9, bytes_accessed=30 * MIB, transcendentals=0),
        name="attention_backward",
    )(g2, x, x1, h1, qkv, p, o, h2, cq, kv, pc, oc, mem, wa[0], wa[1], wo[0], wo[1], gain, gw, ghead)


MESH = pl.DeviceIdType.MESH
OWN = 2


def chip_dims(count):
    nz = 4
    side = math.isqrt(count // nz)
    return nz, count // nz // side, side


class Net:
    def __init__(self, dims, send_sems, recv_sems):
        self.nz, self.ny, self.nx = dims
        self.chip = lax.axis_index("dp")
        self.core = lax.axis_index("mp")
        self.x = lax.rem(self.chip, self.nx)
        self.y = lax.rem(lax.div(self.chip, self.nx), self.ny)
        self.z = lax.div(self.chip, self.nx * self.ny)
        self.place = {"x": self.x, "y": self.y, "z": self.z}
        self.count = {"x": self.nx, "y": self.ny, "z": self.nz}
        self.sibling = {"dp": self.chip, "mp": 1 - self.core}
        self.send_sems, self.recv_sems = send_sems, recv_sems
        self.sent, self.received = 0, 0
        self.unsent = []
        self.ending, self.keeping = False, True

    def at(self, **moved):
        p = {**self.place, **moved}
        return {"dp": (p["z"] * self.ny + p["y"]) * self.nx + p["x"], "mp": self.core}

    def further(self, axis, d):
        return lax.rem(self.place[axis] + d, self.count[axis])

    def on(self, condition, body):
        if condition is True:
            body()
        else:
            pl.when(condition)(body)

    def both(self, *conditions):
        result = True
        for c in conditions:
            if c is not True:
                result = c if result is True else jnp.logical_and(result, c)
        return result

    def inside(self, axis):
        return True if self.count[axis] == OWN else self.place[axis] < OWN

    def goes_inside(self, axis, d):
        return True if self.count[axis] == OWN else self.further(axis, d) < OWN

    def clipped(self, axis):
        return self.place[axis] if self.count[axis] == OWN else jnp.minimum(self.place[axis], OWN - 1)

    def send_sem(self, amount):
        self.sent += amount
        return self.sent - amount

    def recv_sem(self, amount):
        self.received += amount
        return self.received - amount

    def remote(self, src, dst, send_sem, recv_sem, device):
        return pltpu.make_async_remote_copy(
            src_ref=src, dst_ref=dst, send_sem=self.send_sems.at[send_sem],
            recv_sem=self.recv_sems.at[recv_sem], device_id=device, device_id_type=MESH,
        )

    def send(self, condition, src, dst, recv_sem, device):
        sem = self.send_sem(1)
        copy = lambda: self.remote(src, dst, sem, recv_sem, device)
        if self.ending:
            self.on(condition, lambda: copy().wait_send())
            return
        self.on(condition, lambda: copy().start())
        if self.keeping:
            self.unsent.append((condition, copy))

    def landed(self, condition, dst, recv_sem):
        self.on(condition, lambda: self.remote(dst, dst, 0, recv_sem, self.sibling).wait_recv())

    def spread(self, axis, condition, ref, recv_sem):
        for d in range(1, self.count[axis]):
            self.send(condition, ref, ref, recv_sem, self.at(**{axis: self.further(axis, d)}))

    def all_sent(self):
        for condition, copy in self.unsent:
            self.on(condition, lambda copy=copy: copy().wait_send())
        self.unsent = []
        assert self.sent <= self.send_sems.shape[0] and self.received <= self.recv_sems.shape[0]

    def barrier(self):
        partners = [self.sibling]
        for axis in ("x", "y", "z"):
            for d in range(1, self.count[axis]):
                partners.append(self.at(**{axis: self.further(axis, d)}))
        barrier = pltpu.get_barrier_semaphore()
        for partner in partners:
            pl.semaphore_signal(barrier, inc=1, device_id=partner, device_id_type=MESH)
        pl.semaphore_wait(barrier, len(partners))


def add_into(dst, sources, step):
    rows = dst.shape[0]

    def body(i, carry):
        part = pl.ds(pl.multiple_of(i * step, step), step)
        total = dst[part, :].astype(f32)
        for s in sources:
            total = total + s[part, :].astype(f32)
        dst[part, :] = total.astype(bf16)
        return carry

    lax.fori_loop(0, rows // step, body, 0)


HEAD_X, HEAD_Y, HEAD_Z = 1, 0, 0


class EarlySum:
    def __init__(self, net, gw, ghead, wide_out, head_out, scratch):
        (
            self.acc, self.core_in, self.first_in, self.second_in,
            self.head_acc, self.head_core, self.head_first, self.head_second, self.local,
        ) = scratch
        self.net, self.gw, self.ghead, self.wide_out, self.head_out = net, gw, ghead, wide_out, head_out
        n = net
        self.core_sem = n.recv_sem(6)
        self.first_sem = [n.recv_sem(n.nx - 1), n.recv_sem(n.ny - 1)]
        self.second_sem = [n.recv_sem(n.ny - 1), n.recv_sem(n.nx - 1)]
        self.head_first_sem = [n.recv_sem(n.nx - 1), n.recv_sem(n.ny - 1)]
        self.head_second_sem = [n.recv_sem(n.ny - 1), n.recv_sem(n.nx - 1)]
        self.sums = ((0, "x", "y"), (1, "y", "x"))
        self.goal = {"x": HEAD_X, "y": HEAD_Y}

    def head_rows(self, core, f):
        return self.ghead.at[pl.ds(pl.multiple_of(core * HROWS + f * HPART, HPART), HPART)]

    def own_copies(self):
        core = self.net.core
        return [
            pltpu.make_async_copy(self.gw.at[0, m, f], self.acc.at[m, f], self.local.at[2 * m + f])
            for m in range(2)
            for f in range(2)
        ] + [
            pltpu.make_async_copy(self.head_rows(core, f), self.head_acc.at[f], self.local.at[4 + f]) for f in range(2)
        ]

    def start(self):
        self.net.keeping = False
        self.net.barrier()
        for copy in self.own_copies():
            copy.start()
        self.core_sends()

    def core_sends(self):
        n = self.net
        for m in range(2):
            for f in range(2):
                n.send(True, self.gw.at[1, m, f], self.core_in.at[m, f], self.core_sem + 2 * m + f, n.sibling)
        for f in range(2):
            n.send(True, self.head_rows(1 - n.core, f), self.head_core.at[f], self.core_sem + 4 + f, n.sibling)

    def one(self):
        n = self.net
        for copy in self.own_copies():
            copy.wait()
        for m in range(2):
            for f in range(2):
                n.landed(True, self.core_in.at[m, f], self.core_sem + 2 * m + f)
                add_into(self.acc.at[m, f], [self.core_in.at[m, f]], 128)
        for f in range(2):
            n.landed(True, self.head_core.at[f], self.core_sem + 4 + f)
            add_into(self.head_acc.at[f], [self.head_core.at[f]], HPART)
        self.first_sends()

    def first_sends(self):
        n = self.net
        for f, axis, other in self.sums:
            for d in range(1, n.count[axis]):
                target = jnp.minimum(n.further(axis, d), OWN - 1)
                n.send(
                    n.goes_inside(axis, d), self.acc.at[target, f], self.first_in.at[f, d - 1],
                    self.first_sem[f] + d - 1, n.at(**{axis: n.further(axis, d)}),
                )
            goal = self.goal[axis]
            for d in range(1, n.count[axis]):
                n.send(
                    n.place[axis] == (goal + d) % n.count[axis], self.head_acc.at[f],
                    self.head_first.at[f, d - 1], self.head_first_sem[f] + d - 1, n.at(**{axis: goal}),
                )

    def two(self):
        n = self.net
        for f, axis, other in self.sums:
            matrix = n.clipped(axis)

            def take(f=f, axis=axis, matrix=matrix):
                slots = [self.first_in.at[f, d - 1] for d in range(1, n.count[axis])]
                for d in range(1, n.count[axis]):
                    n.landed(True, slots[d - 1], self.first_sem[f] + d - 1)
                add_into(self.acc.at[matrix, f], slots, 128)

            n.on(n.inside(axis), take)

            def take_head(f=f, axis=axis):
                slots = [self.head_first.at[f, d - 1] for d in range(1, n.count[axis])]
                for d in range(1, n.count[axis]):
                    n.landed(True, slots[d - 1], self.head_first_sem[f] + d - 1)
                add_into(self.head_acc.at[f], slots, HPART)

            n.on(n.place[axis] == self.goal[axis], take_head)
        self.second_sends()

    def second_sends(self):
        n = self.net
        for f, axis, other in self.sums:
            matrix = n.clipped(axis)
            distance = lax.rem(n.place[other] - matrix + n.count[other], n.count[other])
            slot = jnp.maximum(distance, 1) - 1
            n.send(
                n.both(n.inside(axis), distance != 0), self.acc.at[matrix, f], self.second_in.at[f, slot],
                self.second_sem[f] + slot, n.at(**{other: matrix}),
            )
            goal = self.goal[other]
            for d in range(1, n.count[other]):
                n.send(
                    n.both(n.place[axis] == self.goal[axis], n.place[other] == (goal + d) % n.count[other]),
                    self.head_acc.at[f], self.head_second.at[f, d - 1], self.head_second_sem[f] + d - 1,
                    n.at(**{other: goal}),
                )

    def columns(self):
        n = self.net
        wide = n.both(n.inside("x"), n.inside("y"), n.x == n.y)
        return wide, n.both(n.x == HEAD_X, n.y == HEAD_Y)

    def out_copies(self):
        n = self.net
        wide, head = self.columns()
        copies = [
            (wide, pltpu.make_async_copy(self.acc.at[n.clipped(axis), f], self.wide_out.at[f], self.local.at[f]))
            for f, axis, other in self.sums
        ]
        return copies + [(head, pltpu.make_async_copy(self.head_acc, self.head_out, self.local.at[4]))]

    def three(self):
        n = self.net
        wide, head = self.columns()
        for f, axis, other in self.sums:

            def take(f=f, axis=axis, other=other):
                slots = [self.second_in.at[f, d - 1] for d in range(1, n.count[other])]
                for d in range(1, n.count[other]):
                    n.landed(True, slots[d - 1], self.second_sem[f] + d - 1)
                add_into(self.acc.at[n.clipped(axis), f], slots, 128)

            n.on(wide, take)

            def take_head(f=f, other=other):
                slots = [self.head_second.at[f, d - 1] for d in range(1, n.count[other])]
                for d in range(1, n.count[other]):
                    n.landed(True, slots[d - 1], self.head_second_sem[f] + d - 1)
                add_into(self.head_acc.at[f], slots, HPART)

            n.on(head, take_head)
        for condition, copy in self.out_copies():
            n.on(condition, copy.start)

    def keep_sends(self):
        self.net.keeping = True

    def end(self):
        for condition, copy in self.out_copies():
            self.net.on(condition, copy.wait)
        self.net.sent, self.net.ending = 0, True
        self.core_sends()
        self.first_sends()
        self.second_sends()


def prepare_kernel(
    dims, lengths_ref, ai_ref, ao_ref, vh_ref, mem_ref,
    wa0, wa1, wo0, wo1, mem_out, wh_ref, total_ref,
    ai_in, ao_in, vh_in, mem_in, ai_low, ao_low, totals,
    load_sems, keep_sems, send_sems, recv_sems,
):
    nz, ny, nx = dims
    chip = lax.axis_index("dp")
    core = lax.axis_index("mp")
    place = {"x": lax.rem(chip, nx), "y": lax.rem(lax.div(chip, nx), ny), "z": lax.div(chip, nx * ny)}
    count = {"x": nx, "y": ny, "z": nz}
    sibling = {"dp": chip, "mp": 1 - core}

    def at(axis, target):
        p = {**place, axis: target}
        return {"dp": (p["z"] * ny + p["y"]) * nx + p["x"], "mp": core}

    arrays = (
        (ai_ref, ai_in, ai_low, wa0, wa1),
        (ao_ref, ao_in, ao_low, wo0, wo1),
    )
    loads = [
        pltpu.make_async_copy(src, dst, load_sems.at[i])
        for i, (src, dst) in enumerate([a[:2] for a in arrays] + [(vh_ref, vh_in), (mem_ref, mem_in)])
    ]
    for load in loads:
        load.start()
    partners = [sibling]
    for axis in ("x", "y", "z"):
        for d in range(1, count[axis]):
            partners.append(at(axis, lax.rem(place[axis] + d, count[axis])))
    barrier = pltpu.get_barrier_semaphore()
    for partner in partners:
        pl.semaphore_signal(barrier, inc=1, device_id=partner, device_id_type=MESH)
    pl.semaphore_wait(barrier, len(partners))

    def remote(src, dst, send_sem, recv_sem, device):
        return pltpu.make_async_remote_copy(
            src_ref=src, dst_ref=dst, send_sem=send_sems.at[send_sem], recv_sem=recv_sems.at[recv_sem],
            device_id=device, device_id_type=MESH,
        )

    tokens = lengths_ref[0]
    for s in range(1, lengths_ref.shape[0]):
        tokens = tokens + lengths_ref[s]

    base = {}
    used = 8
    for axis in ("x", "y", "z"):
        base[axis] = used
        used += count[axis]
    pending = []

    def spread_total(level, axis, value):
        totals[level, place[axis]] = value
        for d in range(1, count[axis]):
            copy = remote(
                totals.at[level, place[axis]], totals.at[level, place[axis]], base[axis] + d,
                base[axis] + place[axis], at(axis, lax.rem(place[axis] + d, count[axis])),
            )
            copy.start()
            pending.append(copy)

    def add_total(level, axis):
        for d in range(1, count[axis]):
            source = lax.rem(place[axis] + d, count[axis])
            remote(
                totals.at[level, source], totals.at[level, source], base[axis] + d,
                base[axis] + source, sibling,
            ).wait_recv()
        value = totals[level, 0]
        for s in range(1, count[axis]):
            value = value + totals[level, s]
        return value

    def memory_moves():
        return (
            (core == 0, pltpu.make_async_copy(mem_in, mem_out.at[pl.ds(0, 1024)], keep_sems.at[4])),
            (
                core == 1,
                pltpu.make_async_copy(mem_in.at[pl.ds(512, 512)], mem_out.at[pl.ds(0, 512)], keep_sems.at[4]),
            ),
            (core == 1, pltpu.make_async_copy(mem_in, mem_out.at[pl.ds(512, 1024)], keep_sems.at[5])),
        )

    def memory_send():
        return remote(mem_in.at[pl.ds(0, 512)], mem_out.at[pl.ds(1024, 512)], 4, 4, sibling)

    spread_total(0, "x", jnp.full((8, 128), tokens.astype(f32)))
    loads[3].wait()
    for condition, copy in memory_moves():
        pl.when(condition)(copy.start)
    pl.when(core == 1)(lambda: memory_send().start())
    sends = []
    keeps = []
    for i, (src, staged, low, mine, others) in enumerate(arrays):
        loads[i].wait()
        low[...] = staged[...].astype(bf16)
        copy = remote(low, others, i, i, sibling)
        copy.start()
        sends.append(copy)
        keep = pltpu.make_async_copy(low, mine, keep_sems.at[i])
        keep.start()
        keeps.append(keep)
        if i < 2:
            spread_total(i + 1, ("y", "z")[i], add_total(i, ("x", "y")[i]))
    loads[2].wait()
    vocab = vh_in.shape[0]
    wh_ref[512:, :] = jnp.zeros((VOC - 512, D), bf16)
    wh_ref[0:vocab, :] = vh_in[...].astype(bf16)
    total_ref[...] = add_total(2, "z")
    for condition, copy in memory_moves():
        pl.when(condition)(copy.wait)
    pl.when(core == 1)(lambda: memory_send().wait_send())
    pl.when(core == 0)(lambda: memory_send().wait_recv())
    for copy in keeps:
        copy.wait()
    for copy in sends:
        copy.wait()
    for copy in pending:
        copy.wait_send()


def run_prepare(dims, lengths, ai, ao, vh, mem):
    hbm = pl.BlockSpec(memory_space=pl.ANY)
    vmem = pl.BlockSpec(memory_space=VMEM)
    weights = [sds(w.shape, bf16) for w in (ai, ao) for _ in range(2)]
    nz, ny, nx = dims
    return pl.pallas_call(
        partial(prepare_kernel, dims),
        in_specs=[pl.BlockSpec(memory_space=pltpu.SMEM)] + [hbm] * 4,
        out_specs=[hbm] * 5 + [vmem, vmem],
        out_shape=weights + [sds((1536, D), bf16), sds((VOC, D), bf16), sds((8, 128), f32)],
        scratch_shapes=[VMEM(w.shape, f32) for w in (ai, ao, vh)]
        + [VMEM(mem.shape, bf16)]
        + [VMEM(w.shape, bf16) for w in (ai, ao)]
        + [
            VMEM((3, max(dims), 8, 128), f32),
            pltpu.SemaphoreType.DMA((6,)), pltpu.SemaphoreType.DMA((6,)),
            pltpu.SemaphoreType.DMA((8 + nx + ny + nz,)), pltpu.SemaphoreType.DMA((8 + nx + ny + nz,)),
        ],
        compiler_params=pltpu.CompilerParams(
            vmem_limit_bytes=60 * MIB, collective_id=1, has_side_effects=True
        ),
        cost_estimate=pl.CostEstimate(flops=10**6, bytes_accessed=14 * MIB, transcendentals=0),
        name="prepare_weights",
    )(lengths, ai, ao, vh, mem)


PIECE = 256
SMALL = 24


def split_two(value):
    high = value.astype(bf16)
    return high, (value - high.astype(f32)).astype(bf16)


def wide_roles(n):
    left = n.x == 0
    return (
        jnp.where(left, 1, 2), jnp.where(left, 0, 3), jnp.where(left, 2, 1), jnp.where(left, 3, 0)
    )


def square_owners(n):
    beside = n.x == n.y
    return (
        jnp.where(beside, jnp.where(n.x == 0, 2, 1), 1),
        jnp.where(beside, jnp.where(n.x == 0, 0, 3), 2),
    )


class SquareBack:
    def __init__(self, net, low, land):
        self.net, self.low, self.land = net, low, land
        self.axes = (("x", "y"), ("y", "x"))
        self.z_sem = [net.recv_sem(2) for _ in range(2)]
        self.one_sem = [net.recv_sem(2 * OWN) for _ in range(2)]
        self.two_sem = [net.recv_sem(2 * OWN) for _ in range(2)]
        self.valid = net.both(net.inside("x"), net.inside("y"))
        self.owners = square_owners(net)

    def chunk(self, f):
        first, second = self.axes[f]
        return self.net.clipped(first) * 2 + self.net.clipped(second)

    def rows(self, p):
        return pl.ds(p * 128, 128)

    def start(self, p):
        n = self.net
        for f in range(2):
            owner = n.both(self.valid, n.z == self.owners[f])

            def keep(f=f):
                self.land[f, self.chunk(f), self.rows(p), :] = self.low[self.rows(p), :]

            n.on(owner, keep)
            n.spread("z", owner, self.land.at[f, self.chunk(f), self.rows(p)], self.z_sem[f] + p)

    def one(self, p):
        n = self.net
        for f in range(2):
            mine = self.land.at[f, self.chunk(f), self.rows(p)]
            n.landed(n.both(self.valid, n.z != self.owners[f]), mine, self.z_sem[f] + p)
            second = self.axes[f][1]
            n.spread(second, self.valid, mine, self.one_sem[f] + p * OWN + n.clipped(second))

    def two(self, p):
        n = self.net
        for f in range(2):
            first, second = self.axes[f]
            for s in range(OWN):
                n.landed(
                    n.both(n.inside(first), n.place[second] != s),
                    self.land.at[f, n.clipped(first) * 2 + s, self.rows(p)], self.one_sem[f] + p * OWN + s,
                )
            n.spread(
                first, n.inside(first), self.land.at[f, pl.ds(n.clipped(first) * 2, 2), self.rows(p)],
                self.two_sem[f] + p * OWN + n.clipped(first),
            )

    def end(self):
        n = self.net
        for p in range(2):
            for f in range(2):
                first = self.axes[f][0]
                for s in range(OWN):
                    n.landed(
                        n.place[first] != s, self.land.at[f, pl.ds(s * 2, 2), self.rows(p)],
                        self.two_sem[f] + p * OWN + s,
                    )


class WideBack:
    def __init__(self, net, low, spot, pieces, rows):
        self.net, self.low, self.spot, self.pieces, self.rows = net, low, spot, pieces, rows
        self.axes = (("x", "y"), ("y", "x"))
        self.hop_sem = net.recv_sem(pieces)
        self.one_sem = net.recv_sem(pieces)
        self.two_sem = [net.recv_sem(OWN) for _ in range(pieces)]
        self.wide = net.both(net.inside("x"), net.inside("y"), net.x == net.y)
        self.owner, self.near, self.middle, self.far = wide_roles(net)

    def stands(self, position):
        return self.net.both(self.wide, self.net.z == position)

    def mine(self, p):
        return self.spot(self.net.clipped("x"), p)

    def start(self, p):
        n = self.net

        def keep():
            self.mine(p)[...] = self.low[pl.ds(p * self.rows, self.rows), :]

        owner = self.stands(self.owner)
        n.on(owner, keep)
        n.send(owner, self.mine(p), self.mine(p), self.hop_sem + p, n.at(z=self.middle))
        n.send(owner, self.mine(p), self.mine(p), self.hop_sem + p, n.at(z=self.near))

    def onward(self, p):
        n = self.net
        here = self.stands(self.middle)
        n.landed(here, self.mine(p), self.hop_sem + p)
        n.send(here, self.mine(p), self.mine(p), self.hop_sem + p, n.at(z=self.far))

    def one(self, p):
        n = self.net
        n.landed(self.stands(self.near), self.mine(p), self.hop_sem + p)
        n.landed(self.stands(self.far), self.mine(p), self.hop_sem + p)
        first, second = self.axes[2 * p // self.pieces]
        n.spread(second, self.wide, self.spot(n.clipped(first), p), self.one_sem + p)

    def two(self, p):
        n = self.net
        first, second = self.axes[2 * p // self.pieces]
        mine = self.spot(n.clipped(first), p)
        n.landed(n.both(n.inside(first), n.place[first] != n.place[second]), mine, self.one_sem + p)
        n.spread(first, n.inside(first), mine, self.two_sem[p] + n.clipped(first))

    def end(self):
        n = self.net
        for p in range(self.pieces):
            first = self.axes[2 * p // self.pieces][0]
            for m in range(OWN):
                n.landed(n.place[first] != m, self.spot(m, p), self.two_sem[p] + m)


class HeadBack:
    def __init__(self, net, low, land):
        self.net, self.low = net, low
        self.hop_sem, self.one_sem, self.two_sem = net.recv_sem(2), net.recv_sem(2), net.recv_sem(2)
        self.core_sem = net.recv_sem(1)
        self.axes = (("x", "y"), ("y", "x"))
        self.goal = {"x": HEAD_X, "y": HEAD_Y}
        self.spots = [
            land.at[pl.ds(pl.multiple_of(net.core * HROWS + p * HPART, HPART), HPART)] for p in range(2)
        ]
        self.mine = land.at[pl.ds(pl.multiple_of(net.core * HROWS, HROWS), HROWS)]
        self.theirs = land.at[pl.ds(pl.multiple_of((1 - net.core) * HROWS, HROWS), HROWS)]
        self.column = net.both(net.x == HEAD_X, net.y == HEAD_Y)

    def hop(self, k):
        n = self.net
        here = n.both(self.column, n.z == k)
        for p in range(2):
            if k == 0:

                def keep(p=p):
                    self.spots[p][...] = self.low[pl.ds(p * HPART, HPART), :]

                n.on(here, keep)
            else:
                n.landed(here, self.spots[p], self.hop_sem + p)
            if k < n.nz - 1:
                n.send(here, self.spots[p], self.spots[p], self.hop_sem + p, n.at(z=k + 1))

    def one(self):
        n = self.net
        for p in range(2):
            n.spread(self.axes[p][1], self.column, self.spots[p], self.one_sem + p)

    def two(self):
        n = self.net
        for p in range(2):
            first, second = self.axes[p]
            plane = n.place[first] == self.goal[first]
            n.landed(n.both(plane, n.place[second] != self.goal[second]), self.spots[p], self.one_sem + p)
            n.spread(first, plane, self.spots[p], self.two_sem + p)

    def three(self):
        n = self.net
        for p in range(2):
            first = self.axes[p][0]
            n.landed(n.place[first] != self.goal[first], self.spots[p], self.two_sem + p)
        n.send(True, self.mine, self.mine, self.core_sem, n.sibling)

    def end(self):
        self.net.landed(True, self.theirs, self.core_sem)


def muon_kernel(
    dims, gs_ref, wide_ref, headg_ref, na_ref, nf_ref, count_ref, dlow_ref, mi_ref, mo_ref, mu_ref, md_ref, mh_ref,
    ms_all, xs_all, mw_all, q_all, mh_all, xh_all, d_in, small_out,
    acc, first_in, second_in, band_in, wide_acc, wide_in, head_acc, head_in, small_buf,
    old_turned, old_plain, old_head, own, gram, gram_in, mats, m_low, x_low,
    ms_land, xs_land, mw_land, q_land, mh_land, xh_land,
    send_sems, recv_sems, local_sems,
):
    n = Net(dims, send_sems, recv_sems)
    nz = n.nz
    x, y, z, core = n.x, n.y, n.z, n.core
    on, both = n.on, n.both
    n.barrier()
    valid = both(n.inside("x"), n.inside("y"))
    wide = both(valid, x == y)
    wide_z, near_z, middle_z, far_z = wide_roles(n)
    wide_owner = both(wide, z == wide_z)
    square_z = square_owners(n)
    owns = [both(valid, z == square_z[f]) for f in range(2)]
    square = jnp.logical_or(owns[0], owns[1])
    task = jnp.where(
        z == square_z[0], n.clipped("x") * 2 + n.clipped("y"), 4 + n.clipped("y") * 2 + n.clipped("x")
    )
    head_column = both(x == HEAD_X, y == HEAD_Y)
    head_owner = both(head_column, z == HEAD_Z)
    axes = (("x", "y"), ("y", "x"))

    first_sem = [n.recv_sem(2 * (n.count[axes[f][0]] - 1)) for f in range(2)]
    second_sem = [n.recv_sem(2 * (n.count[axes[f][1]] - 1)) for f in range(2)]

    def half_rows(p):
        return pl.ds(p * 128, 128)

    for p in range(2):
        for f in range(2):
            axis = axes[f][0]
            for d in range(1, n.count[axis]):
                target = jnp.minimum(n.further(axis, d), OWN - 1)
                n.send(
                    n.goes_inside(axis, d), gs_ref.at[f, pl.ds(target * 2, 2), half_rows(p)],
                    first_in.at[f, d - 1, :, half_rows(p)], first_sem[f] + 2 * (d - 1) + p,
                    n.at(**{axis: n.further(axis, d)}),
                )
    own_copies = [
        pltpu.make_async_copy(gs_ref.at[f], acc.at[f], local_sems.at[f]) for f in range(2)
    ]
    for copy in own_copies:
        copy.start()

    def wide_load():
        return pltpu.make_async_copy(wide_ref, wide_acc, local_sems.at[4])

    def head_load():
        return pltpu.make_async_copy(headg_ref, head_acc, local_sems.at[5])

    def old_copies():
        sem = local_sems.at[6]
        return (
            (both(wide_owner, x == 0), lambda: pltpu.make_async_copy(mu_ref, old_turned, sem)),
            (both(wide_owner, x != 0), lambda: pltpu.make_async_copy(md_ref, old_plain, sem)),
            (
                both(square, task < 6),
                lambda: pltpu.make_async_copy(
                    mi_ref.at[jnp.minimum(task, 5)], old_turned.at[:, pl.ds(0, PIECE)], sem
                ),
            ),
            (
                both(square, task >= 6),
                lambda: pltpu.make_async_copy(
                    mo_ref.at[jnp.maximum(task, 6) - 6], old_plain.at[pl.ds(0, PIECE)], sem
                ),
            ),
            (head_owner, lambda: pltpu.make_async_copy(mh_ref, old_head, sem)),
        )

    on(wide, lambda: wide_load().start())
    on(head_column, lambda: head_load().start())
    for condition, copy in old_copies():
        on(condition, lambda copy=copy: copy().start())
    d_sem = n.recv_sem(1)
    n.send(core == 0, dlow_ref, d_in, d_sem, n.sibling)

    on(wide, lambda: wide_load().wait())
    near_sem, middle_sem, far_sem = n.recv_sem(4), n.recv_sem(4), n.recv_sem(4)

    def piece(k):
        return wide_acc.at[k // 2, pl.ds((k % 2) * PIECE, PIECE)]

    def wide_send(k):
        n.send(both(wide, z == far_z), piece(k), wide_in.at[1, k], far_sem + k, n.at(z=middle_z))
        n.send(both(wide, z == near_z), piece(k), wide_in.at[0, k], near_sem + k, n.at(z=wide_z))

    for k in range(3):
        wide_send(k)

    def wide_pass(k):
        here = both(wide, z == middle_z)

        def take():
            n.landed(True, wide_in.at[1, k], far_sem + k)
            add_into(piece(k), [wide_in.at[1, k]], 128)

        on(here, take)
        n.send(here, piece(k), wide_in.at[1, k], middle_sem + k, n.at(z=wide_z))

    on(head_column, lambda: head_load().wait())
    head_sem = n.recv_sem(2)

    def head_pass(distance):
        here = both(head_column, z == distance)
        for p in range(2):
            if distance < nz - 1:

                def take(p=p):
                    n.landed(True, head_in.at[p], head_sem + p)
                    add_into(head_acc.at[p], [head_in.at[p]], HPART)

                on(here, take)
            n.send(here, head_acc.at[p], head_in.at[p], head_sem + p, n.at(z=distance - 1))

    head_pass(nz - 1)

    small_core = n.recv_sem(1)
    small_sem = {axis: n.recv_sem(n.count[axis]) for axis in ("x", "y", "z")}
    small_buf[0, 0] = jnp.zeros((SMALL, VOC), f32)
    small_buf[0, 0, 0:8, 0:D] = na_ref[...]
    small_buf[0, 0, 8:16, 0:D] = nf_ref[...]
    small_buf[0, 0, 16:24, :] = count_ref[...]
    n.send(True, small_buf.at[0, 0], small_buf.at[0, 1], small_core, n.sibling)

    def small_go(level, axis, value):
        small_buf[level, n.place[axis]] = value
        n.spread(axis, True, small_buf.at[level, n.place[axis]], small_sem[axis] + n.place[axis])

    def small_add(level, axis):
        for d in range(1, n.count[axis]):
            source = n.further(axis, d)
            n.landed(True, small_buf.at[level, source], small_sem[axis] + source)
        total = small_buf[level, 0]
        for s in range(1, n.count[axis]):
            total = total + small_buf[level, s]
        return total

    for copy in own_copies:
        copy.wait()
    n.landed(True, small_buf.at[0, 1], small_core)
    small_go(1, "x", small_buf[0, 0] + small_buf[0, 1])
    wide_pass(0)
    for p in range(2):
        for f in range(2):
            first, second = axes[f]
            mine = n.clipped(first) * 2

            def take(f=f, p=p, first=first, mine=mine):
                for d in range(1, n.count[first]):
                    n.landed(True, first_in.at[f, d - 1, :, half_rows(p)], first_sem[f] + 2 * (d - 1) + p)
                for j in range(2):
                    add_into(
                        acc.at[f, mine + j, half_rows(p)],
                        [first_in.at[f, d - 1, j, half_rows(p)] for d in range(1, n.count[first])], 128,
                    )

            on(n.inside(first), take)
            for d in range(1, n.count[second]):
                target = jnp.minimum(n.further(second, d), OWN - 1)
                n.send(
                    both(n.inside(first), n.goes_inside(second, d)), acc.at[f, mine + target, half_rows(p)],
                    second_in.at[f, d - 1, half_rows(p)], second_sem[f] + 2 * (d - 1) + p,
                    n.at(**{second: n.further(second, d)}),
                )
        wide_pass(1 + p)
        head_pass(2 - p)
    small_go(2, "y", small_add(1, "x"))

    def chunk(f):
        first, second = axes[f]
        return n.clipped(first) * 2 + n.clipped(second)

    band_sem = [n.recv_sem(2 * (nz - 1)) for _ in range(2)]
    for p in range(2):
        for f in range(2):
            second = axes[f][1]

            def take_second(f=f, p=p, second=second):
                for d in range(1, n.count[second]):
                    n.landed(True, second_in.at[f, d - 1, half_rows(p)], second_sem[f] + 2 * (d - 1) + p)
                add_into(
                    acc.at[f, chunk(f), half_rows(p)],
                    [second_in.at[f, d - 1, half_rows(p)] for d in range(1, n.count[second])], 128,
                )

            on(valid, take_second)
            for d in range(1, nz):
                n.send(
                    both(valid, z == lax.rem(square_z[f] + d, nz)), acc.at[f, chunk(f), half_rows(p)],
                    band_in.at[d - 1, half_rows(p)], band_sem[f] + 2 * (d - 1) + p, n.at(z=square_z[f]),
                )
    small_go(3, "z", small_add(2, "y"))
    wide_send(3)

    own[...] = jnp.zeros_like(own)
    for condition, copy in old_copies():
        on(condition, lambda copy=copy: copy().wait())

    def turned(k):
        return jnp.swapaxes(old_turned[:, k * PIECE : (k + 1) * PIECE], 0, 1)

    back_ms = SquareBack(n, m_low, ms_land)
    back_mw = WideBack(
        n, m_low, lambda m, p: mw_land.at[m, p // 2, pl.ds((p % 2) * PIECE, PIECE)], 4, PIECE
    )
    back_mh = HeadBack(n, m_low, mh_land)
    back_xs = SquareBack(n, x_low, xs_land)
    back_q = WideBack(n, x_low, lambda m, p: q_land.at[m, core, p], 2, 128)
    back_xh = HeadBack(n, x_low, xh_land)

    def keep_moment(rows, value):
        own[rows, :] = value
        m_low[rows, :] = value.astype(bf16)

    def finish_wide(k, old):
        total = piece(k)[...].astype(f32) + wide_in[0, k].astype(f32) + wide_in[1, k].astype(f32)
        keep_moment(pl.ds(k * PIECE, PIECE), total + 0.5 * old)

    def wide_moment(k):
        n.landed(wide_owner, wide_in.at[0, k], near_sem + k)
        n.landed(wide_owner, wide_in.at[1, k], middle_sem + k)
        on(both(wide_owner, x == 0), lambda: finish_wide(k, turned(k)))
        on(both(wide_owner, x != 0), lambda: finish_wide(k, old_plain[pl.ds(k * PIECE, PIECE), :]))
        back_mw.start(k)

    def finish_square(p, old):
        f = jnp.where(owns[0], 0, 1)
        mine = jnp.where(owns[0], chunk(0), chunk(1))
        total = acc[f, mine, half_rows(p), :].astype(f32)
        for d in range(1, nz):
            total = total + band_in[d - 1, half_rows(p), :].astype(f32)
        keep_moment(half_rows(p), total + 0.5 * old)

    def square_moment(p):
        for f in range(2):
            for d in range(1, nz):
                n.landed(owns[f], band_in.at[d - 1, half_rows(p)], band_sem[f] + 2 * (d - 1) + p)
        on(
            both(square, task < 6),
            lambda: finish_square(p, jnp.swapaxes(old_turned[:, p * 128 : (p + 1) * 128], 0, 1)),
        )
        on(both(square, task >= 6), lambda: finish_square(p, old_plain[half_rows(p), :]))
        back_ms.start(p)

    def finish_head():
        old_plain[pl.ds(512, 128), :] = jnp.zeros((128, D), f32)
        old_plain[pl.ds(0, old_head.shape[0]), :] = old_head[...]
        for p in range(2):
            here = pl.ds(pl.multiple_of(core * HROWS + p * HPART, HPART), HPART)
            total = head_acc[p].astype(f32) + head_in[p].astype(f32)
            keep_moment(pl.ds(p * HPART, HPART), total + 0.5 * old_plain[here, :])

    wide_moment(0)
    for p in range(2):
        n.landed(head_owner, head_in.at[p], head_sem + p)
    on(head_owner, finish_head)
    back_mh.hop(0)
    square_moment(0)
    wide_moment(1)
    wide_moment(2)
    square_moment(1)
    wide_pass(3)
    wide_moment(3)

    blocks_used = jnp.where(wide_owner, 4, jnp.where(head_owner, 2, 1))
    gram[...] = jnp.zeros_like(gram)

    def gram_step(i, carry):
        high, low = split_two(own[pl.ds(pl.multiple_of(i * PIECE, PIECE), PIECE), :])
        gram[...] += mm_tn(high, high) + (mm_tn(high, low) + mm_tn(low, high))
        return carry

    lax.fori_loop(0, blocks_used, gram_step, 0)
    gram_sem = n.recv_sem(1)
    n.send(True, gram, gram_in, gram_sem, n.sibling)
    small_out[...] = small_add(3, "z")
    n.landed(True, gram_in, gram_sem)

    def eye_rows(first, rows):
        place = lax.broadcasted_iota(jnp.int32, (rows, D), 0) + first
        return (place == lax.broadcasted_iota(jnp.int32, (rows, D), 1)).astype(f32)

    def put(m, value):
        high, low = split_two(value)
        mats[m, 0] = high
        mats[m, 1] = low

    def product(a, b):
        ah, al = mats[a, 0], mats[a, 1]
        left_h, left_l = mats[b, 0, :, 0:256], mats[b, 1, :, 0:256]
        left = mm(ah, left_h) + (mm(ah, left_l) + mm(al, left_h))
        right_h, right_l = mats[b, 0, :, 256:512], mats[b, 1, :, 256:512]
        corner = mm(ah[256:], right_h) + (mm(ah[256:], right_l) + mm(al[256:], right_h))
        right = jnp.concatenate([jnp.swapaxes(left[256:], 0, 1), corner], axis=0)
        return jnp.concatenate([left, right], axis=1)

    both_halves = gram[...] + gram_in[...]
    total = jnp.sum(jnp.sum(both_halves * eye_rows(0, D), axis=0, keepdims=True), axis=1, keepdims=True)
    scale = 1.0 / (jnp.sqrt(total) + 1e-07)
    put(0, both_halves * scale * scale)
    on(square, lambda: own.__setitem__((pl.ds(0, PIECE), slice(None)), own[pl.ds(0, PIECE), :] * scale))
    for iteration in range(NS_STEPS):
        q_now, q_next = (2, 4) if iteration % 2 == 0 else (4, 2)
        a = mats[0, 0].astype(f32) + mats[0, 1].astype(f32)
        put(1, NS_A * eye_rows(0, D) + NS_B * a + NS_C * product(0, 0))

        def update_rows():
            high, low = split_two(own[pl.ds(0, PIECE), :])
            ph, pll = mats[1, 0], mats[1, 1]
            own[pl.ds(0, PIECE), :] = mm(high, ph) + (mm(high, pll) + mm(low, ph))

        def update_q():
            if iteration == 0:
                mats[q_next] = mats[1]
            else:
                put(q_next, product(1, q_now))

        on(square, update_rows)
        on(jnp.logical_not(square), update_q)
        if iteration < NS_STEPS - 1:
            put(3, product(0, 1))
            put(0, product(3, 1))
        if iteration == 0:
            back_ms.one(0)
            back_mh.hop(1)
        if iteration == 1:
            back_ms.one(1)
            back_mw.onward(0)
            back_mw.onward(1)
            back_mh.hop(2)
        if iteration == 2:
            back_ms.two(0)
            back_mw.onward(2)
            back_mw.one(0)
            back_mh.hop(3)
        if iteration == 3:
            back_ms.two(1)
            back_mw.onward(3)
            back_mw.one(1)
            back_mh.one()

    last = 4 if NS_STEPS % 2 == 1 else 2

    def direction():
        part = pl.ds(0, 512)
        high, low = split_two(own[part, :] * scale)
        value = mm(high, mats[last, 0]) + (mm(high, mats[last, 1]) + mm(low, mats[last, 0]))
        x_low[part, :] = value.astype(bf16)

    def wide_polynomial():
        rows = pl.ds(pl.multiple_of(core * PIECE, PIECE), PIECE)
        value = mats[last, 0, rows, :].astype(f32) + mats[last, 1, rows, :].astype(f32)
        x_low[pl.ds(0, PIECE), :] = (value * scale).astype(bf16)

    on(wide_owner, wide_polynomial)
    on(head_owner, direction)

    def keep_rows():
        x_low[pl.ds(0, PIECE), :] = own[pl.ds(0, PIECE), :].astype(bf16)

    on(square, keep_rows)
    back_xs.start(0)
    back_xs.start(1)
    back_q.start(0)
    back_q.start(1)
    back_xh.hop(0)
    back_mw.one(2)
    back_mw.two(0)
    back_mh.two()
    back_q.onward(0)
    back_q.onward(1)
    back_xh.hop(1)
    outs = [
        pltpu.make_async_copy(src, dst, local_sems.at[i])
        for i, (src, dst) in enumerate(
            (
                (ms_land, ms_all), (mh_land, mh_all), (mw_land, mw_all), (xs_land, xs_all), (q_land, q_all),
                (xh_land, xh_all),
            )
        )
    ]
    back_xs.one(0)
    back_xh.hop(2)
    back_mw.one(3)
    back_mw.two(1)
    back_xs.one(1)
    back_q.one(0)
    back_q.one(1)
    back_xs.two(0)
    back_xh.hop(3)
    back_xh.one()
    back_mw.two(2)
    back_xs.two(1)
    back_q.two(0)
    back_q.two(1)
    back_mw.two(3)
    back_xh.two()
    back_mh.three()
    back_ms.end()
    outs[0].start()
    back_mh.end()
    outs[1].start()
    back_mw.end()
    outs[2].start()
    back_q.end()
    q_sem = n.recv_sem(2)
    for m in range(2):
        n.send(True, q_land.at[m, core], q_land.at[m, core], q_sem + m, n.sibling)
    back_xh.three()
    back_xs.end()
    outs[3].start()
    for m in range(2):
        n.landed(True, q_land.at[m, 1 - core], q_sem + m)
    outs[4].start()
    back_xh.end()
    outs[5].start()
    n.landed(core == 1, d_in, d_sem)
    n.all_sent()
    for copy in outs:
        copy.wait()


def run_muon(dims, gs, wide, headg, na, nf, count, dlow, mi, mo, mu, md, mh):
    nz, ny, nx = dims
    hbm = pl.BlockSpec(memory_space=pl.ANY)
    vmem = pl.BlockSpec(memory_space=VMEM)
    slots = max(nx, ny) - 1
    most = max(nx, ny, nz, 2)
    squares = (2, 4, PIECE, D)
    lands = [squares, squares, (2, 2, 512, D), (2, 2, 2, 128, D), (VOC, D), (VOC, D)]
    return pl.pallas_call(
        partial(muon_kernel, dims),
        in_specs=[hbm] * 3 + [vmem] * 3 + [hbm] * 6,
        out_specs=[hbm] * 7 + [vmem],
        out_shape=[sds(s, bf16) for s in lands] + [sds((512, D), bf16), sds((SMALL, VOC), f32)],
        scratch_shapes=[
            VMEM(squares, bf16),
            VMEM((2, slots, 2, PIECE, D), bf16),
            VMEM((2, slots, PIECE, D), bf16),
            VMEM((nz - 1, PIECE, D), bf16),
            VMEM((2, 512, D), bf16),
            VMEM((2, 4, PIECE, D), bf16),
            VMEM((2, HPART, D), bf16),
            VMEM((2, HPART, D), bf16),
            VMEM((4, most, SMALL, VOC), f32),
            VMEM((D, 1024), f32),
            VMEM((1024, D), f32),
            VMEM(mh.shape, f32),
            VMEM((1024, D), f32),
            VMEM((D, D), f32),
            VMEM((D, D), f32),
            VMEM((5, 2, D, D), bf16),
            VMEM((1024, D), bf16),
            VMEM((512, D), bf16),
        ]
        + [VMEM(s, bf16) for s in lands]
        + [
            pltpu.SemaphoreType.DMA((400,)), pltpu.SemaphoreType.DMA((160,)), pltpu.SemaphoreType.DMA((8,)),
        ],
        compiler_params=pltpu.CompilerParams(
            vmem_limit_bytes=60 * MIB, collective_id=0, has_side_effects=True
        ),
        cost_estimate=pl.CostEstimate(flops=20 * 10**9, bytes_accessed=40 * MIB, transcendentals=0),
        name="reduce_muon_spread",
    )(gs, wide, headg, na, nf, count, dlow, mi, mo, mu, md, mh)


def finish_kernel(
    wide_rate, head_rate, core_ref,
    mu, md, mb, q_ref, xb, mh, xh, ai, ao, fi, fo, vh, small, gain, bias, nm, dm, dr,
    mi_out, ni_out, mo_out, no_out, mu_out, nu_out, md_out, nd_out, mh_out, nh_out,
    mn_out, nn_out, counts_out, dm_out,
):
    i = pl.program_id(0)
    same = lax.broadcasted_iota(jnp.int32, (D, D), 0) == lax.broadcasted_iota(jnp.int32, (D, D), 1)
    eye = same.astype(f32).astype(bf16)
    mu_out[...] = mm_nt(eye, mu[0, 0])
    nu_out[...] = fi[...] - wide_rate * mm_nt(q_ref[0], mu[0, 0])
    md_out[...] = md[0, 0].astype(f32)
    nd_out[...] = fo[...] - wide_rate * mm(md[0, 0], q_ref[1])

    @pl.when(i < 3)
    def _():
        for j in range(2):
            mi_out[j] = mm_nt(eye, mb[0, j])
            ni_out[j] = ai[j] - muon_rate * mm_nt(eye, xb[0, j])

    @pl.when(i == 3)
    def _():
        for j in range(2):
            mo_out[j] = mb[0, j].astype(f32)
            no_out[j] = ao[j] - muon_rate * xb[0, j].astype(f32)

    dm_out[...] = jnp.where((core_ref[0] == 0) | (i >= 2), dm[...], dr[...].astype(f32))

    @pl.when(i == 0)
    def _():
        vocab = vh.shape[0]
        mh_out[...] = mh[0:vocab, :].astype(f32)
        nh_out[...] = vh[...] - head_rate * xh[0:vocab, :].astype(f32)
        for kind, old in enumerate((gain, bias)):
            first = 2 * kind
            total = jnp.concatenate([small[first : first + 2, 0:D], small[first + 8 : first + 10, 0:D]], axis=0)
            moment = 0.5 * nm[kind] + total
            mn_out[kind] = moment
            nn_out[kind] = old[...] - vector_rate * moment * lax.rsqrt(
                jnp.mean(moment * moment, axis=-1, keepdims=True) + 1e-06
            )
        counts_out[...] = small[16:17, 0:vocab].astype(jnp.int32)


def run_finish(core, ms, xs, mw, q, m_head, x_head, ai, ao, fi, fo, vh, small, gain, bias, nm, dmem, d_in):
    vocab = vh.shape[0]
    wide_rate = muon_rate * math.sqrt(2 * fi.shape[1] / D)
    head_rate = muon_rate * math.sqrt(vocab / D)

    def spec(shape, index):
        return pl.BlockSpec(shape, index)

    def fixed(shape):
        return pl.BlockSpec(shape, lambda i, c: (0,) * len(shape))

    up = spec((1, 1, 256, D), lambda i, c: (0, i // 2, i % 2, 0))
    down = spec((1, 1, 256, D), lambda i, c: (1, i // 2, i % 2, 0))
    bands = spec((1, 2, 256, D), lambda i, c: (i // 2, i % 2, 0, 0))
    inner = spec((2, D, 256), lambda i, c: (jnp.minimum(i, 2), 0, 0))
    outer = spec((2, 256, D), lambda i, c: (0, 0, 0))
    cols = spec((D, 256), lambda i, c: (0, i))
    rows = spec((256, D), lambda i, c: (i, 0))
    head = fixed((vocab, D))
    shapes = [
        (sds((6, D, 256), f32), inner), (sds((6, D, 256), f32), inner),
        (sds((2, 256, D), f32), outer), (sds((2, 256, D), f32), outer),
        (sds(fi.shape, f32), cols), (sds(fi.shape, f32), cols),
        (sds(fo.shape, f32), rows), (sds(fo.shape, f32), rows),
        (sds((vocab, D), f32), head), (sds((vocab, D), f32), head),
        (sds((2, 4, D), f32), fixed((2, 4, D))), (sds((2, 4, D), f32), fixed((2, 4, D))),
        (sds((1, vocab), jnp.int32), fixed((1, vocab))),
        (sds((1024, D), f32), rows),
    ]
    return pl.pallas_call(
        partial(finish_kernel, wide_rate, head_rate),
        grid_spec=pltpu.PrefetchScalarGridSpec(
            num_scalar_prefetch=1,
            grid=(4,),
            in_specs=[
                up, down, bands, fixed((2, D, D)), bands, fixed((VOC, D)), fixed((VOC, D)),
                inner, outer, cols, rows, head, fixed((SMALL, VOC)), fixed((4, D)), fixed((4, D)), fixed((2, 4, D)),
                spec((256, D), lambda i, c: (jnp.where(c[0] == 0, i, jnp.maximum(i - 2, 0)), 0)),
                spec((256, D), lambda i, c: (jnp.minimum(i, 1), 0)),
            ],
            out_specs=[s[1] for s in shapes],
        ),
        out_shape=[s[0] for s in shapes],
        compiler_params=pltpu.CompilerParams(vmem_limit_bytes=60 * MIB),
        cost_estimate=pl.CostEstimate(flops=10**7, bytes_accessed=40 * MIB, transcendentals=0),
        name="finish_weights",
    )(core, mw, mw, ms, q.reshape(2, D, D), xs, m_head, x_head, ai, ao, fi, fo, vh, small,
      gain, bias, nm, dmem, d_in)


def local(
    residual_in, memory, lengths, targets, attn_in, attn_out, ffn_in, ffn_out, vocab_head,
    norm_gain, norm_bias, attn_in_moment, attn_out_moment, ffn_in_moment, ffn_out_moment,
    head_moment, norm_moment,
):
    dims = chip_dims(lax.axis_size("dp"))
    core = lax.axis_index("mp")
    tokens = residual_in.shape[0] * lax.axis_size("mp") * lax.axis_size("dp")
    vocab = vocab_head.shape[1]
    inner = attn_in.reshape(6, D, 256)
    wa0, wa1, wo0, wo1, mem, wh, total = run_prepare(
        dims, lengths, inner, attn_out, vocab_head.T, memory
    )
    wa, wo = (wa0, wa1), (wo0, wo1)
    h1, qkv, p, o, x1, h2, cq, kv, pc, oc, x2, wi0, wi1, wf0, wf1 = run_forward(
        lengths, residual_in, mem, wa, wo, norm_gain, norm_bias, ffn_in, ffn_out
    )
    wi, wf = (wi0, wi1), (wf0, wf1)
    out, g2, gw, ghead, gnorm_ffn, counts = run_middle(
        lengths, total, x2, targets[:, None], wi, wf, wh, norm_gain, norm_bias, vocab, float(tokens)
    )
    dx, dmem, dlow, gs, gnorm_attn, wide, head_part = run_backward(
        dims, g2, residual_in, x1, h1, qkv, p, o, h2, cq, kv, pc, oc, mem, wa, wo, norm_gain, gw, ghead
    )
    ms, xs, mw, q, head_m, head_x, d_in, small = run_muon(
        dims, gs, wide, head_part, gnorm_attn, gnorm_ffn, counts, dlow,
        attn_in_moment.reshape(6, D, 256), attn_out_moment, ffn_in_moment, ffn_out_moment, head_moment.T,
    )
    (
        moment_in, new_in, moment_out, new_out, moment_up, new_up, moment_down, new_down,
        moment_head, new_head, moment_norms, new_norms, token_counts, memory_grad,
    ) = run_finish(
        core.reshape(1), ms, xs, mw, q, head_m, head_x, inner, attn_out, ffn_in, ffn_out,
        vocab_head.T, small, norm_gain, norm_bias, norm_moment, dmem, d_in,
    )
    return (
        out, dx, memory_grad, moment_in.reshape(attn_in.shape), new_in.reshape(attn_in.shape),
        moment_out, new_out, moment_up, new_up, moment_down, new_down, moment_head.T, new_head.T,
        moment_norms, new_norms,
        token_counts.reshape(vocab),
    )


def solution(mesh):
    rows = P(("dp", "mp"), None)
    placed = (
        rows, rows, P("dp"), P(("dp", "mp")),
        P(None, None, None, "mp"), P(None, "mp", None), P(None, "mp"), P("mp", None), P(), P(), P(),
        P(None, None, None, "mp"), P(None, "mp", None), P(None, "mp"), P("mp", None), P(), P(),
    )
    return jax.shard_map(
        local,
        mesh=mesh,
        in_specs=placed,
        out_specs=(
            rows, rows, rows,
            P(None, None, None, "mp"), P(None, None, None, "mp"),
            P(None, "mp", None), P(None, "mp", None),
            P(None, "mp"), P(None, "mp"), P("mp", None), P("mp", None),
            P(), P(), P(), P(), P(),
        ),
        check_vma=False,
    )
```

```python
from functools import partial
import math

import jax
import jax.numpy as jnp
from jax import lax
from jax.experimental import pallas as pl
from jax.experimental.pallas import tpu as pltpu
from jax.sharding import PartitionSpec as P

HEAD = 64
CAP_S = 64
CAP_M = 128
CAP_L = 256
MEM = 128
SETS = 4
NS_STEPS = 5
NS_A = 3.4445
NS_B = -4.775
NS_C = 2.0315
muon_rate = 0.5
vector_rate = 0.05

D = 512
BLK = 256
WIDE = 512
TALL = 1024
VOC = 640
HROWS = 320
HPART = 160
MIB = 1024 * 1024
bf16 = jnp.bfloat16
f32 = jnp.float32
VMEM = pltpu.VMEM


def mm(a, b):
    return jnp.dot(a, b, preferred_element_type=f32)


def mm_nt(a, b):
    return lax.dot_general(a, b, (((1,), (1,)), ((), ())), preferred_element_type=f32)


def mm_tn(a, b):
    return lax.dot_general(a, b, (((0,), (0,)), ((), ())), preferred_element_type=f32)


def norm_stats(value):
    average = jnp.mean(value, axis=-1, keepdims=True)
    centred = value - average
    variance = jnp.mean(centred * centred, axis=-1, keepdims=True)
    inverse = lax.rsqrt(variance + 1e-05)
    return centred * inverse, inverse


def norm_back(gradient, normed, inverse, gain):
    scaled = gradient * gain
    return inverse * (
        scaled
        - jnp.mean(scaled, axis=-1, keepdims=True)
        - normed * jnp.mean(scaled * normed, axis=-1, keepdims=True)
    )


def lane_masks(width):
    lanes = lax.broadcasted_iota(jnp.int32, (1, width), 1)
    return [(lanes // HEAD == h).astype(f32).astype(bf16) for h in range(width // HEAD)]


def spread(block, masks):
    return jnp.concatenate([block * m for m in masks], axis=0)


def pick(stacked, masks, rows):
    total = stacked[:rows] * masks[0].astype(f32)
    for h in range(1, len(masks)):
        total = total + stacked[h * rows : (h + 1) * rows] * masks[h].astype(f32)
    return total


def softmax_rows(scores):
    top = jnp.max(scores, axis=-1, keepdims=True)
    exps = jnp.exp(scores - top)
    return exps * (1.0 / jnp.sum(exps, axis=-1, keepdims=True))


def mem_slot(core, block, unit):
    on_first = jnp.where(block < 2, 4 * block + unit, 8 + 2 * (block - 2) + unit // 2)
    return jnp.where(core == 0, on_first, block)


def row_limits(core, block, lengths_ref):
    unit = lax.broadcasted_iota(jnp.int32, (BLK, 1), 0) // CAP_S
    low = jnp.zeros((BLK, 1), jnp.int32)
    length = jnp.zeros((BLK, 1), jnp.int32)
    for u in range(BLK // CAP_S):
        on_first = jnp.where(block < 2, u * CAP_S, u // 2 * CAP_M)
        slot = mem_slot(core, block, u) + jnp.where(core == 0, 0, 3 * SETS)
        low = jnp.where(unit == u, jnp.where(core == 0, on_first, 0), low)
        length = jnp.where(unit == u, lengths_ref[slot], length)
    return low, length


def rows_live(core, first, blocks, lengths_ref):
    pieces = []
    for j in range(blocks):
        low, length = row_limits(core, first + j, lengths_ref)
        place = lax.broadcasted_iota(jnp.int32, (BLK, 1), 0)
        pieces.append((place - low < length).astype(f32))
    return jnp.concatenate(pieces, axis=0)


def forward_kernel(
    lengths_ref, x_ref, mem_ref, wa0, wa1, wo0, wo1, gain_ref, bias_ref,
    h1_ref, qkv_ref, p_ref, o_ref, x1_ref, h2_ref, cq_ref, kv_ref, pc_ref, oc_ref, x2_ref,
):
    core = lax.axis_index("mp")
    step = pl.program_id(0)
    wa = (wa0, wa1)

    @pl.when(step == 0)
    def _():
        def fill(i, carry):
            rows = pl.ds(pl.multiple_of(i * WIDE, WIDE), WIDE)
            for half in range(2):
                for which in range(2):
                    kv_ref[rows, pl.ds(which * D + half * 256, 256)] = mm(
                        mem_ref[rows, :], wa[half][4 + which]
                    ).astype(bf16)
            return carry

        lax.fori_loop(0, jnp.where(core == 0, 3, 1), fill, 0)

    normed, _ = norm_stats(x_ref[...].astype(f32))
    h1_ref[...] = (normed * gain_ref[0:1, :] + bias_ref[0:1, :]).astype(bf16)
    for half in range(2):
        for which in range(3):
            qkv_ref[:, pl.ds(which * D + half * 256, 256)] = mm(h1_ref[...], wa[half][which]).astype(bf16)
    pair = lane_masks(128)
    for j in range(WIDE // BLK):
        rows = pl.ds(j * BLK, BLK)
        low, length = row_limits(core, step * (WIDE // BLK) + j, lengths_ref)
        keys = lax.broadcasted_iota(jnp.int32, (BLK, BLK), 1)
        queries = lax.broadcasted_iota(jnp.int32, (BLK, BLK), 0)
        allowed = (keys >= low) & (keys < low + length) & (keys <= queries)
        for i in range(4):
            q = qkv_ref[rows, pl.ds(i * 128, 128)] * jnp.bfloat16(0.125)
            k = qkv_ref[rows, pl.ds(D + i * 128, 128)]
            v = qkv_ref[rows, pl.ds(2 * D + i * 128, 128)]
            scores = mm_nt(spread(q, pair), k).reshape(2, BLK, BLK)
            scores = jnp.where(allowed[None], scores, -1000000000.0)
            probs = softmax_rows(scores).astype(bf16).reshape(2 * BLK, BLK)
            p_ref[j, i] = probs
            o_ref[rows, pl.ds(i * 128, 128)] = pick(mm(probs, v), pair, BLK).astype(bf16)
    x1 = x_ref[...].astype(f32) + mm(o_ref[:, :256], wo0[0]) + mm(o_ref[:, 256:], wo1[0])
    x1_ref[...] = x1
    normed, _ = norm_stats(x1)
    h2_ref[...] = (normed * gain_ref[1:2, :] + bias_ref[1:2, :]).astype(bf16)
    for half in range(2):
        cq_ref[:, pl.ds(half * 256, 256)] = mm(h2_ref[...], wa[half][3]).astype(bf16)
    quad = lane_masks(256)
    for u in range(WIDE // 64):
        rows = pl.ds(u * 64, 64)
        block = step * (WIDE // BLK) + u // 4
        slot = pl.ds(pl.multiple_of(mem_slot(core, block, u % 4) * MEM, MEM), MEM)
        for j in range(2):
            q = cq_ref[rows, pl.ds(j * 256, 256)] * jnp.bfloat16(0.125)
            k = kv_ref[slot, pl.ds(j * 256, 256)]
            v = kv_ref[slot, pl.ds(D + j * 256, 256)]
            probs = softmax_rows(mm_nt(spread(q, quad), k)).astype(bf16)
            pc_ref[u // 4, u % 4 * 2 + j] = probs
            oc_ref[rows, pl.ds(j * 256, 256)] = pick(mm(probs, v), quad, 64).astype(bf16)
    x2_ref[...] = x1_ref[...] + mm(oc_ref[:, :256], wo0[1]) + mm(oc_ref[:, 256:], wo1[1])


def gelu_parts(u):
    z = jnp.abs(u) * math.sqrt(0.5 / math.log(2.0))
    below = 1.0 + (0.3275911 * math.sqrt(math.log(2.0))) * z
    guess = pl.reciprocal(below, approx=True)
    t = guess * (2.0 - below * guess)
    gauss = jnp.exp2(-(z * z))
    tail = gauss * (
        t * (0.127414796 + t * (-0.142248368 + t * (0.7107068705 + t * (-0.7265760135 + t * 0.5307027145))))
    )
    cdf = jnp.where(u < 0, tail, 1.0 - tail)
    return u * cdf, cdf + u * (gauss * (1.0 / math.sqrt(2.0 * math.pi)))


def middle_kernel(
    vocab, tokens, lengths_ref, total_ref, x2_ref, targets_ref, wi0, wi1, wf0, wf1, wh_ref, gain_ref, bias_ref,
    out_ref, g2_ref, gw_ref, ghead_ref, gnorm_ref, count_ref,
    h3_all, a_all, dy_all, du_all, z_all, gl_all, slope,
):
    block = pl.program_id(0)
    rows = pl.ds(pl.multiple_of(block * TALL, TALL), TALL)
    wi = (wi0, wi1)
    wf = (wf0, wf1)
    x2 = x2_ref[...]
    normed2, inverse2 = norm_stats(x2)
    h3 = (normed2 * gain_ref[2:3, :] + bias_ref[2:3, :]).astype(bf16)
    h3_all[rows, :] = h3
    for half in range(2):
        for j in range(2):
            wide = pl.ds(half * 1024 + j * 512, 512)
            active, grad = gelu_parts(mm(h3, wi[half][:, j * 512 : (j + 1) * 512]))
            a_all[rows, wide] = active.astype(bf16)
            slope[:, wide] = grad
    x3 = x2_ref[...] + mm(a_all[rows, 0:1024], wf0[...]) + mm(a_all[rows, 1024:2048], wf1[...])
    out_ref[...] = x3.astype(bf16)
    normed3, inverse3 = norm_stats(x3)
    z = (normed3 * gain_ref[3:4, :] + bias_ref[3:4, :]).astype(bf16)
    z_all[rows, :] = z
    logits = mm_nt(z, wh_ref[...])
    columns = lax.broadcasted_iota(jnp.int32, (TALL, VOC), 1)
    logits = jnp.where(columns < vocab, logits, -1e30)
    probs = softmax_rows(logits)
    onehot = (columns == targets_ref[...]).astype(f32)
    live = rows_live(lax.axis_index("mp"), block * (TALL // BLK), TALL // BLK, lengths_ref)
    gl = (tokens / total_ref[0:1, 0:1] * live * (probs - onehot)).astype(bf16)
    gl_all[rows, :] = gl
    counts = jnp.sum(onehot * live, axis=0, keepdims=True)
    gz = mm(gl, wh_ref[...])
    gain3 = jnp.sum(gz * normed3, axis=0, keepdims=True)
    bias3 = jnp.sum(gz, axis=0, keepdims=True)
    g3 = norm_back(gz, normed3, inverse3, gain_ref[3:4, :])
    dy = g3.astype(bf16)
    dy_all[rows, :] = dy
    g2_ref[...] = g3
    for half in range(2):
        for j in range(2):
            wide = pl.ds(half * 1024 + j * 512, 512)
            back = mm_nt(dy, wf[half][j * 512 : (j + 1) * 512, :])
            du_all[rows, wide] = (slope[:, wide] * back).astype(bf16)
    dh = mm_nt(du_all[rows, 0:1024], wi0[...]) + mm_nt(du_all[rows, 1024:2048], wi1[...])
    normed2, inverse2 = norm_stats(x2_ref[...])
    gain2 = jnp.sum(dh * normed2, axis=0, keepdims=True)
    bias2 = jnp.sum(dh, axis=0, keepdims=True)
    g2_ref[...] = g2_ref[...] + norm_back(dh, normed2, inverse2, gain_ref[2:3, :])

    @pl.when(block == 0)
    def _():
        gnorm_ref[...] = jnp.zeros_like(gnorm_ref)
        count_ref[...] = jnp.zeros_like(count_ref)

    gnorm_ref[0:1, :] += gain2
    gnorm_ref[1:2, :] += gain3
    gnorm_ref[2:3, :] += bias2
    gnorm_ref[3:4, :] += bias3
    count_ref[0:1, :] += counts

    @pl.when(block == pl.num_programs(0) - 1)
    def _():
        for half in range(2):
            for j in range(2):
                col = pl.ds(half * 1024 + j * 512, 512)
                gw_ref[half, 0, j] = mm_tn(du_all[:, col], h3_all[...]).astype(bf16)
                gw_ref[half, 1, j] = mm_tn(a_all[:, col], dy_all[...]).astype(bf16)
        ghead_ref[...] = mm_tn(gl_all[...], z_all[...]).astype(bf16)


def attend_back(queries, keys, values, probs, grads, masks, rows):
    q = spread(queries, masks)
    do = spread(grads, masks)
    dprobs = mm_nt(do, values)
    p = probs.astype(f32)
    weighted = p * dprobs
    ds = (weighted - p * jnp.sum(weighted, axis=-1, keepdims=True)).astype(bf16)
    dv = mm_tn(probs, do)
    dq = pick(mm(ds, keys), masks, rows) * 0.125
    dk = mm_tn(ds, q) * 0.125
    return dq, dk, dv


def backward_kernel(
    dims, g2_ref, x_ref, x1_ref, h1_ref, qkv_ref, p_ref, o_ref, h2_ref, cq_ref, kv_ref, pc_ref, oc_ref,
    mem_ref, wa0, wa1, wo0, wo1, gain_ref, gw_ref, ghead_ref,
    dx_ref, dmem_ref, dlow_ref, gs_ref, gnorm_ref, wide_out, head_out,
    dyc_all, dcq_all, dys_all, dqkv_all, dkv_all, dkv_low,
    early_acc, early_core, early_first, early_second, head_acc, head_core, head_first, head_second,
    gs_away, gs_in, send_sems, recv_sems, local_sems,
):
    core = lax.axis_index("mp")
    block = pl.program_id(0)
    early = EarlySum(
        Net(dims, send_sems, recv_sems), gw_ref, ghead_ref, wide_out, head_out,
        (
            early_acc, early_core, early_first, early_second, head_acc, head_core, head_first, head_second,
            local_sems,
        ),
    )
    band_sem = early.net.recv_sem(4)
    pl.when(block == 0)(early.start)
    rows = pl.ds(pl.multiple_of(block * BLK, BLK), BLK)
    wa = (wa0, wa1)
    wo = (wo0, wo1)

    @pl.when(block == 0)
    def _():
        gnorm_ref[...] = jnp.zeros_like(gnorm_ref)
        dkv_all[...] = jnp.zeros_like(dkv_all)

    g2 = g2_ref[...]
    dyc = g2.astype(bf16)
    dyc_all[rows, :] = dyc
    quad = lane_masks(256)
    for j in range(2):
        lanes = pl.ds(j * 256, 256)
        do = mm_nt(dyc, wo[j][1]).astype(bf16)
        for u in range(4):
            base = pl.multiple_of(block * BLK + u * 64, 64)
            slot = pl.ds(pl.multiple_of(mem_slot(core, block, u) * MEM, MEM), MEM)
            dq, dk, dv = attend_back(
                cq_ref[u * 64 : (u + 1) * 64, lanes],
                kv_ref[slot, lanes],
                kv_ref[slot, pl.ds(D + j * 256, 256)],
                pc_ref[0, u * 2 + j],
                do[u * 64 : (u + 1) * 64],
                quad,
                64,
            )
            dcq_all[pl.ds(base, 64), lanes] = dq.astype(bf16)
            dkv_all[slot, lanes] += dk
            dkv_all[slot, pl.ds(D + j * 256, 256)] += dv
    dcq = dcq_all[rows, :]
    dh = mm_nt(dcq[:, :256], wa0[3]) + mm_nt(dcq[:, 256:], wa1[3])
    normed, inverse = norm_stats(x1_ref[...])
    gnorm_ref[1:2, :] += jnp.sum(dh * normed, axis=0, keepdims=True)
    gnorm_ref[3:4, :] += jnp.sum(dh, axis=0, keepdims=True)
    g1 = g2 + norm_back(dh, normed, inverse, gain_ref[1:2, :])
    pl.when(block == 0)(early.one)
    dys = g1.astype(bf16)
    dys_all[rows, :] = dys
    pair = lane_masks(128)
    for half in range(2):
        do_half = mm_nt(dys, wo[half][0]).astype(bf16)
        for i in range(2):
            first = half * 256 + i * 128
            dq, dk, dv = attend_back(
                qkv_ref[:, pl.ds(first, 128)],
                qkv_ref[:, pl.ds(D + first, 128)],
                qkv_ref[:, pl.ds(2 * D + first, 128)],
                p_ref[0, half * 2 + i],
                do_half[:, i * 128 : (i + 1) * 128],
                pair,
                BLK,
            )
            dqkv_all[rows, pl.ds(first, 128)] = dq.astype(bf16)
            dqkv_all[rows, pl.ds(D + first, 128)] = dk.astype(bf16)
            dqkv_all[rows, pl.ds(2 * D + first, 128)] = dv.astype(bf16)
    dqkv = dqkv_all[rows, :]
    dh = jnp.zeros((BLK, D), f32)
    for half in range(2):
        for which in range(3):
            first = which * D + half * 256
            dh = dh + mm_nt(dqkv[:, first : first + 256], wa[half][which])
    normed, inverse = norm_stats(x_ref[...].astype(f32))
    gnorm_ref[0:1, :] += jnp.sum(dh * normed, axis=0, keepdims=True)
    gnorm_ref[2:3, :] += jnp.sum(dh, axis=0, keepdims=True)
    dx_ref[...] = g1 + norm_back(dh, normed, inverse, gain_ref[0:1, :])
    pl.when(block == 2)(early.two)

    @pl.when(block == pl.num_programs(0) - 1)
    def _():
        def memory_rows(i, carry):
            part = pl.ds(pl.multiple_of(i * BLK, BLK), BLK)
            low = dkv_all[part, :].astype(bf16)
            dkv_low[part, :] = low
            total = jnp.zeros((BLK, D), f32)
            for half in range(2):
                for which in range(2):
                    first = which * D + half * 256
                    total = total + mm_nt(low[:, first : first + 256], wa[half][4 + which])
            dmem_ref[part, :] = total
            return carry

        lax.fori_loop(0, jnp.where(core == 0, 6, 2), memory_rows, 0)

        @pl.when(core != 0)
        def _():
            dkv_low[512:, :] = jnp.zeros((1024, 2 * D), bf16)
            dmem_ref[512:, :] = jnp.zeros((1024, D), f32)

        dlow_ref[...] = dmem_ref[1024:, :].astype(bf16)

        def bands(half, put):
            col = pl.ds(half * 256, 256)
            for which in range(3):
                put(0, which, mm_tn(dqkv_all[:, pl.ds(which * D + half * 256, 256)], h1_ref[...]))
            put(0, 3, mm_tn(dcq_all[:, col], h2_ref[...]))
            for which in range(2):
                put(1, which, mm_tn(dkv_low[:, pl.ds(which * D + half * 256, 256)], mem_ref[...]))
            put(1, 2, mm_tn(o_ref[:, col], dys_all[...]))
            put(1, 3, mm_tn(oc_ref[:, col], dyc_all[...]))

        def put_away(f, j, value):
            gs_away[f, j] = value.astype(bf16)
            if j % 2 == 1:
                pair = pl.ds(j - 1, 2)
                early.net.send(
                    True, gs_away.at[f, pair], gs_in.at[f, pair], band_sem + 2 * f + j // 2, early.net.sibling
                )

        def put_here(f, j, value):
            gs_ref[f, j] = value.astype(bf16)

        early.keep_sends()
        bands(1, put_away)
        bands(0, put_here)
        early.three()
        for f in range(2):
            for j in range(4):
                if j % 2 == 0:
                    early.net.landed(True, gs_in.at[f, pl.ds(j, 2)], band_sem + 2 * f + j // 2)
                add_into(gs_ref.at[f, j], [gs_in.at[f, j]], 128)
        early.net.all_sent()
        early.end()


def whole(shape):
    return pl.BlockSpec(shape, lambda i: (0,) * len(shape), pipeline_mode=pl.Buffered(1))


def by_rows(width):
    return pl.BlockSpec((BLK, width), lambda i: (i, 0))


def wide_rows(width):
    return pl.BlockSpec((WIDE, width), lambda i: (i, 0))


def tall_rows(width):
    return pl.BlockSpec((TALL, width), lambda i: (i, 0))


def sds(shape, dtype):
    return jax.ShapeDtypeStruct(shape, dtype)


def run_forward(lengths, x, mem, wa, wo, gain, bias):
    rows = x.shape[0]
    steps = rows // WIDE
    outs = [
        (sds((rows, D), bf16), wide_rows(D)),
        (sds((rows, 3 * D), bf16), wide_rows(3 * D)),
        (sds((rows // BLK, 4, 512, 256), bf16), pl.BlockSpec((2, 4, 512, 256), lambda i: (i, 0, 0, 0))),
        (sds((rows, D), bf16), wide_rows(D)),
        (sds((rows, D), f32), wide_rows(D)),
        (sds((rows, D), bf16), wide_rows(D)),
        (sds((rows, D), bf16), wide_rows(D)),
        (sds((1536, 2 * D), bf16), whole((1536, 2 * D))),
        (sds((rows // BLK, 8, 256, 128), bf16), pl.BlockSpec((2, 8, 256, 128), lambda i: (i, 0, 0, 0))),
        (sds((rows, D), bf16), wide_rows(D)),
        (sds((rows, D), f32), wide_rows(D)),
    ]
    return pl.pallas_call(
        forward_kernel,
        grid=(steps,),
        in_specs=[
            pl.BlockSpec(memory_space=pltpu.SMEM), wide_rows(D), whole((1536, D)),
            whole((6, D, 256)), whole((6, D, 256)), whole((2, 256, D)), whole((2, 256, D)),
            whole((4, D)), whole((4, D)),
        ],
        out_specs=[o[1] for o in outs],
        out_shape=[o[0] for o in outs],
        compiler_params=pltpu.CompilerParams(vmem_limit_bytes=60 * MIB),
        cost_estimate=pl.CostEstimate(flops=9 * 10**9, bytes_accessed=22 * MIB, transcendentals=3 * 10**6),
        name="layer_forward",
    )(lengths, x, mem, wa[0], wa[1], wo[0], wo[1], gain, bias)


def run_middle(lengths, total, x2, targets, wi, wf, wh, gain, bias, vocab, tokens):
    rows = x2.shape[0]
    steps = rows // TALL
    outs = [
        (sds((rows, D), bf16), tall_rows(D)),
        (sds((rows, D), f32), tall_rows(D)),
        (sds((2, 2, 2, 512, D), bf16), whole((2, 2, 2, 512, D))),
        (sds((VOC, D), bf16), whole((VOC, D))),
        (sds((8, D), f32), whole((8, D))),
        (sds((8, VOC), f32), whole((8, VOC))),
    ]
    return pl.pallas_call(
        partial(middle_kernel, vocab, tokens),
        grid=(steps,),
        in_specs=[
            pl.BlockSpec(memory_space=pltpu.SMEM), whole((8, 128)), tall_rows(D), tall_rows(1),
            whole((D, 1024)), whole((D, 1024)), whole((1024, D)), whole((1024, D)), whole((VOC, D)),
            whole((4, D)), whole((4, D)),
        ],
        out_specs=[o[1] for o in outs],
        out_shape=[o[0] for o in outs],
        scratch_shapes=[
            VMEM((rows, D), bf16), VMEM((rows, 2048), bf16), VMEM((rows, D), bf16),
            VMEM((rows, 2048), bf16), VMEM((rows, D), bf16), VMEM((rows, VOC), bf16),
            VMEM((TALL, 2048), f32),
        ],
        compiler_params=pltpu.CompilerParams(vmem_limit_bytes=60 * MIB),
        cost_estimate=pl.CostEstimate(flops=15 * 10**9, bytes_accessed=18 * MIB, transcendentals=5 * 10**6),
        name="ffn_head",
    )(lengths, total, x2, targets, wi[0], wi[1], wf[0], wf[1], wh, gain, bias)


def run_backward(dims, g2, x, x1, h1, qkv, p, o, h2, cq, kv, pc, oc, mem, wa, wo, gain, gw, ghead):
    rows = x.shape[0]
    steps = rows // BLK
    outs = [
        (sds((rows, D), f32), by_rows(D)),
        (sds((1536, D), f32), whole((1536, D))),
        (sds((512, D), bf16), whole((512, D))),
        (sds((2, 4, 256, D), bf16), whole((2, 4, 256, D))),
        (sds((8, D), f32), whole((8, D))),
        (sds((2, 512, D), bf16), pl.BlockSpec(memory_space=pl.ANY)),
        (sds((2, HPART, D), bf16), pl.BlockSpec(memory_space=pl.ANY)),
    ]
    nz, ny, nx = dims
    slots = max(nx, ny) - 1
    return pl.pallas_call(
        partial(backward_kernel, dims),
        grid=(steps,),
        in_specs=[
            by_rows(D), by_rows(D), by_rows(D), whole((rows, D)), by_rows(3 * D),
            pl.BlockSpec((1, 4, 512, 256), lambda i: (i, 0, 0, 0)), whole((rows, D)), whole((rows, D)),
            by_rows(D), whole((1536, 2 * D)), pl.BlockSpec((1, 8, 256, 128), lambda i: (i, 0, 0, 0)),
            whole((rows, D)), whole((1536, D)),
            whole((6, D, 256)), whole((6, D, 256)), whole((2, 256, D)), whole((2, 256, D)), whole((4, D)),
            pl.BlockSpec(memory_space=pl.ANY), pl.BlockSpec(memory_space=pl.ANY),
        ],
        out_specs=[o_[1] for o_ in outs],
        out_shape=[o_[0] for o_ in outs],
        scratch_shapes=[
            VMEM((rows, D), bf16), VMEM((rows, D), bf16), VMEM((rows, D), bf16),
            VMEM((rows, 3 * D), bf16), VMEM((1536, 2 * D), f32), VMEM((1536, 2 * D), bf16),
            VMEM((2, 2, 512, D), bf16), VMEM((2, 2, 512, D), bf16),
            VMEM((2, slots, 512, D), bf16), VMEM((2, slots, 512, D), bf16),
            VMEM((2, HPART, D), bf16), VMEM((2, HPART, D), bf16),
            VMEM((2, slots, HPART, D), bf16), VMEM((2, slots, HPART, D), bf16),
            VMEM((2, 4, 256, D), bf16), VMEM((2, 4, 256, D), bf16),
            pltpu.SemaphoreType.DMA((48,)), pltpu.SemaphoreType.DMA((40,)), pltpu.SemaphoreType.DMA((6,)),
        ],
        compiler_params=pltpu.CompilerParams(
            vmem_limit_bytes=62 * MIB, collective_id=2, has_side_effects=True,
        ),
        cost_estimate=pl.CostEstimate(flops=18 * 10**9, bytes_accessed=30 * MIB, transcendentals=0),
        name="attention_backward",
    )(g2, x, x1, h1, qkv, p, o, h2, cq, kv, pc, oc, mem, wa[0], wa[1], wo[0], wo[1], gain, gw, ghead)


MESH = pl.DeviceIdType.MESH
OWN = 2


def chip_dims(count):
    nz = 4
    side = math.isqrt(count // nz)
    return nz, count // nz // side, side


class Net:
    def __init__(self, dims, send_sems, recv_sems):
        self.nz, self.ny, self.nx = dims
        self.chip = lax.axis_index("dp")
        self.core = lax.axis_index("mp")
        self.x = lax.rem(self.chip, self.nx)
        self.y = lax.rem(lax.div(self.chip, self.nx), self.ny)
        self.z = lax.div(self.chip, self.nx * self.ny)
        self.place = {"x": self.x, "y": self.y, "z": self.z}
        self.count = {"x": self.nx, "y": self.ny, "z": self.nz}
        self.sibling = {"dp": self.chip, "mp": 1 - self.core}
        self.send_sems, self.recv_sems = send_sems, recv_sems
        self.sent, self.received = 0, 0
        self.unsent = []
        self.ending, self.keeping = False, True

    def at(self, **moved):
        p = {**self.place, **moved}
        return {"dp": (p["z"] * self.ny + p["y"]) * self.nx + p["x"], "mp": self.core}

    def further(self, axis, d):
        return lax.rem(self.place[axis] + d, self.count[axis])

    def on(self, condition, body):
        if condition is True:
            body()
        else:
            pl.when(condition)(body)

    def both(self, *conditions):
        result = True
        for c in conditions:
            if c is not True:
                result = c if result is True else jnp.logical_and(result, c)
        return result

    def inside(self, axis):
        return True if self.count[axis] == OWN else self.place[axis] < OWN

    def goes_inside(self, axis, d):
        return True if self.count[axis] == OWN else self.further(axis, d) < OWN

    def clipped(self, axis):
        return self.place[axis] if self.count[axis] == OWN else jnp.minimum(self.place[axis], OWN - 1)

    def send_sem(self, amount):
        self.sent += amount
        return self.sent - amount

    def recv_sem(self, amount):
        self.received += amount
        return self.received - amount

    def remote(self, src, dst, send_sem, recv_sem, device):
        return pltpu.make_async_remote_copy(
            src_ref=src, dst_ref=dst, send_sem=self.send_sems.at[send_sem],
            recv_sem=self.recv_sems.at[recv_sem], device_id=device, device_id_type=MESH,
        )

    def send(self, condition, src, dst, recv_sem, device):
        sem = self.send_sem(1)
        copy = lambda: self.remote(src, dst, sem, recv_sem, device)
        if self.ending:
            self.on(condition, lambda: copy().wait_send())
            return
        self.on(condition, lambda: copy().start())
        if self.keeping:
            self.unsent.append((condition, copy))

    def landed(self, condition, dst, recv_sem):
        self.on(condition, lambda: self.remote(dst, dst, 0, recv_sem, self.sibling).wait_recv())

    def spread(self, axis, condition, ref, recv_sem):
        for d in range(1, self.count[axis]):
            self.send(condition, ref, ref, recv_sem, self.at(**{axis: self.further(axis, d)}))

    def all_sent(self):
        for condition, copy in self.unsent:
            self.on(condition, lambda copy=copy: copy().wait_send())
        self.unsent = []
        assert self.sent <= self.send_sems.shape[0] and self.received <= self.recv_sems.shape[0]

    def barrier(self):
        partners = [self.sibling]
        for axis in ("x", "y", "z"):
            for d in range(1, self.count[axis]):
                partners.append(self.at(**{axis: self.further(axis, d)}))
        barrier = pltpu.get_barrier_semaphore()
        for partner in partners:
            pl.semaphore_signal(barrier, inc=1, device_id=partner, device_id_type=MESH)
        pl.semaphore_wait(barrier, len(partners))


def add_into(dst, sources, step):
    rows = dst.shape[0]

    def body(i, carry):
        part = pl.ds(pl.multiple_of(i * step, step), step)
        total = dst[part, :].astype(f32)
        for s in sources:
            total = total + s[part, :].astype(f32)
        dst[part, :] = total.astype(bf16)
        return carry

    lax.fori_loop(0, rows // step, body, 0)


HEAD_X, HEAD_Y, HEAD_Z = 1, 0, 0


class EarlySum:
    def __init__(self, net, gw, ghead, wide_out, head_out, scratch):
        (
            self.acc, self.core_in, self.first_in, self.second_in,
            self.head_acc, self.head_core, self.head_first, self.head_second, self.local,
        ) = scratch
        self.net, self.gw, self.ghead, self.wide_out, self.head_out = net, gw, ghead, wide_out, head_out
        n = net
        self.core_sem = n.recv_sem(6)
        self.first_sem = [n.recv_sem(n.nx - 1), n.recv_sem(n.ny - 1)]
        self.second_sem = [n.recv_sem(n.ny - 1), n.recv_sem(n.nx - 1)]
        self.head_first_sem = [n.recv_sem(n.nx - 1), n.recv_sem(n.ny - 1)]
        self.head_second_sem = [n.recv_sem(n.ny - 1), n.recv_sem(n.nx - 1)]
        self.sums = ((0, "x", "y"), (1, "y", "x"))
        self.goal = {"x": HEAD_X, "y": HEAD_Y}

    def head_rows(self, core, f):
        return self.ghead.at[pl.ds(pl.multiple_of(core * HROWS + f * HPART, HPART), HPART)]

    def own_copies(self):
        core = self.net.core
        return [
            pltpu.make_async_copy(self.gw.at[0, m, f], self.acc.at[m, f], self.local.at[2 * m + f])
            for m in range(2)
            for f in range(2)
        ] + [
            pltpu.make_async_copy(self.head_rows(core, f), self.head_acc.at[f], self.local.at[4 + f]) for f in range(2)
        ]

    def start(self):
        self.net.keeping = False
        self.net.barrier()
        for copy in self.own_copies():
            copy.start()
        self.core_sends()

    def core_sends(self):
        n = self.net
        for m in range(2):
            for f in range(2):
                n.send(True, self.gw.at[1, m, f], self.core_in.at[m, f], self.core_sem + 2 * m + f, n.sibling)
        for f in range(2):
            n.send(True, self.head_rows(1 - n.core, f), self.head_core.at[f], self.core_sem + 4 + f, n.sibling)

    def one(self):
        n = self.net
        for copy in self.own_copies():
            copy.wait()
        for m in range(2):
            for f in range(2):
                n.landed(True, self.core_in.at[m, f], self.core_sem + 2 * m + f)
                add_into(self.acc.at[m, f], [self.core_in.at[m, f]], 128)
        for f in range(2):
            n.landed(True, self.head_core.at[f], self.core_sem + 4 + f)
            add_into(self.head_acc.at[f], [self.head_core.at[f]], HPART)
        self.first_sends()

    def first_sends(self):
        n = self.net
        for f, axis, other in self.sums:
            for d in range(1, n.count[axis]):
                target = jnp.minimum(n.further(axis, d), OWN - 1)
                n.send(
                    n.goes_inside(axis, d), self.acc.at[target, f], self.first_in.at[f, d - 1],
                    self.first_sem[f] + d - 1, n.at(**{axis: n.further(axis, d)}),
                )
            goal = self.goal[axis]
            for d in range(1, n.count[axis]):
                n.send(
                    n.place[axis] == (goal + d) % n.count[axis], self.head_acc.at[f],
                    self.head_first.at[f, d - 1], self.head_first_sem[f] + d - 1, n.at(**{axis: goal}),
                )

    def two(self):
        n = self.net
        for f, axis, other in self.sums:
            matrix = n.clipped(axis)

            def take(f=f, axis=axis, matrix=matrix):
                slots = [self.first_in.at[f, d - 1] for d in range(1, n.count[axis])]
                for d in range(1, n.count[axis]):
                    n.landed(True, slots[d - 1], self.first_sem[f] + d - 1)
                add_into(self.acc.at[matrix, f], slots, 128)

            n.on(n.inside(axis), take)

            def take_head(f=f, axis=axis):
                slots = [self.head_first.at[f, d - 1] for d in range(1, n.count[axis])]
                for d in range(1, n.count[axis]):
                    n.landed(True, slots[d - 1], self.head_first_sem[f] + d - 1)
                add_into(self.head_acc.at[f], slots, HPART)

            n.on(n.place[axis] == self.goal[axis], take_head)
        self.second_sends()

    def second_sends(self):
        n = self.net
        for f, axis, other in self.sums:
            matrix = n.clipped(axis)
            distance = lax.rem(n.place[other] - matrix + n.count[other], n.count[other])
            slot = jnp.maximum(distance, 1) - 1
            n.send(
                n.both(n.inside(axis), distance != 0), self.acc.at[matrix, f], self.second_in.at[f, slot],
                self.second_sem[f] + slot, n.at(**{other: matrix}),
            )
            goal = self.goal[other]
            for d in range(1, n.count[other]):
                n.send(
                    n.both(n.place[axis] == self.goal[axis], n.place[other] == (goal + d) % n.count[other]),
                    self.head_acc.at[f], self.head_second.at[f, d - 1], self.head_second_sem[f] + d - 1,
                    n.at(**{other: goal}),
                )

    def columns(self):
        n = self.net
        wide = n.both(n.inside("x"), n.inside("y"), n.x == n.y)
        return wide, n.both(n.x == HEAD_X, n.y == HEAD_Y)

    def out_copies(self):
        n = self.net
        wide, head = self.columns()
        copies = [
            (wide, pltpu.make_async_copy(self.acc.at[n.clipped(axis), f], self.wide_out.at[f], self.local.at[f]))
            for f, axis, other in self.sums
        ]
        return copies + [(head, pltpu.make_async_copy(self.head_acc, self.head_out, self.local.at[4]))]

    def three(self):
        n = self.net
        wide, head = self.columns()
        for f, axis, other in self.sums:

            def take(f=f, axis=axis, other=other):
                slots = [self.second_in.at[f, d - 1] for d in range(1, n.count[other])]
                for d in range(1, n.count[other]):
                    n.landed(True, slots[d - 1], self.second_sem[f] + d - 1)
                add_into(self.acc.at[n.clipped(axis), f], slots, 128)

            n.on(wide, take)

            def take_head(f=f, other=other):
                slots = [self.head_second.at[f, d - 1] for d in range(1, n.count[other])]
                for d in range(1, n.count[other]):
                    n.landed(True, slots[d - 1], self.head_second_sem[f] + d - 1)
                add_into(self.head_acc.at[f], slots, HPART)

            n.on(head, take_head)
        for condition, copy in self.out_copies():
            n.on(condition, copy.start)

    def keep_sends(self):
        self.net.keeping = True

    def end(self):
        for condition, copy in self.out_copies():
            self.net.on(condition, copy.wait)
        self.net.sent, self.net.ending = 0, True
        self.core_sends()
        self.first_sends()
        self.second_sends()


def prepare_kernel(
    dims, lengths_ref, ai_ref, ao_ref, fi_ref, fo_ref, vh_ref, mem_ref,
    wa0, wa1, wo0, wo1, wi0, wi1, wf0, wf1, mem_out, wh_ref, total_ref,
    ai_in, ao_in, fi_in, fo_in, vh_in, mem_in, ai_low, ao_low, fi_low, fo_low, totals,
    load_sems, keep_sems, send_sems, recv_sems,
):
    nz, ny, nx = dims
    chip = lax.axis_index("dp")
    core = lax.axis_index("mp")
    place = {"x": lax.rem(chip, nx), "y": lax.rem(lax.div(chip, nx), ny), "z": lax.div(chip, nx * ny)}
    count = {"x": nx, "y": ny, "z": nz}
    sibling = {"dp": chip, "mp": 1 - core}

    def at(axis, target):
        p = {**place, axis: target}
        return {"dp": (p["z"] * ny + p["y"]) * nx + p["x"], "mp": core}

    arrays = (
        (ai_ref, ai_in, ai_low, wa0, wa1),
        (ao_ref, ao_in, ao_low, wo0, wo1),
        (fi_ref, fi_in, fi_low, wi0, wi1),
        (fo_ref, fo_in, fo_low, wf0, wf1),
    )
    loads = [
        pltpu.make_async_copy(src, dst, load_sems.at[i])
        for i, (src, dst) in enumerate([a[:2] for a in arrays] + [(vh_ref, vh_in), (mem_ref, mem_in)])
    ]
    for load in loads:
        load.start()
    partners = [sibling]
    for axis in ("x", "y", "z"):
        for d in range(1, count[axis]):
            partners.append(at(axis, lax.rem(place[axis] + d, count[axis])))
    barrier = pltpu.get_barrier_semaphore()
    for partner in partners:
        pl.semaphore_signal(barrier, inc=1, device_id=partner, device_id_type=MESH)
    pl.semaphore_wait(barrier, len(partners))

    def remote(src, dst, send_sem, recv_sem, device):
        return pltpu.make_async_remote_copy(
            src_ref=src, dst_ref=dst, send_sem=send_sems.at[send_sem], recv_sem=recv_sems.at[recv_sem],
            device_id=device, device_id_type=MESH,
        )

    tokens = lengths_ref[0]
    for s in range(1, lengths_ref.shape[0]):
        tokens = tokens + lengths_ref[s]

    base = {}
    used = 8
    for axis in ("x", "y", "z"):
        base[axis] = used
        used += count[axis]
    pending = []

    def spread_total(level, axis, value):
        totals[level, place[axis]] = value
        for d in range(1, count[axis]):
            copy = remote(
                totals.at[level, place[axis]], totals.at[level, place[axis]], base[axis] + d,
                base[axis] + place[axis], at(axis, lax.rem(place[axis] + d, count[axis])),
            )
            copy.start()
            pending.append(copy)

    def add_total(level, axis):
        for d in range(1, count[axis]):
            source = lax.rem(place[axis] + d, count[axis])
            remote(
                totals.at[level, source], totals.at[level, source], base[axis] + d,
                base[axis] + source, sibling,
            ).wait_recv()
        value = totals[level, 0]
        for s in range(1, count[axis]):
            value = value + totals[level, s]
        return value

    def memory_moves():
        return (
            (core == 0, pltpu.make_async_copy(mem_in, mem_out.at[pl.ds(0, 1024)], keep_sems.at[4])),
            (
                core == 1,
                pltpu.make_async_copy(mem_in.at[pl.ds(512, 512)], mem_out.at[pl.ds(0, 512)], keep_sems.at[4]),
            ),
            (core == 1, pltpu.make_async_copy(mem_in, mem_out.at[pl.ds(512, 1024)], keep_sems.at[5])),
        )

    def memory_send():
        return remote(mem_in.at[pl.ds(0, 512)], mem_out.at[pl.ds(1024, 512)], 4, 4, sibling)

    spread_total(0, "x", jnp.full((8, 128), tokens.astype(f32)))
    loads[5].wait()
    for condition, copy in memory_moves():
        pl.when(condition)(copy.start)
    pl.when(core == 1)(lambda: memory_send().start())
    sends = []
    keeps = []
    for i, (src, staged, low, mine, others) in enumerate(arrays):
        loads[i].wait()
        low[...] = staged[...].astype(bf16)
        copy = remote(low, others, i, i, sibling)
        copy.start()
        sends.append(copy)
        keep = pltpu.make_async_copy(low, mine, keep_sems.at[i])
        keep.start()
        keeps.append(keep)
        if i < 2:
            spread_total(i + 1, ("y", "z")[i], add_total(i, ("x", "y")[i]))
    loads[4].wait()
    vocab = vh_in.shape[0]
    wh_ref[512:, :] = jnp.zeros((VOC - 512, D), bf16)
    wh_ref[0:vocab, :] = vh_in[...].astype(bf16)
    total_ref[...] = add_total(2, "z")
    for condition, copy in memory_moves():
        pl.when(condition)(copy.wait)
    pl.when(core == 1)(lambda: memory_send().wait_send())
    pl.when(core == 0)(lambda: memory_send().wait_recv())
    for copy in keeps:
        copy.wait()
    for copy in sends:
        copy.wait()
    for copy in pending:
        copy.wait_send()


def run_prepare(dims, lengths, ai, ao, fi, fo, vh, mem):
    hbm = pl.BlockSpec(memory_space=pl.ANY)
    vmem = pl.BlockSpec(memory_space=VMEM)
    weights = [sds(w.shape, bf16) for w in (ai, ao, fi, fo) for _ in range(2)]
    nz, ny, nx = dims
    return pl.pallas_call(
        partial(prepare_kernel, dims),
        in_specs=[pl.BlockSpec(memory_space=pltpu.SMEM)] + [hbm] * 6,
        out_specs=[hbm] * 9 + [vmem, vmem],
        out_shape=weights + [sds((1536, D), bf16), sds((VOC, D), bf16), sds((8, 128), f32)],
        scratch_shapes=[VMEM(w.shape, f32) for w in (ai, ao, fi, fo, vh)]
        + [VMEM(mem.shape, bf16)]
        + [VMEM(w.shape, bf16) for w in (ai, ao, fi, fo)]
        + [
            VMEM((3, max(dims), 8, 128), f32),
            pltpu.SemaphoreType.DMA((6,)), pltpu.SemaphoreType.DMA((6,)),
            pltpu.SemaphoreType.DMA((8 + nx + ny + nz,)), pltpu.SemaphoreType.DMA((8 + nx + ny + nz,)),
        ],
        compiler_params=pltpu.CompilerParams(
            vmem_limit_bytes=60 * MIB, collective_id=1, has_side_effects=True
        ),
        cost_estimate=pl.CostEstimate(flops=10**6, bytes_accessed=24 * MIB, transcendentals=0),
        name="prepare_weights",
    )(lengths, ai, ao, fi, fo, vh, mem)


PIECE = 256
SMALL = 24


def split_two(value):
    high = value.astype(bf16)
    return high, (value - high.astype(f32)).astype(bf16)


def wide_roles(n):
    left = n.x == 0
    return (
        jnp.where(left, 1, 2), jnp.where(left, 0, 3), jnp.where(left, 2, 1), jnp.where(left, 3, 0)
    )


def square_owners(n):
    beside = n.x == n.y
    return (
        jnp.where(beside, jnp.where(n.x == 0, 2, 1), 1),
        jnp.where(beside, jnp.where(n.x == 0, 0, 3), 2),
    )


class SquareBack:
    def __init__(self, net, low, land):
        self.net, self.low, self.land = net, low, land
        self.axes = (("x", "y"), ("y", "x"))
        self.z_sem = [net.recv_sem(2) for _ in range(2)]
        self.one_sem = [net.recv_sem(2 * OWN) for _ in range(2)]
        self.two_sem = [net.recv_sem(2 * OWN) for _ in range(2)]
        self.valid = net.both(net.inside("x"), net.inside("y"))
        self.owners = square_owners(net)

    def chunk(self, f):
        first, second = self.axes[f]
        return self.net.clipped(first) * 2 + self.net.clipped(second)

    def rows(self, p):
        return pl.ds(p * 128, 128)

    def start(self, p):
        n = self.net
        for f in range(2):
            owner = n.both(self.valid, n.z == self.owners[f])

            def keep(f=f):
                self.land[f, self.chunk(f), self.rows(p), :] = self.low[self.rows(p), :]

            n.on(owner, keep)
            n.spread("z", owner, self.land.at[f, self.chunk(f), self.rows(p)], self.z_sem[f] + p)

    def one(self, p):
        n = self.net
        for f in range(2):
            mine = self.land.at[f, self.chunk(f), self.rows(p)]
            n.landed(n.both(self.valid, n.z != self.owners[f]), mine, self.z_sem[f] + p)
            second = self.axes[f][1]
            n.spread(second, self.valid, mine, self.one_sem[f] + p * OWN + n.clipped(second))

    def two(self, p):
        n = self.net
        for f in range(2):
            first, second = self.axes[f]
            for s in range(OWN):
                n.landed(
                    n.both(n.inside(first), n.place[second] != s),
                    self.land.at[f, n.clipped(first) * 2 + s, self.rows(p)], self.one_sem[f] + p * OWN + s,
                )
            n.spread(
                first, n.inside(first), self.land.at[f, pl.ds(n.clipped(first) * 2, 2), self.rows(p)],
                self.two_sem[f] + p * OWN + n.clipped(first),
            )

    def end(self):
        n = self.net
        for p in range(2):
            for f in range(2):
                first = self.axes[f][0]
                for s in range(OWN):
                    n.landed(
                        n.place[first] != s, self.land.at[f, pl.ds(s * 2, 2), self.rows(p)],
                        self.two_sem[f] + p * OWN + s,
                    )


class WideBack:
    def __init__(self, net, low, spot, pieces, rows):
        self.net, self.low, self.spot, self.pieces, self.rows = net, low, spot, pieces, rows
        self.axes = (("x", "y"), ("y", "x"))
        self.hop_sem = net.recv_sem(pieces)
        self.one_sem = net.recv_sem(pieces)
        self.two_sem = [net.recv_sem(OWN) for _ in range(pieces)]
        self.wide = net.both(net.inside("x"), net.inside("y"), net.x == net.y)
        self.owner, self.near, self.middle, self.far = wide_roles(net)

    def stands(self, position):
        return self.net.both(self.wide, self.net.z == position)

    def mine(self, p):
        return self.spot(self.net.clipped("x"), p)

    def start(self, p):
        n = self.net

        def keep():
            self.mine(p)[...] = self.low[pl.ds(p * self.rows, self.rows), :]

        owner = self.stands(self.owner)
        n.on(owner, keep)
        n.send(owner, self.mine(p), self.mine(p), self.hop_sem + p, n.at(z=self.middle))
        n.send(owner, self.mine(p), self.mine(p), self.hop_sem + p, n.at(z=self.near))

    def onward(self, p):
        n = self.net
        here = self.stands(self.middle)
        n.landed(here, self.mine(p), self.hop_sem + p)
        n.send(here, self.mine(p), self.mine(p), self.hop_sem + p, n.at(z=self.far))

    def one(self, p):
        n = self.net
        n.landed(self.stands(self.near), self.mine(p), self.hop_sem + p)
        n.landed(self.stands(self.far), self.mine(p), self.hop_sem + p)
        first, second = self.axes[2 * p // self.pieces]
        n.spread(second, self.wide, self.spot(n.clipped(first), p), self.one_sem + p)

    def two(self, p):
        n = self.net
        first, second = self.axes[2 * p // self.pieces]
        mine = self.spot(n.clipped(first), p)
        n.landed(n.both(n.inside(first), n.place[first] != n.place[second]), mine, self.one_sem + p)
        n.spread(first, n.inside(first), mine, self.two_sem[p] + n.clipped(first))

    def end(self):
        n = self.net
        for p in range(self.pieces):
            first = self.axes[2 * p // self.pieces][0]
            for m in range(OWN):
                n.landed(n.place[first] != m, self.spot(m, p), self.two_sem[p] + m)


class HeadBack:
    def __init__(self, net, low, land):
        self.net, self.low = net, low
        self.hop_sem, self.one_sem, self.two_sem = net.recv_sem(2), net.recv_sem(2), net.recv_sem(2)
        self.core_sem = net.recv_sem(1)
        self.axes = (("x", "y"), ("y", "x"))
        self.goal = {"x": HEAD_X, "y": HEAD_Y}
        self.spots = [
            land.at[pl.ds(pl.multiple_of(net.core * HROWS + p * HPART, HPART), HPART)] for p in range(2)
        ]
        self.mine = land.at[pl.ds(pl.multiple_of(net.core * HROWS, HROWS), HROWS)]
        self.theirs = land.at[pl.ds(pl.multiple_of((1 - net.core) * HROWS, HROWS), HROWS)]
        self.column = net.both(net.x == HEAD_X, net.y == HEAD_Y)

    def hop(self, k):
        n = self.net
        here = n.both(self.column, n.z == k)
        for p in range(2):
            if k == 0:

                def keep(p=p):
                    self.spots[p][...] = self.low[pl.ds(p * HPART, HPART), :]

                n.on(here, keep)
            else:
                n.landed(here, self.spots[p], self.hop_sem + p)
            if k < n.nz - 1:
                n.send(here, self.spots[p], self.spots[p], self.hop_sem + p, n.at(z=k + 1))

    def one(self):
        n = self.net
        for p in range(2):
            n.spread(self.axes[p][1], self.column, self.spots[p], self.one_sem + p)

    def two(self):
        n = self.net
        for p in range(2):
            first, second = self.axes[p]
            plane = n.place[first] == self.goal[first]
            n.landed(n.both(plane, n.place[second] != self.goal[second]), self.spots[p], self.one_sem + p)
            n.spread(first, plane, self.spots[p], self.two_sem + p)

    def three(self):
        n = self.net
        for p in range(2):
            first = self.axes[p][0]
            n.landed(n.place[first] != self.goal[first], self.spots[p], self.two_sem + p)
        n.send(True, self.mine, self.mine, self.core_sem, n.sibling)

    def end(self):
        self.net.landed(True, self.theirs, self.core_sem)


def muon_kernel(
    dims, gs_ref, wide_ref, headg_ref, na_ref, nf_ref, count_ref, dlow_ref, mi_ref, mo_ref, mu_ref, md_ref, mh_ref,
    ms_all, xs_all, mw_all, q_all, mh_all, xh_all, d_in, small_out,
    acc, first_in, second_in, band_in, wide_acc, wide_in, head_acc, head_in, small_buf,
    old_turned, old_plain, old_head, own, gram, gram_in, mats, m_low, x_low,
    ms_land, xs_land, mw_land, q_land, mh_land, xh_land,
    send_sems, recv_sems, local_sems,
):
    n = Net(dims, send_sems, recv_sems)
    nz = n.nz
    x, y, z, core = n.x, n.y, n.z, n.core
    on, both = n.on, n.both
    n.barrier()
    valid = both(n.inside("x"), n.inside("y"))
    wide = both(valid, x == y)
    wide_z, near_z, middle_z, far_z = wide_roles(n)
    wide_owner = both(wide, z == wide_z)
    square_z = square_owners(n)
    owns = [both(valid, z == square_z[f]) for f in range(2)]
    square = jnp.logical_or(owns[0], owns[1])
    task = jnp.where(
        z == square_z[0], n.clipped("x") * 2 + n.clipped("y"), 4 + n.clipped("y") * 2 + n.clipped("x")
    )
    head_column = both(x == HEAD_X, y == HEAD_Y)
    head_owner = both(head_column, z == HEAD_Z)
    axes = (("x", "y"), ("y", "x"))

    first_sem = [n.recv_sem(2 * (n.count[axes[f][0]] - 1)) for f in range(2)]
    second_sem = [n.recv_sem(2 * (n.count[axes[f][1]] - 1)) for f in range(2)]

    def half_rows(p):
        return pl.ds(p * 128, 128)

    for p in range(2):
        for f in range(2):
            axis = axes[f][0]
            for d in range(1, n.count[axis]):
                target = jnp.minimum(n.further(axis, d), OWN - 1)
                n.send(
                    n.goes_inside(axis, d), gs_ref.at[f, pl.ds(target * 2, 2), half_rows(p)],
                    first_in.at[f, d - 1, :, half_rows(p)], first_sem[f] + 2 * (d - 1) + p,
                    n.at(**{axis: n.further(axis, d)}),
                )
    own_copies = [
        pltpu.make_async_copy(gs_ref.at[f], acc.at[f], local_sems.at[f]) for f in range(2)
    ]
    for copy in own_copies:
        copy.start()

    def wide_load():
        return pltpu.make_async_copy(wide_ref, wide_acc, local_sems.at[4])

    def head_load():
        return pltpu.make_async_copy(headg_ref, head_acc, local_sems.at[5])

    def old_copies():
        sem = local_sems.at[6]
        return (
            (both(wide_owner, x == 0), lambda: pltpu.make_async_copy(mu_ref, old_turned, sem)),
            (both(wide_owner, x != 0), lambda: pltpu.make_async_copy(md_ref, old_plain, sem)),
            (
                both(square, task < 6),
                lambda: pltpu.make_async_copy(
                    mi_ref.at[jnp.minimum(task, 5)], old_turned.at[:, pl.ds(0, PIECE)], sem
                ),
            ),
            (
                both(square, task >= 6),
                lambda: pltpu.make_async_copy(
                    mo_ref.at[jnp.maximum(task, 6) - 6], old_plain.at[pl.ds(0, PIECE)], sem
                ),
            ),
            (head_owner, lambda: pltpu.make_async_copy(mh_ref, old_head, sem)),
        )

    on(wide, lambda: wide_load().start())
    on(head_column, lambda: head_load().start())
    for condition, copy in old_copies():
        on(condition, lambda copy=copy: copy().start())
    d_sem = n.recv_sem(1)
    n.send(core == 0, dlow_ref, d_in, d_sem, n.sibling)

    on(wide, lambda: wide_load().wait())
    near_sem, middle_sem, far_sem = n.recv_sem(4), n.recv_sem(4), n.recv_sem(4)

    def piece(k):
        return wide_acc.at[k // 2, pl.ds((k % 2) * PIECE, PIECE)]

    for k in range(4):
        n.send(both(wide, z == far_z), piece(k), wide_in.at[1, k], far_sem + k, n.at(z=middle_z))
        n.send(both(wide, z == near_z), piece(k), wide_in.at[0, k], near_sem + k, n.at(z=wide_z))

    def wide_pass(k):
        here = both(wide, z == middle_z)

        def take():
            n.landed(True, wide_in.at[1, k], far_sem + k)
            add_into(piece(k), [wide_in.at[1, k]], 128)

        on(here, take)
        n.send(here, piece(k), wide_in.at[1, k], middle_sem + k, n.at(z=wide_z))

    on(head_column, lambda: head_load().wait())
    head_sem = n.recv_sem(2)

    def head_pass(distance):
        here = both(head_column, z == distance)
        for p in range(2):
            if distance < nz - 1:

                def take(p=p):
                    n.landed(True, head_in.at[p], head_sem + p)
                    add_into(head_acc.at[p], [head_in.at[p]], HPART)

                on(here, take)
            n.send(here, head_acc.at[p], head_in.at[p], head_sem + p, n.at(z=distance - 1))

    head_pass(nz - 1)

    small_core = n.recv_sem(1)
    small_sem = {axis: n.recv_sem(n.count[axis]) for axis in ("x", "y", "z")}
    small_buf[0, 0] = jnp.zeros((SMALL, VOC), f32)
    small_buf[0, 0, 0:8, 0:D] = na_ref[...]
    small_buf[0, 0, 8:16, 0:D] = nf_ref[...]
    small_buf[0, 0, 16:24, :] = count_ref[...]
    n.send(True, small_buf.at[0, 0], small_buf.at[0, 1], small_core, n.sibling)

    def small_go(level, axis, value):
        small_buf[level, n.place[axis]] = value
        n.spread(axis, True, small_buf.at[level, n.place[axis]], small_sem[axis] + n.place[axis])

    def small_add(level, axis):
        for d in range(1, n.count[axis]):
            source = n.further(axis, d)
            n.landed(True, small_buf.at[level, source], small_sem[axis] + source)
        total = small_buf[level, 0]
        for s in range(1, n.count[axis]):
            total = total + small_buf[level, s]
        return total

    for copy in own_copies:
        copy.wait()
    n.landed(True, small_buf.at[0, 1], small_core)
    small_go(1, "x", small_buf[0, 0] + small_buf[0, 1])
    wide_pass(0)
    for p in range(2):
        for f in range(2):
            first, second = axes[f]
            mine = n.clipped(first) * 2

            def take(f=f, p=p, first=first, mine=mine):
                for d in range(1, n.count[first]):
                    n.landed(True, first_in.at[f, d - 1, :, half_rows(p)], first_sem[f] + 2 * (d - 1) + p)
                for j in range(2):
                    add_into(
                        acc.at[f, mine + j, half_rows(p)],
                        [first_in.at[f, d - 1, j, half_rows(p)] for d in range(1, n.count[first])], 128,
                    )

            on(n.inside(first), take)
            for d in range(1, n.count[second]):
                target = jnp.minimum(n.further(second, d), OWN - 1)
                n.send(
                    both(n.inside(first), n.goes_inside(second, d)), acc.at[f, mine + target, half_rows(p)],
                    second_in.at[f, d - 1, half_rows(p)], second_sem[f] + 2 * (d - 1) + p,
                    n.at(**{second: n.further(second, d)}),
                )
        wide_pass(1 + p)
        head_pass(2 - p)
    small_go(2, "y", small_add(1, "x"))

    def chunk(f):
        first, second = axes[f]
        return n.clipped(first) * 2 + n.clipped(second)

    band_sem = [n.recv_sem(2 * (nz - 1)) for _ in range(2)]
    for p in range(2):
        for f in range(2):
            second = axes[f][1]

            def take_second(f=f, p=p, second=second):
                for d in range(1, n.count[second]):
                    n.landed(True, second_in.at[f, d - 1, half_rows(p)], second_sem[f] + 2 * (d - 1) + p)
                add_into(
                    acc.at[f, chunk(f), half_rows(p)],
                    [second_in.at[f, d - 1, half_rows(p)] for d in range(1, n.count[second])], 128,
                )

            on(valid, take_second)
            for d in range(1, nz):
                n.send(
                    both(valid, z == lax.rem(square_z[f] + d, nz)), acc.at[f, chunk(f), half_rows(p)],
                    band_in.at[d - 1, half_rows(p)], band_sem[f] + 2 * (d - 1) + p, n.at(z=square_z[f]),
                )
    small_go(3, "z", small_add(2, "y"))
    wide_pass(3)

    own[...] = jnp.zeros_like(own)
    for condition, copy in old_copies():
        on(condition, lambda copy=copy: copy().wait())

    def turned(k):
        return jnp.swapaxes(old_turned[:, k * PIECE : (k + 1) * PIECE], 0, 1)

    back_ms = SquareBack(n, m_low, ms_land)
    back_mw = WideBack(
        n, m_low, lambda m, p: mw_land.at[m, p // 2, pl.ds((p % 2) * PIECE, PIECE)], 4, PIECE
    )
    back_mh = HeadBack(n, m_low, mh_land)
    back_xs = SquareBack(n, x_low, xs_land)
    back_q = WideBack(n, x_low, lambda m, p: q_land.at[m, core, p], 2, 128)
    back_xh = HeadBack(n, x_low, xh_land)

    def keep_moment(rows, value):
        own[rows, :] = value
        m_low[rows, :] = value.astype(bf16)

    def finish_wide(k, old):
        total = piece(k)[...].astype(f32) + wide_in[0, k].astype(f32) + wide_in[1, k].astype(f32)
        keep_moment(pl.ds(k * PIECE, PIECE), total + 0.5 * old)

    def wide_moment(k):
        n.landed(wide_owner, wide_in.at[0, k], near_sem + k)
        n.landed(wide_owner, wide_in.at[1, k], middle_sem + k)
        on(both(wide_owner, x == 0), lambda: finish_wide(k, turned(k)))
        on(both(wide_owner, x != 0), lambda: finish_wide(k, old_plain[pl.ds(k * PIECE, PIECE), :]))
        back_mw.start(k)

    def finish_square(p, old):
        f = jnp.where(owns[0], 0, 1)
        mine = jnp.where(owns[0], chunk(0), chunk(1))
        total = acc[f, mine, half_rows(p), :].astype(f32)
        for d in range(1, nz):
            total = total + band_in[d - 1, half_rows(p), :].astype(f32)
        keep_moment(half_rows(p), total + 0.5 * old)

    def square_moment(p):
        for f in range(2):
            for d in range(1, nz):
                n.landed(owns[f], band_in.at[d - 1, half_rows(p)], band_sem[f] + 2 * (d - 1) + p)
        on(
            both(square, task < 6),
            lambda: finish_square(p, jnp.swapaxes(old_turned[:, p * 128 : (p + 1) * 128], 0, 1)),
        )
        on(both(square, task >= 6), lambda: finish_square(p, old_plain[half_rows(p), :]))
        back_ms.start(p)

    def finish_head():
        old_plain[pl.ds(512, 128), :] = jnp.zeros((128, D), f32)
        old_plain[pl.ds(0, old_head.shape[0]), :] = old_head[...]
        for p in range(2):
            here = pl.ds(pl.multiple_of(core * HROWS + p * HPART, HPART), HPART)
            total = head_acc[p].astype(f32) + head_in[p].astype(f32)
            keep_moment(pl.ds(p * HPART, HPART), total + 0.5 * old_plain[here, :])

    wide_moment(0)
    for p in range(2):
        n.landed(head_owner, head_in.at[p], head_sem + p)
    on(head_owner, finish_head)
    back_mh.hop(0)
    square_moment(0)
    wide_moment(1)
    wide_moment(2)
    square_moment(1)
    wide_moment(3)

    blocks_used = jnp.where(wide_owner, 4, jnp.where(head_owner, 2, 1))
    gram[...] = jnp.zeros_like(gram)

    def gram_step(i, carry):
        high, low = split_two(own[pl.ds(pl.multiple_of(i * PIECE, PIECE), PIECE), :])
        gram[...] += mm_tn(high, high) + (mm_tn(high, low) + mm_tn(low, high))
        return carry

    lax.fori_loop(0, blocks_used, gram_step, 0)
    gram_sem = n.recv_sem(1)
    n.send(True, gram, gram_in, gram_sem, n.sibling)
    small_out[...] = small_add(3, "z")
    n.landed(True, gram_in, gram_sem)

    def eye_rows(first, rows):
        place = lax.broadcasted_iota(jnp.int32, (rows, D), 0) + first
        return (place == lax.broadcasted_iota(jnp.int32, (rows, D), 1)).astype(f32)

    def put(m, value):
        high, low = split_two(value)
        mats[m, 0] = high
        mats[m, 1] = low

    def product(a, b):
        ah, al = mats[a, 0], mats[a, 1]
        left_h, left_l = mats[b, 0, :, 0:256], mats[b, 1, :, 0:256]
        left = mm(ah, left_h) + (mm(ah, left_l) + mm(al, left_h))
        right_h, right_l = mats[b, 0, :, 256:512], mats[b, 1, :, 256:512]
        corner = mm(ah[256:], right_h) + (mm(ah[256:], right_l) + mm(al[256:], right_h))
        right = jnp.concatenate([jnp.swapaxes(left[256:], 0, 1), corner], axis=0)
        return jnp.concatenate([left, right], axis=1)

    busy = jnp.logical_or(square, jnp.logical_or(wide_owner, head_owner))
    total = jnp.sum(
        jnp.sum((gram[...] + gram_in[...]) * eye_rows(0, D), axis=0, keepdims=True), axis=1, keepdims=True
    )
    scale = 1.0 / (jnp.sqrt(total) + 1e-07)

    def newton_schulz(iteration):
        q_now, q_next = (2, 4) if iteration % 2 == 0 else (4, 2)
        if iteration == 0:
            put(0, (gram[...] + gram_in[...]) * scale * scale)

            def begin_rows():
                own[pl.ds(0, PIECE), :] = own[pl.ds(0, PIECE), :] * scale

            on(square, begin_rows)
        a = mats[0, 0].astype(f32) + mats[0, 1].astype(f32)
        put(1, NS_A * eye_rows(0, D) + NS_B * a + NS_C * product(0, 0))

        def update_rows():
            high, low = split_two(own[pl.ds(0, PIECE), :])
            ph, pll = mats[1, 0], mats[1, 1]
            own[pl.ds(0, PIECE), :] = mm(high, ph) + (mm(high, pll) + mm(low, ph))

        def update_q():
            if iteration == 0:
                mats[q_next] = mats[1]
            else:
                put(q_next, product(1, q_now))

        on(square, update_rows)
        on(jnp.logical_not(square), update_q)
        if iteration < NS_STEPS - 1:
            put(3, product(0, 1))
            put(0, product(3, 1))

    for iteration in range(NS_STEPS):
        on(busy, partial(newton_schulz, iteration))
        if iteration == 0:
            back_ms.one(0)
            back_mh.hop(1)
        if iteration == 1:
            back_ms.one(1)
            back_mw.onward(0)
            back_mw.onward(1)
            back_mh.hop(2)
        if iteration == 2:
            back_ms.two(0)
            back_mw.onward(2)
            back_mw.one(0)
            back_mh.hop(3)
        if iteration == 3:
            back_ms.two(1)
            back_mw.onward(3)
            back_mw.one(1)
            back_mh.one()

    last = 4 if NS_STEPS % 2 == 1 else 2

    def direction():
        part = pl.ds(0, 512)
        high, low = split_two(own[part, :] * scale)
        value = mm(high, mats[last, 0]) + (mm(high, mats[last, 1]) + mm(low, mats[last, 0]))
        x_low[part, :] = value.astype(bf16)

    def wide_polynomial():
        rows = pl.ds(pl.multiple_of(core * PIECE, PIECE), PIECE)
        value = mats[last, 0, rows, :].astype(f32) + mats[last, 1, rows, :].astype(f32)
        x_low[pl.ds(0, PIECE), :] = (value * scale).astype(bf16)

    on(wide_owner, wide_polynomial)
    on(head_owner, direction)

    def keep_rows():
        x_low[pl.ds(0, PIECE), :] = own[pl.ds(0, PIECE), :].astype(bf16)

    on(square, keep_rows)
    back_xs.start(0)
    back_xs.start(1)
    back_q.start(0)
    back_q.start(1)
    back_xh.hop(0)
    back_mw.one(2)
    back_mw.two(0)
    back_mh.two()
    back_q.onward(0)
    back_q.onward(1)
    back_xh.hop(1)
    outs = [
        pltpu.make_async_copy(src, dst, local_sems.at[i])
        for i, (src, dst) in enumerate(
            (
                (ms_land, ms_all), (mh_land, mh_all), (mw_land, mw_all), (xs_land, xs_all), (q_land, q_all),
                (xh_land, xh_all),
            )
        )
    ]
    back_xs.one(0)
    back_xh.hop(2)
    back_mw.one(3)
    back_mw.two(1)
    back_xs.one(1)
    back_q.one(0)
    back_q.one(1)
    back_xs.two(0)
    back_xh.hop(3)
    back_xh.one()
    back_mw.two(2)
    back_xs.two(1)
    back_q.two(0)
    back_q.two(1)
    back_mw.two(3)
    back_xh.two()
    back_mh.three()
    back_ms.end()
    outs[0].start()
    back_mh.end()
    outs[1].start()
    back_mw.end()
    outs[2].start()
    back_q.end()
    q_sem = n.recv_sem(2)
    for m in range(2):
        n.send(True, q_land.at[m, core], q_land.at[m, core], q_sem + m, n.sibling)
    back_xh.three()
    back_xs.end()
    outs[3].start()
    for m in range(2):
        n.landed(True, q_land.at[m, 1 - core], q_sem + m)
    outs[4].start()
    back_xh.end()
    outs[5].start()
    n.landed(core == 1, d_in, d_sem)
    n.all_sent()
    for copy in outs:
        copy.wait()


def run_muon(dims, gs, wide, headg, na, nf, count, dlow, mi, mo, mu, md, mh):
    nz, ny, nx = dims
    hbm = pl.BlockSpec(memory_space=pl.ANY)
    vmem = pl.BlockSpec(memory_space=VMEM)
    slots = max(nx, ny) - 1
    most = max(nx, ny, nz, 2)
    squares = (2, 4, PIECE, D)
    lands = [squares, squares, (2, 2, 512, D), (2, 2, 2, 128, D), (VOC, D), (VOC, D)]
    return pl.pallas_call(
        partial(muon_kernel, dims),
        in_specs=[hbm] * 3 + [vmem] * 3 + [hbm] * 6,
        out_specs=[hbm] * 7 + [vmem],
        out_shape=[sds(s, bf16) for s in lands] + [sds((512, D), bf16), sds((SMALL, VOC), f32)],
        scratch_shapes=[
            VMEM(squares, bf16),
            VMEM((2, slots, 2, PIECE, D), bf16),
            VMEM((2, slots, PIECE, D), bf16),
            VMEM((nz - 1, PIECE, D), bf16),
            VMEM((2, 512, D), bf16),
            VMEM((2, 4, PIECE, D), bf16),
            VMEM((2, HPART, D), bf16),
            VMEM((2, HPART, D), bf16),
            VMEM((4, most, SMALL, VOC), f32),
            VMEM((D, 1024), f32),
            VMEM((1024, D), f32),
            VMEM(mh.shape, f32),
            VMEM((1024, D), f32),
            VMEM((D, D), f32),
            VMEM((D, D), f32),
            VMEM((5, 2, D, D), bf16),
            VMEM((1024, D), bf16),
            VMEM((512, D), bf16),
        ]
        + [VMEM(s, bf16) for s in lands]
        + [
            pltpu.SemaphoreType.DMA((400,)), pltpu.SemaphoreType.DMA((160,)), pltpu.SemaphoreType.DMA((8,)),
        ],
        compiler_params=pltpu.CompilerParams(
            vmem_limit_bytes=60 * MIB, collective_id=0, has_side_effects=True
        ),
        cost_estimate=pl.CostEstimate(flops=20 * 10**9, bytes_accessed=40 * MIB, transcendentals=0),
        name="reduce_muon_spread",
    )(gs, wide, headg, na, nf, count, dlow, mi, mo, mu, md, mh)


def finish_kernel(
    wide_rate, head_rate, core_ref,
    mu, md, mb, q_ref, xb, mh, xh, ai, ao, fi, fo, vh, small, gain, bias, nm, dm, dr,
    mi_out, ni_out, mo_out, no_out, mu_out, nu_out, md_out, nd_out, mh_out, nh_out,
    mn_out, nn_out, counts_out, dm_out,
):
    i = pl.program_id(0)
    same = lax.broadcasted_iota(jnp.int32, (D, D), 0) == lax.broadcasted_iota(jnp.int32, (D, D), 1)
    eye = same.astype(f32).astype(bf16)
    mu_out[...] = mm_nt(eye, mu[0, 0])
    nu_out[...] = fi[...] - wide_rate * mm_nt(q_ref[0], mu[0, 0])
    md_out[...] = md[0, 0].astype(f32)
    nd_out[...] = fo[...] - wide_rate * mm(md[0, 0], q_ref[1])

    @pl.when(i < 3)
    def _():
        for j in range(2):
            mi_out[j] = mm_nt(eye, mb[0, j])
            ni_out[j] = ai[j] - muon_rate * mm_nt(eye, xb[0, j])

    @pl.when(i == 3)
    def _():
        for j in range(2):
            mo_out[j] = mb[0, j].astype(f32)
            no_out[j] = ao[j] - muon_rate * xb[0, j].astype(f32)

    dm_out[...] = jnp.where((core_ref[0] == 0) | (i >= 2), dm[...], dr[...].astype(f32))

    @pl.when(i == 0)
    def _():
        vocab = vh.shape[0]
        mh_out[...] = mh[0:vocab, :].astype(f32)
        nh_out[...] = vh[...] - head_rate * xh[0:vocab, :].astype(f32)
        for kind, old in enumerate((gain, bias)):
            first = 2 * kind
            total = jnp.concatenate([small[first : first + 2, 0:D], small[first + 8 : first + 10, 0:D]], axis=0)
            moment = 0.5 * nm[kind] + total
            mn_out[kind] = moment
            nn_out[kind] = old[...] - vector_rate * moment * lax.rsqrt(
                jnp.mean(moment * moment, axis=-1, keepdims=True) + 1e-06
            )
        counts_out[...] = small[16:17, 0:vocab].astype(jnp.int32)


def run_finish(core, ms, xs, mw, q, m_head, x_head, ai, ao, fi, fo, vh, small, gain, bias, nm, dmem, d_in):
    vocab = vh.shape[0]
    wide_rate = muon_rate * math.sqrt(2 * fi.shape[1] / D)
    head_rate = muon_rate * math.sqrt(vocab / D)

    def spec(shape, index):
        return pl.BlockSpec(shape, index)

    def fixed(shape):
        return pl.BlockSpec(shape, lambda i, c: (0,) * len(shape))

    up = spec((1, 1, 256, D), lambda i, c: (0, i // 2, i % 2, 0))
    down = spec((1, 1, 256, D), lambda i, c: (1, i // 2, i % 2, 0))
    bands = spec((1, 2, 256, D), lambda i, c: (i // 2, i % 2, 0, 0))
    inner = spec((2, D, 256), lambda i, c: (jnp.minimum(i, 2), 0, 0))
    outer = spec((2, 256, D), lambda i, c: (0, 0, 0))
    cols = spec((D, 256), lambda i, c: (0, i))
    rows = spec((256, D), lambda i, c: (i, 0))
    head = fixed((vocab, D))
    shapes = [
        (sds((6, D, 256), f32), inner), (sds((6, D, 256), f32), inner),
        (sds((2, 256, D), f32), outer), (sds((2, 256, D), f32), outer),
        (sds(fi.shape, f32), cols), (sds(fi.shape, f32), cols),
        (sds(fo.shape, f32), rows), (sds(fo.shape, f32), rows),
        (sds((vocab, D), f32), head), (sds((vocab, D), f32), head),
        (sds((2, 4, D), f32), fixed((2, 4, D))), (sds((2, 4, D), f32), fixed((2, 4, D))),
        (sds((1, vocab), jnp.int32), fixed((1, vocab))),
        (sds((1024, D), f32), rows),
    ]
    return pl.pallas_call(
        partial(finish_kernel, wide_rate, head_rate),
        grid_spec=pltpu.PrefetchScalarGridSpec(
            num_scalar_prefetch=1,
            grid=(4,),
            in_specs=[
                up, down, bands, fixed((2, D, D)), bands, fixed((VOC, D)), fixed((VOC, D)),
                inner, outer, cols, rows, head, fixed((SMALL, VOC)), fixed((4, D)), fixed((4, D)), fixed((2, 4, D)),
                spec((256, D), lambda i, c: (jnp.where(c[0] == 0, i, jnp.maximum(i - 2, 0)), 0)),
                spec((256, D), lambda i, c: (jnp.minimum(i, 1), 0)),
            ],
            out_specs=[s[1] for s in shapes],
        ),
        out_shape=[s[0] for s in shapes],
        compiler_params=pltpu.CompilerParams(vmem_limit_bytes=60 * MIB),
        cost_estimate=pl.CostEstimate(flops=10**7, bytes_accessed=40 * MIB, transcendentals=0),
        name="finish_weights",
    )(core, mw, mw, ms, q.reshape(2, D, D), xs, m_head, x_head, ai, ao, fi, fo, vh, small,
      gain, bias, nm, dmem, d_in)


def local(
    residual_in, memory, lengths, targets, attn_in, attn_out, ffn_in, ffn_out, vocab_head,
    norm_gain, norm_bias, attn_in_moment, attn_out_moment, ffn_in_moment, ffn_out_moment,
    head_moment, norm_moment,
):
    dims = chip_dims(lax.axis_size("dp"))
    core = lax.axis_index("mp")
    tokens = residual_in.shape[0] * lax.axis_size("mp") * lax.axis_size("dp")
    vocab = vocab_head.shape[1]
    inner = attn_in.reshape(6, D, 256)
    wa0, wa1, wo0, wo1, wi0, wi1, wf0, wf1, mem, wh, total = run_prepare(
        dims, lengths, inner, attn_out, ffn_in, ffn_out, vocab_head.T, memory
    )
    wa, wo, wi, wf = (wa0, wa1), (wo0, wo1), (wi0, wi1), (wf0, wf1)
    h1, qkv, p, o, x1, h2, cq, kv, pc, oc, x2 = run_forward(
        lengths, residual_in, mem, wa, wo, norm_gain, norm_bias
    )
    out, g2, gw, ghead, gnorm_ffn, counts = run_middle(
        lengths, total, x2, targets[:, None], wi, wf, wh, norm_gain, norm_bias, vocab, float(tokens)
    )
    dx, dmem, dlow, gs, gnorm_attn, wide, head_part = run_backward(
        dims, g2, residual_in, x1, h1, qkv, p, o, h2, cq, kv, pc, oc, mem, wa, wo, norm_gain, gw, ghead
    )
    ms, xs, mw, q, head_m, head_x, d_in, small = run_muon(
        dims, gs, wide, head_part, gnorm_attn, gnorm_ffn, counts, dlow,
        attn_in_moment.reshape(6, D, 256), attn_out_moment, ffn_in_moment, ffn_out_moment, head_moment.T,
    )
    (
        moment_in, new_in, moment_out, new_out, moment_up, new_up, moment_down, new_down,
        moment_head, new_head, moment_norms, new_norms, token_counts, memory_grad,
    ) = run_finish(
        core.reshape(1), ms, xs, mw, q, head_m, head_x, inner, attn_out, ffn_in, ffn_out,
        vocab_head.T, small, norm_gain, norm_bias, norm_moment, dmem, d_in,
    )
    return (
        out, dx, memory_grad, moment_in.reshape(attn_in.shape), new_in.reshape(attn_in.shape),
        moment_out, new_out, moment_up, new_up, moment_down, new_down, moment_head.T, new_head.T,
        moment_norms, new_norms,
        token_counts.reshape(vocab),
    )


def solution(mesh):
    rows = P(("dp", "mp"), None)
    placed = (
        rows, rows, P("dp"), P(("dp", "mp")),
        P(None, None, None, "mp"), P(None, "mp", None), P(None, "mp"), P("mp", None), P(), P(), P(),
        P(None, None, None, "mp"), P(None, "mp", None), P(None, "mp"), P("mp", None), P(), P(),
    )
    return jax.shard_map(
        local,
        mesh=mesh,
        in_specs=placed,
        out_specs=(
            rows, rows, rows,
            P(None, None, None, "mp"), P(None, None, None, "mp"),
            P(None, "mp", None), P(None, "mp", None),
            P(None, "mp"), P(None, "mp"), P("mp", None), P("mp", None),
            P(), P(), P(), P(), P(),
        ),
        check_vma=False,
    )
```

```python
from functools import partial
import math

import jax
import jax.numpy as jnp
from jax import lax
from jax.experimental import pallas as pl
from jax.experimental.pallas import tpu as pltpu
from jax.sharding import PartitionSpec as P

HEAD = 64
CAP_S = 64
CAP_M = 128
CAP_L = 256
MEM = 128
SETS = 4
NS_STEPS = 5
NS_A = 3.4445
NS_B = -4.775
NS_C = 2.0315
muon_rate = 0.5
vector_rate = 0.05

D = 512
BLK = 256
WIDE = 512
TALL = 1024
VOC = 640
HROWS = 320
HPART = 160
MIB = 1024 * 1024
bf16 = jnp.bfloat16
f32 = jnp.float32
VMEM = pltpu.VMEM


def mm(a, b):
    return jnp.dot(a, b, preferred_element_type=f32)


def mm_nt(a, b):
    return lax.dot_general(a, b, (((1,), (1,)), ((), ())), preferred_element_type=f32)


def mm_tn(a, b):
    return lax.dot_general(a, b, (((0,), (0,)), ((), ())), preferred_element_type=f32)


def norm_stats(value):
    average = jnp.mean(value, axis=-1, keepdims=True)
    centred = value - average
    variance = jnp.mean(centred * centred, axis=-1, keepdims=True)
    inverse = lax.rsqrt(variance + 1e-05)
    return centred * inverse, inverse


def norm_back(gradient, normed, inverse, gain):
    scaled = gradient * gain
    return inverse * (
        scaled
        - jnp.mean(scaled, axis=-1, keepdims=True)
        - normed * jnp.mean(scaled * normed, axis=-1, keepdims=True)
    )


def lane_masks(width):
    lanes = lax.broadcasted_iota(jnp.int32, (1, width), 1)
    return [(lanes // HEAD == h).astype(f32).astype(bf16) for h in range(width // HEAD)]


def spread(block, masks):
    return jnp.concatenate([block * m for m in masks], axis=0)


def pick(stacked, masks, rows):
    total = stacked[:rows] * masks[0].astype(f32)
    for h in range(1, len(masks)):
        total = total + stacked[h * rows : (h + 1) * rows] * masks[h].astype(f32)
    return total


def softmax_rows(scores):
    top = jnp.max(scores, axis=-1, keepdims=True)
    exps = jnp.exp(scores - top)
    return exps * (1.0 / jnp.sum(exps, axis=-1, keepdims=True))


def mem_slot(core, block, unit):
    on_first = jnp.where(block < 2, 4 * block + unit, 8 + 2 * (block - 2) + unit // 2)
    return jnp.where(core == 0, on_first, block)


def row_limits(core, block, lengths_ref):
    unit = lax.broadcasted_iota(jnp.int32, (BLK, 1), 0) // CAP_S
    low = jnp.zeros((BLK, 1), jnp.int32)
    length = jnp.zeros((BLK, 1), jnp.int32)
    for u in range(BLK // CAP_S):
        on_first = jnp.where(block < 2, u * CAP_S, u // 2 * CAP_M)
        slot = mem_slot(core, block, u) + jnp.where(core == 0, 0, 3 * SETS)
        low = jnp.where(unit == u, jnp.where(core == 0, on_first, 0), low)
        length = jnp.where(unit == u, lengths_ref[slot], length)
    return low, length


def rows_live(core, first, blocks, lengths_ref):
    pieces = []
    for j in range(blocks):
        low, length = row_limits(core, first + j, lengths_ref)
        place = lax.broadcasted_iota(jnp.int32, (BLK, 1), 0)
        pieces.append((place - low < length).astype(f32))
    return jnp.concatenate(pieces, axis=0)


def forward_kernel(
    lengths_ref, x_ref, mem_ref, wa0, wa1, wo0, wo1, gain_ref, bias_ref,
    h1_ref, qkv_ref, p_ref, o_ref, x1_ref, h2_ref, cq_ref, kv_ref, pc_ref, oc_ref, x2_ref,
):
    core = lax.axis_index("mp")
    step = pl.program_id(0)
    wa = (wa0, wa1)

    @pl.when(step == 0)
    def _():
        def fill(i, carry):
            rows = pl.ds(pl.multiple_of(i * WIDE, WIDE), WIDE)
            for half in range(2):
                for which in range(2):
                    kv_ref[rows, pl.ds(which * D + half * 256, 256)] = mm(
                        mem_ref[rows, :], wa[half][4 + which]
                    ).astype(bf16)
            return carry

        lax.fori_loop(0, jnp.where(core == 0, 3, 1), fill, 0)

    normed, _ = norm_stats(x_ref[...].astype(f32))
    h1_ref[...] = (normed * gain_ref[0:1, :] + bias_ref[0:1, :]).astype(bf16)
    for half in range(2):
        for which in range(3):
            qkv_ref[:, pl.ds(which * D + half * 256, 256)] = mm(h1_ref[...], wa[half][which]).astype(bf16)
    pair = lane_masks(128)
    for j in range(WIDE // BLK):
        rows = pl.ds(j * BLK, BLK)
        low, length = row_limits(core, step * (WIDE // BLK) + j, lengths_ref)
        keys = lax.broadcasted_iota(jnp.int32, (BLK, BLK), 1)
        queries = lax.broadcasted_iota(jnp.int32, (BLK, BLK), 0)
        allowed = (keys >= low) & (keys < low + length) & (keys <= queries)
        for i in range(4):
            q = qkv_ref[rows, pl.ds(i * 128, 128)] * jnp.bfloat16(0.125)
            k = qkv_ref[rows, pl.ds(D + i * 128, 128)]
            v = qkv_ref[rows, pl.ds(2 * D + i * 128, 128)]
            scores = mm_nt(spread(q, pair), k).reshape(2, BLK, BLK)
            scores = jnp.where(allowed[None], scores, -1000000000.0)
            probs = softmax_rows(scores).astype(bf16).reshape(2 * BLK, BLK)
            p_ref[j, i] = probs
            o_ref[rows, pl.ds(i * 128, 128)] = pick(mm(probs, v), pair, BLK).astype(bf16)
    x1 = x_ref[...].astype(f32) + mm(o_ref[:, :256], wo0[0]) + mm(o_ref[:, 256:], wo1[0])
    x1_ref[...] = x1
    normed, _ = norm_stats(x1)
    h2_ref[...] = (normed * gain_ref[1:2, :] + bias_ref[1:2, :]).astype(bf16)
    for half in range(2):
        cq_ref[:, pl.ds(half * 256, 256)] = mm(h2_ref[...], wa[half][3]).astype(bf16)
    quad = lane_masks(256)
    for u in range(WIDE // 64):
        rows = pl.ds(u * 64, 64)
        block = step * (WIDE // BLK) + u // 4
        slot = pl.ds(pl.multiple_of(mem_slot(core, block, u % 4) * MEM, MEM), MEM)
        for j in range(2):
            q = cq_ref[rows, pl.ds(j * 256, 256)] * jnp.bfloat16(0.125)
            k = kv_ref[slot, pl.ds(j * 256, 256)]
            v = kv_ref[slot, pl.ds(D + j * 256, 256)]
            probs = softmax_rows(mm_nt(spread(q, quad), k)).astype(bf16)
            pc_ref[u // 4, u % 4 * 2 + j] = probs
            oc_ref[rows, pl.ds(j * 256, 256)] = pick(mm(probs, v), quad, 64).astype(bf16)
    x2_ref[...] = x1_ref[...] + mm(oc_ref[:, :256], wo0[1]) + mm(oc_ref[:, 256:], wo1[1])


def gelu_parts(u):
    z = jnp.abs(u) * math.sqrt(0.5 / math.log(2.0))
    below = 1.0 + (0.3275911 * math.sqrt(math.log(2.0))) * z
    guess = pl.reciprocal(below, approx=True)
    t = guess * (2.0 - below * guess)
    gauss = jnp.exp2(-(z * z))
    tail = gauss * (
        t * (0.127414796 + t * (-0.142248368 + t * (0.7107068705 + t * (-0.7265760135 + t * 0.5307027145))))
    )
    cdf = jnp.where(u < 0, tail, 1.0 - tail)
    return u * cdf, cdf + u * (gauss * (1.0 / math.sqrt(2.0 * math.pi)))


def middle_kernel(
    vocab, tokens, lengths_ref, total_ref, x2_ref, targets_ref, wi0, wi1, wf0, wf1, wh_ref, gain_ref, bias_ref,
    out_ref, g2_ref, gw_ref, ghead_ref, gnorm_ref, count_ref,
    h3_all, a_all, dy_all, du_all, z_all, gl_all, slope,
):
    block = pl.program_id(0)
    rows = pl.ds(pl.multiple_of(block * TALL, TALL), TALL)
    wi = (wi0, wi1)
    wf = (wf0, wf1)
    x2 = x2_ref[...]
    normed2, inverse2 = norm_stats(x2)
    h3 = (normed2 * gain_ref[2:3, :] + bias_ref[2:3, :]).astype(bf16)
    h3_all[rows, :] = h3
    for half in range(2):
        for j in range(2):
            wide = pl.ds(half * 1024 + j * 512, 512)
            active, grad = gelu_parts(mm(h3, wi[half][:, j * 512 : (j + 1) * 512]))
            a_all[rows, wide] = active.astype(bf16)
            slope[:, wide] = grad
    x3 = x2_ref[...] + mm(a_all[rows, 0:1024], wf0[...]) + mm(a_all[rows, 1024:2048], wf1[...])
    out_ref[...] = x3.astype(bf16)
    normed3, inverse3 = norm_stats(x3)
    z = (normed3 * gain_ref[3:4, :] + bias_ref[3:4, :]).astype(bf16)
    z_all[rows, :] = z
    logits = mm_nt(z, wh_ref[...])
    columns = lax.broadcasted_iota(jnp.int32, (TALL, VOC), 1)
    logits = jnp.where(columns < vocab, logits, -1e30)
    probs = softmax_rows(logits)
    onehot = (columns == targets_ref[...]).astype(f32)
    live = rows_live(lax.axis_index("mp"), block * (TALL // BLK), TALL // BLK, lengths_ref)
    gl = (tokens / total_ref[0:1, 0:1] * live * (probs - onehot)).astype(bf16)
    gl_all[rows, :] = gl
    counts = jnp.sum(onehot * live, axis=0, keepdims=True)
    gz = mm(gl, wh_ref[...])
    gain3 = jnp.sum(gz * normed3, axis=0, keepdims=True)
    bias3 = jnp.sum(gz, axis=0, keepdims=True)
    g3 = norm_back(gz, normed3, inverse3, gain_ref[3:4, :])
    dy = g3.astype(bf16)
    dy_all[rows, :] = dy
    g2_ref[...] = g3
    for half in range(2):
        for j in range(2):
            wide = pl.ds(half * 1024 + j * 512, 512)
            back = mm_nt(dy, wf[half][j * 512 : (j + 1) * 512, :])
            du_all[rows, wide] = (slope[:, wide] * back).astype(bf16)
    dh = mm_nt(du_all[rows, 0:1024], wi0[...]) + mm_nt(du_all[rows, 1024:2048], wi1[...])
    normed2, inverse2 = norm_stats(x2_ref[...])
    gain2 = jnp.sum(dh * normed2, axis=0, keepdims=True)
    bias2 = jnp.sum(dh, axis=0, keepdims=True)
    g2_ref[...] = g2_ref[...] + norm_back(dh, normed2, inverse2, gain_ref[2:3, :])

    @pl.when(block == 0)
    def _():
        gnorm_ref[...] = jnp.zeros_like(gnorm_ref)
        count_ref[...] = jnp.zeros_like(count_ref)

    gnorm_ref[0:1, :] += gain2
    gnorm_ref[1:2, :] += gain3
    gnorm_ref[2:3, :] += bias2
    gnorm_ref[3:4, :] += bias3
    count_ref[0:1, :] += counts

    @pl.when(block == pl.num_programs(0) - 1)
    def _():
        for half in range(2):
            for j in range(2):
                col = pl.ds(half * 1024 + j * 512, 512)
                gw_ref[half, 0, j] = mm_tn(du_all[:, col], h3_all[...]).astype(bf16)
                gw_ref[half, 1, j] = mm_tn(a_all[:, col], dy_all[...]).astype(bf16)
        ghead_ref[...] = mm_tn(gl_all[...], z_all[...]).astype(bf16)


def attend_back(queries, keys, values, probs, grads, masks, rows):
    q = spread(queries, masks)
    do = spread(grads, masks)
    dprobs = mm_nt(do, values)
    p = probs.astype(f32)
    weighted = p * dprobs
    ds = (weighted - p * jnp.sum(weighted, axis=-1, keepdims=True)).astype(bf16)
    dv = mm_tn(probs, do)
    dq = pick(mm(ds, keys), masks, rows) * 0.125
    dk = mm_tn(ds, q) * 0.125
    return dq, dk, dv


def backward_kernel(
    dims, g2_ref, x_ref, x1_ref, h1_ref, qkv_ref, p_ref, o_ref, h2_ref, cq_ref, kv_ref, pc_ref, oc_ref,
    mem_ref, wa0, wa1, wo0, wo1, gain_ref, gw_ref, ghead_ref,
    dx_ref, dmem_ref, dlow_ref, gs_ref, gnorm_ref, wide_out, head_out,
    dyc_all, dcq_all, dys_all, dqkv_all, dkv_all, dkv_low,
    early_acc, early_core, early_first, early_second, head_acc, head_core, head_first, head_second,
    gs_away, gs_in, send_sems, recv_sems, local_sems,
):
    core = lax.axis_index("mp")
    block = pl.program_id(0)
    early = EarlySum(
        Net(dims, send_sems, recv_sems), gw_ref, ghead_ref, wide_out, head_out,
        (
            early_acc, early_core, early_first, early_second, head_acc, head_core, head_first, head_second,
            local_sems,
        ),
    )
    band_sem = early.net.recv_sem(4)
    pl.when(block == 0)(early.start)
    rows = pl.ds(pl.multiple_of(block * BLK, BLK), BLK)
    wa = (wa0, wa1)
    wo = (wo0, wo1)

    @pl.when(block == 0)
    def _():
        gnorm_ref[...] = jnp.zeros_like(gnorm_ref)
        dkv_all[...] = jnp.zeros_like(dkv_all)

    g2 = g2_ref[...]
    dyc = g2.astype(bf16)
    dyc_all[rows, :] = dyc
    quad = lane_masks(256)
    for j in range(2):
        lanes = pl.ds(j * 256, 256)
        do = mm_nt(dyc, wo[j][1]).astype(bf16)
        for u in range(4):
            base = pl.multiple_of(block * BLK + u * 64, 64)
            slot = pl.ds(pl.multiple_of(mem_slot(core, block, u) * MEM, MEM), MEM)
            dq, dk, dv = attend_back(
                cq_ref[u * 64 : (u + 1) * 64, lanes],
                kv_ref[slot, lanes],
                kv_ref[slot, pl.ds(D + j * 256, 256)],
                pc_ref[0, u * 2 + j],
                do[u * 64 : (u + 1) * 64],
                quad,
                64,
            )
            dcq_all[pl.ds(base, 64), lanes] = dq.astype(bf16)
            dkv_all[slot, lanes] += dk
            dkv_all[slot, pl.ds(D + j * 256, 256)] += dv
    dcq = dcq_all[rows, :]
    dh = mm_nt(dcq[:, :256], wa0[3]) + mm_nt(dcq[:, 256:], wa1[3])
    normed, inverse = norm_stats(x1_ref[...])
    gnorm_ref[1:2, :] += jnp.sum(dh * normed, axis=0, keepdims=True)
    gnorm_ref[3:4, :] += jnp.sum(dh, axis=0, keepdims=True)
    g1 = g2 + norm_back(dh, normed, inverse, gain_ref[1:2, :])
    pl.when(block == 0)(early.one)
    dys = g1.astype(bf16)
    dys_all[rows, :] = dys
    pair = lane_masks(128)
    for half in range(2):
        do_half = mm_nt(dys, wo[half][0]).astype(bf16)
        for i in range(2):
            first = half * 256 + i * 128
            dq, dk, dv = attend_back(
                qkv_ref[:, pl.ds(first, 128)],
                qkv_ref[:, pl.ds(D + first, 128)],
                qkv_ref[:, pl.ds(2 * D + first, 128)],
                p_ref[0, half * 2 + i],
                do_half[:, i * 128 : (i + 1) * 128],
                pair,
                BLK,
            )
            dqkv_all[rows, pl.ds(first, 128)] = dq.astype(bf16)
            dqkv_all[rows, pl.ds(D + first, 128)] = dk.astype(bf16)
            dqkv_all[rows, pl.ds(2 * D + first, 128)] = dv.astype(bf16)
    dqkv = dqkv_all[rows, :]
    dh = jnp.zeros((BLK, D), f32)
    for half in range(2):
        for which in range(3):
            first = which * D + half * 256
            dh = dh + mm_nt(dqkv[:, first : first + 256], wa[half][which])
    normed, inverse = norm_stats(x_ref[...].astype(f32))
    gnorm_ref[0:1, :] += jnp.sum(dh * normed, axis=0, keepdims=True)
    gnorm_ref[2:3, :] += jnp.sum(dh, axis=0, keepdims=True)
    dx_ref[...] = g1 + norm_back(dh, normed, inverse, gain_ref[0:1, :])
    pl.when(block == 2)(early.two)

    @pl.when(block == pl.num_programs(0) - 1)
    def _():
        def memory_rows(i, carry):
            part = pl.ds(pl.multiple_of(i * BLK, BLK), BLK)
            low = dkv_all[part, :].astype(bf16)
            dkv_low[part, :] = low
            total = jnp.zeros((BLK, D), f32)
            for half in range(2):
                for which in range(2):
                    first = which * D + half * 256
                    total = total + mm_nt(low[:, first : first + 256], wa[half][4 + which])
            dmem_ref[part, :] = total
            return carry

        lax.fori_loop(0, jnp.where(core == 0, 6, 2), memory_rows, 0)

        @pl.when(core != 0)
        def _():
            dkv_low[512:, :] = jnp.zeros((1024, 2 * D), bf16)
            dmem_ref[512:, :] = jnp.zeros((1024, D), f32)

        dlow_ref[...] = dmem_ref[1024:, :].astype(bf16)

        def bands(half, put):
            col = pl.ds(half * 256, 256)
            for which in range(3):
                put(0, which, mm_tn(dqkv_all[:, pl.ds(which * D + half * 256, 256)], h1_ref[...]))
            put(0, 3, mm_tn(dcq_all[:, col], h2_ref[...]))
            for which in range(2):
                put(1, which, mm_tn(dkv_low[:, pl.ds(which * D + half * 256, 256)], mem_ref[...]))
            put(1, 2, mm_tn(o_ref[:, col], dys_all[...]))
            put(1, 3, mm_tn(oc_ref[:, col], dyc_all[...]))

        def put_away(f, j, value):
            gs_away[f, j] = value.astype(bf16)
            if j % 2 == 1:
                pair = pl.ds(j - 1, 2)
                early.net.send(
                    True, gs_away.at[f, pair], gs_in.at[f, pair], band_sem + 2 * f + j // 2, early.net.sibling
                )

        def put_here(f, j, value):
            gs_ref[f, j] = value.astype(bf16)

        early.keep_sends()
        bands(1, put_away)
        bands(0, put_here)
        early.three()
        for f in range(2):
            for j in range(4):
                if j % 2 == 0:
                    early.net.landed(True, gs_in.at[f, pl.ds(j, 2)], band_sem + 2 * f + j // 2)
                add_into(gs_ref.at[f, j], [gs_in.at[f, j]], 128)
        early.net.all_sent()
        early.end()


def whole(shape):
    return pl.BlockSpec(shape, lambda i: (0,) * len(shape), pipeline_mode=pl.Buffered(1))


def by_rows(width):
    return pl.BlockSpec((BLK, width), lambda i: (i, 0))


def wide_rows(width):
    return pl.BlockSpec((WIDE, width), lambda i: (i, 0))


def tall_rows(width):
    return pl.BlockSpec((TALL, width), lambda i: (i, 0))


def sds(shape, dtype):
    return jax.ShapeDtypeStruct(shape, dtype)


def run_forward(lengths, x, mem, wa, wo, gain, bias):
    rows = x.shape[0]
    steps = rows // WIDE
    outs = [
        (sds((rows, D), bf16), wide_rows(D)),
        (sds((rows, 3 * D), bf16), wide_rows(3 * D)),
        (sds((rows // BLK, 4, 512, 256), bf16), pl.BlockSpec((2, 4, 512, 256), lambda i: (i, 0, 0, 0))),
        (sds((rows, D), bf16), wide_rows(D)),
        (sds((rows, D), f32), wide_rows(D)),
        (sds((rows, D), bf16), wide_rows(D)),
        (sds((rows, D), bf16), wide_rows(D)),
        (sds((1536, 2 * D), bf16), whole((1536, 2 * D))),
        (sds((rows // BLK, 8, 256, 128), bf16), pl.BlockSpec((2, 8, 256, 128), lambda i: (i, 0, 0, 0))),
        (sds((rows, D), bf16), wide_rows(D)),
        (sds((rows, D), f32), wide_rows(D)),
    ]
    return pl.pallas_call(
        forward_kernel,
        grid=(steps,),
        in_specs=[
            pl.BlockSpec(memory_space=pltpu.SMEM), wide_rows(D), whole((1536, D)),
            whole((6, D, 256)), whole((6, D, 256)), whole((2, 256, D)), whole((2, 256, D)),
            whole((4, D)), whole((4, D)),
        ],
        out_specs=[o[1] for o in outs],
        out_shape=[o[0] for o in outs],
        compiler_params=pltpu.CompilerParams(vmem_limit_bytes=60 * MIB),
        cost_estimate=pl.CostEstimate(flops=9 * 10**9, bytes_accessed=22 * MIB, transcendentals=3 * 10**6),
        name="layer_forward",
    )(lengths, x, mem, wa[0], wa[1], wo[0], wo[1], gain, bias)


def run_middle(lengths, total, x2, targets, wi, wf, wh, gain, bias, vocab, tokens):
    rows = x2.shape[0]
    steps = rows // TALL
    outs = [
        (sds((rows, D), bf16), tall_rows(D)),
        (sds((rows, D), f32), tall_rows(D)),
        (sds((2, 2, 2, 512, D), bf16), whole((2, 2, 2, 512, D))),
        (sds((VOC, D), bf16), whole((VOC, D))),
        (sds((8, D), f32), whole((8, D))),
        (sds((8, VOC), f32), whole((8, VOC))),
    ]
    return pl.pallas_call(
        partial(middle_kernel, vocab, tokens),
        grid=(steps,),
        in_specs=[
            pl.BlockSpec(memory_space=pltpu.SMEM), whole((8, 128)), tall_rows(D), tall_rows(1),
            whole((D, 1024)), whole((D, 1024)), whole((1024, D)), whole((1024, D)), whole((VOC, D)),
            whole((4, D)), whole((4, D)),
        ],
        out_specs=[o[1] for o in outs],
        out_shape=[o[0] for o in outs],
        scratch_shapes=[
            VMEM((rows, D), bf16), VMEM((rows, 2048), bf16), VMEM((rows, D), bf16),
            VMEM((rows, 2048), bf16), VMEM((rows, D), bf16), VMEM((rows, VOC), bf16),
            VMEM((TALL, 2048), f32),
        ],
        compiler_params=pltpu.CompilerParams(vmem_limit_bytes=60 * MIB),
        cost_estimate=pl.CostEstimate(flops=15 * 10**9, bytes_accessed=18 * MIB, transcendentals=5 * 10**6),
        name="ffn_head",
    )(lengths, total, x2, targets, wi[0], wi[1], wf[0], wf[1], wh, gain, bias)


def run_backward(dims, g2, x, x1, h1, qkv, p, o, h2, cq, kv, pc, oc, mem, wa, wo, gain, gw, ghead):
    rows = x.shape[0]
    steps = rows // BLK
    outs = [
        (sds((rows, D), f32), by_rows(D)),
        (sds((1536, D), f32), whole((1536, D))),
        (sds((512, D), bf16), whole((512, D))),
        (sds((2, 4, 256, D), bf16), whole((2, 4, 256, D))),
        (sds((8, D), f32), whole((8, D))),
        (sds((2, 512, D), bf16), pl.BlockSpec(memory_space=pl.ANY)),
        (sds((2, HPART, D), bf16), pl.BlockSpec(memory_space=pl.ANY)),
    ]
    nz, ny, nx = dims
    slots = max(nx, ny) - 1
    return pl.pallas_call(
        partial(backward_kernel, dims),
        grid=(steps,),
        in_specs=[
            by_rows(D), by_rows(D), by_rows(D), whole((rows, D)), by_rows(3 * D),
            pl.BlockSpec((1, 4, 512, 256), lambda i: (i, 0, 0, 0)), whole((rows, D)), whole((rows, D)),
            by_rows(D), whole((1536, 2 * D)), pl.BlockSpec((1, 8, 256, 128), lambda i: (i, 0, 0, 0)),
            whole((rows, D)), whole((1536, D)),
            whole((6, D, 256)), whole((6, D, 256)), whole((2, 256, D)), whole((2, 256, D)), whole((4, D)),
            pl.BlockSpec(memory_space=pl.ANY), pl.BlockSpec(memory_space=pl.ANY),
        ],
        out_specs=[o_[1] for o_ in outs],
        out_shape=[o_[0] for o_ in outs],
        scratch_shapes=[
            VMEM((rows, D), bf16), VMEM((rows, D), bf16), VMEM((rows, D), bf16),
            VMEM((rows, 3 * D), bf16), VMEM((1536, 2 * D), f32), VMEM((1536, 2 * D), bf16),
            VMEM((2, 2, 512, D), bf16), VMEM((2, 2, 512, D), bf16),
            VMEM((2, slots, 512, D), bf16), VMEM((2, slots, 512, D), bf16),
            VMEM((2, HPART, D), bf16), VMEM((2, HPART, D), bf16),
            VMEM((2, slots, HPART, D), bf16), VMEM((2, slots, HPART, D), bf16),
            VMEM((2, 4, 256, D), bf16), VMEM((2, 4, 256, D), bf16),
            pltpu.SemaphoreType.DMA((48,)), pltpu.SemaphoreType.DMA((40,)), pltpu.SemaphoreType.DMA((6,)),
        ],
        compiler_params=pltpu.CompilerParams(
            vmem_limit_bytes=62 * MIB, collective_id=2, has_side_effects=True,
        ),
        cost_estimate=pl.CostEstimate(flops=18 * 10**9, bytes_accessed=30 * MIB, transcendentals=0),
        name="attention_backward",
    )(g2, x, x1, h1, qkv, p, o, h2, cq, kv, pc, oc, mem, wa[0], wa[1], wo[0], wo[1], gain, gw, ghead)


MESH = pl.DeviceIdType.MESH
OWN = 2


def chip_dims(count):
    nz = 4
    side = math.isqrt(count // nz)
    return nz, count // nz // side, side


class Net:
    def __init__(self, dims, send_sems, recv_sems):
        self.nz, self.ny, self.nx = dims
        self.chip = lax.axis_index("dp")
        self.core = lax.axis_index("mp")
        self.x = lax.rem(self.chip, self.nx)
        self.y = lax.rem(lax.div(self.chip, self.nx), self.ny)
        self.z = lax.div(self.chip, self.nx * self.ny)
        self.place = {"x": self.x, "y": self.y, "z": self.z}
        self.count = {"x": self.nx, "y": self.ny, "z": self.nz}
        self.sibling = {"dp": self.chip, "mp": 1 - self.core}
        self.send_sems, self.recv_sems = send_sems, recv_sems
        self.sent, self.received = 0, 0
        self.unsent = []
        self.ending, self.keeping = False, True

    def at(self, **moved):
        p = {**self.place, **moved}
        return {"dp": (p["z"] * self.ny + p["y"]) * self.nx + p["x"], "mp": self.core}

    def further(self, axis, d):
        return lax.rem(self.place[axis] + d, self.count[axis])

    def on(self, condition, body):
        if condition is True:
            body()
        else:
            pl.when(condition)(body)

    def both(self, *conditions):
        result = True
        for c in conditions:
            if c is not True:
                result = c if result is True else jnp.logical_and(result, c)
        return result

    def inside(self, axis):
        return True if self.count[axis] == OWN else self.place[axis] < OWN

    def goes_inside(self, axis, d):
        return True if self.count[axis] == OWN else self.further(axis, d) < OWN

    def clipped(self, axis):
        return self.place[axis] if self.count[axis] == OWN else jnp.minimum(self.place[axis], OWN - 1)

    def send_sem(self, amount):
        self.sent += amount
        return self.sent - amount

    def recv_sem(self, amount):
        self.received += amount
        return self.received - amount

    def remote(self, src, dst, send_sem, recv_sem, device):
        return pltpu.make_async_remote_copy(
            src_ref=src, dst_ref=dst, send_sem=self.send_sems.at[send_sem],
            recv_sem=self.recv_sems.at[recv_sem], device_id=device, device_id_type=MESH,
        )

    def send(self, condition, src, dst, recv_sem, device):
        sem = self.send_sem(1)
        copy = lambda: self.remote(src, dst, sem, recv_sem, device)
        if self.ending:
            self.on(condition, lambda: copy().wait_send())
            return
        self.on(condition, lambda: copy().start())
        if self.keeping:
            self.unsent.append((condition, copy))

    def landed(self, condition, dst, recv_sem):
        self.on(condition, lambda: self.remote(dst, dst, 0, recv_sem, self.sibling).wait_recv())

    def spread(self, axis, condition, ref, recv_sem):
        for d in range(1, self.count[axis]):
            self.send(condition, ref, ref, recv_sem, self.at(**{axis: self.further(axis, d)}))

    def all_sent(self):
        for condition, copy in self.unsent:
            self.on(condition, lambda copy=copy: copy().wait_send())
        self.unsent = []
        assert self.sent <= self.send_sems.shape[0] and self.received <= self.recv_sems.shape[0]

    def barrier(self):
        partners = [self.sibling]
        for axis in ("x", "y", "z"):
            for d in range(1, self.count[axis]):
                partners.append(self.at(**{axis: self.further(axis, d)}))
        barrier = pltpu.get_barrier_semaphore()
        for partner in partners:
            pl.semaphore_signal(barrier, inc=1, device_id=partner, device_id_type=MESH)
        pl.semaphore_wait(barrier, len(partners))


def add_into(dst, sources, step):
    rows = dst.shape[0]

    def body(i, carry):
        part = pl.ds(pl.multiple_of(i * step, step), step)
        total = dst[part, :].astype(f32)
        for s in sources:
            total = total + s[part, :].astype(f32)
        dst[part, :] = total.astype(bf16)
        return carry

    lax.fori_loop(0, rows // step, body, 0)


HEAD_X, HEAD_Y, HEAD_Z = 1, 0, 0


class EarlySum:
    def __init__(self, net, gw, ghead, wide_out, head_out, scratch):
        (
            self.acc, self.core_in, self.first_in, self.second_in,
            self.head_acc, self.head_core, self.head_first, self.head_second, self.local,
        ) = scratch
        self.net, self.gw, self.ghead, self.wide_out, self.head_out = net, gw, ghead, wide_out, head_out
        n = net
        self.core_sem = n.recv_sem(6)
        self.first_sem = [n.recv_sem(n.nx - 1), n.recv_sem(n.ny - 1)]
        self.second_sem = [n.recv_sem(n.ny - 1), n.recv_sem(n.nx - 1)]
        self.head_first_sem = [n.recv_sem(n.nx - 1), n.recv_sem(n.ny - 1)]
        self.head_second_sem = [n.recv_sem(n.ny - 1), n.recv_sem(n.nx - 1)]
        self.sums = ((0, "x", "y"), (1, "y", "x"))
        self.goal = {"x": HEAD_X, "y": HEAD_Y}

    def head_rows(self, core, f):
        return self.ghead.at[pl.ds(pl.multiple_of(core * HROWS + f * HPART, HPART), HPART)]

    def own_copies(self):
        core = self.net.core
        return [
            pltpu.make_async_copy(self.gw.at[0, m, f], self.acc.at[m, f], self.local.at[2 * m + f])
            for m in range(2)
            for f in range(2)
        ] + [
            pltpu.make_async_copy(self.head_rows(core, f), self.head_acc.at[f], self.local.at[4 + f]) for f in range(2)
        ]

    def start(self):
        self.net.keeping = False
        self.net.barrier()
        for copy in self.own_copies():
            copy.start()
        self.core_sends()

    def core_sends(self):
        n = self.net
        for m in range(2):
            for f in range(2):
                n.send(True, self.gw.at[1, m, f], self.core_in.at[m, f], self.core_sem + 2 * m + f, n.sibling)
        for f in range(2):
            n.send(True, self.head_rows(1 - n.core, f), self.head_core.at[f], self.core_sem + 4 + f, n.sibling)

    def one(self):
        n = self.net
        for copy in self.own_copies():
            copy.wait()
        for m in range(2):
            for f in range(2):
                n.landed(True, self.core_in.at[m, f], self.core_sem + 2 * m + f)
                add_into(self.acc.at[m, f], [self.core_in.at[m, f]], 128)
        for f in range(2):
            n.landed(True, self.head_core.at[f], self.core_sem + 4 + f)
            add_into(self.head_acc.at[f], [self.head_core.at[f]], HPART)
        self.first_sends()

    def first_sends(self):
        n = self.net
        for f, axis, other in self.sums:
            for d in range(1, n.count[axis]):
                target = jnp.minimum(n.further(axis, d), OWN - 1)
                n.send(
                    n.goes_inside(axis, d), self.acc.at[target, f], self.first_in.at[f, d - 1],
                    self.first_sem[f] + d - 1, n.at(**{axis: n.further(axis, d)}),
                )
            goal = self.goal[axis]
            for d in range(1, n.count[axis]):
                n.send(
                    n.place[axis] == (goal + d) % n.count[axis], self.head_acc.at[f],
                    self.head_first.at[f, d - 1], self.head_first_sem[f] + d - 1, n.at(**{axis: goal}),
                )

    def two(self):
        n = self.net
        for f, axis, other in self.sums:
            matrix = n.clipped(axis)

            def take(f=f, axis=axis, matrix=matrix):
                slots = [self.first_in.at[f, d - 1] for d in range(1, n.count[axis])]
                for d in range(1, n.count[axis]):
                    n.landed(True, slots[d - 1], self.first_sem[f] + d - 1)
                add_into(self.acc.at[matrix, f], slots, 128)

            n.on(n.inside(axis), take)

            def take_head(f=f, axis=axis):
                slots = [self.head_first.at[f, d - 1] for d in range(1, n.count[axis])]
                for d in range(1, n.count[axis]):
                    n.landed(True, slots[d - 1], self.head_first_sem[f] + d - 1)
                add_into(self.head_acc.at[f], slots, HPART)

            n.on(n.place[axis] == self.goal[axis], take_head)
        self.second_sends()

    def second_sends(self):
        n = self.net
        for f, axis, other in self.sums:
            matrix = n.clipped(axis)
            distance = lax.rem(n.place[other] - matrix + n.count[other], n.count[other])
            slot = jnp.maximum(distance, 1) - 1
            n.send(
                n.both(n.inside(axis), distance != 0), self.acc.at[matrix, f], self.second_in.at[f, slot],
                self.second_sem[f] + slot, n.at(**{other: matrix}),
            )
            goal = self.goal[other]
            for d in range(1, n.count[other]):
                n.send(
                    n.both(n.place[axis] == self.goal[axis], n.place[other] == (goal + d) % n.count[other]),
                    self.head_acc.at[f], self.head_second.at[f, d - 1], self.head_second_sem[f] + d - 1,
                    n.at(**{other: goal}),
                )

    def columns(self):
        n = self.net
        wide = n.both(n.inside("x"), n.inside("y"), n.x == n.y)
        return wide, n.both(n.x == HEAD_X, n.y == HEAD_Y)

    def out_copies(self):
        n = self.net
        wide, head = self.columns()
        copies = [
            (wide, pltpu.make_async_copy(self.acc.at[n.clipped(axis), f], self.wide_out.at[f], self.local.at[f]))
            for f, axis, other in self.sums
        ]
        return copies + [(head, pltpu.make_async_copy(self.head_acc, self.head_out, self.local.at[4]))]

    def three(self):
        n = self.net
        wide, head = self.columns()
        for f, axis, other in self.sums:

            def take(f=f, axis=axis, other=other):
                slots = [self.second_in.at[f, d - 1] for d in range(1, n.count[other])]
                for d in range(1, n.count[other]):
                    n.landed(True, slots[d - 1], self.second_sem[f] + d - 1)
                add_into(self.acc.at[n.clipped(axis), f], slots, 128)

            n.on(wide, take)

            def take_head(f=f, other=other):
                slots = [self.head_second.at[f, d - 1] for d in range(1, n.count[other])]
                for d in range(1, n.count[other]):
                    n.landed(True, slots[d - 1], self.head_second_sem[f] + d - 1)
                add_into(self.head_acc.at[f], slots, HPART)

            n.on(head, take_head)
        for condition, copy in self.out_copies():
            n.on(condition, copy.start)

    def keep_sends(self):
        self.net.keeping = True

    def end(self):
        for condition, copy in self.out_copies():
            self.net.on(condition, copy.wait)
        self.net.sent, self.net.ending = 0, True
        self.core_sends()
        self.first_sends()
        self.second_sends()


def prepare_kernel(
    dims, lengths_ref, ai_ref, ao_ref, fi_ref, fo_ref, vh_ref, mem_ref,
    wa0, wa1, wo0, wo1, wi0, wi1, wf0, wf1, mem_out, wh_ref, total_ref,
    ai_in, ao_in, fi_in, fo_in, vh_in, mem_in, ai_low, ao_low, fi_low, fo_low, totals,
    load_sems, keep_sems, send_sems, recv_sems,
):
    nz, ny, nx = dims
    chip = lax.axis_index("dp")
    core = lax.axis_index("mp")
    place = {"x": lax.rem(chip, nx), "y": lax.rem(lax.div(chip, nx), ny), "z": lax.div(chip, nx * ny)}
    count = {"x": nx, "y": ny, "z": nz}
    sibling = {"dp": chip, "mp": 1 - core}

    def at(axis, target):
        p = {**place, axis: target}
        return {"dp": (p["z"] * ny + p["y"]) * nx + p["x"], "mp": core}

    arrays = (
        (ai_ref, ai_in, ai_low, wa0, wa1),
        (ao_ref, ao_in, ao_low, wo0, wo1),
        (fi_ref, fi_in, fi_low, wi0, wi1),
        (fo_ref, fo_in, fo_low, wf0, wf1),
    )
    loads = [
        pltpu.make_async_copy(src, dst, load_sems.at[i])
        for i, (src, dst) in enumerate([a[:2] for a in arrays] + [(vh_ref, vh_in), (mem_ref, mem_in)])
    ]
    for load in loads:
        load.start()
    partners = [sibling]
    for axis in ("x", "y", "z"):
        for d in range(1, count[axis]):
            partners.append(at(axis, lax.rem(place[axis] + d, count[axis])))
    barrier = pltpu.get_barrier_semaphore()
    for partner in partners:
        pl.semaphore_signal(barrier, inc=1, device_id=partner, device_id_type=MESH)
    pl.semaphore_wait(barrier, len(partners))

    def remote(src, dst, send_sem, recv_sem, device):
        return pltpu.make_async_remote_copy(
            src_ref=src, dst_ref=dst, send_sem=send_sems.at[send_sem], recv_sem=recv_sems.at[recv_sem],
            device_id=device, device_id_type=MESH,
        )

    tokens = lengths_ref[0]
    for s in range(1, lengths_ref.shape[0]):
        tokens = tokens + lengths_ref[s]

    base = {}
    used = 8
    for axis in ("x", "y", "z"):
        base[axis] = used
        used += count[axis]
    pending = []

    def spread_total(level, axis, value):
        totals[level, place[axis]] = value
        for d in range(1, count[axis]):
            copy = remote(
                totals.at[level, place[axis]], totals.at[level, place[axis]], base[axis] + d,
                base[axis] + place[axis], at(axis, lax.rem(place[axis] + d, count[axis])),
            )
            copy.start()
            pending.append(copy)

    def add_total(level, axis):
        for d in range(1, count[axis]):
            source = lax.rem(place[axis] + d, count[axis])
            remote(
                totals.at[level, source], totals.at[level, source], base[axis] + d,
                base[axis] + source, sibling,
            ).wait_recv()
        value = totals[level, 0]
        for s in range(1, count[axis]):
            value = value + totals[level, s]
        return value

    def memory_moves():
        return (
            (core == 0, pltpu.make_async_copy(mem_in, mem_out.at[pl.ds(0, 1024)], keep_sems.at[4])),
            (
                core == 1,
                pltpu.make_async_copy(mem_in.at[pl.ds(512, 512)], mem_out.at[pl.ds(0, 512)], keep_sems.at[4]),
            ),
            (core == 1, pltpu.make_async_copy(mem_in, mem_out.at[pl.ds(512, 1024)], keep_sems.at[5])),
        )

    def memory_send():
        return remote(mem_in.at[pl.ds(0, 512)], mem_out.at[pl.ds(1024, 512)], 4, 4, sibling)

    spread_total(0, "x", jnp.full((8, 128), tokens.astype(f32)))
    loads[5].wait()
    for condition, copy in memory_moves():
        pl.when(condition)(copy.start)
    pl.when(core == 1)(lambda: memory_send().start())
    sends = []
    keeps = []
    for i, (src, staged, low, mine, others) in enumerate(arrays):
        loads[i].wait()
        low[...] = staged[...].astype(bf16)
        copy = remote(low, others, i, i, sibling)
        copy.start()
        sends.append(copy)
        keep = pltpu.make_async_copy(low, mine, keep_sems.at[i])
        keep.start()
        keeps.append(keep)
        if i < 2:
            spread_total(i + 1, ("y", "z")[i], add_total(i, ("x", "y")[i]))
    loads[4].wait()
    vocab = vh_in.shape[0]
    wh_ref[512:, :] = jnp.zeros((VOC - 512, D), bf16)
    wh_ref[0:vocab, :] = vh_in[...].astype(bf16)
    total_ref[...] = add_total(2, "z")
    for condition, copy in memory_moves():
        pl.when(condition)(copy.wait)
    pl.when(core == 1)(lambda: memory_send().wait_send())
    pl.when(core == 0)(lambda: memory_send().wait_recv())
    for copy in keeps:
        copy.wait()
    for copy in sends:
        copy.wait()
    for copy in pending:
        copy.wait_send()


def run_prepare(dims, lengths, ai, ao, fi, fo, vh, mem):
    hbm = pl.BlockSpec(memory_space=pl.ANY)
    vmem = pl.BlockSpec(memory_space=VMEM)
    weights = [sds(w.shape, bf16) for w in (ai, ao, fi, fo) for _ in range(2)]
    nz, ny, nx = dims
    return pl.pallas_call(
        partial(prepare_kernel, dims),
        in_specs=[pl.BlockSpec(memory_space=pltpu.SMEM)] + [hbm] * 6,
        out_specs=[hbm] * 9 + [vmem, vmem],
        out_shape=weights + [sds((1536, D), bf16), sds((VOC, D), bf16), sds((8, 128), f32)],
        scratch_shapes=[VMEM(w.shape, f32) for w in (ai, ao, fi, fo, vh)]
        + [VMEM(mem.shape, bf16)]
        + [VMEM(w.shape, bf16) for w in (ai, ao, fi, fo)]
        + [
            VMEM((3, max(dims), 8, 128), f32),
            pltpu.SemaphoreType.DMA((6,)), pltpu.SemaphoreType.DMA((6,)),
            pltpu.SemaphoreType.DMA((8 + nx + ny + nz,)), pltpu.SemaphoreType.DMA((8 + nx + ny + nz,)),
        ],
        compiler_params=pltpu.CompilerParams(
            vmem_limit_bytes=60 * MIB, collective_id=1, has_side_effects=True
        ),
        cost_estimate=pl.CostEstimate(flops=10**6, bytes_accessed=24 * MIB, transcendentals=0),
        name="prepare_weights",
    )(lengths, ai, ao, fi, fo, vh, mem)


PIECE = 256
SMALL = 24


def split_two(value):
    high = value.astype(bf16)
    return high, (value - high.astype(f32)).astype(bf16)


def wide_roles(n):
    left = n.x == 0
    return (
        jnp.where(left, 1, 2), jnp.where(left, 0, 3), jnp.where(left, 2, 1), jnp.where(left, 3, 0)
    )


def square_owners(n):
    beside = n.x == n.y
    return (
        jnp.where(beside, jnp.where(n.x == 0, 2, 1), 1),
        jnp.where(beside, jnp.where(n.x == 0, 0, 3), 2),
    )


class SquareBack:
    def __init__(self, net, low, land):
        self.net, self.low, self.land = net, low, land
        self.axes = (("x", "y"), ("y", "x"))
        self.z_sem = [net.recv_sem(2) for _ in range(2)]
        self.one_sem = [net.recv_sem(2 * OWN) for _ in range(2)]
        self.two_sem = [net.recv_sem(2 * OWN) for _ in range(2)]
        self.valid = net.both(net.inside("x"), net.inside("y"))
        self.owners = square_owners(net)

    def chunk(self, f):
        first, second = self.axes[f]
        return self.net.clipped(first) * 2 + self.net.clipped(second)

    def rows(self, p):
        return pl.ds(p * 128, 128)

    def start(self, p):
        n = self.net
        for f in range(2):
            owner = n.both(self.valid, n.z == self.owners[f])

            def keep(f=f):
                self.land[f, self.chunk(f), self.rows(p), :] = self.low[self.rows(p), :]

            n.on(owner, keep)
            n.spread("z", owner, self.land.at[f, self.chunk(f), self.rows(p)], self.z_sem[f] + p)

    def one(self, p):
        n = self.net
        for f in range(2):
            mine = self.land.at[f, self.chunk(f), self.rows(p)]
            n.landed(n.both(self.valid, n.z != self.owners[f]), mine, self.z_sem[f] + p)
            second = self.axes[f][1]
            n.spread(second, self.valid, mine, self.one_sem[f] + p * OWN + n.clipped(second))

    def two(self, p):
        n = self.net
        for f in range(2):
            first, second = self.axes[f]
            for s in range(OWN):
                n.landed(
                    n.both(n.inside(first), n.place[second] != s),
                    self.land.at[f, n.clipped(first) * 2 + s, self.rows(p)], self.one_sem[f] + p * OWN + s,
                )
            n.spread(
                first, n.inside(first), self.land.at[f, pl.ds(n.clipped(first) * 2, 2), self.rows(p)],
                self.two_sem[f] + p * OWN + n.clipped(first),
            )

    def end(self):
        n = self.net
        for p in range(2):
            for f in range(2):
                first = self.axes[f][0]
                for s in range(OWN):
                    n.landed(
                        n.place[first] != s, self.land.at[f, pl.ds(s * 2, 2), self.rows(p)],
                        self.two_sem[f] + p * OWN + s,
                    )


class WideBack:
    def __init__(self, net, low, spot, pieces, rows):
        self.net, self.low, self.spot, self.pieces, self.rows = net, low, spot, pieces, rows
        self.axes = (("x", "y"), ("y", "x"))
        self.hop_sem = net.recv_sem(pieces)
        self.one_sem = net.recv_sem(pieces)
        self.two_sem = [net.recv_sem(OWN) for _ in range(pieces)]
        self.wide = net.both(net.inside("x"), net.inside("y"), net.x == net.y)
        self.owner, self.near, self.middle, self.far = wide_roles(net)

    def stands(self, position):
        return self.net.both(self.wide, self.net.z == position)

    def mine(self, p):
        return self.spot(self.net.clipped("x"), p)

    def start(self, p):
        n = self.net

        def keep():
            self.mine(p)[...] = self.low[pl.ds(p * self.rows, self.rows), :]

        owner = self.stands(self.owner)
        n.on(owner, keep)
        n.send(owner, self.mine(p), self.mine(p), self.hop_sem + p, n.at(z=self.middle))
        n.send(owner, self.mine(p), self.mine(p), self.hop_sem + p, n.at(z=self.near))

    def onward(self, p):
        n = self.net
        here = self.stands(self.middle)
        n.landed(here, self.mine(p), self.hop_sem + p)
        n.send(here, self.mine(p), self.mine(p), self.hop_sem + p, n.at(z=self.far))

    def one(self, p):
        n = self.net
        n.landed(self.stands(self.near), self.mine(p), self.hop_sem + p)
        n.landed(self.stands(self.far), self.mine(p), self.hop_sem + p)
        first, second = self.axes[p % 2]
        n.spread(second, self.wide, self.spot(n.clipped(first), p), self.one_sem + p)

    def two(self, p):
        n = self.net
        first, second = self.axes[p % 2]
        mine = self.spot(n.clipped(first), p)
        n.landed(n.both(n.inside(first), n.place[first] != n.place[second]), mine, self.one_sem + p)
        n.spread(first, n.inside(first), mine, self.two_sem[p] + n.clipped(first))

    def end(self):
        n = self.net
        for p in range(self.pieces):
            first = self.axes[p % 2][0]
            for m in range(OWN):
                n.landed(n.place[first] != m, self.spot(m, p), self.two_sem[p] + m)


class HeadBack:
    def __init__(self, net, low, land):
        self.net, self.low = net, low
        self.hop_sem, self.one_sem, self.two_sem = net.recv_sem(2), net.recv_sem(2), net.recv_sem(2)
        self.core_sem = net.recv_sem(1)
        self.axes = (("x", "y"), ("y", "x"))
        self.goal = {"x": HEAD_X, "y": HEAD_Y}
        self.spots = [
            land.at[pl.ds(pl.multiple_of(net.core * HROWS + p * HPART, HPART), HPART)] for p in range(2)
        ]
        self.mine = land.at[pl.ds(pl.multiple_of(net.core * HROWS, HROWS), HROWS)]
        self.theirs = land.at[pl.ds(pl.multiple_of((1 - net.core) * HROWS, HROWS), HROWS)]
        self.column = net.both(net.x == HEAD_X, net.y == HEAD_Y)

    def hop(self, k):
        n = self.net
        here = n.both(self.column, n.z == k)
        for p in range(2):
            if k == 0:

                def keep(p=p):
                    self.spots[p][...] = self.low[pl.ds(p * HPART, HPART), :]

                n.on(here, keep)
            else:
                n.landed(here, self.spots[p], self.hop_sem + p)
            if k < n.nz - 1:
                n.send(here, self.spots[p], self.spots[p], self.hop_sem + p, n.at(z=k + 1))

    def one(self):
        n = self.net
        for p in range(2):
            n.spread(self.axes[p][1], self.column, self.spots[p], self.one_sem + p)

    def two(self):
        n = self.net
        for p in range(2):
            first, second = self.axes[p]
            plane = n.place[first] == self.goal[first]
            n.landed(n.both(plane, n.place[second] != self.goal[second]), self.spots[p], self.one_sem + p)
            n.spread(first, plane, self.spots[p], self.two_sem + p)

    def three(self):
        n = self.net
        for p in range(2):
            first = self.axes[p][0]
            n.landed(n.place[first] != self.goal[first], self.spots[p], self.two_sem + p)
        n.send(True, self.mine, self.mine, self.core_sem, n.sibling)

    def end(self):
        self.net.landed(True, self.theirs, self.core_sem)


def muon_kernel(
    dims, gs_ref, wide_ref, headg_ref, na_ref, nf_ref, count_ref, dlow_ref, mi_ref, mo_ref, mu_ref, md_ref, mh_ref,
    ms_all, xs_all, mw_all, q_all, mh_all, xh_all, d_in, small_out,
    acc, first_in, second_in, band_in, wide_acc, wide_in, head_acc, head_in, small_buf,
    old_turned, old_plain, old_head, own, gram, gram_in, mats, m_low, x_low,
    ms_land, xs_land, mw_land, q_land, mh_land, xh_land,
    send_sems, recv_sems, local_sems,
):
    n = Net(dims, send_sems, recv_sems)
    nz = n.nz
    x, y, z, core = n.x, n.y, n.z, n.core
    on, both = n.on, n.both
    n.barrier()
    valid = both(n.inside("x"), n.inside("y"))
    wide = both(valid, x == y)
    wide_z, near_z, middle_z, far_z = wide_roles(n)
    wide_owner = both(wide, z == wide_z)
    square_z = square_owners(n)
    owns = [both(valid, z == square_z[f]) for f in range(2)]
    square = jnp.logical_or(owns[0], owns[1])
    task = jnp.where(
        z == square_z[0], n.clipped("x") * 2 + n.clipped("y"), 4 + n.clipped("y") * 2 + n.clipped("x")
    )
    head_column = both(x == HEAD_X, y == HEAD_Y)
    head_owner = both(head_column, z == HEAD_Z)
    axes = (("x", "y"), ("y", "x"))

    first_sem = [n.recv_sem(2 * (n.count[axes[f][0]] - 1)) for f in range(2)]
    second_sem = [n.recv_sem(2 * (n.count[axes[f][1]] - 1)) for f in range(2)]

    def half_rows(p):
        return pl.ds(p * 128, 128)

    for p in range(2):
        for f in range(2):
            axis = axes[f][0]
            for d in range(1, n.count[axis]):
                target = jnp.minimum(n.further(axis, d), OWN - 1)
                n.send(
                    n.goes_inside(axis, d), gs_ref.at[f, pl.ds(target * 2, 2), half_rows(p)],
                    first_in.at[f, d - 1, :, half_rows(p)], first_sem[f] + 2 * (d - 1) + p,
                    n.at(**{axis: n.further(axis, d)}),
                )
    own_copies = [
        pltpu.make_async_copy(gs_ref.at[f], acc.at[f], local_sems.at[f]) for f in range(2)
    ]
    for copy in own_copies:
        copy.start()

    def wide_load():
        return pltpu.make_async_copy(wide_ref, wide_acc, local_sems.at[4])

    def head_load():
        return pltpu.make_async_copy(headg_ref, head_acc, local_sems.at[5])

    def old_copies():
        sem = local_sems.at[6]
        return (
            (both(wide_owner, x == 0), lambda: pltpu.make_async_copy(mu_ref, old_turned, sem)),
            (both(wide_owner, x != 0), lambda: pltpu.make_async_copy(md_ref, old_plain, sem)),
            (
                both(square, task < 6),
                lambda: pltpu.make_async_copy(
                    mi_ref.at[jnp.minimum(task, 5)], old_turned.at[:, pl.ds(0, PIECE)], sem
                ),
            ),
            (
                both(square, task >= 6),
                lambda: pltpu.make_async_copy(
                    mo_ref.at[jnp.maximum(task, 6) - 6], old_plain.at[pl.ds(0, PIECE)], sem
                ),
            ),
            (head_owner, lambda: pltpu.make_async_copy(mh_ref, old_head, sem)),
        )

    on(wide, lambda: wide_load().start())
    on(head_column, lambda: head_load().start())
    for condition, copy in old_copies():
        on(condition, lambda copy=copy: copy().start())
    d_sem = n.recv_sem(1)
    n.send(core == 0, dlow_ref, d_in, d_sem, n.sibling)

    on(wide, lambda: wide_load().wait())
    near_sem, middle_sem, far_sem = n.recv_sem(4), n.recv_sem(4), n.recv_sem(4)

    def piece(k):
        return wide_acc.at[k // 2, pl.ds((k % 2) * PIECE, PIECE)]

    for k in range(4):
        n.send(both(wide, z == far_z), piece(k), wide_in.at[1, k], far_sem + k, n.at(z=middle_z))
        n.send(both(wide, z == near_z), piece(k), wide_in.at[0, k], near_sem + k, n.at(z=wide_z))

    def wide_pass(k):
        here = both(wide, z == middle_z)

        def take():
            n.landed(True, wide_in.at[1, k], far_sem + k)
            add_into(piece(k), [wide_in.at[1, k]], 128)

        on(here, take)
        n.send(here, piece(k), wide_in.at[1, k], middle_sem + k, n.at(z=wide_z))

    on(head_column, lambda: head_load().wait())
    head_sem = n.recv_sem(2)

    def head_pass(distance):
        here = both(head_column, z == distance)
        for p in range(2):
            if distance < nz - 1:

                def take(p=p):
                    n.landed(True, head_in.at[p], head_sem + p)
                    add_into(head_acc.at[p], [head_in.at[p]], HPART)

                on(here, take)
            n.send(here, head_acc.at[p], head_in.at[p], head_sem + p, n.at(z=distance - 1))

    head_pass(nz - 1)

    small_core = n.recv_sem(1)
    small_sem = {axis: n.recv_sem(n.count[axis]) for axis in ("x", "y", "z")}
    small_buf[0, 0] = jnp.zeros((SMALL, VOC), f32)
    small_buf[0, 0, 0:8, 0:D] = na_ref[...]
    small_buf[0, 0, 8:16, 0:D] = nf_ref[...]
    small_buf[0, 0, 16:24, :] = count_ref[...]
    n.send(True, small_buf.at[0, 0], small_buf.at[0, 1], small_core, n.sibling)

    def small_go(level, axis, value):
        small_buf[level, n.place[axis]] = value
        n.spread(axis, True, small_buf.at[level, n.place[axis]], small_sem[axis] + n.place[axis])

    def small_add(level, axis):
        for d in range(1, n.count[axis]):
            source = n.further(axis, d)
            n.landed(True, small_buf.at[level, source], small_sem[axis] + source)
        total = small_buf[level, 0]
        for s in range(1, n.count[axis]):
            total = total + small_buf[level, s]
        return total

    for copy in own_copies:
        copy.wait()
    n.landed(True, small_buf.at[0, 1], small_core)
    small_go(1, "x", small_buf[0, 0] + small_buf[0, 1])
    wide_pass(0)
    for p in range(2):
        for f in range(2):
            first, second = axes[f]
            mine = n.clipped(first) * 2

            def take(f=f, p=p, first=first, mine=mine):
                for d in range(1, n.count[first]):
                    n.landed(True, first_in.at[f, d - 1, :, half_rows(p)], first_sem[f] + 2 * (d - 1) + p)
                for j in range(2):
                    add_into(
                        acc.at[f, mine + j, half_rows(p)],
                        [first_in.at[f, d - 1, j, half_rows(p)] for d in range(1, n.count[first])], 128,
                    )

            on(n.inside(first), take)
            for d in range(1, n.count[second]):
                target = jnp.minimum(n.further(second, d), OWN - 1)
                n.send(
                    both(n.inside(first), n.goes_inside(second, d)), acc.at[f, mine + target, half_rows(p)],
                    second_in.at[f, d - 1, half_rows(p)], second_sem[f] + 2 * (d - 1) + p,
                    n.at(**{second: n.further(second, d)}),
                )
        wide_pass(1 + p)
        head_pass(2 - p)
    small_go(2, "y", small_add(1, "x"))

    def chunk(f):
        first, second = axes[f]
        return n.clipped(first) * 2 + n.clipped(second)

    band_sem = [n.recv_sem(2 * (nz - 1)) for _ in range(2)]
    for p in range(2):
        for f in range(2):
            second = axes[f][1]

            def take_second(f=f, p=p, second=second):
                for d in range(1, n.count[second]):
                    n.landed(True, second_in.at[f, d - 1, half_rows(p)], second_sem[f] + 2 * (d - 1) + p)
                add_into(
                    acc.at[f, chunk(f), half_rows(p)],
                    [second_in.at[f, d - 1, half_rows(p)] for d in range(1, n.count[second])], 128,
                )

            on(valid, take_second)
            for d in range(1, nz):
                n.send(
                    both(valid, z == lax.rem(square_z[f] + d, nz)), acc.at[f, chunk(f), half_rows(p)],
                    band_in.at[d - 1, half_rows(p)], band_sem[f] + 2 * (d - 1) + p, n.at(z=square_z[f]),
                )
    small_go(3, "z", small_add(2, "y"))
    wide_pass(3)

    own[...] = jnp.zeros_like(own)
    for condition, copy in old_copies():
        on(condition, lambda copy=copy: copy().wait())

    def turned(k):
        return jnp.swapaxes(old_turned[:, k * PIECE : (k + 1) * PIECE], 0, 1)

    back_ms = SquareBack(n, m_low, ms_land)
    back_mw = WideBack(
        n, m_low, lambda m, p: mw_land.at[m, p // 2, pl.ds((p % 2) * PIECE, PIECE)], 4, PIECE
    )
    back_mh = HeadBack(n, m_low, mh_land)
    back_xs = SquareBack(n, x_low, xs_land)
    back_q = WideBack(n, x_low, lambda m, p: q_land.at[m, core, p], 2, 128)
    back_xh = HeadBack(n, x_low, xh_land)

    def keep_moment(rows, value):
        own[rows, :] = value
        m_low[rows, :] = value.astype(bf16)

    def finish_wide(k, old):
        total = piece(k)[...].astype(f32) + wide_in[0, k].astype(f32) + wide_in[1, k].astype(f32)
        keep_moment(pl.ds(k * PIECE, PIECE), total + 0.5 * old)

    def wide_moment(k):
        n.landed(wide_owner, wide_in.at[0, k], near_sem + k)
        n.landed(wide_owner, wide_in.at[1, k], middle_sem + k)
        on(both(wide_owner, x == 0), lambda: finish_wide(k, turned(k)))
        on(both(wide_owner, x != 0), lambda: finish_wide(k, old_plain[pl.ds(k * PIECE, PIECE), :]))
        back_mw.start(k)

    def finish_square(p, old):
        f = jnp.where(owns[0], 0, 1)
        mine = jnp.where(owns[0], chunk(0), chunk(1))
        total = acc[f, mine, half_rows(p), :].astype(f32)
        for d in range(1, nz):
            total = total + band_in[d - 1, half_rows(p), :].astype(f32)
        keep_moment(half_rows(p), total + 0.5 * old)

    def square_moment(p):
        for f in range(2):
            for d in range(1, nz):
                n.landed(owns[f], band_in.at[d - 1, half_rows(p)], band_sem[f] + 2 * (d - 1) + p)
        on(
            both(square, task < 6),
            lambda: finish_square(p, jnp.swapaxes(old_turned[:, p * 128 : (p + 1) * 128], 0, 1)),
        )
        on(both(square, task >= 6), lambda: finish_square(p, old_plain[half_rows(p), :]))
        back_ms.start(p)

    def finish_head():
        old_plain[pl.ds(512, 128), :] = jnp.zeros((128, D), f32)
        old_plain[pl.ds(0, old_head.shape[0]), :] = old_head[...]
        for p in range(2):
            here = pl.ds(pl.multiple_of(core * HROWS + p * HPART, HPART), HPART)
            total = head_acc[p].astype(f32) + head_in[p].astype(f32)
            keep_moment(pl.ds(p * HPART, HPART), total + 0.5 * old_plain[here, :])

    wide_moment(0)
    for p in range(2):
        n.landed(head_owner, head_in.at[p], head_sem + p)
    on(head_owner, finish_head)
    back_mh.hop(0)
    square_moment(0)
    wide_moment(1)
    wide_moment(2)
    square_moment(1)
    wide_moment(3)

    blocks_used = jnp.where(wide_owner, 4, jnp.where(head_owner, 2, 1))
    gram[...] = jnp.zeros_like(gram)

    def gram_step(i, carry):
        high, low = split_two(own[pl.ds(pl.multiple_of(i * PIECE, PIECE), PIECE), :])
        gram[...] += mm_tn(high, high) + (mm_tn(high, low) + mm_tn(low, high))
        return carry

    lax.fori_loop(0, blocks_used, gram_step, 0)
    gram_sem = n.recv_sem(1)
    n.send(True, gram, gram_in, gram_sem, n.sibling)
    small_out[...] = small_add(3, "z")
    n.landed(True, gram_in, gram_sem)

    def eye_rows(first, rows):
        place = lax.broadcasted_iota(jnp.int32, (rows, D), 0) + first
        return (place == lax.broadcasted_iota(jnp.int32, (rows, D), 1)).astype(f32)

    def put(m, value):
        high, low = split_two(value)
        mats[m, 0] = high
        mats[m, 1] = low

    def product(a, b):
        ah, al = mats[a, 0], mats[a, 1]
        left_h, left_l = mats[b, 0, :, 0:256], mats[b, 1, :, 0:256]
        left = mm(ah, left_h) + (mm(ah, left_l) + mm(al, left_h))
        right_h, right_l = mats[b, 0, :, 256:512], mats[b, 1, :, 256:512]
        corner = mm(ah[256:], right_h) + (mm(ah[256:], right_l) + mm(al[256:], right_h))
        right = jnp.concatenate([jnp.swapaxes(left[256:], 0, 1), corner], axis=0)
        return jnp.concatenate([left, right], axis=1)

    busy = jnp.logical_or(square, jnp.logical_or(wide_owner, head_owner))
    total = jnp.sum(
        jnp.sum((gram[...] + gram_in[...]) * eye_rows(0, D), axis=0, keepdims=True), axis=1, keepdims=True
    )
    scale = 1.0 / (jnp.sqrt(total) + 1e-07)

    def newton_schulz(iteration):
        q_now, q_next = (2, 4) if iteration % 2 == 0 else (4, 2)
        if iteration == 0:
            put(0, (gram[...] + gram_in[...]) * scale * scale)

            def begin_rows():
                own[pl.ds(0, PIECE), :] = own[pl.ds(0, PIECE), :] * scale

            on(square, begin_rows)
        a = mats[0, 0].astype(f32) + mats[0, 1].astype(f32)
        put(1, NS_A * eye_rows(0, D) + NS_B * a + NS_C * product(0, 0))

        def update_rows():
            high, low = split_two(own[pl.ds(0, PIECE), :])
            ph, pll = mats[1, 0], mats[1, 1]
            own[pl.ds(0, PIECE), :] = mm(high, ph) + (mm(high, pll) + mm(low, ph))

        def update_q():
            if iteration == 0:
                mats[q_next] = mats[1]
            else:
                put(q_next, product(1, q_now))

        on(square, update_rows)
        on(jnp.logical_not(square), update_q)
        if iteration < NS_STEPS - 1:
            put(3, product(0, 1))
            put(0, product(3, 1))

    for iteration in range(NS_STEPS):
        on(busy, partial(newton_schulz, iteration))
        if iteration == 0:
            back_ms.one(0)
            back_mh.hop(1)
        if iteration == 1:
            back_ms.one(1)
            back_mw.onward(0)
            back_mw.onward(1)
            back_mh.hop(2)
        if iteration == 2:
            back_ms.two(0)
            back_mw.onward(2)
            back_mw.one(0)
            back_mh.hop(3)
        if iteration == 3:
            back_ms.two(1)
            back_mw.onward(3)
            back_mw.one(1)
            back_mh.one()

    last = 4 if NS_STEPS % 2 == 1 else 2

    def direction():
        part = pl.ds(0, 512)
        high, low = split_two(own[part, :] * scale)
        value = mm(high, mats[last, 0]) + (mm(high, mats[last, 1]) + mm(low, mats[last, 0]))
        x_low[part, :] = value.astype(bf16)

    def wide_polynomial():
        rows = pl.ds(pl.multiple_of(core * PIECE, PIECE), PIECE)
        value = mats[last, 0, rows, :].astype(f32) + mats[last, 1, rows, :].astype(f32)
        x_low[pl.ds(0, PIECE), :] = (value * scale).astype(bf16)

    on(wide_owner, wide_polynomial)
    on(head_owner, direction)

    def keep_rows():
        x_low[pl.ds(0, PIECE), :] = own[pl.ds(0, PIECE), :].astype(bf16)

    on(square, keep_rows)
    back_xs.start(0)
    back_xs.start(1)
    back_q.start(0)
    back_q.start(1)
    back_xh.hop(0)
    back_mw.one(2)
    back_mw.two(0)
    back_mh.two()
    back_q.onward(0)
    back_q.onward(1)
    back_xh.hop(1)
    outs = [
        pltpu.make_async_copy(src, dst, local_sems.at[i])
        for i, (src, dst) in enumerate(
            (
                (ms_land, ms_all), (mh_land, mh_all), (mw_land, mw_all), (xs_land, xs_all), (q_land, q_all),
                (xh_land, xh_all),
            )
        )
    ]
    back_xs.one(0)
    back_xh.hop(2)
    back_mw.one(3)
    back_mw.two(1)
    back_xs.one(1)
    back_q.one(0)
    back_q.one(1)
    back_xs.two(0)
    back_xh.hop(3)
    back_xh.one()
    back_mw.two(2)
    back_xs.two(1)
    back_q.two(0)
    back_q.two(1)
    back_mw.two(3)
    back_xh.two()
    back_mh.three()
    back_ms.end()
    outs[0].start()
    back_mh.end()
    outs[1].start()
    back_mw.end()
    outs[2].start()
    back_q.end()
    q_sem = n.recv_sem(2)
    for m in range(2):
        n.send(True, q_land.at[m, core], q_land.at[m, core], q_sem + m, n.sibling)
    back_xh.three()
    back_xs.end()
    outs[3].start()
    for m in range(2):
        n.landed(True, q_land.at[m, 1 - core], q_sem + m)
    outs[4].start()
    back_xh.end()
    outs[5].start()
    n.landed(core == 1, d_in, d_sem)
    n.all_sent()
    for copy in outs:
        copy.wait()


def run_muon(dims, gs, wide, headg, na, nf, count, dlow, mi, mo, mu, md, mh):
    nz, ny, nx = dims
    hbm = pl.BlockSpec(memory_space=pl.ANY)
    vmem = pl.BlockSpec(memory_space=VMEM)
    slots = max(nx, ny) - 1
    most = max(nx, ny, nz, 2)
    squares = (2, 4, PIECE, D)
    lands = [squares, squares, (2, 2, 512, D), (2, 2, 2, 128, D), (VOC, D), (VOC, D)]
    return pl.pallas_call(
        partial(muon_kernel, dims),
        in_specs=[hbm] * 3 + [vmem] * 3 + [hbm] * 6,
        out_specs=[hbm] * 7 + [vmem],
        out_shape=[sds(s, bf16) for s in lands] + [sds((512, D), bf16), sds((SMALL, VOC), f32)],
        scratch_shapes=[
            VMEM(squares, bf16),
            VMEM((2, slots, 2, PIECE, D), bf16),
            VMEM((2, slots, PIECE, D), bf16),
            VMEM((nz - 1, PIECE, D), bf16),
            VMEM((2, 512, D), bf16),
            VMEM((2, 4, PIECE, D), bf16),
            VMEM((2, HPART, D), bf16),
            VMEM((2, HPART, D), bf16),
            VMEM((4, most, SMALL, VOC), f32),
            VMEM((D, 1024), f32),
            VMEM((1024, D), f32),
            VMEM(mh.shape, f32),
            VMEM((1024, D), f32),
            VMEM((D, D), f32),
            VMEM((D, D), f32),
            VMEM((5, 2, D, D), bf16),
            VMEM((1024, D), bf16),
            VMEM((512, D), bf16),
        ]
        + [VMEM(s, bf16) for s in lands]
        + [
            pltpu.SemaphoreType.DMA((400,)), pltpu.SemaphoreType.DMA((160,)), pltpu.SemaphoreType.DMA((8,)),
        ],
        compiler_params=pltpu.CompilerParams(
            vmem_limit_bytes=60 * MIB, collective_id=0, has_side_effects=True
        ),
        cost_estimate=pl.CostEstimate(flops=20 * 10**9, bytes_accessed=40 * MIB, transcendentals=0),
        name="reduce_muon_spread",
    )(gs, wide, headg, na, nf, count, dlow, mi, mo, mu, md, mh)


def finish_kernel(
    wide_rate, head_rate, core_ref,
    mu, md, mb, q_ref, xb, mh, xh, ai, ao, fi, fo, vh, small, gain, bias, nm, dm, dr,
    mi_out, ni_out, mo_out, no_out, mu_out, nu_out, md_out, nd_out, mh_out, nh_out,
    mn_out, nn_out, counts_out, dm_out,
):
    i = pl.program_id(0)
    same = lax.broadcasted_iota(jnp.int32, (D, D), 0) == lax.broadcasted_iota(jnp.int32, (D, D), 1)
    eye = same.astype(f32).astype(bf16)
    mu_out[...] = mm_nt(eye, mu[0, 0])
    nu_out[...] = fi[...] - wide_rate * mm_nt(q_ref[0], mu[0, 0])
    md_out[...] = md[0, 0].astype(f32)
    nd_out[...] = fo[...] - wide_rate * mm(md[0, 0], q_ref[1])

    @pl.when(i < 3)
    def _():
        for j in range(2):
            mi_out[j] = mm_nt(eye, mb[0, j])
            ni_out[j] = ai[j] - muon_rate * mm_nt(eye, xb[0, j])

    @pl.when(i == 3)
    def _():
        for j in range(2):
            mo_out[j] = mb[0, j].astype(f32)
            no_out[j] = ao[j] - muon_rate * xb[0, j].astype(f32)

    dm_out[...] = jnp.where((core_ref[0] == 0) | (i >= 2), dm[...], dr[...].astype(f32))

    @pl.when(i == 0)
    def _():
        vocab = vh.shape[0]
        mh_out[...] = mh[0:vocab, :].astype(f32)
        nh_out[...] = vh[...] - head_rate * xh[0:vocab, :].astype(f32)
        for kind, old in enumerate((gain, bias)):
            first = 2 * kind
            total = jnp.concatenate([small[first : first + 2, 0:D], small[first + 8 : first + 10, 0:D]], axis=0)
            moment = 0.5 * nm[kind] + total
            mn_out[kind] = moment
            nn_out[kind] = old[...] - vector_rate * moment * lax.rsqrt(
                jnp.mean(moment * moment, axis=-1, keepdims=True) + 1e-06
            )
        counts_out[...] = small[16:17, 0:vocab].astype(jnp.int32)


def run_finish(core, ms, xs, mw, q, m_head, x_head, ai, ao, fi, fo, vh, small, gain, bias, nm, dmem, d_in):
    vocab = vh.shape[0]
    wide_rate = muon_rate * math.sqrt(2 * fi.shape[1] / D)
    head_rate = muon_rate * math.sqrt(vocab / D)

    def spec(shape, index):
        return pl.BlockSpec(shape, index)

    def fixed(shape):
        return pl.BlockSpec(shape, lambda i, c: (0,) * len(shape))

    up = spec((1, 1, 256, D), lambda i, c: (0, i // 2, i % 2, 0))
    down = spec((1, 1, 256, D), lambda i, c: (1, i // 2, i % 2, 0))
    bands = spec((1, 2, 256, D), lambda i, c: (i // 2, i % 2, 0, 0))
    inner = spec((2, D, 256), lambda i, c: (jnp.minimum(i, 2), 0, 0))
    outer = spec((2, 256, D), lambda i, c: (0, 0, 0))
    cols = spec((D, 256), lambda i, c: (0, i))
    rows = spec((256, D), lambda i, c: (i, 0))
    head = fixed((vocab, D))
    shapes = [
        (sds((6, D, 256), f32), inner), (sds((6, D, 256), f32), inner),
        (sds((2, 256, D), f32), outer), (sds((2, 256, D), f32), outer),
        (sds(fi.shape, f32), cols), (sds(fi.shape, f32), cols),
        (sds(fo.shape, f32), rows), (sds(fo.shape, f32), rows),
        (sds((vocab, D), f32), head), (sds((vocab, D), f32), head),
        (sds((2, 4, D), f32), fixed((2, 4, D))), (sds((2, 4, D), f32), fixed((2, 4, D))),
        (sds((1, vocab), jnp.int32), fixed((1, vocab))),
        (sds((1024, D), f32), rows),
    ]
    return pl.pallas_call(
        partial(finish_kernel, wide_rate, head_rate),
        grid_spec=pltpu.PrefetchScalarGridSpec(
            num_scalar_prefetch=1,
            grid=(4,),
            in_specs=[
                up, down, bands, fixed((2, D, D)), bands, fixed((VOC, D)), fixed((VOC, D)),
                inner, outer, cols, rows, head, fixed((SMALL, VOC)), fixed((4, D)), fixed((4, D)), fixed((2, 4, D)),
                spec((256, D), lambda i, c: (jnp.where(c[0] == 0, i, jnp.maximum(i - 2, 0)), 0)),
                spec((256, D), lambda i, c: (jnp.minimum(i, 1), 0)),
            ],
            out_specs=[s[1] for s in shapes],
        ),
        out_shape=[s[0] for s in shapes],
        compiler_params=pltpu.CompilerParams(vmem_limit_bytes=60 * MIB),
        cost_estimate=pl.CostEstimate(flops=10**7, bytes_accessed=40 * MIB, transcendentals=0),
        name="finish_weights",
    )(core, mw, mw, ms, q.reshape(2, D, D), xs, m_head, x_head, ai, ao, fi, fo, vh, small,
      gain, bias, nm, dmem, d_in)


def local(
    residual_in, memory, lengths, targets, attn_in, attn_out, ffn_in, ffn_out, vocab_head,
    norm_gain, norm_bias, attn_in_moment, attn_out_moment, ffn_in_moment, ffn_out_moment,
    head_moment, norm_moment,
):
    dims = chip_dims(lax.axis_size("dp"))
    core = lax.axis_index("mp")
    tokens = residual_in.shape[0] * lax.axis_size("mp") * lax.axis_size("dp")
    vocab = vocab_head.shape[1]
    inner = attn_in.reshape(6, D, 256)
    wa0, wa1, wo0, wo1, wi0, wi1, wf0, wf1, mem, wh, total = run_prepare(
        dims, lengths, inner, attn_out, ffn_in, ffn_out, vocab_head.T, memory
    )
    wa, wo, wi, wf = (wa0, wa1), (wo0, wo1), (wi0, wi1), (wf0, wf1)
    h1, qkv, p, o, x1, h2, cq, kv, pc, oc, x2 = run_forward(
        lengths, residual_in, mem, wa, wo, norm_gain, norm_bias
    )
    out, g2, gw, ghead, gnorm_ffn, counts = run_middle(
        lengths, total, x2, targets[:, None], wi, wf, wh, norm_gain, norm_bias, vocab, float(tokens)
    )
    dx, dmem, dlow, gs, gnorm_attn, wide, head_part = run_backward(
        dims, g2, residual_in, x1, h1, qkv, p, o, h2, cq, kv, pc, oc, mem, wa, wo, norm_gain, gw, ghead
    )
    ms, xs, mw, q, head_m, head_x, d_in, small = run_muon(
        dims, gs, wide, head_part, gnorm_attn, gnorm_ffn, counts, dlow,
        attn_in_moment.reshape(6, D, 256), attn_out_moment, ffn_in_moment, ffn_out_moment, head_moment.T,
    )
    (
        moment_in, new_in, moment_out, new_out, moment_up, new_up, moment_down, new_down,
        moment_head, new_head, moment_norms, new_norms, token_counts, memory_grad,
    ) = run_finish(
        core.reshape(1), ms, xs, mw, q, head_m, head_x, inner, attn_out, ffn_in, ffn_out,
        vocab_head.T, small, norm_gain, norm_bias, norm_moment, dmem, d_in,
    )
    return (
        out, dx, memory_grad, moment_in.reshape(attn_in.shape), new_in.reshape(attn_in.shape),
        moment_out, new_out, moment_up, new_up, moment_down, new_down, moment_head.T, new_head.T,
        moment_norms, new_norms,
        token_counts.reshape(vocab),
    )


def solution(mesh):
    rows = P(("dp", "mp"), None)
    placed = (
        rows, rows, P("dp"), P(("dp", "mp")),
        P(None, None, None, "mp"), P(None, "mp", None), P(None, "mp"), P("mp", None), P(), P(), P(),
        P(None, None, None, "mp"), P(None, "mp", None), P(None, "mp"), P("mp", None), P(), P(),
    )
    return jax.shard_map(
        local,
        mesh=mesh,
        in_specs=placed,
        out_specs=(
            rows, rows, rows,
            P(None, None, None, "mp"), P(None, None, None, "mp"),
            P(None, "mp", None), P(None, "mp", None),
            P(None, "mp"), P(None, "mp"), P("mp", None), P("mp", None),
            P(), P(), P(), P(), P(),
        ),
        check_vma=False,
    )
```
